32 devices in a mesh: expert: 2 (over y), context: 4 (over x, core), dp: 4 (over z).
Axes of the slice: x: 2, y: 2, z: 4, core: 2. Of those that a mesh axis runs over, the one named last changes fastest.
Arguments:
- inputs: bfloat16 [8, 3072, 1536], P(('expert', 'dp'), 'context'), may hold values from -6 to 6
- cotangent: bfloat16 [8, 3072, 1536], P(('expert', 'dp'), 'context'), may hold values from -6 to 6
- routes: int32 [8, 3072, 4], P(('expert', 'dp'), 'context'), may hold values from 0 to 31, all different within a row; in each aligned block of 768 rows (0 to 767, 768 to 1535, ..., all dimensions but the last counted through in order) at most 103 rows name the same one
- attn_q: float32 [1536, 1536], P('dp'), may hold values from -0.15625 to 0.15625
- attn_k: float32 [1536, 256], P('dp'), may hold values from -0.15625 to 0.15625
- attn_v: float32 [1536, 256], P('dp'), may hold values from -0.15625 to 0.15625
- attn_o: float32 [1536, 1536], P('dp'), may hold values from -0.625 to 0.625
- norm_attn: float32 [1536], P('dp'), may hold values from 0.5 to 1.5
- norm_moe: float32 [1536], P('dp'), may hold values from 0.5 to 1.5
- router: float32 [1536, 32], P('dp'), may hold values from -0.109375 to 0.109375
- expert_gate: float32 [1536, 32, 768], P('dp', 'expert'), may hold values from -0.15625 to 0.15625
- expert_up: float32 [1536, 32, 768], P('dp', 'expert'), may hold values from -0.15625 to 0.15625
- expert_down: float32 [768, 32, 1536], P('dp', 'expert'), may hold values from -0.4375 to 0.4375
Outputs:
- output: bfloat16 [8, 3072, 1536], P(('expert', 'dp'), 'context')
- grad_inputs: bfloat16 [8, 3072, 1536], P(('expert', 'dp'), 'context')
- grad_attn_q: float32 [1536, 1536], P('dp')
- grad_attn_k: float32 [1536, 256], P('dp')
- grad_attn_v: float32 [1536, 256], P('dp')
- grad_attn_o: float32 [1536, 1536], P('dp')
- grad_norm_attn: float32 [1536], P('dp')
- grad_norm_moe: float32 [1536], P('dp')
- grad_router: float32 [1536, 32], P('dp')
- grad_expert_gate: float32 [1536, 32, 768], P('dp', 'expert')
- grad_expert_up: float32 [1536, 32, 768], P('dp', 'expert')
- grad_expert_down: float32 [768, 32, 1536], P('dp', 'expert')
The draws below stay inside these ranges and needn't reach their ends.
Inputs may be any that keep to these rules, and one draw needn't show every extreme that they name: `routes`: each row names 4 different experts. In the 768 rows of one block no expert is named more than 103 times, a bound that some block reaches.
All inputs are finite; a program needn't handle non-finite values.
Results may differ from the reference program's by a relative error of at most 0.02.
Values may be sent and summed in bfloat16 or wider, within the bound.
A program may use at most 576 MiB of HBM per device.

```python
import math
import jax
import jax.numpy as jnp
import numpy as np
from jax import lax

D = 1536
HEADS = 12
KVH = 2
HD = 128
FF = 768
EXPERTS = 32
TOP = 4
PBLK = 256
CONT = 512
TOK_DEV = 768
PROMPT = 1024
SPAN = 3072
GROUPS = 8
CAP = 103
N_CONTEXT = 4


def steps_of(stream_key, dims, cuts, least, top_value):
    level, own = 1.0, jax.random.fold_in(stream_key, 6)
    for dim, shards_of in cuts:
        steps = jnp.exp(jax.random.uniform(jax.random.fold_in(own, dim), (shards_of,), jnp.float32, least / len(cuts), top_value / len(cuts)))
        level = level * jnp.repeat(steps, dims[dim] // shards_of).reshape([-1 if axis == dim else 1 for axis in range(len(dims))])
    return level


def deal_out(rng, own, number, rows, number_of, top, most, slope):
    sequence = jax.random.permutation(rng, number_of)
    packed, common = portions_of(number_of, rows * top, most, slope, True), portions_of(number_of, rows * top, most, slope, False)
    places = jnp.arange(number_of)

    def named(sizes, offset_by):
        used = int((sizes > 0).sum())
        fixed = max(1, used // 4)
        passed = fixed + (places - fixed + offset_by * (used - fixed)) % max(1, number_of - fixed)
        return jnp.zeros((number_of,), jnp.int32).at[sequence[jnp.where(places < fixed, places, passed)]].set(jnp.asarray(sizes, jnp.int32))

    sizes = jnp.where(number % 4 == 0, named(packed, number // 4), named(common, number - number // 4 - 1))
    mixed = jax.random.permutation(jax.random.fold_in(own, 3), number_of)
    giver, sink = mixed[0:number_of // 2 * 2:2], mixed[1:number_of // 2 * 2:2]
    room = jnp.minimum(sizes[giver] - 1, most - sizes[sink]) // 2
    room = jnp.where((giver == sequence[0]) | (sink == sequence[0]) | (sizes[sink] == 0), 0, jnp.maximum(room, 0))
    passed = jax.random.randint(jax.random.fold_in(own, 4), (number_of // 2,), 0, 1 << 20) % (room + 1)
    sizes = sizes.at[giver].add(-passed).at[sink].add(passed)
    members = jnp.searchsorted(jnp.cumsum(sizes), jnp.arange(rows * top), side="right").astype(jnp.int32)
    listing = members.reshape(top, rows).T
    listing = listing[jax.random.permutation(jax.random.fold_in(own, 1), rows)]
    offset_by = jax.random.randint(jax.random.fold_in(own, 2), (rows, 1), 0, top)
    return jnp.take_along_axis(listing, (jnp.arange(top)[None, :] + offset_by) % top, axis=1)


def portions_of(count, total, most, skew, full):
    loads = [(1 << 20) // math.isqrt(grade ** skew) + 1 for grade in range(1, count + 1)]
    largest = most if full else min(most, max(-(-total // count), total * loads[0] // sum(loads)))
    least = 1 if total - largest >= count - 1 else 0
    given, surplus = [largest] + [least] * (count - 1), total - largest - least * (count - 1)
    while surplus > 0:
        candidates = [i for i in range(1, count) if given[i] < largest] or [i for i in range(1, count) if given[i] < most]
        mass, left = sum([loads[i] for i in candidates]), surplus
        for i in candidates:
            addition = min(most - given[i], max(1, left * loads[i] // mass), surplus)
            given[i] = given[i] + addition
            surplus = surplus - addition
    return np.array(given)


def scatter_about(key, extent, deviation, reach, shards=(), kind=jnp.bfloat16):
    array = deviation * jax.random.normal(key, extent, jnp.float32)
    if shards:
        array = array * steps_of(key, extent, shards, -0.22, 0.18)
    return jnp.clip(array, -reach, reach).astype(kind)


def setup_inputs(seed: int = 0) -> dict:
    splits = jax.random.split(jax.random.key(seed), 14)
    inputs = scatter_about(splits[0], (GROUPS, SPAN, D), 1.0, 6.0, ((0, 8), (1, 4)))
    cotangent = scatter_about(splits[1], (GROUPS, SPAN, D), 1.0, 6.0, ((0, 8), (1, 4)))
    routes_keys = jax.random.split(jax.random.fold_in(splits[2], 1), GROUPS * SPAN // TOK_DEV)
    routes_turns = jax.random.permutation(jax.random.fold_in(splits[2], 3), GROUPS * SPAN // TOK_DEV)
    routes = jax.vmap(lambda own, number: deal_out(jax.random.fold_in(splits[2], 2), own, number, TOK_DEV, EXPERTS, TOP, CAP, 1))(routes_keys, routes_turns).reshape((GROUPS, SPAN, TOP))
    attn_q = scatter_about(splits[3], (D, D), D ** -0.5, 0.15625, ((0, 4),), jnp.float32)
    attn_k = scatter_about(splits[4], (D, KVH * HD), D ** -0.5, 0.15625, ((0, 4),), jnp.float32)
    attn_v = scatter_about(splits[5], (D, KVH * HD), D ** -0.5, 0.15625, ((0, 4),), jnp.float32)
    attn_o = scatter_about(splits[6], (D, D), (D // 16) ** -0.5, 0.625, ((0, 4),), jnp.float32)
    norm_attn = jnp.clip(1.0 + 0.1 * jax.random.normal(splits[7], (D,), jnp.float32), 0.5, 1.5)
    norm_moe = jnp.clip(1.0 + 0.1 * jax.random.normal(splits[8], (D,), jnp.float32), 0.5, 1.5)
    router = scatter_about(splits[9], (D, EXPERTS), (2 * D) ** -0.5, 0.109375, ((0, 4),), jnp.float32)
    expert_gate = scatter_about(splits[10], (D, EXPERTS, FF), D ** -0.5, 0.15625, ((0, 4), (1, 2)), jnp.float32)
    expert_up = scatter_about(splits[11], (D, EXPERTS, FF), D ** -0.5, 0.15625, ((0, 4), (1, 2)), jnp.float32)
    expert_down = scatter_about(splits[12], (FF, EXPERTS, D), (FF // 4) ** -0.5, 0.4375, ((0, 4), (1, 2)), jnp.float32)
    return {"inputs": inputs, "cotangent": cotangent, "routes": routes, "attn_q": attn_q, "attn_k": attn_k, "attn_v": attn_v, "attn_o": attn_o, "norm_attn": norm_attn, "norm_moe": norm_moe, "router": router, "expert_gate": expert_gate, "expert_up": expert_up, "expert_down": expert_down}


@jax.custom_vjp
def low(v):
    return lax.optimization_barrier(v.astype(jnp.bfloat16)).astype(jnp.float32)

@jax.custom_vjp
def low_back(v):
    return v

def low_keep(v):
    return (low(v), None)

def low_pass(kept, grad):
    return (grad,)

def back_keep(v):
    return (v, None)

def back_low(kept, grad):
    return (low(grad),)
low.defvjp(low_keep, low_pass)
low_back.defvjp(back_keep, back_low)
epsilon = 1e-06
rope_base = 1000000.0
masked_score = -1e+30
highest = lax.Precision.HIGHEST

def rms_scale(values, gain):
    return values * lax.rsqrt(lax.optimization_barrier(jnp.mean(values * values, axis=-1, keepdims=True)) + epsilon) * gain

def angle_table(positions):
    steps_half = jnp.arange(HD // 2, dtype=jnp.float32)
    inverse = jnp.exp(steps_half * (-2.0 * math.log(rope_base) / HD))
    return positions.astype(jnp.float32)[..., None] * inverse

def rotary(values, angles, direction):
    halfway = values.shape[-1] // 2
    cosine = jnp.cos(angles)[..., None, :]
    sine_part = direction * jnp.sin(angles)[..., None, :]
    leading = values[..., :halfway]
    trailing = values[..., halfway:]
    return jnp.concatenate([leading * cosine - trailing * sine_part, trailing * cosine + leading * sine_part], axis=-1)

def visible(query_pos, key_pos, prompt_len):
    query_cont = jnp.arange(query_pos.shape[0]) >= PBLK
    key_prompt = jnp.arange(key_pos.shape[0]) < prompt_len
    return (key_pos[None, :] <= query_pos[:, None]) & (key_prompt[None, :] | query_cont[:, None])

def gating(logit_rows, route_rows):
    picker = (route_rows[:, :, None] == jnp.arange(EXPERTS, dtype=jnp.int32)[None, None, :]).astype(logit_rows.dtype)
    chosen = lax.optimization_barrier(jnp.sum(picker * logit_rows[:, None, :], axis=-1))
    return jax.nn.softmax(chosen, axis=-1)

def gated(gate_pre, up_pre):
    return jax.nn.silu(gate_pre) * up_pre

def expert_slots(flat_experts):
    picker = (flat_experts[:, None] == jnp.arange(EXPERTS, dtype=jnp.int32)[None, :]).astype(jnp.int32)
    earlier = (jnp.cumsum(picker, axis=0) - picker).astype(jnp.int32)
    return lax.optimization_barrier(jnp.sum(earlier * picker, axis=1)).astype(jnp.int32)

def slot_sources(destination):
    assignments = TOK_DEV * TOP
    empty_table = jnp.full((EXPERTS * CAP,), assignments, dtype=jnp.int32)
    return empty_table.at[destination].set(jnp.arange(assignments, dtype=jnp.int32))

def group_layer(lowered, x_group, route_group):
    w_query, w_key, w_value, w_out, gain_one, gain_two, w_router, w_gate, w_up, w_down = lowered
    group_width = HEADS // KVH
    score_scale = 1.0 / math.sqrt(HD)
    normed_one = low(rms_scale(x_group, gain_one))
    q_proj = low_back(jnp.dot(normed_one, w_query, precision=highest))
    k_proj = low_back(jnp.dot(normed_one, w_key, precision=highest))
    v_proj = low_back(jnp.dot(normed_one, w_value, precision=highest))
    block_ids = jnp.arange(N_CONTEXT, dtype=jnp.int32)[:, None]
    prompt_part = block_ids * PBLK + jnp.arange(PBLK, dtype=jnp.int32)[None, :]
    cont_part = jnp.broadcast_to(PROMPT + jnp.arange(CONT, dtype=jnp.int32)[None, :], (N_CONTEXT, CONT))
    block_pos = jnp.concatenate([prompt_part, cont_part], axis=1)
    angles = angle_table(block_pos)
    queries = low(rotary(q_proj.reshape(N_CONTEXT, TOK_DEV, HEADS, HD), angles, 1.0) * score_scale)
    queries = queries.reshape(N_CONTEXT, TOK_DEV, KVH, group_width, HD)
    keys_rot = low(rotary(k_proj.reshape(N_CONTEXT, TOK_DEV, KVH, HD), angles, 1.0))
    values_low = low(v_proj).reshape(N_CONTEXT, TOK_DEV, KVH, HD)
    prompt_keys = keys_rot[:, :PBLK].reshape(PROMPT, KVH, HD)
    prompt_values = values_low[:, :PBLK].reshape(PROMPT, KVH, HD)
    key_pos = jnp.concatenate([jnp.arange(PROMPT, dtype=jnp.int32), PROMPT + jnp.arange(CONT, dtype=jnp.int32)])

    def attend_block(pieces):
        query_block, key_tail, value_tail, query_pos = pieces
        all_keys = jnp.concatenate([prompt_keys, key_tail], axis=0)
        all_values = jnp.concatenate([prompt_values, value_tail], axis=0)
        allowed = visible(query_pos, key_pos, PROMPT)
        scores = low_back(jnp.einsum('tign,kin->igtk', query_block, all_keys, precision=highest))
        scores = jnp.where(allowed[None, None], scores, masked_score)
        attn_probs = low(jax.nn.softmax(scores, axis=-1))
        return jnp.einsum('igtk,kin->tign', attn_probs, all_values, precision=highest)
    attended = lax.map(jax.checkpoint(attend_block), (queries, keys_rot[:, PBLK:], values_low[:, PBLK:], block_pos))
    attended_low = low(low_back(attended.reshape(SPAN, D)))
    mid_rows = x_group + low_back(jnp.dot(attended_low, w_out, precision=highest))
    normed_two = low(rms_scale(mid_rows, gain_two))
    logits = low_back(jnp.dot(normed_two, w_router, precision=highest))
    gate_weights = gating(logits, route_group)
    flat_experts = route_group.reshape(N_CONTEXT, TOK_DEV * TOP)
    slot_rank = jax.vmap(expert_slots)(flat_experts)
    destination = (flat_experts * CAP + slot_rank).astype(jnp.int32)
    source = jax.vmap(slot_sources)(destination)
    filled = source < TOK_DEV * TOP
    source_token = jnp.minimum(source, TOK_DEV * TOP - 1) // TOP
    block_rows = normed_two.reshape(N_CONTEXT, TOK_DEV, D)
    buffer_rows = low_back(jnp.where(filled[..., None], block_rows[block_ids, source_token], 0.0))
    buffer_rows = buffer_rows.reshape(N_CONTEXT, EXPERTS, CAP, D)
    gate_pre = low_back(jnp.einsum('cerd,def->cerf', buffer_rows, w_gate, precision=highest))
    up_pre = low_back(jnp.einsum('cerd,def->cerf', buffer_rows, w_up, precision=highest))
    activation = low(gated(gate_pre, up_pre))
    expert_rows = low(low_back(jnp.einsum('cerf,fed->cerd', activation, w_down, precision=highest)))
    expert_rows = expert_rows.reshape(N_CONTEXT, EXPERTS * CAP, D)
    picked = expert_rows[block_ids, destination].reshape(SPAN, TOP, D)
    return mid_rows + lax.optimization_barrier(jnp.sum(gate_weights[:, :, None] * picked, axis=1))

def reference(inputs, cotangent, routes, attn_q, attn_k, attn_v, attn_o, norm_attn, norm_moe, router, expert_gate, expert_up, expert_down):
    masters = (attn_q, attn_k, attn_v, attn_o, norm_attn, norm_moe, router, expert_gate, expert_up, expert_down)

    def forward(x_all, weights):
        lowered = tuple((low(master) for master in weights))

        def run_group(pieces):
            return jax.checkpoint(group_layer)(lowered, pieces[0], pieces[1])
        return lax.map(run_group, (x_all, routes))
    outputs, pullback = jax.vjp(forward, inputs.astype(jnp.float32), masters)
    grad_x, grad_masters = pullback(cotangent.astype(jnp.float32))
    return (outputs.astype(jnp.bfloat16), grad_x.astype(jnp.bfloat16), grad_masters[0], grad_masters[1], grad_masters[2], grad_masters[3], grad_masters[4], grad_masters[5], grad_masters[6], grad_masters[7], grad_masters[8], grad_masters[9])
```

```python
import functools
import math

import jax
import jax.numpy as jnp
from jax import lax
from jax.experimental import pallas as pl
from jax.experimental.pallas import tpu as pltpu
from jax.sharding import PartitionSpec as P

D = 1536
HEADS = 12
KVH = 2
HD = 128
EXPERTS = 32
TOP = 4
PBLK = 256
CONT = 512
CAP = 103


epsilon = 1e-06
rope_base = 1000000.0
masked_score = -1e30


def rms_scale(values, gain):
    return values * lax.rsqrt(jnp.mean(values * values, axis=-1, keepdims=True) + epsilon) * gain


def angle_table(positions):
    steps_half = jnp.arange(HD // 2, dtype=jnp.float32)
    inverse = jnp.exp(steps_half * (-2.0 * math.log(rope_base) / HD))
    return positions.astype(jnp.float32)[..., None] * inverse


def rotary(values, angles, direction):
    halfway = values.shape[-1] // 2
    cosine = jnp.cos(angles)[..., None, :]
    sine_part = direction * jnp.sin(angles)[..., None, :]
    leading = values[..., :halfway]
    trailing = values[..., halfway:]
    return jnp.concatenate(
        [leading * cosine - trailing * sine_part, trailing * cosine + leading * sine_part], axis=-1
    )


def visible(query_pos, key_pos, prompt_len):
    query_cont = jnp.arange(query_pos.shape[0]) >= PBLK
    key_prompt = jnp.arange(key_pos.shape[0]) < prompt_len
    return (key_pos[None, :] <= query_pos[:, None]) & (key_prompt[None, :] | query_cont[:, None])


def gating(logit_rows, route_rows):
    picker = (route_rows[:, :, None] == jnp.arange(EXPERTS, dtype=jnp.int32)[None, None, :]).astype(
        logit_rows.dtype
    )
    chosen = jnp.sum(picker * logit_rows[:, None, :], axis=-1)
    return jax.nn.softmax(chosen, axis=-1)


def gated(gate_pre, up_pre):
    return jax.nn.silu(gate_pre) * up_pre


def expert_slots(flat_experts):
    picker = (flat_experts[:, None] == jnp.arange(EXPERTS, dtype=jnp.int32)[None, :]).astype(
        jnp.int32
    )
    earlier = jnp.cumsum(picker, axis=0) - picker
    return jnp.sum(earlier * picker, axis=1)


def local(
    inputs,
    cotangent,
    routes,
    attn_q,
    attn_k,
    attn_v,
    attn_o,
    norm_attn,
    norm_moe,
    router,
    expert_gate,
    expert_up,
    expert_down,
):
    low_type = jnp.bfloat16
    full_type = jnp.float32
    w_query, w_key, w_value, w_out, gain_first, gain_second, w_router, w_gate, w_up, w_down = (
        lax.all_gather(attn_q.astype(low_type), "dp", axis=0, tiled=True),
        lax.all_gather(attn_k.astype(low_type), "dp", axis=0, tiled=True),
        lax.all_gather(attn_v.astype(low_type), "dp", axis=0, tiled=True),
        lax.all_gather(attn_o.astype(low_type), "dp", axis=0, tiled=True),
        lax.all_gather(norm_attn.astype(low_type), "dp", axis=0, tiled=True),
        lax.all_gather(norm_moe.astype(low_type), "dp", axis=0, tiled=True),
        lax.all_gather(router.astype(low_type), "dp", axis=0, tiled=True),
        lax.all_gather(expert_gate.astype(low_type), "dp", axis=0, tiled=True),
        lax.all_gather(expert_up.astype(low_type), "dp", axis=0, tiled=True),
        lax.all_gather(expert_down.astype(low_type), "dp", axis=0, tiled=True),
    )
    n_context = lax.axis_size("context")
    n_expert = lax.axis_size("expert")
    block_index = lax.axis_index("context")
    prompt_len = PBLK * n_context
    tokens = inputs.shape[1]
    local_experts = w_gate.shape[1]
    group_width = HEADS // KVH
    score_scale = 1.0 / math.sqrt(HD)
    gain_one = gain_first.astype(full_type)
    gain_two = gain_second.astype(full_type)
    x_rows = inputs[0].astype(full_type)
    positions = jnp.concatenate(
        [
            block_index * PBLK + jnp.arange(PBLK, dtype=jnp.int32),
            prompt_len + jnp.arange(CONT, dtype=jnp.int32),
        ]
    )
    angles = angle_table(positions)
    normed_one = rms_scale(x_rows, gain_one).astype(low_type)
    q_proj = jnp.dot(normed_one, w_query, preferred_element_type=full_type)
    k_proj = jnp.dot(normed_one, w_key, preferred_element_type=full_type)
    v_proj = jnp.dot(normed_one, w_value, preferred_element_type=full_type)
    queries = (rotary(q_proj.reshape(tokens, HEADS, HD), angles, 1.0) * score_scale).astype(
        low_type
    )
    queries = queries.reshape(tokens, KVH, group_width, HD)
    keys_own = rotary(k_proj.reshape(tokens, KVH, HD), angles, 1.0).astype(low_type)
    values_own = v_proj.astype(low_type).reshape(tokens, KVH, HD)
    prompt_keys, prompt_values = (
        lax.all_gather(keys_own[:PBLK], "context", axis=0, tiled=True),
        lax.all_gather(values_own[:PBLK], "context", axis=0, tiled=True),
    )
    all_keys = jnp.concatenate([prompt_keys, keys_own[PBLK:]], axis=0)
    all_values = jnp.concatenate([prompt_values, values_own[PBLK:]], axis=0)
    key_pos = jnp.concatenate(
        [jnp.arange(prompt_len, dtype=jnp.int32), prompt_len + jnp.arange(CONT, dtype=jnp.int32)]
    )
    allowed = visible(positions, key_pos, prompt_len)
    head_outs = []
    log_totals = []
    for kv_head in range(KVH):
        scores = jnp.einsum(
            "tgn,kn->gtk",
            queries[:, kv_head],
            all_keys[:, kv_head],
            preferred_element_type=full_type,
        )
        scores = jnp.where(allowed[None], scores, masked_score)
        top_score = jnp.max(scores, axis=-1, keepdims=True)
        unnormed = jnp.exp(scores - top_score)
        totals = jnp.sum(unnormed, axis=-1, keepdims=True)
        attn_probs = (unnormed / totals).astype(low_type)
        head_outs.append(
            jnp.einsum(
                "gtk,kn->tgn", attn_probs, all_values[:, kv_head], preferred_element_type=full_type
            )
        )
        log_totals.append(top_score + jnp.log(totals))
    attended_low = jnp.stack(head_outs, axis=1).reshape(tokens, D).astype(low_type)
    mid_rows = x_rows + jnp.dot(attended_low, w_out, preferred_element_type=full_type)
    normed_two = rms_scale(mid_rows, gain_two).astype(low_type)
    logits = jnp.dot(normed_two, w_router, preferred_element_type=full_type)
    route_rows = routes[0]
    gate_weights = gating(logits, route_rows)
    flat_experts = route_rows.reshape(-1)
    slot_rank = expert_slots(flat_experts)
    destination = (
        flat_experts % local_experts * n_expert + flat_experts // local_experts
    ) * CAP + slot_rank
    capacity_rows = local_experts * n_expert * CAP
    assignments = tokens * TOP
    source = (
        jnp.full((capacity_rows,), assignments, dtype=jnp.int32)
        .at[destination]
        .set(jnp.arange(assignments, dtype=jnp.int32))
    )
    filled = source < assignments
    source_row = jnp.minimum(source, assignments - 1)
    send_rows = jnp.where(filled[:, None], normed_two[source_row // TOP], jnp.zeros((), low_type))
    received = lax.all_to_all(
        send_rows.reshape(local_experts, n_expert, CAP, D),
        "expert",
        split_axis=1,
        concat_axis=1,
        tiled=True,
    )
    received = received.reshape(local_experts, n_expert * CAP, D)
    gate_pre = jnp.einsum("lrd,dlf->lrf", received, w_gate, preferred_element_type=full_type)
    up_pre = jnp.einsum("lrd,dlf->lrf", received, w_up, preferred_element_type=full_type)
    activation = gated(gate_pre, up_pre).astype(low_type)
    expert_rows = jnp.einsum(
        "lrf,fld->lrd", activation, w_down, preferred_element_type=full_type
    ).astype(low_type)
    returned = lax.all_to_all(
        expert_rows.reshape(local_experts, n_expert, CAP, D),
        "expert",
        split_axis=1,
        concat_axis=1,
        tiled=True,
    )
    returned = returned.reshape(capacity_rows, D)
    picked = returned[destination].reshape(tokens, TOP, D)
    moe_out = jnp.sum(gate_weights[:, :, None] * picked.astype(full_type), axis=1)
    result = (mid_rows + moe_out).astype(low_type)
    grad_out = cotangent[0].astype(full_type)
    slot_grads = (
        (gate_weights[:, :, None] * grad_out[:, None, :]).reshape(assignments, D).astype(low_type)
    )
    send_grads = jnp.where(filled[:, None], slot_grads[source_row], jnp.zeros((), low_type))
    grad_rows = lax.all_to_all(
        send_grads.reshape(local_experts, n_expert, CAP, D),
        "expert",
        split_axis=1,
        concat_axis=1,
        tiled=True,
    )
    grad_rows = grad_rows.reshape(local_experts, n_expert * CAP, D)
    grad_gates = jnp.sum(picked.astype(full_type) * grad_out[:, None, :], axis=-1)
    grad_wdown = jnp.einsum("lrf,lrd->fld", activation, grad_rows, preferred_element_type=full_type)
    grad_act = jnp.einsum("lrd,fld->lrf", grad_rows, w_down, preferred_element_type=full_type)
    primal_gate, gated_back = jax.vjp(gated, gate_pre, up_pre)
    grad_gpre, grad_upre = gated_back(grad_act)
    grad_gpre = grad_gpre.astype(low_type)
    grad_upre = grad_upre.astype(low_type)
    grad_wgate = jnp.einsum("lrd,lrf->dlf", received, grad_gpre, preferred_element_type=full_type)
    grad_wup = jnp.einsum("lrd,lrf->dlf", received, grad_upre, preferred_element_type=full_type)
    grad_recv = jnp.einsum("lrf,dlf->lrd", grad_gpre, w_gate, preferred_element_type=full_type)
    grad_recv = (
        grad_recv + jnp.einsum("lrf,dlf->lrd", grad_upre, w_up, preferred_element_type=full_type)
    ).astype(low_type)
    back_rows = lax.all_to_all(
        grad_recv.reshape(local_experts, n_expert, CAP, D),
        "expert",
        split_axis=1,
        concat_axis=1,
        tiled=True,
    )
    back_rows = back_rows.reshape(capacity_rows, D)
    grad_normed_two = jnp.sum(
        back_rows[destination].reshape(tokens, TOP, D).astype(full_type), axis=1
    )

    def gate_of(logit_rows):
        return gating(logit_rows, route_rows)

    primal_gates, gate_back = jax.vjp(gate_of, logits)
    grad_logits = gate_back(grad_gates)[0].astype(low_type)
    grad_wrouter = jnp.einsum(
        "td,te->de", normed_two, grad_logits, preferred_element_type=full_type
    )
    grad_normed_two = grad_normed_two + jnp.einsum(
        "te,de->td", grad_logits, w_router, preferred_element_type=full_type
    )
    primal_two, norm_back_two = jax.vjp(rms_scale, mid_rows, gain_two)
    grad_mid_norm, grad_gain_two = norm_back_two(grad_normed_two)
    grad_mid = grad_out + grad_mid_norm
    grad_attn = grad_mid.astype(low_type)
    grad_wout = jnp.einsum("td,te->de", attended_low, grad_attn, preferred_element_type=full_type)
    grad_attended = jnp.einsum(
        "te,de->td", grad_attn, w_out, preferred_element_type=full_type
    ).astype(low_type)
    grad_attended = grad_attended.reshape(tokens, KVH, group_width, HD)
    query_grads = []
    key_grads = []
    value_grads = []
    for kv_head in range(KVH):
        scores = jnp.einsum(
            "tgn,kn->gtk",
            queries[:, kv_head],
            all_keys[:, kv_head],
            preferred_element_type=full_type,
        )
        scores = jnp.where(allowed[None], scores, masked_score)
        exact_probs = jnp.exp(scores - log_totals[kv_head])
        grad_probs = jnp.einsum(
            "tgn,kn->gtk",
            grad_attended[:, kv_head],
            all_values[:, kv_head],
            preferred_element_type=full_type,
        )
        row_dots = jnp.sum(exact_probs * grad_probs, axis=-1, keepdims=True)
        grad_scores = (exact_probs * (grad_probs - row_dots)).astype(low_type)
        query_grads.append(
            jnp.einsum(
                "gtk,kn->tgn", grad_scores, all_keys[:, kv_head], preferred_element_type=full_type
            )
        )
        key_grads.append(
            jnp.einsum(
                "gtk,tgn->kn", grad_scores, queries[:, kv_head], preferred_element_type=full_type
            )
        )
        value_grads.append(
            jnp.einsum(
                "gtk,tgn->kn",
                exact_probs.astype(low_type),
                grad_attended[:, kv_head],
                preferred_element_type=full_type,
            )
        )
    grad_queries = jnp.stack(query_grads, axis=1).reshape(tokens, HEADS, HD)
    grad_keys = jnp.stack(key_grads, axis=1)
    grad_values = jnp.stack(value_grads, axis=1)
    prompt_key_grad, prompt_value_grad = (
        lax.psum_scatter(
            grad_keys[:prompt_len].astype(jnp.bfloat16), "context", scatter_dimension=0, tiled=True
        ).astype(jnp.float32),
        lax.psum_scatter(
            grad_values[:prompt_len].astype(jnp.bfloat16),
            "context",
            scatter_dimension=0,
            tiled=True,
        ).astype(jnp.float32),
    )
    own_key_grad = jnp.concatenate([prompt_key_grad, grad_keys[prompt_len:]], axis=0)
    own_value_grad = jnp.concatenate([prompt_value_grad, grad_values[prompt_len:]], axis=0)
    grad_qproj = (
        rotary(grad_queries * score_scale, angles, -1.0).reshape(tokens, D).astype(low_type)
    )
    grad_kproj = rotary(own_key_grad, angles, -1.0).reshape(tokens, KVH * HD).astype(low_type)
    grad_vproj = own_value_grad.reshape(tokens, KVH * HD).astype(low_type)
    grad_wquery = jnp.einsum("td,te->de", normed_one, grad_qproj, preferred_element_type=full_type)
    grad_wkey = jnp.einsum("td,te->de", normed_one, grad_kproj, preferred_element_type=full_type)
    grad_wvalue = jnp.einsum("td,te->de", normed_one, grad_vproj, preferred_element_type=full_type)
    grad_normed_one = jnp.einsum("te,de->td", grad_qproj, w_query, preferred_element_type=full_type)
    grad_normed_one = grad_normed_one + jnp.einsum(
        "te,de->td", grad_kproj, w_key, preferred_element_type=full_type
    )
    grad_normed_one = grad_normed_one + jnp.einsum(
        "te,de->td", grad_vproj, w_value, preferred_element_type=full_type
    )
    primal_one, norm_back_one = jax.vjp(rms_scale, x_rows, gain_one)
    grad_x_norm, grad_gain_one = norm_back_one(grad_normed_one)
    grad_inputs = (grad_mid + grad_x_norm).astype(low_type)
    shares = (
        lax.psum_scatter(
            grad_wquery.astype(jnp.bfloat16), "dp", scatter_dimension=0, tiled=True
        ).astype(jnp.float32),
        lax.psum_scatter(
            grad_wkey.astype(jnp.bfloat16), "dp", scatter_dimension=0, tiled=True
        ).astype(jnp.float32),
        lax.psum_scatter(
            grad_wvalue.astype(jnp.bfloat16), "dp", scatter_dimension=0, tiled=True
        ).astype(jnp.float32),
        lax.psum_scatter(
            grad_wout.astype(jnp.bfloat16), "dp", scatter_dimension=0, tiled=True
        ).astype(jnp.float32),
        lax.psum_scatter(
            grad_gain_one.astype(jnp.bfloat16), "dp", scatter_dimension=0, tiled=True
        ).astype(jnp.float32),
        lax.psum_scatter(
            grad_gain_two.astype(jnp.bfloat16), "dp", scatter_dimension=0, tiled=True
        ).astype(jnp.float32),
        lax.psum_scatter(
            grad_wrouter.astype(jnp.bfloat16), "dp", scatter_dimension=0, tiled=True
        ).astype(jnp.float32),
        lax.psum_scatter(
            grad_wgate.astype(jnp.bfloat16), "dp", scatter_dimension=0, tiled=True
        ).astype(jnp.float32),
        lax.psum_scatter(
            grad_wup.astype(jnp.bfloat16), "dp", scatter_dimension=0, tiled=True
        ).astype(jnp.float32),
        lax.psum_scatter(
            grad_wdown.astype(jnp.bfloat16), "dp", scatter_dimension=0, tiled=True
        ).astype(jnp.float32),
    )
    dense_sum = lax.psum(
        (shares[0], shares[1], shares[2], shares[3], shares[4], shares[5], shares[6]),
        ("expert", "context"),
    )
    expert_sum = (
        lax.psum(shares[7].astype(jnp.bfloat16), "context").astype(jnp.float32),
        lax.psum(shares[8].astype(jnp.bfloat16), "context").astype(jnp.float32),
        lax.psum(shares[9].astype(jnp.bfloat16), "context").astype(jnp.float32),
    )
    totals_all = tuple(dense_sum) + tuple(expert_sum)
    return (
        result[None],
        grad_inputs[None],
        totals_all[0],
        totals_all[1],
        totals_all[2],
        totals_all[3],
        totals_all[4],
        totals_all[5],
        totals_all[6],
        totals_all[7],
        totals_all[8],
        totals_all[9],
    )


BF = jnp.bfloat16
F32 = jnp.float32
SLOTS = 104
PLANE = ("expert", "context")
VMEM_BYTES = 60 * 1024 * 1024


def mxu(lhs, rhs, contract=((1,), (0,))):
    return lax.dot_general(lhs, rhs, (contract, ((), ())), preferred_element_type=F32)


def grant(bytes_wanted=VMEM_BYTES):
    return pltpu.CompilerParams(vmem_limit_bytes=bytes_wanted)


def turn(values, cosine, sine):
    return values * cosine + pltpu.roll(values, HD // 2, 1) * sine


def project_kernel(x_ref, gain_ref, w_ref, cos_ref, sin_ref, out_ref, normed_ref):
    step = pl.program_id(0)

    @pl.when(step == 0)
    def _():
        rows = x_ref[...].astype(F32)
        scale = lax.rsqrt(jnp.mean(rows * rows, axis=-1, keepdims=True) + epsilon)
        normed_ref[...] = (rows * scale * gain_ref[...]).astype(BF)

    product = mxu(normed_ref[...], w_ref[...])
    is_query = step < HEADS // 2
    is_value = step == HEADS // 2 + KVH // 2
    cosine = jnp.where(is_value, 1.0, cos_ref[...])
    sine = jnp.where(is_value, 0.0, sin_ref[...])
    factor = jnp.where(is_query, 1.0 / math.sqrt(HD), 1.0)
    for half in range(2):
        part = product[:, half * HD : (half + 1) * HD]
        out_ref[:, half * HD : (half + 1) * HD] = (turn(part, cosine, sine) * factor).astype(BF)


def project(x_low, gain, w_qkv, cosine, sine):
    tokens, width = x_low.shape[0], w_qkv.shape[1]
    whole = lambda j: (0, 0)
    return pl.pallas_call(
        project_kernel,
        grid=(width // (2 * HD),),
        in_specs=[
            pl.BlockSpec((tokens, D), whole),
            pl.BlockSpec((1, D), whole),
            pl.BlockSpec((D, 2 * HD), lambda j: (0, j)),
            pl.BlockSpec((tokens, HD), whole),
            pl.BlockSpec((tokens, HD), whole),
        ],
        out_specs=[
            pl.BlockSpec((tokens, 2 * HD), lambda j: (0, j)),
            pl.BlockSpec((tokens, D), whole),
        ],
        out_shape=[
            jax.ShapeDtypeStruct((tokens, width), BF),
            jax.ShapeDtypeStruct((tokens, D), BF),
        ],
        compiler_params=grant(),
        name="project",
    )(x_low, gain, w_qkv, cosine, sine)


def row_blocks(prompt_len):
    blocks = [(0, prompt_len)]
    for start in range(0, CONT, PBLK):
        blocks.append((PBLK + start, prompt_len + start + PBLK))
    return blocks


def masked_scores(scores, first_row, prompt_len, block_index):
    row = lax.broadcasted_iota(jnp.int32, scores.shape, 0)
    column = lax.broadcasted_iota(jnp.int32, scores.shape, 1)
    if first_row == 0:
        limit = row + block_index * PBLK
    else:
        limit = row + (prompt_len + first_row - PBLK)
    return jnp.where(column <= limit, scores, masked_score)


def attend_kernel(prompt_len, block_ref, q_ref, k_ref, v_ref, out_ref, log_ref):
    for first_row, keys in row_blocks(prompt_len):
        rows = slice(first_row, first_row + PBLK)
        scores = mxu(q_ref[rows, :], k_ref[:keys, :], ((1,), (1,)))
        scores = masked_scores(scores, first_row, prompt_len, block_ref[0])
        top = jnp.max(scores, axis=-1, keepdims=True)
        unnormed = jnp.exp(scores - top)
        total = jnp.sum(unnormed, axis=-1, keepdims=True)
        mixed = mxu(unnormed.astype(BF), v_ref[:keys, :]) / total
        out_ref[rows, :] = mixed.astype(BF)
        log_ref[0, rows, :] = top + jnp.log(total)


def attend(block_index, qkv, keys_values, prompt_len):
    tokens, key_rows = qkv.shape[0], keys_values.shape[0]
    width = HEADS // KVH
    return pl.pallas_call(
        functools.partial(attend_kernel, prompt_len),
        grid=(HEADS,),
        in_specs=[
            pl.BlockSpec(memory_space=pltpu.SMEM),
            pl.BlockSpec((tokens, HD), lambda h: (0, h)),
            pl.BlockSpec((key_rows, HD), lambda h: (0, h // width)),
            pl.BlockSpec((key_rows, HD), lambda h: (0, KVH + h // width)),
        ],
        out_specs=[
            pl.BlockSpec((tokens, HD), lambda h: (0, h)),
            pl.BlockSpec((1, tokens, 1), lambda h: (h, 0, 0)),
        ],
        out_shape=[
            jax.ShapeDtypeStruct((tokens, D), BF),
            jax.ShapeDtypeStruct((HEADS, tokens, 1), F32),
        ],
        compiler_params=grant(),
        name="attend",
    )(block_index, qkv, keys_values, keys_values)


def attend_back_kernel(
    prompt_len, block_ref, q_ref, k_ref, v_ref, do_ref, log_ref, cos_ref, sin_ref, dq_ref, dk_ref, dv_ref
):
    @pl.when(pl.program_id(1) == 0)
    def _():
        dk_ref[...] = jnp.zeros_like(dk_ref)
        dv_ref[...] = jnp.zeros_like(dv_ref)

    for first_row, keys in row_blocks(prompt_len):
        rows = slice(first_row, first_row + PBLK)
        queries, grads = q_ref[rows, :], do_ref[rows, :]
        scores = mxu(queries, k_ref[:keys, :], ((1,), (1,)))
        scores = masked_scores(scores, first_row, prompt_len, block_ref[0])
        probs = jnp.exp(scores - log_ref[0, rows, :])
        grad_probs = mxu(grads, v_ref[:keys, :], ((1,), (1,)))
        dots = jnp.sum(probs * grad_probs, axis=-1, keepdims=True)
        grad_scores = (probs * (grad_probs - dots)).astype(BF)
        grad_query = mxu(grad_scores, k_ref[:keys, :])
        grad_query = turn(grad_query, cos_ref[rows, :], -sin_ref[rows, :]) * (1.0 / math.sqrt(HD))
        dq_ref[rows, :] = grad_query.astype(BF)
        dk_ref[:keys, :] += mxu(grad_scores, queries, ((0,), (0,)))
        dv_ref[:keys, :] += mxu(probs.astype(BF), grads, ((0,), (0,)))


def attend_back(block_index, qkv, keys_values, grad_heads, logs, cosine, sine, prompt_len):
    tokens, key_rows = qkv.shape[0], keys_values.shape[0]
    width = HEADS // KVH
    head = lambda i, g: (0, i * width + g)
    whole = lambda i, g: (0, 0)
    return pl.pallas_call(
        functools.partial(attend_back_kernel, prompt_len),
        grid=(KVH, width),
        in_specs=[
            pl.BlockSpec(memory_space=pltpu.SMEM),
            pl.BlockSpec((tokens, HD), head),
            pl.BlockSpec((key_rows, HD), lambda i, g: (0, i)),
            pl.BlockSpec((key_rows, HD), lambda i, g: (0, KVH + i)),
            pl.BlockSpec((tokens, HD), head),
            pl.BlockSpec((1, tokens, 1), lambda i, g: (i * width + g, 0, 0)),
            pl.BlockSpec((tokens, HD), whole),
            pl.BlockSpec((tokens, HD), whole),
        ],
        out_specs=[
            pl.BlockSpec((tokens, HD), head),
            pl.BlockSpec((key_rows, HD), lambda i, g: (0, i)),
            pl.BlockSpec((key_rows, HD), lambda i, g: (0, i)),
        ],
        out_shape=[
            jax.ShapeDtypeStruct((tokens, D), BF),
            jax.ShapeDtypeStruct((key_rows, KVH * HD), F32),
            jax.ShapeDtypeStruct((key_rows, KVH * HD), F32),
        ],
        compiler_params=grant(),
        name="attend_back",
    )(block_index, qkv, keys_values, keys_values, grad_heads, logs, cosine, sine)


def segment_matrix(parts, transposed):
    shape = (parts * SLOTS, parts) if transposed else (parts, parts * SLOTS)
    long = lax.broadcasted_iota(jnp.int32, shape, 0 if transposed else 1)
    short = lax.broadcasted_iota(jnp.int32, shape, 1 if transposed else 0)
    inside = (long >= short * SLOTS) & (long < (short + 1) * SLOTS)
    return jnp.where(inside, 1.0, 0.0).astype(BF)


def slot_matrix(ranks, parts, transposed):
    if transposed:
        spread = mxu(segment_matrix(parts, True), ranks)
        slot = lax.broadcasted_iota(jnp.int32, (parts * SLOTS, 1), 0)
    else:
        spread = mxu(ranks, segment_matrix(parts, False))
        slot = lax.broadcasted_iota(jnp.int32, (1, parts * SLOTS), 1)
    for part in range(parts - 1, 0, -1):
        slot = jnp.where(slot >= part * SLOTS, slot - SLOTS, slot)
    return jnp.where(spread == slot.astype(F32), 1.0, 0.0).astype(BF)


def spread_kernel(parts, rank0_ref, rank1_ref, rows_ref, out0_ref, out1_ref):
    for rank_ref, out_ref in ((rank0_ref, out0_ref), (rank1_ref, out1_ref)):
        chooser = slot_matrix(rank_ref[0], parts, True)
        out_ref[...] = mxu(chooser, rows_ref[...]).astype(BF)


def spread_rows(rank0, rank1, rows):
    dests, tokens = rank0.shape
    steps = 2
    parts = dests // steps
    rank0 = rank0.reshape(steps, parts, tokens)
    rank1 = rank1.reshape(steps, parts, tokens)
    ranks = pl.BlockSpec((1, parts, tokens), lambda j: (j, 0, 0))
    block = pl.BlockSpec((parts * SLOTS, D), lambda j: (j, 0))
    shape = jax.ShapeDtypeStruct((dests * SLOTS, D), BF)
    return pl.pallas_call(
        functools.partial(spread_kernel, parts),
        grid=(steps,),
        in_specs=[ranks, ranks, pl.BlockSpec((tokens, D), lambda j: (0, 0))],
        out_specs=[block, block],
        out_shape=[shape, shape],
        compiler_params=grant(),
        name="spread_rows",
    )(rank0, rank1, rows)


def collect_kernel(parts, rank0_ref, rank1_ref, rows0_ref, rows1_ref, out_ref):
    total = mxu(slot_matrix(rank0_ref[...], parts, False), rows0_ref[...])
    total = total + mxu(slot_matrix(rank1_ref[...], parts, False), rows1_ref[...])
    out_ref[...] = total.astype(out_ref.dtype)


def collect_rows(rank0, rank1, rows0, rows1, kind):
    tokens, dests = rank0.shape
    step = PBLK
    ranks = pl.BlockSpec((step, dests), lambda j: (j, 0))
    slots = pl.BlockSpec((dests * SLOTS, D), lambda j: (0, 0))
    return pl.pallas_call(
        functools.partial(collect_kernel, dests),
        grid=(tokens // step,),
        in_specs=[ranks, ranks, slots, slots],
        out_specs=pl.BlockSpec((step, D), lambda j: (j, 0)),
        out_shape=jax.ShapeDtypeStruct((tokens, D), kind),
        compiler_params=grant(),
        name="collect_rows",
    )(rank0, rank1, rows0, rows1)


def expert_kernel(n_dp, half_steps, *refs):
    (z_ref, xo_ref, xp_ref, go_ref, gp_ref, so_ref, sp_ref) = refs[:7]
    pieces = refs[7 : 7 + 3 * n_dp]
    outs = refs[7 + 3 * n_dp :]
    (yo_ref, yp_ref, bo_ref, bp_ref, do_ref, dp_ref, xc_ref, a_ref, dg_ref, du_ref, de_ref) = outs[:11]
    weights = outs[11:]
    wg_ref, wu_ref, wd_ref = weights
    step = pl.program_id(0)
    own = step < half_steps

    @pl.when(step == 0)
    def _():
        for which in range(3):
            for flip in range(n_dp):
                piece = pieces[which * n_dp + flip]
                size = piece.shape[1]
                start = pl.multiple_of((z_ref[0] ^ flip) * size, 64)
                weights[which][pl.ds(start, size), :] = piece[0]

    rows = jnp.where(own, xo_ref[...], xp_ref[...])
    cot = jnp.where(own, go_ref[...], gp_ref[...])
    share = jnp.where(own, so_ref[...], sp_ref[...])
    xc_ref[...] = rows
    gate_pre = mxu(rows, wg_ref[...])
    up_pre = mxu(rows, wu_ref[...])
    sigma = 1.0 / (1.0 + jnp.exp(-gate_pre))
    silu = gate_pre * sigma
    act = (silu * up_pre).astype(BF)
    a_ref[...] = act
    cot_full = cot.astype(F32)
    weighted = (cot_full * share).astype(BF)
    de_ref[...] = weighted
    result = mxu(act, wd_ref[...])
    dots = jnp.sum(result.astype(BF).astype(F32) * cot_full, axis=-1, keepdims=True)
    scaled = (result * share).astype(BF)
    grad_act = mxu(weighted, wd_ref[...], ((1,), (1,)))
    grad_gate = (grad_act * up_pre * sigma * (1.0 + gate_pre * (1.0 - sigma))).astype(BF)
    grad_up = (grad_act * silu).astype(BF)
    dg_ref[...] = grad_gate
    du_ref[...] = grad_up
    back = mxu(grad_gate, wg_ref[...], ((1,), (1,))) + mxu(grad_up, wu_ref[...], ((1,), (1,)))
    back = back.astype(BF)

    @pl.when(own)
    def _():
        yo_ref[...] = scaled
        bo_ref[...] = back
        do_ref[...] = dots

    @pl.when(jnp.logical_not(own))
    def _():
        yp_ref[...] = scaled
        bp_ref[...] = back
        dp_ref[...] = dots


def run_expert(which, z_index, x_own, x_par, g_own, g_par, s_own, s_par, gate_pieces, up_pieces, down_pieces):
    half_rows = x_own.shape[0]
    step_rows = half_rows // 2
    half_steps = 2
    n_dp = len(gate_pieces)
    full_hidden = gate_pieces[0].shape[2]
    own_map = lambda j: (jnp.minimum(j, half_steps - 1), 0)
    par_map = lambda j: (jnp.maximum(j - half_steps, 0), 0)
    all_map = lambda j: (j, 0)
    piece_map = lambda j: (which, 0, 0)

    def pair(width):
        return [pl.BlockSpec((step_rows, width), own_map), pl.BlockSpec((step_rows, width), par_map)]

    def piece_specs(pieces):
        return [
            pl.BlockSpec((1,) + p.shape[1:], piece_map, pipeline_mode=pl.Buffered(1)) for p in pieces
        ]

    wide = pl.BlockSpec((step_rows, D), all_map)
    narrow = pl.BlockSpec((step_rows, full_hidden), all_map)
    half_shape = jax.ShapeDtypeStruct((half_rows, D), BF)
    dot_shape = jax.ShapeDtypeStruct((half_rows, 1), F32)
    wide_shape = jax.ShapeDtypeStruct((2 * half_rows, D), BF)
    narrow_shape = jax.ShapeDtypeStruct((2 * half_rows, full_hidden), BF)
    return pl.pallas_call(
        functools.partial(expert_kernel, n_dp, half_steps),
        grid=(2 * half_steps,),
        in_specs=[pl.BlockSpec(memory_space=pltpu.SMEM)]
        + pair(D)
        + pair(D)
        + pair(1)
        + piece_specs(gate_pieces)
        + piece_specs(up_pieces)
        + piece_specs(down_pieces),
        out_specs=pair(D) + pair(D) + pair(1) + [wide, narrow, narrow, narrow, wide],
        out_shape=[half_shape] * 4
        + [dot_shape] * 2
        + [wide_shape, narrow_shape, narrow_shape, narrow_shape, wide_shape],
        scratch_shapes=[
            pltpu.VMEM((D, full_hidden), BF),
            pltpu.VMEM((D, full_hidden), BF),
            pltpu.VMEM((full_hidden, D), BF),
        ],
        compiler_params=grant(62 * 1024 * 1024),
        name="experts",
    )(z_index, x_own, x_par, g_own, g_par, s_own, s_par, *gate_pieces, *up_pieces, *down_pieces)


def flip_permute(value, axis, size, flip):
    return lax.ppermute(value, axis, [(i, i ^ flip) for i in range(size)])


def plane_exchange(rows):
    plane = lax.axis_size("expert") * lax.axis_size("context")
    parted = rows.reshape(plane, rows.shape[0] // plane, *rows.shape[1:])
    moved = lax.all_to_all(parted, PLANE, split_axis=0, concat_axis=0, tiled=True)
    return moved.reshape(rows.shape)


def gather_dense(shard):
    n_context, n_expert = lax.axis_size("context"), lax.axis_size("expert")
    plane = n_context * n_expert
    here = lax.axis_index("expert") * n_context + lax.axis_index("context")
    rows = shard.shape[0] // plane
    part = lax.dynamic_slice_in_dim(shard, here * rows, rows, 0)
    part = lax.all_gather(part, "dp", axis=0, tiled=False)
    whole = lax.all_gather(part, PLANE, axis=1, tiled=False)
    return whole.reshape(-1, shard.shape[1])


def scatter_dense(share):
    n_context, n_expert, n_dp = lax.axis_size("context"), lax.axis_size("expert"), lax.axis_size("dp")
    plane = n_context * n_expert
    width = share.shape[1]
    rows = share.shape[0] // (plane * n_dp)
    parts = share.astype(BF).reshape(n_dp, plane, rows, width)
    parts = lax.psum_scatter(parts, PLANE, scatter_dimension=1, tiled=True)
    parts = lax.psum_scatter(parts.reshape(n_dp, rows, width), "dp", scatter_dimension=0, tiled=True)
    whole = lax.all_gather(parts.reshape(rows, width), PLANE, axis=0, tiled=True)
    return whole.astype(F32)


def local_paired(
    inputs,
    cotangent,
    routes,
    attn_q,
    attn_k,
    attn_v,
    attn_o,
    norm_attn,
    norm_moe,
    router,
    expert_gate,
    expert_up,
    expert_down,
):
    n_context, n_expert, n_dp = lax.axis_size("context"), lax.axis_size("expert"), lax.axis_size("dp")
    plane = n_context * n_expert
    tokens = inputs.shape[1]
    block_index = lax.axis_index("context")
    z_index = lax.axis_index("dp")
    parity = z_index % 2
    prompt_len = PBLK * n_context
    x_low = inputs[0]
    cot_low = cotangent[0]
    route_rows = routes[0]

    small = jnp.concatenate(
        [router, norm_attn[:, None], norm_moe[:, None]], axis=1
    ).astype(BF)
    small = jnp.pad(small, ((0, 0), (0, 128 - small.shape[1])))
    shard_in = jnp.concatenate([attn_q.astype(BF), attn_k.astype(BF), attn_v.astype(BF), small], axis=1)
    whole_in = gather_dense(shard_in)
    w_out = gather_dense(attn_o.astype(BF))
    qkv_width = D + 2 * KVH * HD
    w_qkv = whole_in[:, :qkv_width]
    w_router = whole_in[:, qkv_width : qkv_width + EXPERTS]
    gain_one = whole_in[:, qkv_width + EXPERTS].astype(F32)
    gain_two = whole_in[:, qkv_width + EXPERTS + 1].astype(F32)

    per_device = expert_gate.shape[1] // n_context

    def weight_pieces(weight):
        mine = lax.dynamic_slice_in_dim(weight, block_index * per_device, per_device, 1)
        mine = mine.astype(BF).transpose(1, 0, 2)
        mine = mine.reshape(2, per_device // 2, mine.shape[1], mine.shape[2])
        same = lax.dynamic_index_in_dim(mine, parity, 0, keepdims=False)
        other = lax.dynamic_index_in_dim(mine, 1 - parity, 0, keepdims=False)
        return [same] + [
            flip_permute(other if flip % 2 else same, "dp", n_dp, flip) for flip in range(1, n_dp)
        ]

    gate_pieces, up_pieces, down_pieces = (
        weight_pieces(expert_gate),
        weight_pieces(expert_up),
        weight_pieces(expert_down),
    )

    partner_routes = flip_permute(route_rows, "dp", n_dp, 1)

    def ranks_of(rows):
        named = jnp.sum(
            (rows[:, :, None] == jnp.arange(EXPERTS, dtype=jnp.int32)[None, None, :]).astype(F32), axis=1
        )
        order = jnp.arange(tokens, dtype=jnp.int32)
        before = (order[None, :] < order[:, None]).astype(BF)
        count = mxu(before, named.astype(BF))
        return named > 0, jnp.where(named > 0, count, -1.0)

    named, own_ranks = ranks_of(route_rows)
    partner_ranks = ranks_of(partner_routes)[1]

    def mine_of(table):
        parted = table.reshape(tokens, plane, 2, 2)
        return lax.dynamic_index_in_dim(parted, parity, 2, keepdims=False)

    own_sel = mine_of(own_ranks)
    partner_sel = mine_of(partner_ranks)
    own_pair = [own_sel[:, :, i].astype(BF) for i in range(2)]
    partner_pair = [partner_sel[:, :, i].astype(BF) for i in range(2)]

    def dispatch(rows, ranks):
        slots = spread_rows(ranks[0].T, ranks[1].T, rows)
        return [plane_exchange(s) for s in slots]

    partner_cot = flip_permute(cot_low, "dp", n_dp, 1)
    cot_own = dispatch(cot_low, own_pair)
    cot_partner = dispatch(partner_cot, partner_pair)

    positions = jnp.concatenate(
        [
            block_index * PBLK + jnp.arange(PBLK, dtype=jnp.int32),
            prompt_len + jnp.arange(CONT, dtype=jnp.int32),
        ]
    )
    angles = angle_table(positions)
    cos_half, sin_half = jnp.cos(angles), jnp.sin(angles)
    cosine = jnp.concatenate([cos_half, cos_half], axis=1)
    sine = jnp.concatenate([-sin_half, sin_half], axis=1)
    block_word = block_index.astype(jnp.int32).reshape(1)
    z_word = z_index.astype(jnp.int32).reshape(1)
    qkv, normed_one = project(x_low, gain_one[None, :], w_qkv, cosine, sine)
    keys_own = qkv[:, D:]
    prompt_kv = lax.all_gather(keys_own[:PBLK], "context", axis=0, tiled=True)
    keys_values = jnp.concatenate([prompt_kv, keys_own[PBLK:]], axis=0)
    attended, logs = attend(block_word, qkv, keys_values, prompt_len)
    x_rows = x_low.astype(F32)
    mid_rows = x_rows + mxu(attended, w_out)
    normed_two = rms_scale(mid_rows, gain_two).astype(BF)

    partner_normed = flip_permute(normed_two, "dp", n_dp, 1)
    rows_own = dispatch(normed_two, own_pair)
    rows_partner = dispatch(partner_normed, partner_pair)
    logits = mxu(normed_two, w_router)
    top_logit = jnp.max(jnp.where(named, logits, masked_score), axis=1, keepdims=True)
    raised = jnp.where(named, jnp.exp(jnp.where(named, logits - top_logit, 0.0)), 0.0)
    gates = raised / jnp.sum(raised, axis=1, keepdims=True)

    slot_ids = jnp.arange(SLOTS, dtype=F32)
    hits = own_ranks.T[:, None, :] == slot_ids[None, :, None]
    slot_gates = jnp.sum(jnp.where(hits, gates.T[:, None, :], 0.0), axis=-1)
    slot_gates = slot_gates.reshape(plane, 2, 2, SLOTS)
    own_gates = lax.dynamic_index_in_dim(slot_gates, parity, 1, keepdims=False)
    other_gates = lax.dynamic_index_in_dim(slot_gates, 1 - parity, 1, keepdims=False)
    partner_gates = flip_permute(other_gates, "dp", n_dp, 1)
    both_gates = jnp.stack([own_gates, partner_gates], axis=1)
    both_gates = lax.all_to_all(both_gates, PLANE, split_axis=0, concat_axis=0, tiled=True)

    shares = []
    returned = []
    for i in range(2):
        column = lambda side: both_gates[:, side, i].reshape(plane * SLOTS, 1)
        returned.append(
            run_expert(
                i,
                z_word,
                rows_own[i],
                rows_partner[i],
                cot_own[i],
                cot_partner[i],
                column(0),
                column(1),
                gate_pieces,
                up_pieces,
                down_pieces,
            )
        )

    back_partner = [plane_exchange(r[3]) for r in returned]
    back_own = [plane_exchange(r[2]) for r in returned]
    dots = jnp.stack(
        [
            jnp.stack([r[4].reshape(plane, SLOTS), r[5].reshape(plane, SLOTS)], axis=1) for r in returned
        ],
        axis=2,
    )
    dots = lax.all_to_all(dots, PLANE, split_axis=0, concat_axis=0, tiled=True)
    other_dots = flip_permute(dots[:, 1], "dp", n_dp, 1)
    all_dots = jnp.where(
        parity == 0,
        jnp.stack([dots[:, 0], other_dots], axis=1),
        jnp.stack([other_dots, dots[:, 0]], axis=1),
    ).reshape(EXPERTS, SLOTS)
    grad_gates = jnp.sum(
        jnp.where(own_ranks[:, :, None] == slot_ids[None, None, :], all_dots[None], 0.0), axis=-1
    )
    for_partner = collect_rows(partner_pair[0], partner_pair[1], back_partner[0], back_partner[1], BF)
    from_partner = flip_permute(for_partner, "dp", n_dp, 1)
    grad_normed_two = collect_rows(own_pair[0], own_pair[1], back_own[0], back_own[1], F32)
    grad_normed_two = grad_normed_two + from_partner.astype(F32)
    grad_logits = gates * (grad_gates - jnp.sum(gates * grad_gates, axis=1, keepdims=True))
    grad_logits = grad_logits.astype(BF)
    grad_wrouter = mxu(normed_two, grad_logits, ((0,), (0,)))
    grad_normed_two = grad_normed_two + mxu(grad_logits, w_router, ((1,), (1,)))
    grad_out = cot_low.astype(F32)
    norm_back_two = jax.vjp(rms_scale, mid_rows, gain_two)[1]
    grad_mid_norm, grad_gain_two = norm_back_two(grad_normed_two)
    grad_mid = grad_out + grad_mid_norm
    grad_attn = grad_mid.astype(BF)
    grad_attended = mxu(grad_attn, w_out, ((1,), (1,))).astype(BF)
    grad_wout = mxu(attended, grad_attn, ((0,), (0,)))

    def weight_shares(index_lhs, index_rhs):
        made = [mxu(r[index_lhs], r[index_rhs], ((0,), (0,))).astype(BF) for r in returned]
        made = jnp.stack(made, axis=0)
        made = made.reshape(2, n_dp, made.shape[1] // n_dp, made.shape[2])

        def quarter(flip):
            return lax.dynamic_index_in_dim(made, z_index ^ flip, 1, keepdims=False)

        got = [quarter(0)] + [
            flip_permute(quarter(flip), "dp", n_dp, flip) for flip in range(1, n_dp)
        ]
        same = sum(got[flip].astype(F32) for flip in range(0, n_dp, 2)).astype(BF)
        other = sum(got[flip].astype(F32) for flip in range(1, n_dp, 2)).astype(BF)
        four = jnp.where(
            parity == 0, jnp.concatenate([same, other], axis=0), jnp.concatenate([other, same], axis=0)
        )
        everything = lax.all_gather(four, "context", axis=0, tiled=True)
        return everything.transpose(1, 0, 2).astype(F32)

    grad_wdown = weight_shares(7, 10)
    grad_wgate = weight_shares(6, 8)
    grad_wup = weight_shares(6, 9)

    grad_qproj, grad_keys, grad_values = attend_back(
        block_word, qkv, keys_values, grad_attended, logs, cosine, sine, prompt_len
    )
    grad_kv = jnp.concatenate([grad_keys, grad_values], axis=1)
    prompt_share = lax.psum_scatter(
        grad_kv[:prompt_len].astype(BF), "context", scatter_dimension=0, tiled=True
    ).astype(F32)
    grad_kv = jnp.concatenate([prompt_share, grad_kv[prompt_len:]], axis=0)
    grad_kproj = rotary(grad_kv[:, : KVH * HD].reshape(tokens, KVH, HD), angles, -1.0)
    grad_kv = jnp.concatenate([grad_kproj.reshape(tokens, KVH * HD), grad_kv[:, KVH * HD :]], axis=1)
    grad_qkv = jnp.concatenate([grad_qproj, grad_kv.astype(BF)], axis=1)
    grad_wqkv = mxu(normed_one, grad_qkv, ((0,), (0,)))
    grad_normed_one = mxu(grad_qkv, w_qkv, ((1,), (1,)))
    norm_back_one = jax.vjp(rms_scale, x_rows, gain_one)[1]
    grad_x_norm, grad_gain_one = norm_back_one(grad_normed_one)
    grad_inputs = (grad_mid + grad_x_norm).astype(BF)

    out_partner = [plane_exchange(r[1]) for r in returned]
    out_own = [plane_exchange(r[0]) for r in returned]
    out_for_partner = collect_rows(partner_pair[0], partner_pair[1], out_partner[0], out_partner[1], BF)
    out_from_partner = flip_permute(out_for_partner, "dp", n_dp, 1)
    moe_out = collect_rows(own_pair[0], own_pair[1], out_own[0], out_own[1], F32)
    result = (mid_rows + moe_out + out_from_partner.astype(F32)).astype(BF)

    grad_small = jnp.concatenate(
        [grad_wrouter, grad_gain_one[:, None], grad_gain_two[:, None]], axis=1
    )
    grad_small = jnp.pad(grad_small, ((0, 0), (0, 128 - grad_small.shape[1])))
    total_out = scatter_dense(grad_wout)
    total_in = scatter_dense(jnp.concatenate([grad_wqkv, grad_small], axis=1))
    return (
        result[None],
        grad_inputs[None],
        total_in[:, :D],
        total_in[:, D : D + KVH * HD],
        total_in[:, D + KVH * HD : qkv_width],
        total_out,
        total_in[:, qkv_width + EXPERTS],
        total_in[:, qkv_width + EXPERTS + 1],
        total_in[:, qkv_width : qkv_width + EXPERTS],
        grad_wgate,
        grad_wup,
        grad_wdown,
    )


def paired_plan(mesh):
    n_expert, n_context, n_dp = mesh.shape["expert"], mesh.shape["context"], mesh.shape["dp"]
    owners = 2 * n_expert * n_context
    small_axes = all(size & (size - 1) == 0 for size in (n_expert, n_context, n_dp))
    return small_axes and n_dp % 2 == 0 and EXPERTS == 2 * owners


def solution(mesh):
    in_specs = (
        P(("expert", "dp"), "context", None),
        P(("expert", "dp"), "context", None),
        P(("expert", "dp"), "context", None),
        P("dp", None),
        P("dp", None),
        P("dp", None),
        P("dp", None),
        P("dp"),
        P("dp"),
        P("dp", None),
        P("dp", "expert", None),
        P("dp", "expert", None),
        P("dp", "expert", None),
    )
    out_specs = (
        P(("expert", "dp"), "context", None),
        P(("expert", "dp"), "context", None),
        P("dp", None),
        P("dp", None),
        P("dp", None),
        P("dp", None),
        P("dp"),
        P("dp"),
        P("dp", None),
        P("dp", "expert", None),
        P("dp", "expert", None),
        P("dp", "expert", None),
    )
    chosen = local_paired if paired_plan(mesh) else local
    return jax.shard_map(chosen, mesh=mesh, in_specs=in_specs, out_specs=out_specs, check_vma=False)
```

```python
import functools
import math

import jax
import jax.numpy as jnp
from jax import lax
from jax.experimental import pallas as pl
from jax.experimental.pallas import tpu as pltpu
from jax.sharding import PartitionSpec as P

D = 1536
HEADS = 12
KVH = 2
HD = 128
EXPERTS = 32
TOP = 4
PBLK = 256
CONT = 512
CAP = 103


epsilon = 1e-06
rope_base = 1000000.0
masked_score = -1e30


def rms_scale(values, gain):
    return values * lax.rsqrt(jnp.mean(values * values, axis=-1, keepdims=True) + epsilon) * gain


def angle_table(positions):
    steps_half = jnp.arange(HD // 2, dtype=jnp.float32)
    inverse = jnp.exp(steps_half * (-2.0 * math.log(rope_base) / HD))
    return positions.astype(jnp.float32)[..., None] * inverse


def rotary(values, angles, direction):
    halfway = values.shape[-1] // 2
    cosine = jnp.cos(angles)[..., None, :]
    sine_part = direction * jnp.sin(angles)[..., None, :]
    leading = values[..., :halfway]
    trailing = values[..., halfway:]
    return jnp.concatenate(
        [leading * cosine - trailing * sine_part, trailing * cosine + leading * sine_part], axis=-1
    )


def visible(query_pos, key_pos, prompt_len):
    query_cont = jnp.arange(query_pos.shape[0]) >= PBLK
    key_prompt = jnp.arange(key_pos.shape[0]) < prompt_len
    return (key_pos[None, :] <= query_pos[:, None]) & (key_prompt[None, :] | query_cont[:, None])


def gating(logit_rows, route_rows):
    picker = (route_rows[:, :, None] == jnp.arange(EXPERTS, dtype=jnp.int32)[None, None, :]).astype(
        logit_rows.dtype
    )
    chosen = jnp.sum(picker * logit_rows[:, None, :], axis=-1)
    return jax.nn.softmax(chosen, axis=-1)


def gated(gate_pre, up_pre):
    return jax.nn.silu(gate_pre) * up_pre


def expert_slots(flat_experts):
    picker = (flat_experts[:, None] == jnp.arange(EXPERTS, dtype=jnp.int32)[None, :]).astype(
        jnp.int32
    )
    earlier = jnp.cumsum(picker, axis=0) - picker
    return jnp.sum(earlier * picker, axis=1)


def local(
    inputs,
    cotangent,
    routes,
    attn_q,
    attn_k,
    attn_v,
    attn_o,
    norm_attn,
    norm_moe,
    router,
    expert_gate,
    expert_up,
    expert_down,
):
    low_type = jnp.bfloat16
    full_type = jnp.float32
    w_query, w_key, w_value, w_out, gain_first, gain_second, w_router, w_gate, w_up, w_down = (
        lax.all_gather(attn_q.astype(low_type), "dp", axis=0, tiled=True),
        lax.all_gather(attn_k.astype(low_type), "dp", axis=0, tiled=True),
        lax.all_gather(attn_v.astype(low_type), "dp", axis=0, tiled=True),
        lax.all_gather(attn_o.astype(low_type), "dp", axis=0, tiled=True),
        lax.all_gather(norm_attn.astype(low_type), "dp", axis=0, tiled=True),
        lax.all_gather(norm_moe.astype(low_type), "dp", axis=0, tiled=True),
        lax.all_gather(router.astype(low_type), "dp", axis=0, tiled=True),
        lax.all_gather(expert_gate.astype(low_type), "dp", axis=0, tiled=True),
        lax.all_gather(expert_up.astype(low_type), "dp", axis=0, tiled=True),
        lax.all_gather(expert_down.astype(low_type), "dp", axis=0, tiled=True),
    )
    n_context = lax.axis_size("context")
    n_expert = lax.axis_size("expert")
    block_index = lax.axis_index("context")
    prompt_len = PBLK * n_context
    tokens = inputs.shape[1]
    local_experts = w_gate.shape[1]
    group_width = HEADS // KVH
    score_scale = 1.0 / math.sqrt(HD)
    gain_one = gain_first.astype(full_type)
    gain_two = gain_second.astype(full_type)
    x_rows = inputs[0].astype(full_type)
    positions = jnp.concatenate(
        [
            block_index * PBLK + jnp.arange(PBLK, dtype=jnp.int32),
            prompt_len + jnp.arange(CONT, dtype=jnp.int32),
        ]
    )
    angles = angle_table(positions)
    normed_one = rms_scale(x_rows, gain_one).astype(low_type)
    q_proj = jnp.dot(normed_one, w_query, preferred_element_type=full_type)
    k_proj = jnp.dot(normed_one, w_key, preferred_element_type=full_type)
    v_proj = jnp.dot(normed_one, w_value, preferred_element_type=full_type)
    queries = (rotary(q_proj.reshape(tokens, HEADS, HD), angles, 1.0) * score_scale).astype(
        low_type
    )
    queries = queries.reshape(tokens, KVH, group_width, HD)
    keys_own = rotary(k_proj.reshape(tokens, KVH, HD), angles, 1.0).astype(low_type)
    values_own = v_proj.astype(low_type).reshape(tokens, KVH, HD)
    prompt_keys, prompt_values = (
        lax.all_gather(keys_own[:PBLK], "context", axis=0, tiled=True),
        lax.all_gather(values_own[:PBLK], "context", axis=0, tiled=True),
    )
    all_keys = jnp.concatenate([prompt_keys, keys_own[PBLK:]], axis=0)
    all_values = jnp.concatenate([prompt_values, values_own[PBLK:]], axis=0)
    key_pos = jnp.concatenate(
        [jnp.arange(prompt_len, dtype=jnp.int32), prompt_len + jnp.arange(CONT, dtype=jnp.int32)]
    )
    allowed = visible(positions, key_pos, prompt_len)
    head_outs = []
    log_totals = []
    for kv_head in range(KVH):
        scores = jnp.einsum(
            "tgn,kn->gtk",
            queries[:, kv_head],
            all_keys[:, kv_head],
            preferred_element_type=full_type,
        )
        scores = jnp.where(allowed[None], scores, masked_score)
        top_score = jnp.max(scores, axis=-1, keepdims=True)
        unnormed = jnp.exp(scores - top_score)
        totals = jnp.sum(unnormed, axis=-1, keepdims=True)
        attn_probs = (unnormed / totals).astype(low_type)
        head_outs.append(
            jnp.einsum(
                "gtk,kn->tgn", attn_probs, all_values[:, kv_head], preferred_element_type=full_type
            )
        )
        log_totals.append(top_score + jnp.log(totals))
    attended_low = jnp.stack(head_outs, axis=1).reshape(tokens, D).astype(low_type)
    mid_rows = x_rows + jnp.dot(attended_low, w_out, preferred_element_type=full_type)
    normed_two = rms_scale(mid_rows, gain_two).astype(low_type)
    logits = jnp.dot(normed_two, w_router, preferred_element_type=full_type)
    route_rows = routes[0]
    gate_weights = gating(logits, route_rows)
    flat_experts = route_rows.reshape(-1)
    slot_rank = expert_slots(flat_experts)
    destination = (
        flat_experts % local_experts * n_expert + flat_experts // local_experts
    ) * CAP + slot_rank
    capacity_rows = local_experts * n_expert * CAP
    assignments = tokens * TOP
    source = (
        jnp.full((capacity_rows,), assignments, dtype=jnp.int32)
        .at[destination]
        .set(jnp.arange(assignments, dtype=jnp.int32))
    )
    filled = source < assignments
    source_row = jnp.minimum(source, assignments - 1)
    send_rows = jnp.where(filled[:, None], normed_two[source_row // TOP], jnp.zeros((), low_type))
    received = lax.all_to_all(
        send_rows.reshape(local_experts, n_expert, CAP, D),
        "expert",
        split_axis=1,
        concat_axis=1,
        tiled=True,
    )
    received = received.reshape(local_experts, n_expert * CAP, D)
    gate_pre = jnp.einsum("lrd,dlf->lrf", received, w_gate, preferred_element_type=full_type)
    up_pre = jnp.einsum("lrd,dlf->lrf", received, w_up, preferred_element_type=full_type)
    activation = gated(gate_pre, up_pre).astype(low_type)
    expert_rows = jnp.einsum(
        "lrf,fld->lrd", activation, w_down, preferred_element_type=full_type
    ).astype(low_type)
    returned = lax.all_to_all(
        expert_rows.reshape(local_experts, n_expert, CAP, D),
        "expert",
        split_axis=1,
        concat_axis=1,
        tiled=True,
    )
    returned = returned.reshape(capacity_rows, D)
    picked = returned[destination].reshape(tokens, TOP, D)
    moe_out = jnp.sum(gate_weights[:, :, None] * picked.astype(full_type), axis=1)
    result = (mid_rows + moe_out).astype(low_type)
    grad_out = cotangent[0].astype(full_type)
    slot_grads = (
        (gate_weights[:, :, None] * grad_out[:, None, :]).reshape(assignments, D).astype(low_type)
    )
    send_grads = jnp.where(filled[:, None], slot_grads[source_row], jnp.zeros((), low_type))
    grad_rows = lax.all_to_all(
        send_grads.reshape(local_experts, n_expert, CAP, D),
        "expert",
        split_axis=1,
        concat_axis=1,
        tiled=True,
    )
    grad_rows = grad_rows.reshape(local_experts, n_expert * CAP, D)
    grad_gates = jnp.sum(picked.astype(full_type) * grad_out[:, None, :], axis=-1)
    grad_wdown = jnp.einsum("lrf,lrd->fld", activation, grad_rows, preferred_element_type=full_type)
    grad_act = jnp.einsum("lrd,fld->lrf", grad_rows, w_down, preferred_element_type=full_type)
    primal_gate, gated_back = jax.vjp(gated, gate_pre, up_pre)
    grad_gpre, grad_upre = gated_back(grad_act)
    grad_gpre = grad_gpre.astype(low_type)
    grad_upre = grad_upre.astype(low_type)
    grad_wgate = jnp.einsum("lrd,lrf->dlf", received, grad_gpre, preferred_element_type=full_type)
    grad_wup = jnp.einsum("lrd,lrf->dlf", received, grad_upre, preferred_element_type=full_type)
    grad_recv = jnp.einsum("lrf,dlf->lrd", grad_gpre, w_gate, preferred_element_type=full_type)
    grad_recv = (
        grad_recv + jnp.einsum("lrf,dlf->lrd", grad_upre, w_up, preferred_element_type=full_type)
    ).astype(low_type)
    back_rows = lax.all_to_all(
        grad_recv.reshape(local_experts, n_expert, CAP, D),
        "expert",
        split_axis=1,
        concat_axis=1,
        tiled=True,
    )
    back_rows = back_rows.reshape(capacity_rows, D)
    grad_normed_two = jnp.sum(
        back_rows[destination].reshape(tokens, TOP, D).astype(full_type), axis=1
    )

    def gate_of(logit_rows):
        return gating(logit_rows, route_rows)

    primal_gates, gate_back = jax.vjp(gate_of, logits)
    grad_logits = gate_back(grad_gates)[0].astype(low_type)
    grad_wrouter = jnp.einsum(
        "td,te->de", normed_two, grad_logits, preferred_element_type=full_type
    )
    grad_normed_two = grad_normed_two + jnp.einsum(
        "te,de->td", grad_logits, w_router, preferred_element_type=full_type
    )
    primal_two, norm_back_two = jax.vjp(rms_scale, mid_rows, gain_two)
    grad_mid_norm, grad_gain_two = norm_back_two(grad_normed_two)
    grad_mid = grad_out + grad_mid_norm
    grad_attn = grad_mid.astype(low_type)
    grad_wout = jnp.einsum("td,te->de", attended_low, grad_attn, preferred_element_type=full_type)
    grad_attended = jnp.einsum(
        "te,de->td", grad_attn, w_out, preferred_element_type=full_type
    ).astype(low_type)
    grad_attended = grad_attended.reshape(tokens, KVH, group_width, HD)
    query_grads = []
    key_grads = []
    value_grads = []
    for kv_head in range(KVH):
        scores = jnp.einsum(
            "tgn,kn->gtk",
            queries[:, kv_head],
            all_keys[:, kv_head],
            preferred_element_type=full_type,
        )
        scores = jnp.where(allowed[None], scores, masked_score)
        exact_probs = jnp.exp(scores - log_totals[kv_head])
        grad_probs = jnp.einsum(
            "tgn,kn->gtk",
            grad_attended[:, kv_head],
            all_values[:, kv_head],
            preferred_element_type=full_type,
        )
        row_dots = jnp.sum(exact_probs * grad_probs, axis=-1, keepdims=True)
        grad_scores = (exact_probs * (grad_probs - row_dots)).astype(low_type)
        query_grads.append(
            jnp.einsum(
                "gtk,kn->tgn", grad_scores, all_keys[:, kv_head], preferred_element_type=full_type
            )
        )
        key_grads.append(
            jnp.einsum(
                "gtk,tgn->kn", grad_scores, queries[:, kv_head], preferred_element_type=full_type
            )
        )
        value_grads.append(
            jnp.einsum(
                "gtk,tgn->kn",
                exact_probs.astype(low_type),
                grad_attended[:, kv_head],
                preferred_element_type=full_type,
            )
        )
    grad_queries = jnp.stack(query_grads, axis=1).reshape(tokens, HEADS, HD)
    grad_keys = jnp.stack(key_grads, axis=1)
    grad_values = jnp.stack(value_grads, axis=1)
    prompt_key_grad, prompt_value_grad = (
        lax.psum_scatter(
            grad_keys[:prompt_len].astype(jnp.bfloat16), "context", scatter_dimension=0, tiled=True
        ).astype(jnp.float32),
        lax.psum_scatter(
            grad_values[:prompt_len].astype(jnp.bfloat16),
            "context",
            scatter_dimension=0,
            tiled=True,
        ).astype(jnp.float32),
    )
    own_key_grad = jnp.concatenate([prompt_key_grad, grad_keys[prompt_len:]], axis=0)
    own_value_grad = jnp.concatenate([prompt_value_grad, grad_values[prompt_len:]], axis=0)
    grad_qproj = (
        rotary(grad_queries * score_scale, angles, -1.0).reshape(tokens, D).astype(low_type)
    )
    grad_kproj = rotary(own_key_grad, angles, -1.0).reshape(tokens, KVH * HD).astype(low_type)
    grad_vproj = own_value_grad.reshape(tokens, KVH * HD).astype(low_type)
    grad_wquery = jnp.einsum("td,te->de", normed_one, grad_qproj, preferred_element_type=full_type)
    grad_wkey = jnp.einsum("td,te->de", normed_one, grad_kproj, preferred_element_type=full_type)
    grad_wvalue = jnp.einsum("td,te->de", normed_one, grad_vproj, preferred_element_type=full_type)
    grad_normed_one = jnp.einsum("te,de->td", grad_qproj, w_query, preferred_element_type=full_type)
    grad_normed_one = grad_normed_one + jnp.einsum(
        "te,de->td", grad_kproj, w_key, preferred_element_type=full_type
    )
    grad_normed_one = grad_normed_one + jnp.einsum(
        "te,de->td", grad_vproj, w_value, preferred_element_type=full_type
    )
    primal_one, norm_back_one = jax.vjp(rms_scale, x_rows, gain_one)
    grad_x_norm, grad_gain_one = norm_back_one(grad_normed_one)
    grad_inputs = (grad_mid + grad_x_norm).astype(low_type)
    shares = (
        lax.psum_scatter(
            grad_wquery.astype(jnp.bfloat16), "dp", scatter_dimension=0, tiled=True
        ).astype(jnp.float32),
        lax.psum_scatter(
            grad_wkey.astype(jnp.bfloat16), "dp", scatter_dimension=0, tiled=True
        ).astype(jnp.float32),
        lax.psum_scatter(
            grad_wvalue.astype(jnp.bfloat16), "dp", scatter_dimension=0, tiled=True
        ).astype(jnp.float32),
        lax.psum_scatter(
            grad_wout.astype(jnp.bfloat16), "dp", scatter_dimension=0, tiled=True
        ).astype(jnp.float32),
        lax.psum_scatter(
            grad_gain_one.astype(jnp.bfloat16), "dp", scatter_dimension=0, tiled=True
        ).astype(jnp.float32),
        lax.psum_scatter(
            grad_gain_two.astype(jnp.bfloat16), "dp", scatter_dimension=0, tiled=True
        ).astype(jnp.float32),
        lax.psum_scatter(
            grad_wrouter.astype(jnp.bfloat16), "dp", scatter_dimension=0, tiled=True
        ).astype(jnp.float32),
        lax.psum_scatter(
            grad_wgate.astype(jnp.bfloat16), "dp", scatter_dimension=0, tiled=True
        ).astype(jnp.float32),
        lax.psum_scatter(
            grad_wup.astype(jnp.bfloat16), "dp", scatter_dimension=0, tiled=True
        ).astype(jnp.float32),
        lax.psum_scatter(
            grad_wdown.astype(jnp.bfloat16), "dp", scatter_dimension=0, tiled=True
        ).astype(jnp.float32),
    )
    dense_sum = lax.psum(
        (shares[0], shares[1], shares[2], shares[3], shares[4], shares[5], shares[6]),
        ("expert", "context"),
    )
    expert_sum = (
        lax.psum(shares[7].astype(jnp.bfloat16), "context").astype(jnp.float32),
        lax.psum(shares[8].astype(jnp.bfloat16), "context").astype(jnp.float32),
        lax.psum(shares[9].astype(jnp.bfloat16), "context").astype(jnp.float32),
    )
    totals_all = tuple(dense_sum) + tuple(expert_sum)
    return (
        result[None],
        grad_inputs[None],
        totals_all[0],
        totals_all[1],
        totals_all[2],
        totals_all[3],
        totals_all[4],
        totals_all[5],
        totals_all[6],
        totals_all[7],
        totals_all[8],
        totals_all[9],
    )


BF = jnp.bfloat16
F32 = jnp.float32
SLOTS = 112
MESH_ID = pl.DeviceIdType.MESH
PLANE = ("expert", "context")
VMEM_BYTES = 60 * 1024 * 1024


def mxu(lhs, rhs, contract=((1,), (0,))):
    return lax.dot_general(lhs, rhs, (contract, ((), ())), preferred_element_type=F32)


def grant(bytes_wanted=VMEM_BYTES):
    return pltpu.CompilerParams(vmem_limit_bytes=bytes_wanted)


def turn(values, cosine, sine):
    return values * cosine + pltpu.roll(values, HD // 2, 1) * sine


def project_kernel(x_ref, gain_ref, w_ref, cos_ref, sin_ref, out_ref, normed_ref):
    step = pl.program_id(0)

    @pl.when(step == 0)
    def _():
        rows = x_ref[...].astype(F32)
        scale = lax.rsqrt(jnp.mean(rows * rows, axis=-1, keepdims=True) + epsilon)
        normed_ref[...] = (rows * scale * gain_ref[...]).astype(BF)

    product = mxu(normed_ref[...], w_ref[...])
    is_query = step < HEADS // 2
    is_value = step == HEADS // 2 + KVH // 2
    cosine = jnp.where(is_value, 1.0, cos_ref[...])
    sine = jnp.where(is_value, 0.0, sin_ref[...])
    factor = jnp.where(is_query, 1.0 / math.sqrt(HD), 1.0)
    for half in range(2):
        part = product[:, half * HD : (half + 1) * HD]
        out_ref[:, half * HD : (half + 1) * HD] = (turn(part, cosine, sine) * factor).astype(BF)


def project(x_low, gain, w_qkv, cosine, sine):
    tokens, width = x_low.shape[0], w_qkv.shape[1]
    whole = lambda j: (0, 0)
    return pl.pallas_call(
        project_kernel,
        grid=(width // (2 * HD),),
        in_specs=[
            pl.BlockSpec((tokens, D), whole),
            pl.BlockSpec((1, D), whole),
            pl.BlockSpec((D, 2 * HD), lambda j: (0, j)),
            pl.BlockSpec((tokens, HD), whole),
            pl.BlockSpec((tokens, HD), whole),
        ],
        out_specs=[
            pl.BlockSpec((tokens, 2 * HD), lambda j: (0, j)),
            pl.BlockSpec((tokens, D), whole),
        ],
        out_shape=[
            jax.ShapeDtypeStruct((tokens, width), BF),
            jax.ShapeDtypeStruct((tokens, D), BF),
        ],
        compiler_params=grant(),
        name="project",
    )(x_low, gain, w_qkv, cosine, sine)


def row_blocks(prompt_len):
    blocks = [(0, prompt_len)]
    for start in range(0, CONT, PBLK):
        blocks.append((PBLK + start, prompt_len + start + PBLK))
    return blocks


def masked_scores(scores, first_row, prompt_len, block_index):
    row = lax.broadcasted_iota(jnp.int32, scores.shape, 0)
    column = lax.broadcasted_iota(jnp.int32, scores.shape, 1)
    if first_row == 0:
        limit = row + block_index * PBLK
    else:
        limit = row + (prompt_len + first_row - PBLK)
    return jnp.where(column <= limit, scores, masked_score)


def attend_kernel(prompt_len, block_ref, q_ref, k_ref, v_ref, out_ref, log_ref):
    for first_row, keys in row_blocks(prompt_len):
        rows = slice(first_row, first_row + PBLK)
        scores = mxu(q_ref[rows, :], k_ref[:keys, :], ((1,), (1,)))
        scores = masked_scores(scores, first_row, prompt_len, block_ref[0])
        top = jnp.max(scores, axis=-1, keepdims=True)
        unnormed = jnp.exp(scores - top)
        total = jnp.sum(unnormed, axis=-1, keepdims=True)
        mixed = mxu(unnormed.astype(BF), v_ref[:keys, :]) / total
        out_ref[rows, :] = mixed.astype(BF)
        log_ref[0, rows, :] = top + jnp.log(total)


def attend(block_index, qkv, keys_values, prompt_len):
    tokens, key_rows = qkv.shape[0], keys_values.shape[0]
    width = HEADS // KVH
    return pl.pallas_call(
        functools.partial(attend_kernel, prompt_len),
        grid=(HEADS,),
        in_specs=[
            pl.BlockSpec(memory_space=pltpu.SMEM),
            pl.BlockSpec((tokens, HD), lambda h: (0, h)),
            pl.BlockSpec((key_rows, HD), lambda h: (0, h // width)),
            pl.BlockSpec((key_rows, HD), lambda h: (0, KVH + h // width)),
        ],
        out_specs=[
            pl.BlockSpec((tokens, HD), lambda h: (0, h)),
            pl.BlockSpec((1, tokens, 1), lambda h: (h, 0, 0)),
        ],
        out_shape=[
            jax.ShapeDtypeStruct((tokens, D), BF),
            jax.ShapeDtypeStruct((HEADS, tokens, 1), F32),
        ],
        compiler_params=grant(),
        name="attend",
    )(block_index, qkv, keys_values, keys_values)


def attend_back_kernel(
    prompt_len, block_ref, q_ref, k_ref, v_ref, do_ref, log_ref, cos_ref, sin_ref, dq_ref, dk_ref, dv_ref
):
    @pl.when(pl.program_id(1) == 0)
    def _():
        dk_ref[...] = jnp.zeros_like(dk_ref)
        dv_ref[...] = jnp.zeros_like(dv_ref)

    for first_row, keys in row_blocks(prompt_len):
        rows = slice(first_row, first_row + PBLK)
        queries, grads = q_ref[rows, :], do_ref[rows, :]
        scores = mxu(queries, k_ref[:keys, :], ((1,), (1,)))
        scores = masked_scores(scores, first_row, prompt_len, block_ref[0])
        probs = jnp.exp(scores - log_ref[0, rows, :])
        grad_probs = mxu(grads, v_ref[:keys, :], ((1,), (1,)))
        dots = jnp.sum(probs * grad_probs, axis=-1, keepdims=True)
        grad_scores = (probs * (grad_probs - dots)).astype(BF)
        grad_query = mxu(grad_scores, k_ref[:keys, :])
        grad_query = turn(grad_query, cos_ref[rows, :], -sin_ref[rows, :]) * (1.0 / math.sqrt(HD))
        dq_ref[rows, :] = grad_query.astype(BF)
        dk_ref[:keys, :] += mxu(grad_scores, queries, ((0,), (0,)))
        dv_ref[:keys, :] += mxu(probs.astype(BF), grads, ((0,), (0,)))


def attend_back(block_index, qkv, keys_values, grad_heads, logs, cosine, sine, prompt_len):
    tokens, key_rows = qkv.shape[0], keys_values.shape[0]
    width = HEADS // KVH
    head = lambda i, g: (0, i * width + g)
    whole = lambda i, g: (0, 0)
    return pl.pallas_call(
        functools.partial(attend_back_kernel, prompt_len),
        grid=(KVH, width),
        in_specs=[
            pl.BlockSpec(memory_space=pltpu.SMEM),
            pl.BlockSpec((tokens, HD), head),
            pl.BlockSpec((key_rows, HD), lambda i, g: (0, i)),
            pl.BlockSpec((key_rows, HD), lambda i, g: (0, KVH + i)),
            pl.BlockSpec((tokens, HD), head),
            pl.BlockSpec((1, tokens, 1), lambda i, g: (i * width + g, 0, 0)),
            pl.BlockSpec((tokens, HD), whole),
            pl.BlockSpec((tokens, HD), whole),
        ],
        out_specs=[
            pl.BlockSpec((tokens, HD), head),
            pl.BlockSpec((key_rows, HD), lambda i, g: (0, i)),
            pl.BlockSpec((key_rows, HD), lambda i, g: (0, i)),
        ],
        out_shape=[
            jax.ShapeDtypeStruct((tokens, D), BF),
            jax.ShapeDtypeStruct((key_rows, KVH * HD), F32),
            jax.ShapeDtypeStruct((key_rows, KVH * HD), F32),
        ],
        compiler_params=grant(),
        name="attend_back",
    )(block_index, qkv, keys_values, keys_values, grad_heads, logs, cosine, sine)


def segment_matrix(parts, transposed):
    shape = (parts * SLOTS, parts) if transposed else (parts, parts * SLOTS)
    long = lax.broadcasted_iota(jnp.int32, shape, 0 if transposed else 1)
    short = lax.broadcasted_iota(jnp.int32, shape, 1 if transposed else 0)
    inside = (long >= short * SLOTS) & (long < (short + 1) * SLOTS)
    return jnp.where(inside, 1.0, 0.0).astype(BF)


def slot_matrix(ranks, parts, transposed):
    if transposed:
        spread = mxu(segment_matrix(parts, True), ranks)
        slot = lax.broadcasted_iota(jnp.int32, (parts * SLOTS, 1), 0)
    else:
        spread = mxu(ranks, segment_matrix(parts, False))
        slot = lax.broadcasted_iota(jnp.int32, (1, parts * SLOTS), 1)
    for part in range(parts - 1, 0, -1):
        slot = jnp.where(slot >= part * SLOTS, slot - SLOTS, slot)
    return jnp.where(spread == slot.astype(F32), 1.0, 0.0).astype(BF)


def spread_kernel(parts, rank0_ref, rank1_ref, rows_ref, out0_ref, out1_ref):
    for rank_ref, out_ref in ((rank0_ref, out0_ref), (rank1_ref, out1_ref)):
        chooser = slot_matrix(rank_ref[0], parts, True)
        out_ref[...] = mxu(chooser, rows_ref[...]).astype(BF)


def spread_rows(rank0, rank1, rows):
    dests, tokens = rank0.shape
    steps = 2
    parts = dests // steps
    rank0 = rank0.reshape(steps, parts, tokens)
    rank1 = rank1.reshape(steps, parts, tokens)
    ranks = pl.BlockSpec((1, parts, tokens), lambda j: (j, 0, 0))
    block = pl.BlockSpec((parts * SLOTS, D), lambda j: (j, 0))
    shape = jax.ShapeDtypeStruct((dests * SLOTS, D), BF)
    return pl.pallas_call(
        functools.partial(spread_kernel, parts),
        grid=(steps,),
        in_specs=[ranks, ranks, pl.BlockSpec((tokens, D), lambda j: (0, 0))],
        out_specs=[block, block],
        out_shape=[shape, shape],
        compiler_params=grant(),
        name="spread_rows",
    )(rank0, rank1, rows)


def collect_kernel(parts, rank0_ref, rank1_ref, rows0_ref, rows1_ref, out_ref):
    total = mxu(slot_matrix(rank0_ref[...], parts, False), rows0_ref[...])
    total = total + mxu(slot_matrix(rank1_ref[...], parts, False), rows1_ref[...])
    out_ref[...] = total.astype(out_ref.dtype)


def collect_rows(rank0, rank1, rows0, rows1, kind):
    tokens, dests = rank0.shape
    step = PBLK
    ranks = pl.BlockSpec((step, dests), lambda j: (j, 0))
    slots = pl.BlockSpec((dests * SLOTS, D), lambda j: (0, 0))
    return pl.pallas_call(
        functools.partial(collect_kernel, dests),
        grid=(tokens // step,),
        in_specs=[ranks, ranks, slots, slots],
        out_specs=pl.BlockSpec((step, D), lambda j: (j, 0)),
        out_shape=jax.ShapeDtypeStruct((tokens, D), kind),
        compiler_params=grant(),
        name="collect_rows",
    )(rank0, rank1, rows0, rows1)


def expert_kernel(n_dp, half_steps, *refs):
    (z_ref, xo_ref, xp_ref, go_ref, gp_ref, so_ref, sp_ref) = refs[:7]
    pieces = refs[7 : 7 + 3 * n_dp]
    outs = refs[7 + 3 * n_dp :]
    (yo_ref, yp_ref, bo_ref, bp_ref, do_ref, dp_ref, xc_ref, a_ref, dg_ref, du_ref, de_ref) = outs[:11]
    weights = outs[11:]
    wg_ref, wu_ref, wd_ref = weights
    step = pl.program_id(0)
    own = step < half_steps

    @pl.when(step == 0)
    def _():
        for which in range(3):
            for flip in range(n_dp):
                piece = pieces[which * n_dp + flip]
                size = piece.shape[1]
                start = pl.multiple_of((z_ref[0] ^ flip) * size, 64)
                weights[which][pl.ds(start, size), :] = piece[0]

    rows = jnp.where(own, xo_ref[...], xp_ref[...])
    cot = jnp.where(own, go_ref[...], gp_ref[...])
    share = jnp.where(own, so_ref[...], sp_ref[...])
    xc_ref[...] = rows
    gate_pre = mxu(rows, wg_ref[...])
    up_pre = mxu(rows, wu_ref[...])
    sigma = 1.0 / (1.0 + jnp.exp(-gate_pre))
    silu = gate_pre * sigma
    act = (silu * up_pre).astype(BF)
    a_ref[...] = act
    cot_full = cot.astype(F32)
    weighted = (cot_full * share).astype(BF)
    de_ref[...] = weighted
    result = mxu(act, wd_ref[...])
    dots = jnp.sum(result.astype(BF).astype(F32) * cot_full, axis=-1, keepdims=True)
    scaled = (result * share).astype(BF)
    grad_act = mxu(weighted, wd_ref[...], ((1,), (1,)))
    grad_gate = (grad_act * up_pre * sigma * (1.0 + gate_pre * (1.0 - sigma))).astype(BF)
    grad_up = (grad_act * silu).astype(BF)
    dg_ref[...] = grad_gate
    du_ref[...] = grad_up
    back = mxu(grad_gate, wg_ref[...], ((1,), (1,))) + mxu(grad_up, wu_ref[...], ((1,), (1,)))
    back = back.astype(BF)

    @pl.when(own)
    def _():
        yo_ref[...] = scaled
        bo_ref[...] = back
        do_ref[...] = dots

    @pl.when(jnp.logical_not(own))
    def _():
        yp_ref[...] = scaled
        bp_ref[...] = back
        dp_ref[...] = dots


def run_expert(which, z_index, x_own, x_par, g_own, g_par, s_own, s_par, gate_pieces, up_pieces, down_pieces):
    half_rows = x_own.shape[0]
    step_rows = half_rows // 2
    half_steps = 2
    n_dp = len(gate_pieces)
    full_hidden = gate_pieces[0].shape[2]
    own_map = lambda j: (jnp.minimum(j, half_steps - 1), 0)
    par_map = lambda j: (jnp.maximum(j - half_steps, 0), 0)
    all_map = lambda j: (j, 0)
    piece_map = lambda j: (which, 0, 0)

    def pair(width):
        return [pl.BlockSpec((step_rows, width), own_map), pl.BlockSpec((step_rows, width), par_map)]

    def piece_specs(pieces):
        return [
            pl.BlockSpec((1,) + p.shape[1:], piece_map, pipeline_mode=pl.Buffered(1)) for p in pieces
        ]

    wide = pl.BlockSpec((step_rows, D), all_map)
    narrow = pl.BlockSpec((step_rows, full_hidden), all_map)
    half_shape = jax.ShapeDtypeStruct((half_rows, D), BF)
    dot_shape = jax.ShapeDtypeStruct((half_rows, 1), F32)
    wide_shape = jax.ShapeDtypeStruct((2 * half_rows, D), BF)
    narrow_shape = jax.ShapeDtypeStruct((2 * half_rows, full_hidden), BF)
    return pl.pallas_call(
        functools.partial(expert_kernel, n_dp, half_steps),
        grid=(2 * half_steps,),
        in_specs=[pl.BlockSpec(memory_space=pltpu.SMEM)]
        + pair(D)
        + pair(D)
        + pair(1)
        + piece_specs(gate_pieces)
        + piece_specs(up_pieces)
        + piece_specs(down_pieces),
        out_specs=pair(D) + pair(D) + pair(1) + [wide, narrow, narrow, narrow, wide],
        out_shape=[half_shape] * 4
        + [dot_shape] * 2
        + [wide_shape, narrow_shape, narrow_shape, narrow_shape, wide_shape],
        scratch_shapes=[
            pltpu.VMEM((D, full_hidden), BF),
            pltpu.VMEM((D, full_hidden), BF),
            pltpu.VMEM((full_hidden, D), BF),
        ],
        compiler_params=grant(62 * 1024 * 1024),
        name="experts",
    )(z_index, x_own, x_par, g_own, g_par, s_own, s_par, *gate_pieces, *up_pieces, *down_pieces)


def plane_peer(index):
    n_context = lax.axis_size("context")
    return {"expert": index // n_context, "context": index % n_context}


def plane_here():
    return lax.axis_index("expert") * lax.axis_size("context") + lax.axis_index("context")


def greet(peers):
    barrier = pltpu.get_barrier_semaphore()
    for peer in peers:
        pl.semaphore_signal(barrier, inc=1, device_id=peer, device_id_type=MESH_ID)
    pl.semaphore_wait(barrier, len(peers))


def plane_and_partner(plane):
    here = plane_here()
    return [plane_peer(here ^ flip) for flip in range(1, plane)] + [{"dp": lax.axis_index("dp") ^ 1}]


def remote(source, target, send, receive, peer):
    return pltpu.make_async_remote_copy(
        src_ref=source,
        dst_ref=target,
        send_sem=send,
        recv_sem=receive,
        device_id=peer,
        device_id_type=MESH_ID,
    )


def gather_kernel(
    n_dp, in_ref, out_part_ref, whole_ref, out_ref, local_sems, z_send, o_send, o_recv, sends, recvs
):
    here = plane_here()
    z_index = lax.axis_index("dp")
    z_peer = lambda flip: {"dp": z_index ^ flip}
    greet([z_peer(flip) for flip in range(1, n_dp)] + [plane_peer(here ^ flip) for flip in (1, 2, 4)])
    keep = [
        pltpu.make_async_copy(in_ref, whole_ref.at[z_index, here], local_sems.at[0]),
        pltpu.make_async_copy(out_part_ref, out_ref.at[z_index], local_sems.at[1]),
    ]
    for copy in keep:
        copy.start()
    started = []
    for flip in range(1, n_dp):
        started.append(
            remote(in_ref, whole_ref.at[z_index, here], z_send.at[flip], recvs.at[z_index, here], z_peer(flip))
        )
        started[-1].start()
    for flip in range(1, n_dp):
        started.append(
            remote(out_part_ref, out_ref.at[z_index], o_send.at[flip], o_recv.at[z_index], z_peer(flip))
        )
        started[-1].start()

    def pass_on(lane, flip, z_from, place, source=None):
        block = whole_ref.at[z_from, place]
        move = remote(
            block if source is None else source,
            block,
            sends.at[lane, z_from, place],
            recvs.at[z_from, place],
            plane_peer(here ^ flip),
        )
        move.start()
        started.append(move)

    def landed(z_from, place):
        block = whole_ref.at[z_from, place]
        remote(block, block, z_send.at[0], recvs.at[z_from, place], z_peer(1)).wait_recv()

    froms = [z_index ^ flip for flip in range(n_dp)]
    for n, z_from in enumerate(froms):
        if n > 0:
            landed(z_from, here)
        source = in_ref if n == 0 else None
        pass_on(0, 2, z_from, here, source)
        pass_on(1, 4, z_from, here, source)
        pass_on(2, 1, z_from, here, source)
    for n, z_from in enumerate(froms):
        landed(z_from, here ^ 2)
        if n % 2 == 1:
            pass_on(1, 4, z_from, here ^ 2)
        pass_on(2, 1, z_from, here ^ 2)
        landed(z_from, here ^ 4)
        if n % 2 == 0:
            pass_on(0, 2, z_from, here ^ 4)
        pass_on(2, 1, z_from, here ^ 4)
    for z_from in froms:
        landed(z_from, here ^ 6)
        pass_on(2, 1, z_from, here ^ 6)
    for place in (1, 3, 5, 7):
        for z_from in froms:
            landed(z_from, here ^ place)
    for flip in range(1, n_dp):
        z_from = z_index ^ flip
        remote(out_part_ref, out_ref.at[z_from], o_send.at[0], o_recv.at[z_from], z_peer(1)).wait_recv()
    for move in started:
        move.wait_send()
    for copy in keep:
        copy.wait()


def gather_parts(part_in, part_out, n_dp, plane):
    anywhere = pl.BlockSpec(memory_space=pl.ANY)
    return pl.pallas_call(
        functools.partial(gather_kernel, n_dp),
        in_specs=[anywhere] * 2,
        out_specs=[anywhere] * 2,
        out_shape=[
            jax.ShapeDtypeStruct((n_dp, plane) + part_in.shape, BF),
            jax.ShapeDtypeStruct((n_dp,) + part_out.shape, BF),
        ],
        scratch_shapes=[
            pltpu.SemaphoreType.DMA((2,)),
            pltpu.SemaphoreType.DMA((n_dp,)),
            pltpu.SemaphoreType.DMA((n_dp,)),
            pltpu.SemaphoreType.DMA((n_dp,)),
            pltpu.SemaphoreType.DMA((3, n_dp, plane)),
            pltpu.SemaphoreType.DMA((n_dp, plane)),
        ],
        compiler_params=pltpu.CompilerParams(collective_id=3, has_side_effects=True),
        name="gather_parts",
    )(part_in, part_out)


RIDING = ((0, 2), (1, 1), (1, 2), (1, 3), (2, 1), (2, 2), (2, 3))


def dispatch_kernel(
    plane,
    n_dp,
    normed_ref,
    cot_ref,
    cot_partner_ref,
    own_rank_ref,
    partner_rank_ref,
    *refs,
):
    riders = len(RIDING)
    sources, refs = refs[:riders], refs[riders:]
    outs, targets, refs = refs[:8], refs[8 : 8 + riders], refs[8 + riders :]
    stage, normed_partner, pair_sems, local_sems, send_sems, recv_sems, ride_send, ride_recv = refs
    z_index = lax.axis_index("dp")
    here = plane_here()
    partner = {"dp": lax.axis_index("dp") ^ 1}
    greet(plane_and_partner(plane) + [{"dp": z_index ^ flip} for flip in range(2, n_dp)])
    pair = remote(normed_ref, normed_partner, pair_sems.at[0], pair_sems.at[1], partner)
    pair.start()
    rides = [
        remote(source, target, ride_send.at[n], ride_recv.at[n], {"dp": z_index ^ flip})
        for n, (source, target, (_, flip)) in enumerate(zip(sources, targets, RIDING))
    ]
    for ride in rides:
        ride.start()
    plans = (
        (0, normed_ref, own_rank_ref),
        (2, cot_ref, own_rank_ref),
        (6, cot_partner_ref, partner_rank_ref),
        (4, normed_partner, partner_rank_ref),
    )
    for base, rows_ref, rank_ref in plans:
        if base == 4:
            pair.wait()
        for expert in range(2):
            slot = base + expert
            chooser = slot_matrix(rank_ref[expert], plane, True)
            stage[slot] = mxu(chooser, rows_ref[...]).astype(BF).reshape(plane, SLOTS, D)
            pltpu.make_async_copy(stage.at[slot, here], outs[slot].at[here], local_sems.at[slot]).start()

            def begin(flip, carry):
                peer = here ^ flip
                remote(
                    stage.at[slot, peer],
                    outs[slot].at[here],
                    send_sems.at[slot, peer],
                    recv_sems.at[slot, here],
                    plane_peer(peer),
                ).start()
                return carry

            lax.fori_loop(1, plane, begin, 0)
    for slot in range(8):
        pltpu.make_async_copy(stage.at[slot, here], outs[slot].at[here], local_sems.at[slot]).wait()

        def finish(flip, carry):
            peer = here ^ flip
            done = remote(
                stage.at[slot, peer],
                outs[slot].at[peer],
                send_sems.at[slot, peer],
                recv_sems.at[slot, peer],
                plane_peer(peer),
            )
            done.wait_send()
            done.wait_recv()
            return carry

        lax.fori_loop(1, plane, finish, 0)
    for ride in rides:
        ride.wait()


def dispatch_rows(normed, cot, cot_partner, own_ranks, partner_ranks, riders, n_dp):
    plane, tokens = own_ranks.shape[1:]
    vmem = pl.BlockSpec(memory_space=pltpu.VMEM)
    anywhere = pl.BlockSpec(memory_space=pl.ANY)
    return pl.pallas_call(
        functools.partial(dispatch_kernel, plane, n_dp),
        in_specs=[vmem] * 5 + [anywhere] * len(riders),
        out_specs=[anywhere] * (8 + len(riders)),
        out_shape=[jax.ShapeDtypeStruct((plane, SLOTS, D), BF)] * 8
        + [jax.ShapeDtypeStruct(rider.shape, rider.dtype) for rider in riders],
        scratch_shapes=[
            pltpu.VMEM((8, plane, SLOTS, D), BF),
            pltpu.VMEM((tokens, D), BF),
            pltpu.SemaphoreType.DMA((2,)),
            pltpu.SemaphoreType.DMA((8,)),
            pltpu.SemaphoreType.DMA((8, plane)),
            pltpu.SemaphoreType.DMA((8, plane)),
            pltpu.SemaphoreType.DMA((len(riders),)),
            pltpu.SemaphoreType.DMA((len(riders),)),
        ],
        compiler_params=pltpu.CompilerParams(
            vmem_limit_bytes=VMEM_BYTES, collective_id=1, has_side_effects=True
        ),
        cost_estimate=pl.CostEstimate(flops=2 * 10**10, bytes_accessed=7 * 10**8, transcendentals=0),
        name="dispatch_rows",
    )(normed, cot, cot_partner, own_ranks, partner_ranks, *riders)


HOMING = ((0, 2), (0, 3), (1, 2), (0, 1))


def return_kernel(plane, n_dp, own_rank_ref, partner_rank_ref, *refs):
    back = refs[:4]
    operands = (refs[4:9], refs[9:14])
    total_ref, gate_ref, up_ref, down_ref = refs[14:18]
    homes = refs[18 : 18 + len(HOMING)]
    (
        held,
        to_partner,
        of_partner,
        rows_buf,
        weighted_buf,
        act_buf,
        grad_gate_buf,
        grad_up_buf,
        stage,
        load_sems,
        store_sems,
        pair_sems,
        local_sems,
        send_sems,
        recv_sems,
        home_send,
        home_recv,
    ) = refs[18 + len(HOMING) :]
    here = plane_here()
    z_index = lax.axis_index("dp")
    greet(plane_and_partner(plane) + [{"dp": z_index ^ flip} for flip in range(2, n_dp)])
    share_refs = (gate_ref, up_ref, down_ref)
    homing = [
        remote(
            share_refs[which].at[flip],
            home,
            home_send.at[n],
            home_recv.at[n],
            {"dp": z_index ^ flip},
        )
        for n, (home, (which, flip)) in enumerate(zip(homes, HOMING))
    ]

    order = [(side, expert) for side in (1, 0) for expert in range(2)]
    for side, expert in order:
        slot = 2 * side + expert
        source = back[2 * expert + side]
        pltpu.make_async_copy(source.at[here], held.at[slot, here], local_sems.at[slot]).start()

        def begin(flip, carry):
            peer = here ^ flip
            remote(
                source.at[peer],
                held.at[slot, here],
                send_sems.at[slot, peer],
                recv_sems.at[slot, here],
                plane_peer(peer),
            ).start()
            return carry

        lax.fori_loop(1, plane, begin, 0)

    def send_home(which):
        for move, (matrix, _) in zip(homing, HOMING):
            if matrix == which:
                move.start()

    buffers = (rows_buf, weighted_buf, act_buf, grad_gate_buf, grad_up_buf)
    quarter = D // n_dp
    for expert in range(2):
        loads = [
            pltpu.make_async_copy(source, buffer, load_sems.at[n])
            for n, (source, buffer) in enumerate(zip(operands[expert], buffers))
        ]
        for load in loads:
            load.start()
        for load in loads:
            load.wait()

        def of_rows(q, carry):
            columns = pl.ds(pl.multiple_of(q * quarter, 128), quarter)
            place = z_index ^ q
            for n, (grad_buf, out_ref) in enumerate(((grad_gate_buf, gate_ref), (grad_up_buf, up_ref))):
                made = mxu(rows_buf[:, columns], grad_buf[...], ((0,), (0,)))
                stage[n] = made.astype(BF)
                pltpu.make_async_copy(stage.at[n], out_ref.at[place, expert], store_sems.at[n]).start()
            for n, out_ref in enumerate((gate_ref, up_ref)):
                pltpu.make_async_copy(stage.at[n], out_ref.at[place, expert], store_sems.at[n]).wait()
            return carry

        lax.fori_loop(0, n_dp, of_rows, 0)
        if expert == 1:
            send_home(0)
            send_home(1)

        width = act_buf.shape[1]
        rows = width // n_dp
        for q in range(0, n_dp, 2):
            made = mxu(act_buf[:, q * rows : (q + 2) * rows], weighted_buf[...], ((0,), (0,))).astype(BF)
            stores = []
            for half in range(2):
                part = made[half * rows : (half + 1) * rows]
                stage[half, :rows] = part[:, :width]
                stage[half, rows:] = part[:, width:]
                place = z_index ^ (q + half)
                stores.append(
                    pltpu.make_async_copy(stage.at[half], down_ref.at[place, expert], store_sems.at[half])
                )
                stores[-1].start()
            for store in stores:
                store.wait()
    send_home(2)

    def arrive(side):
        for expert in range(2):
            slot = 2 * side + expert
            source = back[2 * expert + side]
            pltpu.make_async_copy(source.at[here], held.at[slot, here], local_sems.at[slot]).wait()

            def finish(flip, carry):
                peer = here ^ flip
                done = remote(
                    source.at[peer],
                    held.at[slot, peer],
                    send_sems.at[slot, peer],
                    recv_sems.at[slot, peer],
                    plane_peer(peer),
                )
                done.wait_send()
                done.wait_recv()
                return carry

            lax.fori_loop(1, plane, finish, 0)

    def collect(rank_ref, side, target, kind):
        def block(n, carry):
            rows = pl.ds(pl.multiple_of(n * PBLK, PBLK), PBLK)
            made = jnp.zeros((PBLK, D), F32)
            for expert in range(2):
                chooser = slot_matrix(rank_ref[expert, rows, :], plane, False)
                made = made + mxu(chooser, held[2 * side + expert].reshape(plane * SLOTS, D))
            target[rows, :] = made.astype(kind)
            return carry

        lax.fori_loop(0, total_ref.shape[0] // PBLK, block, 0)

    arrive(1)
    collect(partner_rank_ref, 1, to_partner, BF)
    pair = remote(to_partner, of_partner, pair_sems.at[0], pair_sems.at[1], {"dp": z_index ^ 1})
    pair.start()
    arrive(0)
    collect(own_rank_ref, 0, total_ref, F32)
    pair.wait()
    total_ref[...] += of_partner[...].astype(F32)
    for move in homing:
        move.wait()


def return_rows(own_ranks, partner_ranks, back, operands, n_dp):
    tokens, plane = own_ranks.shape[1:]
    slot_rows, hidden = operands[0][2].shape
    quarter = D // n_dp
    vmem = pl.BlockSpec(memory_space=pltpu.VMEM)
    anywhere = pl.BlockSpec(memory_space=pl.ANY)
    shares = jax.ShapeDtypeStruct((n_dp, 2, quarter, hidden), BF)
    return pl.pallas_call(
        functools.partial(return_kernel, plane, n_dp),
        in_specs=[vmem, vmem] + [anywhere] * 14,
        out_specs=[vmem] + [anywhere] * (3 + len(HOMING)),
        out_shape=[jax.ShapeDtypeStruct((tokens, D), F32), shares, shares, shares]
        + [jax.ShapeDtypeStruct(shares.shape[1:], BF)] * len(HOMING),
        scratch_shapes=[
            pltpu.VMEM((4, plane, SLOTS, D), BF),
            pltpu.VMEM((tokens, D), BF),
            pltpu.VMEM((tokens, D), BF),
            pltpu.VMEM((slot_rows, D), BF),
            pltpu.VMEM((slot_rows, D), BF),
            pltpu.VMEM((slot_rows, hidden), BF),
            pltpu.VMEM((slot_rows, hidden), BF),
            pltpu.VMEM((slot_rows, hidden), BF),
            pltpu.VMEM((2, quarter, hidden), BF),
            pltpu.SemaphoreType.DMA((5,)),
            pltpu.SemaphoreType.DMA((2,)),
            pltpu.SemaphoreType.DMA((2,)),
            pltpu.SemaphoreType.DMA((4,)),
            pltpu.SemaphoreType.DMA((4, plane)),
            pltpu.SemaphoreType.DMA((4, plane)),
            pltpu.SemaphoreType.DMA((len(HOMING),)),
            pltpu.SemaphoreType.DMA((len(HOMING),)),
        ],
        compiler_params=pltpu.CompilerParams(
            vmem_limit_bytes=VMEM_BYTES, collective_id=2, has_side_effects=True
        ),
        cost_estimate=pl.CostEstimate(flops=3 * 10**10, bytes_accessed=4 * 10**8, transcendentals=0),
        name="return_rows",
    )(own_ranks, partner_ranks, *back, *operands[0], *operands[1])


def finish_kernel(in_ref, out_ref):
    out_ref[...] = jnp.swapaxes(in_ref[...].astype(F32), 0, 1)


def finish_down_kernel(in_ref, out_ref):
    half = out_ref.shape[2] // 2
    for side in range(2):
        out_ref[:, :, side * half : (side + 1) * half] = jnp.swapaxes(in_ref[:, side].astype(F32), 0, 1)


def finish_weight(parts, down):
    experts, rows, width = parts.shape
    step = 32
    if down:
        rows = rows // 2
        parts = parts.reshape(experts, 2, rows, width)
        spec = pl.BlockSpec((experts, 2, step, width), lambda j: (0, 0, j, 0))
        width = 2 * width
    else:
        spec = pl.BlockSpec((experts, step, width), lambda j: (0, j, 0))
    return pl.pallas_call(
        finish_down_kernel if down else finish_kernel,
        grid=(rows // step,),
        in_specs=[spec],
        out_specs=pl.BlockSpec((step, experts, width), lambda j: (j, 0, 0)),
        out_shape=jax.ShapeDtypeStruct((rows, experts, width), F32),
        compiler_params=grant(),
        name="finish_weight",
    )(parts)


def tie(*values):
    return lax.optimization_barrier(values)


def flip_permute(value, axis, size, flip):
    return lax.ppermute(value, axis, [(i, i ^ flip) for i in range(size)])


def plane_exchange(rows):
    plane = lax.axis_size("expert") * lax.axis_size("context")
    parted = rows.reshape(plane, rows.shape[0] // plane, *rows.shape[1:])
    moved = lax.all_to_all(parted, PLANE, split_axis=0, concat_axis=0, tiled=True)
    return moved.reshape(rows.shape)


def gather_dense(shard):
    n_context, n_expert = lax.axis_size("context"), lax.axis_size("expert")
    plane = n_context * n_expert
    here = lax.axis_index("expert") * n_context + lax.axis_index("context")
    rows = shard.shape[0] // plane
    part = lax.dynamic_slice_in_dim(shard, here * rows, rows, 0)
    part = lax.all_gather(part, "dp", axis=0, tiled=False)
    whole = lax.all_gather(part, PLANE, axis=1, tiled=False)
    return whole.reshape(-1, shard.shape[1])


def scatter_dense(share):
    n_context, n_expert, n_dp = lax.axis_size("context"), lax.axis_size("expert"), lax.axis_size("dp")
    plane = n_context * n_expert
    width = share.shape[1]
    rows = share.shape[0] // (plane * n_dp)
    parts = share.astype(BF).reshape(n_dp, plane, rows, width)
    parts = lax.psum_scatter(parts, PLANE, scatter_dimension=1, tiled=True)
    parts = lax.psum_scatter(parts.reshape(n_dp, rows, width), "dp", scatter_dimension=0, tiled=True)
    whole = lax.all_gather(parts.reshape(rows, width), PLANE, axis=0, tiled=True)
    return whole.astype(F32)


def local_paired(
    inputs,
    cotangent,
    routes,
    attn_q,
    attn_k,
    attn_v,
    attn_o,
    norm_attn,
    norm_moe,
    router,
    expert_gate,
    expert_up,
    expert_down,
):
    n_context, n_expert, n_dp = lax.axis_size("context"), lax.axis_size("expert"), lax.axis_size("dp")
    plane = n_context * n_expert
    tokens = inputs.shape[1]
    block_index = lax.axis_index("context")
    z_index = lax.axis_index("dp")
    parity = z_index % 2
    prompt_len = PBLK * n_context
    x_low = inputs[0]
    cot_low = cotangent[0]
    route_rows = routes[0]

    small = jnp.concatenate(
        [router, norm_attn[:, None], norm_moe[:, None]], axis=1
    ).astype(BF)
    small = jnp.pad(small, ((0, 0), (0, 128 - small.shape[1])))
    shard_in = jnp.concatenate([attn_q.astype(BF), attn_k.astype(BF), attn_v.astype(BF), small], axis=1)
    here = lax.axis_index("expert") * n_context + block_index
    part_rows = attn_q.shape[0] // plane
    part_of = lambda shard: lax.dynamic_slice_in_dim(shard, here * part_rows, part_rows, 0)
    whole_in, out_parts = gather_parts(part_of(shard_in), part_of(attn_o).astype(BF), n_dp, plane)
    whole_in = whole_in.reshape(-1, shard_in.shape[1])
    w_out = lax.all_gather(out_parts, PLANE, axis=1, tiled=False).reshape(-1, D)
    qkv_width = D + 2 * KVH * HD
    w_qkv = whole_in[:, :qkv_width]
    w_router = whole_in[:, qkv_width : qkv_width + EXPERTS]
    gain_one = whole_in[:, qkv_width + EXPERTS].astype(F32)
    gain_two = whole_in[:, qkv_width + EXPERTS + 1].astype(F32)

    per_device = expert_gate.shape[1] // n_context

    def weight_pieces(weight):
        mine = lax.dynamic_slice_in_dim(weight, block_index * per_device, per_device, 1)
        mine = mine.astype(BF).transpose(1, 0, 2)
        mine = mine.reshape(2, per_device // 2, mine.shape[1], mine.shape[2])
        same = lax.dynamic_index_in_dim(mine, parity, 0, keepdims=False)
        other = lax.dynamic_index_in_dim(mine, 1 - parity, 0, keepdims=False)
        return same, other

    weight_halves = [weight_pieces(weight) for weight in (expert_gate, expert_up, expert_down)]
    pieces = [[halves[0]] + [None] * (n_dp - 1) for halves in weight_halves]
    for flip in (1, 3):
        pieces[0][flip] = flip_permute(weight_halves[0][flip % 2], "dp", n_dp, flip)

    partner_routes = flip_permute(route_rows, "dp", n_dp, 1)

    def ranks_of(rows):
        named = jnp.sum(
            (rows[:, :, None] == jnp.arange(EXPERTS, dtype=jnp.int32)[None, None, :]).astype(F32), axis=1
        )
        order = jnp.arange(tokens, dtype=jnp.int32)
        before = (order[None, :] < order[:, None]).astype(BF)
        count = mxu(before, named.astype(BF))
        return named > 0, jnp.where(named > 0, count, -1.0)

    named, own_ranks = ranks_of(route_rows)
    partner_ranks = ranks_of(partner_routes)[1]

    def mine_of(table):
        parted = table.reshape(tokens, plane, 2, 2)
        return lax.dynamic_index_in_dim(parted, parity, 2, keepdims=False)

    own_sel = mine_of(own_ranks)
    partner_sel = mine_of(partner_ranks)
    own_pair = [own_sel[:, :, i].astype(BF) for i in range(2)]
    partner_pair = [partner_sel[:, :, i].astype(BF) for i in range(2)]

    own_ranks_t = jnp.stack(own_pair, axis=0).transpose(0, 2, 1)
    partner_ranks_t = jnp.stack(partner_pair, axis=0).transpose(0, 2, 1)
    partner_cot = flip_permute(cot_low, "dp", n_dp, 1)

    positions = jnp.concatenate(
        [
            block_index * PBLK + jnp.arange(PBLK, dtype=jnp.int32),
            prompt_len + jnp.arange(CONT, dtype=jnp.int32),
        ]
    )
    angles = angle_table(positions)
    cos_half, sin_half = jnp.cos(angles), jnp.sin(angles)
    cosine = jnp.concatenate([cos_half, cos_half], axis=1)
    sine = jnp.concatenate([-sin_half, sin_half], axis=1)
    block_word = block_index.astype(jnp.int32).reshape(1)
    z_word = z_index.astype(jnp.int32).reshape(1)
    qkv, normed_one = project(x_low, gain_one[None, :], w_qkv, cosine, sine)
    keys_own = qkv[:, D:]
    prompt_kv = lax.all_gather(keys_own[:PBLK], "context", axis=0, tiled=True)
    keys_values = jnp.concatenate([prompt_kv, keys_own[PBLK:]], axis=0)
    attended, logs = attend(block_word, qkv, keys_values, prompt_len)
    x_rows = x_low.astype(F32)
    mid_rows = x_rows + mxu(attended, w_out)
    normed_two = rms_scale(mid_rows, gain_two).astype(BF)

    normed_two, partner_cot, pieces[0][1], pieces[0][3] = tie(
        normed_two, partner_cot, pieces[0][1], pieces[0][3]
    )
    riders = [weight_halves[which][flip % 2] for which, flip in RIDING]
    moved = dispatch_rows(
        normed_two, cot_low, partner_cot, own_ranks_t, partner_ranks_t, riders, n_dp
    )
    for (which, flip), piece in zip(RIDING, moved[8:]):
        pieces[which][flip] = piece
    moved = moved[:8]
    moved = [m.reshape(plane * SLOTS, D) for m in moved]
    rows_own, cot_own, rows_partner, cot_partner = moved[0:2], moved[2:4], moved[4:6], moved[6:8]
    logits = mxu(normed_two, w_router)
    top_logit = jnp.max(jnp.where(named, logits, masked_score), axis=1, keepdims=True)
    raised = jnp.where(named, jnp.exp(jnp.where(named, logits - top_logit, 0.0)), 0.0)
    gates = raised / jnp.sum(raised, axis=1, keepdims=True)

    slot_ids = jnp.arange(SLOTS, dtype=F32)
    hits = own_ranks.T[:, None, :] == slot_ids[None, :, None]
    slot_gates = jnp.sum(jnp.where(hits, gates.T[:, None, :], 0.0), axis=-1)
    slot_gates = slot_gates.reshape(plane, 2, 2, SLOTS)
    own_gates = lax.dynamic_index_in_dim(slot_gates, parity, 1, keepdims=False)
    other_gates = lax.dynamic_index_in_dim(slot_gates, 1 - parity, 1, keepdims=False)
    partner_gates = flip_permute(other_gates, "dp", n_dp, 1)
    both_gates = jnp.stack([own_gates, partner_gates], axis=1)
    both_gates = lax.all_to_all(both_gates, PLANE, split_axis=0, concat_axis=0, tiled=True)

    shares = []
    returned = []
    for i in range(2):
        column = lambda side: both_gates[:, side, i].reshape(plane * SLOTS, 1)
        returned.append(
            run_expert(
                i,
                z_word,
                rows_own[i],
                rows_partner[i],
                cot_own[i],
                cot_partner[i],
                column(0),
                column(1),
                *pieces,
            )
        )

    parted = lambda rows: rows.reshape(plane, SLOTS, D)
    grad_normed_two, gate_share, up_share, down_share, *homes = return_rows(
        jnp.stack(own_pair, axis=0),
        jnp.stack(partner_pair, axis=0),
        [parted(rows) for r in returned for rows in (r[2], r[3])],
        [(r[6], r[10], r[7], r[8], r[9]) for r in returned],
        n_dp,
    )
    grad_normed_two, *rows_out = tie(
        grad_normed_two, *[rows for r in returned for rows in (r[0], r[1])]
    )
    dots = jnp.stack(
        [
            jnp.stack([r[4].reshape(plane, SLOTS), r[5].reshape(plane, SLOTS)], axis=1) for r in returned
        ],
        axis=2,
    )
    dots = lax.all_to_all(dots, PLANE, split_axis=0, concat_axis=0, tiled=True)
    other_dots = flip_permute(dots[:, 1], "dp", n_dp, 1)
    all_dots = jnp.where(
        parity == 0,
        jnp.stack([dots[:, 0], other_dots], axis=1),
        jnp.stack([other_dots, dots[:, 0]], axis=1),
    ).reshape(EXPERTS, SLOTS)
    grad_gates = jnp.sum(
        jnp.where(own_ranks[:, :, None] == slot_ids[None, None, :], all_dots[None], 0.0), axis=-1
    )
    grad_logits = gates * (grad_gates - jnp.sum(gates * grad_gates, axis=1, keepdims=True))
    grad_logits = grad_logits.astype(BF)
    grad_wrouter = mxu(normed_two, grad_logits, ((0,), (0,)))
    grad_normed_two = grad_normed_two + mxu(grad_logits, w_router, ((1,), (1,)))
    grad_out = cot_low.astype(F32)
    norm_back_two = jax.vjp(rms_scale, mid_rows, gain_two)[1]
    grad_mid_norm, grad_gain_two = norm_back_two(grad_normed_two)
    grad_mid = grad_out + grad_mid_norm
    grad_attn = grad_mid.astype(BF)
    grad_attended = mxu(grad_attn, w_out, ((1,), (1,))).astype(BF)
    grad_wout = mxu(attended, grad_attn, ((0,), (0,)))

    home_of = dict(zip(HOMING, homes))

    def move_share(which, share):
        got = [share[0]] + [None] * (n_dp - 1)
        for flip in range(1, n_dp):
            got[flip] = home_of.get((which, flip))
            if got[flip] is None:
                got[flip] = flip_permute(share[flip], "dp", n_dp, flip)
        same = sum(got[flip].astype(F32) for flip in range(0, n_dp, 2)).astype(BF)
        other = sum(got[flip].astype(F32) for flip in range(1, n_dp, 2)).astype(BF)
        return jnp.where(
            parity == 0, jnp.concatenate([same, other], axis=0), jnp.concatenate([other, same], axis=0)
        )

    gate_four = move_share(0, gate_share)
    up_four = move_share(1, up_share)
    down_four = move_share(2, down_share)

    grad_qproj, grad_keys, grad_values = attend_back(
        block_word, qkv, keys_values, grad_attended, logs, cosine, sine, prompt_len
    )
    grad_qproj, grad_keys, grad_values, gate_four = tie(grad_qproj, grad_keys, grad_values, gate_four)
    grad_kv = jnp.concatenate([grad_keys, grad_values], axis=1)
    prompt_share = lax.psum_scatter(
        grad_kv[:prompt_len].astype(BF), "context", scatter_dimension=0, tiled=True
    ).astype(F32)
    grad_kv = jnp.concatenate([prompt_share, grad_kv[prompt_len:]], axis=0)
    grad_kproj = rotary(grad_kv[:, : KVH * HD].reshape(tokens, KVH, HD), angles, -1.0)
    grad_kv = jnp.concatenate([grad_kproj.reshape(tokens, KVH * HD), grad_kv[:, KVH * HD :]], axis=1)
    grad_qkv = jnp.concatenate([grad_qproj, grad_kv.astype(BF)], axis=1)
    grad_wqkv = mxu(normed_one, grad_qkv, ((0,), (0,)))
    grad_normed_one = mxu(grad_qkv, w_qkv, ((1,), (1,)))
    grad_wqkv, grad_normed_one, up_four = tie(grad_wqkv, grad_normed_one, up_four)
    norm_back_one = jax.vjp(rms_scale, x_rows, gain_one)[1]
    grad_x_norm, grad_gain_one = norm_back_one(grad_normed_one)
    grad_inputs = (grad_mid + grad_x_norm).astype(BF)

    out_partner = [plane_exchange(rows) for rows in rows_out[1::2]]
    out_own = [plane_exchange(rows) for rows in rows_out[0::2]]
    out_for_partner = collect_rows(partner_pair[0], partner_pair[1], out_partner[0], out_partner[1], BF)
    out_from_partner = flip_permute(out_for_partner, "dp", n_dp, 1)
    moe_out = collect_rows(own_pair[0], own_pair[1], out_own[0], out_own[1], F32)
    result = (mid_rows + moe_out + out_from_partner.astype(F32)).astype(BF)

    grad_small = jnp.concatenate(
        [grad_wrouter, grad_gain_one[:, None], grad_gain_two[:, None]], axis=1
    )
    grad_small = jnp.pad(grad_small, ((0, 0), (0, 128 - grad_small.shape[1])))
    total_out = scatter_dense(grad_wout)
    total_in = scatter_dense(jnp.concatenate([grad_wqkv, grad_small], axis=1))
    return (
        result[None],
        grad_inputs[None],
        total_in[:, :D],
        total_in[:, D : D + KVH * HD],
        total_in[:, D + KVH * HD : qkv_width],
        total_out,
        total_in[:, qkv_width + EXPERTS],
        total_in[:, qkv_width + EXPERTS + 1],
        total_in[:, qkv_width : qkv_width + EXPERTS],
        finish_weight(lax.all_gather(gate_four, "context", axis=0, tiled=True), False),
        finish_weight(lax.all_gather(up_four, "context", axis=0, tiled=True), False),
        finish_weight(lax.all_gather(down_four, "context", axis=0, tiled=True), True),
    )


def paired_plan(mesh):
    n_expert, n_context, n_dp = mesh.shape["expert"], mesh.shape["context"], mesh.shape["dp"]
    owners = 2 * n_expert * n_context
    small_axes = all(size & (size - 1) == 0 for size in (n_expert, n_context, n_dp))
    return small_axes and n_dp % 2 == 0 and EXPERTS == 2 * owners


def solution(mesh):
    in_specs = (
        P(("expert", "dp"), "context", None),
        P(("expert", "dp"), "context", None),
        P(("expert", "dp"), "context", None),
        P("dp", None),
        P("dp", None),
        P("dp", None),
        P("dp", None),
        P("dp"),
        P("dp"),
        P("dp", None),
        P("dp", "expert", None),
        P("dp", "expert", None),
        P("dp", "expert", None),
    )
    out_specs = (
        P(("expert", "dp"), "context", None),
        P(("expert", "dp"), "context", None),
        P("dp", None),
        P("dp", None),
        P("dp", None),
        P("dp", None),
        P("dp"),
        P("dp"),
        P("dp", None),
        P("dp", "expert", None),
        P("dp", "expert", None),
        P("dp", "expert", None),
    )
    chosen = local_paired if paired_plan(mesh) else local
    return jax.shard_map(chosen, mesh=mesh, in_specs=in_specs, out_specs=out_specs, check_vma=False)
```

```python
import functools
import math

import jax
import jax.numpy as jnp
from jax import lax
from jax.experimental import pallas as pl
from jax.experimental.pallas import tpu as pltpu
from jax.sharding import PartitionSpec as P

D = 1536
HEADS = 12
KVH = 2
HD = 128
EXPERTS = 32
TOP = 4
PBLK = 256
CONT = 512
CAP = 103


epsilon = 1e-06
rope_base = 1000000.0
masked_score = -1e30


def rms_scale(values, gain):
    return values * lax.rsqrt(jnp.mean(values * values, axis=-1, keepdims=True) + epsilon) * gain


def angle_table(positions):
    steps_half = jnp.arange(HD // 2, dtype=jnp.float32)
    inverse = jnp.exp(steps_half * (-2.0 * math.log(rope_base) / HD))
    return positions.astype(jnp.float32)[..., None] * inverse


def rotary(values, angles, direction):
    halfway = values.shape[-1] // 2
    cosine = jnp.cos(angles)[..., None, :]
    sine_part = direction * jnp.sin(angles)[..., None, :]
    leading = values[..., :halfway]
    trailing = values[..., halfway:]
    return jnp.concatenate(
        [leading * cosine - trailing * sine_part, trailing * cosine + leading * sine_part], axis=-1
    )


def visible(query_pos, key_pos, prompt_len):
    query_cont = jnp.arange(query_pos.shape[0]) >= PBLK
    key_prompt = jnp.arange(key_pos.shape[0]) < prompt_len
    return (key_pos[None, :] <= query_pos[:, None]) & (key_prompt[None, :] | query_cont[:, None])


def gating(logit_rows, route_rows):
    picker = (route_rows[:, :, None] == jnp.arange(EXPERTS, dtype=jnp.int32)[None, None, :]).astype(
        logit_rows.dtype
    )
    chosen = jnp.sum(picker * logit_rows[:, None, :], axis=-1)
    return jax.nn.softmax(chosen, axis=-1)


def gated(gate_pre, up_pre):
    return jax.nn.silu(gate_pre) * up_pre


def expert_slots(flat_experts):
    picker = (flat_experts[:, None] == jnp.arange(EXPERTS, dtype=jnp.int32)[None, :]).astype(
        jnp.int32
    )
    earlier = jnp.cumsum(picker, axis=0) - picker
    return jnp.sum(earlier * picker, axis=1)


def local(
    inputs,
    cotangent,
    routes,
    attn_q,
    attn_k,
    attn_v,
    attn_o,
    norm_attn,
    norm_moe,
    router,
    expert_gate,
    expert_up,
    expert_down,
):
    low_type = jnp.bfloat16
    full_type = jnp.float32
    w_query, w_key, w_value, w_out, gain_first, gain_second, w_router, w_gate, w_up, w_down = (
        lax.all_gather(attn_q.astype(low_type), "dp", axis=0, tiled=True),
        lax.all_gather(attn_k.astype(low_type), "dp", axis=0, tiled=True),
        lax.all_gather(attn_v.astype(low_type), "dp", axis=0, tiled=True),
        lax.all_gather(attn_o.astype(low_type), "dp", axis=0, tiled=True),
        lax.all_gather(norm_attn.astype(low_type), "dp", axis=0, tiled=True),
        lax.all_gather(norm_moe.astype(low_type), "dp", axis=0, tiled=True),
        lax.all_gather(router.astype(low_type), "dp", axis=0, tiled=True),
        lax.all_gather(expert_gate.astype(low_type), "dp", axis=0, tiled=True),
        lax.all_gather(expert_up.astype(low_type), "dp", axis=0, tiled=True),
        lax.all_gather(expert_down.astype(low_type), "dp", axis=0, tiled=True),
    )
    n_context = lax.axis_size("context")
    n_expert = lax.axis_size("expert")
    block_index = lax.axis_index("context")
    prompt_len = PBLK * n_context
    tokens = inputs.shape[1]
    local_experts = w_gate.shape[1]
    group_width = HEADS // KVH
    score_scale = 1.0 / math.sqrt(HD)
    gain_one = gain_first.astype(full_type)
    gain_two = gain_second.astype(full_type)
    x_rows = inputs[0].astype(full_type)
    positions = jnp.concatenate(
        [
            block_index * PBLK + jnp.arange(PBLK, dtype=jnp.int32),
            prompt_len + jnp.arange(CONT, dtype=jnp.int32),
        ]
    )
    angles = angle_table(positions)
    normed_one = rms_scale(x_rows, gain_one).astype(low_type)
    q_proj = jnp.dot(normed_one, w_query, preferred_element_type=full_type)
    k_proj = jnp.dot(normed_one, w_key, preferred_element_type=full_type)
    v_proj = jnp.dot(normed_one, w_value, preferred_element_type=full_type)
    queries = (rotary(q_proj.reshape(tokens, HEADS, HD), angles, 1.0) * score_scale).astype(
        low_type
    )
    queries = queries.reshape(tokens, KVH, group_width, HD)
    keys_own = rotary(k_proj.reshape(tokens, KVH, HD), angles, 1.0).astype(low_type)
    values_own = v_proj.astype(low_type).reshape(tokens, KVH, HD)
    prompt_keys, prompt_values = (
        lax.all_gather(keys_own[:PBLK], "context", axis=0, tiled=True),
        lax.all_gather(values_own[:PBLK], "context", axis=0, tiled=True),
    )
    all_keys = jnp.concatenate([prompt_keys, keys_own[PBLK:]], axis=0)
    all_values = jnp.concatenate([prompt_values, values_own[PBLK:]], axis=0)
    key_pos = jnp.concatenate(
        [jnp.arange(prompt_len, dtype=jnp.int32), prompt_len + jnp.arange(CONT, dtype=jnp.int32)]
    )
    allowed = visible(positions, key_pos, prompt_len)
    head_outs = []
    log_totals = []
    for kv_head in range(KVH):
        scores = jnp.einsum(
            "tgn,kn->gtk",
            queries[:, kv_head],
            all_keys[:, kv_head],
            preferred_element_type=full_type,
        )
        scores = jnp.where(allowed[None], scores, masked_score)
        top_score = jnp.max(scores, axis=-1, keepdims=True)
        unnormed = jnp.exp(scores - top_score)
        totals = jnp.sum(unnormed, axis=-1, keepdims=True)
        attn_probs = (unnormed / totals).astype(low_type)
        head_outs.append(
            jnp.einsum(
                "gtk,kn->tgn", attn_probs, all_values[:, kv_head], preferred_element_type=full_type
            )
        )
        log_totals.append(top_score + jnp.log(totals))
    attended_low = jnp.stack(head_outs, axis=1).reshape(tokens, D).astype(low_type)
    mid_rows = x_rows + jnp.dot(attended_low, w_out, preferred_element_type=full_type)
    normed_two = rms_scale(mid_rows, gain_two).astype(low_type)
    logits = jnp.dot(normed_two, w_router, preferred_element_type=full_type)
    route_rows = routes[0]
    gate_weights = gating(logits, route_rows)
    flat_experts = route_rows.reshape(-1)
    slot_rank = expert_slots(flat_experts)
    destination = (
        flat_experts % local_experts * n_expert + flat_experts // local_experts
    ) * CAP + slot_rank
    capacity_rows = local_experts * n_expert * CAP
    assignments = tokens * TOP
    source = (
        jnp.full((capacity_rows,), assignments, dtype=jnp.int32)
        .at[destination]
        .set(jnp.arange(assignments, dtype=jnp.int32))
    )
    filled = source < assignments
    source_row = jnp.minimum(source, assignments - 1)
    send_rows = jnp.where(filled[:, None], normed_two[source_row // TOP], jnp.zeros((), low_type))
    received = lax.all_to_all(
        send_rows.reshape(local_experts, n_expert, CAP, D),
        "expert",
        split_axis=1,
        concat_axis=1,
        tiled=True,
    )
    received = received.reshape(local_experts, n_expert * CAP, D)
    gate_pre = jnp.einsum("lrd,dlf->lrf", received, w_gate, preferred_element_type=full_type)
    up_pre = jnp.einsum("lrd,dlf->lrf", received, w_up, preferred_element_type=full_type)
    activation = gated(gate_pre, up_pre).astype(low_type)
    expert_rows = jnp.einsum(
        "lrf,fld->lrd", activation, w_down, preferred_element_type=full_type
    ).astype(low_type)
    returned = lax.all_to_all(
        expert_rows.reshape(local_experts, n_expert, CAP, D),
        "expert",
        split_axis=1,
        concat_axis=1,
        tiled=True,
    )
    returned = returned.reshape(capacity_rows, D)
    picked = returned[destination].reshape(tokens, TOP, D)
    moe_out = jnp.sum(gate_weights[:, :, None] * picked.astype(full_type), axis=1)
    result = (mid_rows + moe_out).astype(low_type)
    grad_out = cotangent[0].astype(full_type)
    slot_grads = (
        (gate_weights[:, :, None] * grad_out[:, None, :]).reshape(assignments, D).astype(low_type)
    )
    send_grads = jnp.where(filled[:, None], slot_grads[source_row], jnp.zeros((), low_type))
    grad_rows = lax.all_to_all(
        send_grads.reshape(local_experts, n_expert, CAP, D),
        "expert",
        split_axis=1,
        concat_axis=1,
        tiled=True,
    )
    grad_rows = grad_rows.reshape(local_experts, n_expert * CAP, D)
    grad_gates = jnp.sum(picked.astype(full_type) * grad_out[:, None, :], axis=-1)
    grad_wdown = jnp.einsum("lrf,lrd->fld", activation, grad_rows, preferred_element_type=full_type)
    grad_act = jnp.einsum("lrd,fld->lrf", grad_rows, w_down, preferred_element_type=full_type)
    primal_gate, gated_back = jax.vjp(gated, gate_pre, up_pre)
    grad_gpre, grad_upre = gated_back(grad_act)
    grad_gpre = grad_gpre.astype(low_type)
    grad_upre = grad_upre.astype(low_type)
    grad_wgate = jnp.einsum("lrd,lrf->dlf", received, grad_gpre, preferred_element_type=full_type)
    grad_wup = jnp.einsum("lrd,lrf->dlf", received, grad_upre, preferred_element_type=full_type)
    grad_recv = jnp.einsum("lrf,dlf->lrd", grad_gpre, w_gate, preferred_element_type=full_type)
    grad_recv = (
        grad_recv + jnp.einsum("lrf,dlf->lrd", grad_upre, w_up, preferred_element_type=full_type)
    ).astype(low_type)
    back_rows = lax.all_to_all(
        grad_recv.reshape(local_experts, n_expert, CAP, D),
        "expert",
        split_axis=1,
        concat_axis=1,
        tiled=True,
    )
    back_rows = back_rows.reshape(capacity_rows, D)
    grad_normed_two = jnp.sum(
        back_rows[destination].reshape(tokens, TOP, D).astype(full_type), axis=1
    )

    def gate_of(logit_rows):
        return gating(logit_rows, route_rows)

    primal_gates, gate_back = jax.vjp(gate_of, logits)
    grad_logits = gate_back(grad_gates)[0].astype(low_type)
    grad_wrouter = jnp.einsum(
        "td,te->de", normed_two, grad_logits, preferred_element_type=full_type
    )
    grad_normed_two = grad_normed_two + jnp.einsum(
        "te,de->td", grad_logits, w_router, preferred_element_type=full_type
    )
    primal_two, norm_back_two = jax.vjp(rms_scale, mid_rows, gain_two)
    grad_mid_norm, grad_gain_two = norm_back_two(grad_normed_two)
    grad_mid = grad_out + grad_mid_norm
    grad_attn = grad_mid.astype(low_type)
    grad_wout = jnp.einsum("td,te->de", attended_low, grad_attn, preferred_element_type=full_type)
    grad_attended = jnp.einsum(
        "te,de->td", grad_attn, w_out, preferred_element_type=full_type
    ).astype(low_type)
    grad_attended = grad_attended.reshape(tokens, KVH, group_width, HD)
    query_grads = []
    key_grads = []
    value_grads = []
    for kv_head in range(KVH):
        scores = jnp.einsum(
            "tgn,kn->gtk",
            queries[:, kv_head],
            all_keys[:, kv_head],
            preferred_element_type=full_type,
        )
        scores = jnp.where(allowed[None], scores, masked_score)
        exact_probs = jnp.exp(scores - log_totals[kv_head])
        grad_probs = jnp.einsum(
            "tgn,kn->gtk",
            grad_attended[:, kv_head],
            all_values[:, kv_head],
            preferred_element_type=full_type,
        )
        row_dots = jnp.sum(exact_probs * grad_probs, axis=-1, keepdims=True)
        grad_scores = (exact_probs * (grad_probs - row_dots)).astype(low_type)
        query_grads.append(
            jnp.einsum(
                "gtk,kn->tgn", grad_scores, all_keys[:, kv_head], preferred_element_type=full_type
            )
        )
        key_grads.append(
            jnp.einsum(
                "gtk,tgn->kn", grad_scores, queries[:, kv_head], preferred_element_type=full_type
            )
        )
        value_grads.append(
            jnp.einsum(
                "gtk,tgn->kn",
                exact_probs.astype(low_type),
                grad_attended[:, kv_head],
                preferred_element_type=full_type,
            )
        )
    grad_queries = jnp.stack(query_grads, axis=1).reshape(tokens, HEADS, HD)
    grad_keys = jnp.stack(key_grads, axis=1)
    grad_values = jnp.stack(value_grads, axis=1)
    prompt_key_grad, prompt_value_grad = (
        lax.psum_scatter(
            grad_keys[:prompt_len].astype(jnp.bfloat16), "context", scatter_dimension=0, tiled=True
        ).astype(jnp.float32),
        lax.psum_scatter(
            grad_values[:prompt_len].astype(jnp.bfloat16),
            "context",
            scatter_dimension=0,
            tiled=True,
        ).astype(jnp.float32),
    )
    own_key_grad = jnp.concatenate([prompt_key_grad, grad_keys[prompt_len:]], axis=0)
    own_value_grad = jnp.concatenate([prompt_value_grad, grad_values[prompt_len:]], axis=0)
    grad_qproj = (
        rotary(grad_queries * score_scale, angles, -1.0).reshape(tokens, D).astype(low_type)
    )
    grad_kproj = rotary(own_key_grad, angles, -1.0).reshape(tokens, KVH * HD).astype(low_type)
    grad_vproj = own_value_grad.reshape(tokens, KVH * HD).astype(low_type)
    grad_wquery = jnp.einsum("td,te->de", normed_one, grad_qproj, preferred_element_type=full_type)
    grad_wkey = jnp.einsum("td,te->de", normed_one, grad_kproj, preferred_element_type=full_type)
    grad_wvalue = jnp.einsum("td,te->de", normed_one, grad_vproj, preferred_element_type=full_type)
    grad_normed_one = jnp.einsum("te,de->td", grad_qproj, w_query, preferred_element_type=full_type)
    grad_normed_one = grad_normed_one + jnp.einsum(
        "te,de->td", grad_kproj, w_key, preferred_element_type=full_type
    )
    grad_normed_one = grad_normed_one + jnp.einsum(
        "te,de->td", grad_vproj, w_value, preferred_element_type=full_type
    )
    primal_one, norm_back_one = jax.vjp(rms_scale, x_rows, gain_one)
    grad_x_norm, grad_gain_one = norm_back_one(grad_normed_one)
    grad_inputs = (grad_mid + grad_x_norm).astype(low_type)
    shares = (
        lax.psum_scatter(
            grad_wquery.astype(jnp.bfloat16), "dp", scatter_dimension=0, tiled=True
        ).astype(jnp.float32),
        lax.psum_scatter(
            grad_wkey.astype(jnp.bfloat16), "dp", scatter_dimension=0, tiled=True
        ).astype(jnp.float32),
        lax.psum_scatter(
            grad_wvalue.astype(jnp.bfloat16), "dp", scatter_dimension=0, tiled=True
        ).astype(jnp.float32),
        lax.psum_scatter(
            grad_wout.astype(jnp.bfloat16), "dp", scatter_dimension=0, tiled=True
        ).astype(jnp.float32),
        lax.psum_scatter(
            grad_gain_one.astype(jnp.bfloat16), "dp", scatter_dimension=0, tiled=True
        ).astype(jnp.float32),
        lax.psum_scatter(
            grad_gain_two.astype(jnp.bfloat16), "dp", scatter_dimension=0, tiled=True
        ).astype(jnp.float32),
        lax.psum_scatter(
            grad_wrouter.astype(jnp.bfloat16), "dp", scatter_dimension=0, tiled=True
        ).astype(jnp.float32),
        lax.psum_scatter(
            grad_wgate.astype(jnp.bfloat16), "dp", scatter_dimension=0, tiled=True
        ).astype(jnp.float32),
        lax.psum_scatter(
            grad_wup.astype(jnp.bfloat16), "dp", scatter_dimension=0, tiled=True
        ).astype(jnp.float32),
        lax.psum_scatter(
            grad_wdown.astype(jnp.bfloat16), "dp", scatter_dimension=0, tiled=True
        ).astype(jnp.float32),
    )
    dense_sum = lax.psum(
        (shares[0], shares[1], shares[2], shares[3], shares[4], shares[5], shares[6]),
        ("expert", "context"),
    )
    expert_sum = (
        lax.psum(shares[7].astype(jnp.bfloat16), "context").astype(jnp.float32),
        lax.psum(shares[8].astype(jnp.bfloat16), "context").astype(jnp.float32),
        lax.psum(shares[9].astype(jnp.bfloat16), "context").astype(jnp.float32),
    )
    totals_all = tuple(dense_sum) + tuple(expert_sum)
    return (
        result[None],
        grad_inputs[None],
        totals_all[0],
        totals_all[1],
        totals_all[2],
        totals_all[3],
        totals_all[4],
        totals_all[5],
        totals_all[6],
        totals_all[7],
        totals_all[8],
        totals_all[9],
    )


BF = jnp.bfloat16
F32 = jnp.float32
SLOTS = 112
MESH_ID = pl.DeviceIdType.MESH
PLANE = ("expert", "context")
VMEM_BYTES = 60 * 1024 * 1024


def mxu(lhs, rhs, contract=((1,), (0,))):
    return lax.dot_general(lhs, rhs, (contract, ((), ())), preferred_element_type=F32)


def grant(bytes_wanted=VMEM_BYTES):
    return pltpu.CompilerParams(vmem_limit_bytes=bytes_wanted)


def turn(values, cosine, sine):
    return values * cosine + pltpu.roll(values, HD // 2, 1) * sine


def project_kernel(x_ref, gain_ref, w_ref, cos_ref, sin_ref, out_ref, normed_ref):
    step = pl.program_id(0)

    @pl.when(step == 0)
    def _():
        rows = x_ref[...].astype(F32)
        scale = lax.rsqrt(jnp.mean(rows * rows, axis=-1, keepdims=True) + epsilon)
        normed_ref[...] = (rows * scale * gain_ref[...]).astype(BF)

    product = mxu(normed_ref[...], w_ref[...])
    is_query = step < HEADS // 2
    is_value = step == HEADS // 2 + KVH // 2
    cosine = jnp.where(is_value, 1.0, cos_ref[...])
    sine = jnp.where(is_value, 0.0, sin_ref[...])
    factor = jnp.where(is_query, 1.0 / math.sqrt(HD), 1.0)
    for half in range(2):
        part = product[:, half * HD : (half + 1) * HD]
        out_ref[:, half * HD : (half + 1) * HD] = (turn(part, cosine, sine) * factor).astype(BF)


def project(x_low, gain, w_in, width, cosine, sine):
    tokens = x_low.shape[0]
    whole = lambda j: (0, 0)
    return pl.pallas_call(
        project_kernel,
        grid=(width // (2 * HD),),
        in_specs=[
            pl.BlockSpec((tokens, D), whole),
            pl.BlockSpec((1, D), whole),
            pl.BlockSpec((D, 2 * HD), lambda j: (0, j)),
            pl.BlockSpec((tokens, HD), whole),
            pl.BlockSpec((tokens, HD), whole),
        ],
        out_specs=[
            pl.BlockSpec((tokens, 2 * HD), lambda j: (0, j)),
            pl.BlockSpec((tokens, D), whole),
        ],
        out_shape=[
            jax.ShapeDtypeStruct((tokens, width), BF),
            jax.ShapeDtypeStruct((tokens, D), BF),
        ],
        compiler_params=grant(),
        name="project",
    )(x_low, gain, w_in, cosine, sine)


def row_blocks(prompt_len):
    blocks = [(0, prompt_len)]
    for start in range(0, CONT, PBLK):
        blocks.append((PBLK + start, prompt_len + start + PBLK))
    return blocks


def masked_scores(scores, first_row, prompt_len, block_index):
    row = lax.broadcasted_iota(jnp.int32, scores.shape, 0)
    column = lax.broadcasted_iota(jnp.int32, scores.shape, 1)
    if first_row == 0:
        limit = row + block_index * PBLK
    else:
        limit = row + (prompt_len + first_row - PBLK)
    return jnp.where(column <= limit, scores, masked_score)


def attend_kernel(prompt_len, block_ref, q_ref, k_ref, v_ref, out_ref, log_ref):
    for first_row, keys in row_blocks(prompt_len):
        rows = slice(first_row, first_row + PBLK)
        scores = mxu(q_ref[rows, :], k_ref[:keys, :], ((1,), (1,)))
        scores = masked_scores(scores, first_row, prompt_len, block_ref[0])
        top = jnp.max(scores, axis=-1, keepdims=True)
        unnormed = jnp.exp(scores - top)
        total = jnp.sum(unnormed, axis=-1, keepdims=True)
        mixed = mxu(unnormed.astype(BF), v_ref[:keys, :]) / total
        out_ref[rows, :] = mixed.astype(BF)
        lane = lax.broadcasted_iota(jnp.int32, (PBLK, log_ref.shape[1]), 1)
        kept = jnp.where(pl.program_id(0) == 0, 0.0, log_ref[rows, :])
        log_ref[rows, :] = jnp.where(lane == pl.program_id(0), top + jnp.log(total), kept)


def attend(block_index, qkv, keys_values, prompt_len):
    tokens, key_rows = qkv.shape[0], keys_values.shape[0]
    width = HEADS // KVH
    return pl.pallas_call(
        functools.partial(attend_kernel, prompt_len),
        grid=(HEADS,),
        in_specs=[
            pl.BlockSpec(memory_space=pltpu.SMEM),
            pl.BlockSpec((tokens, HD), lambda h: (0, h)),
            pl.BlockSpec((key_rows, HD), lambda h: (0, h // width)),
            pl.BlockSpec((key_rows, HD), lambda h: (0, KVH + h // width)),
        ],
        out_specs=[
            pl.BlockSpec((tokens, HD), lambda h: (0, h)),
            pl.BlockSpec((tokens, 128), lambda h: (0, 0)),
        ],
        out_shape=[
            jax.ShapeDtypeStruct((tokens, D), BF),
            jax.ShapeDtypeStruct((tokens, 128), F32),
        ],
        compiler_params=grant(),
        name="attend",
    )(block_index, qkv, keys_values, keys_values)


def segment_matrix(parts, transposed):
    shape = (parts * SLOTS, parts) if transposed else (parts, parts * SLOTS)
    long = lax.broadcasted_iota(jnp.int32, shape, 0 if transposed else 1)
    short = lax.broadcasted_iota(jnp.int32, shape, 1 if transposed else 0)
    inside = (long >= short * SLOTS) & (long < (short + 1) * SLOTS)
    return jnp.where(inside, 1.0, 0.0).astype(BF)


def slot_matrix(ranks, parts, transposed):
    if transposed:
        spread = mxu(segment_matrix(parts, True), ranks)
        slot = lax.broadcasted_iota(jnp.int32, (parts * SLOTS, 1), 0)
    else:
        spread = mxu(ranks, segment_matrix(parts, False))
        slot = lax.broadcasted_iota(jnp.int32, (1, parts * SLOTS), 1)
    for part in range(parts - 1, 0, -1):
        slot = jnp.where(slot >= part * SLOTS, slot - SLOTS, slot)
    return jnp.where(spread == slot.astype(F32), 1.0, 0.0).astype(BF)


def collect_kernel(parts, rank0_ref, rank1_ref, rows0_ref, rows1_ref, out_ref):
    total = mxu(slot_matrix(rank0_ref[...], parts, False), rows0_ref[...])
    total = total + mxu(slot_matrix(rank1_ref[...], parts, False), rows1_ref[...])
    out_ref[...] = total.astype(out_ref.dtype)


def collect_rows(rank0, rank1, rows0, rows1, kind):
    tokens, dests = rank0.shape
    step = PBLK
    ranks = pl.BlockSpec((step, dests), lambda j: (j, 0))
    slots = pl.BlockSpec((dests * SLOTS, D), lambda j: (0, 0))
    return pl.pallas_call(
        functools.partial(collect_kernel, dests),
        grid=(tokens // step,),
        in_specs=[ranks, ranks, slots, slots],
        out_specs=pl.BlockSpec((step, D), lambda j: (j, 0)),
        out_shape=jax.ShapeDtypeStruct((tokens, D), kind),
        compiler_params=grant(),
        name="collect_rows",
    )(rank0, rank1, rows0, rows1)


def plane_exchange(slot, source, target, local_sems, send_sems, recv_sems):
    here = plane_here()
    plane = source.shape[0]

    def begin():
        pltpu.make_async_copy(source.at[here], target.at[here], local_sems.at[slot]).start()

        def one(flip, carry):
            peer = here ^ flip
            remote(
                source.at[peer],
                target.at[here],
                send_sems.at[slot, peer],
                recv_sems.at[slot, here],
                plane_peer(peer),
            ).start()
            return carry

        lax.fori_loop(1, plane, one, 0)

    def finish():
        pltpu.make_async_copy(source.at[here], target.at[here], local_sems.at[slot]).wait()

        def one(flip, carry):
            peer = here ^ flip
            done = remote(
                source.at[peer],
                target.at[peer],
                send_sems.at[slot, peer],
                recv_sems.at[slot, peer],
                plane_peer(peer),
            )
            done.wait_send()
            done.wait_recv()
            return carry

        lax.fori_loop(1, plane, one, 0)

    return begin, finish


ALL_FLIPS = (2, 3, 1)
RIDE_DISPATCH = ((0, 3, 0),) + tuple((m, f, 0) for m in (1, 2) for f in ALL_FLIPS)
RIDE_FIRST = ((0, 3, 1),) + tuple((m, f, 1) for m in (1, 2) for f in ALL_FLIPS)
HOME_SECOND = tuple((m, f, 0) for m in (0, 1) for f in ALL_FLIPS) + ((2, 2, 0),)
HOME_RETURN = ((2, 3, 0), (0, 2, 1), (0, 3, 1), (1, 2, 1), (2, 1, 0), (0, 1, 1))
HOME_BACKWARD = ((1, 3, 1), (2, 2, 1), (2, 3, 1), (1, 1, 1), (2, 1, 1))


def pick(array, index):
    return array if index is None else array.at[index]


def picked_shape(array, index):
    return array.shape if index is None else array.shape[1:]


def dp_moves(sources, targets, riders, sends, recvs):
    z_index = lax.axis_index("dp")
    return [
        remote(pick(source, index), target, sends.at[n], recvs.at[n], {"dp": z_index ^ flip})
        for n, (source, target, (index, flip)) in enumerate(zip(sources, targets, riders))
    ]


def dp_peers(n_dp):
    return [{"dp": lax.axis_index("dp") ^ flip} for flip in range(1, n_dp)]


def expert_kernel(plane, n_dp, half_steps, picks, riders, *refs):
    (xo_ref, xp_ref, go_ref, gp_ref, so_ref, sp_ref), refs = refs[:6], refs[6:]
    pieces, refs = refs[: 3 * n_dp], refs[3 * n_dp :]
    carried, refs = refs[:4], refs[4:]
    sources, refs = refs[: len(riders)], refs[len(riders) :]
    (yo_ref, yp_ref, bo_ref, bp_ref, do_ref, dp_ref, gate_ref, up_ref, down_ref), refs = refs[:9], refs[9:]
    landed, refs = refs[:4], refs[4:]
    targets, refs = refs[: len(riders)], refs[len(riders) :]
    (wg_ref, wu_ref, wd_ref, x_all, de_all, a_all, dg_all, du_all, stage), sems = refs[:9], refs[9:]
    weight_sems, store_sems, local_sems, send_sems, recv_sems, ride_send, ride_recv = sems
    weights = (wg_ref, wu_ref, wd_ref)
    z_index = lax.axis_index("dp")
    step = pl.program_id(0)
    own = step < half_steps
    rows_of_step = xo_ref.shape[0]
    exchanges = [
        plane_exchange(n, source, target, local_sems, send_sems, recv_sems)
        for n, (source, target) in enumerate(zip(carried, landed))
    ]
    moves = dp_moves(sources, targets, riders, ride_send, ride_recv)

    @pl.when(step == 0)
    def _():
        here = plane_here()
        greet([plane_peer(here ^ flip) for flip in range(1, plane)] + dp_peers(n_dp))
        loads = []
        for n, piece in enumerate(pieces):
            source = pick(piece, picks[n])
            size = source.shape[0]
            start = pl.multiple_of((z_index ^ (n % n_dp)) * size, 64)
            loads.append(
                pltpu.make_async_copy(source, weights[n // n_dp].at[pl.ds(start, size)], weight_sems.at[n])
            )
            loads[-1].start()
        for begin, _ in exchanges:
            begin()
        for move in moves:
            move.start()
        for load in loads:
            load.wait()

    rows = jnp.where(own, xo_ref[...], xp_ref[...])
    cot = jnp.where(own, go_ref[...], gp_ref[...])
    share = jnp.where(own, so_ref[...], sp_ref[...])
    place = pl.ds(pl.multiple_of(step * rows_of_step, 32), rows_of_step)
    x_all[place, :] = rows
    gate_pre = mxu(rows, wg_ref[...])
    up_pre = mxu(rows, wu_ref[...])
    sigma = 1.0 / (1.0 + jnp.exp(-gate_pre))
    silu = gate_pre * sigma
    act = (silu * up_pre).astype(BF)
    a_all[place, :] = act
    cot_full = cot.astype(F32)
    weighted = (cot_full * share).astype(BF)
    de_all[place, :] = weighted
    result = mxu(act, wd_ref[...])
    dots = jnp.sum(result.astype(BF).astype(F32) * cot_full, axis=-1, keepdims=True)
    scaled = (result * share).astype(BF)
    grad_act = mxu(weighted, wd_ref[...], ((1,), (1,)))
    grad_gate = (grad_act * up_pre * sigma * (1.0 + gate_pre * (1.0 - sigma))).astype(BF)
    grad_up = (grad_act * silu).astype(BF)
    dg_all[place, :] = grad_gate
    du_all[place, :] = grad_up
    back = mxu(grad_gate, wg_ref[...], ((1,), (1,))) + mxu(grad_up, wu_ref[...], ((1,), (1,)))
    back = back.astype(BF)

    @pl.when(own)
    def _():
        yo_ref[...] = scaled
        bo_ref[...] = back
        do_ref[...] = dots

    @pl.when(jnp.logical_not(own))
    def _():
        yp_ref[...] = scaled
        bp_ref[...] = back
        dp_ref[...] = dots

    @pl.when(step == 2 * half_steps - 1)
    def _():
        quarter = D // n_dp
        hidden = a_all.shape[1]

        def of_rows(q, carry):
            columns = pl.ds(pl.multiple_of(q * quarter, 128), quarter)
            stores = []
            for n, (grads, out_ref) in enumerate(((dg_all, gate_ref), (du_all, up_ref))):
                stage[n] = mxu(x_all[:, columns], grads[...], ((0,), (0,))).astype(BF)
                stores.append(pltpu.make_async_copy(stage.at[n], out_ref.at[z_index ^ q], store_sems.at[n]))
                stores[-1].start()
            for store in stores:
                store.wait()
            return carry

        lax.fori_loop(0, n_dp, of_rows, 0)
        size = hidden // n_dp
        for q in range(0, n_dp, 2):
            made = mxu(a_all[:, q * size : (q + 2) * size], de_all[...], ((0,), (0,))).astype(BF)
            stores = []
            for half in range(2):
                part = made[half * size : (half + 1) * size]
                stage[half, :size] = part[:, :hidden]
                stage[half, size:] = part[:, hidden:]
                stores.append(
                    pltpu.make_async_copy(
                        stage.at[half], down_ref.at[z_index ^ (q + half)], store_sems.at[half]
                    )
                )
                stores[-1].start()
            for store in stores:
                store.wait()
        for _, finish in exchanges:
            finish()
        for move in moves:
            move.wait()


def run_expert(name, number, rows, cots, gates, pieces, carried, riders):
    half_rows = rows[0].shape[0]
    half_steps = 4
    step_rows = half_rows // half_steps
    plane = carried[0].shape[0]
    n_dp = lax.axis_size("dp")
    hidden = picked_shape(*pieces[0])[1]
    own_map = lambda j: (jnp.minimum(j, half_steps - 1), 0)
    par_map = lambda j: (jnp.maximum(j - half_steps, 0), 0)
    anywhere = pl.BlockSpec(memory_space=pl.ANY)

    def pair(width):
        return [pl.BlockSpec((step_rows, width), own_map), pl.BlockSpec((step_rows, width), par_map)]

    shape = jax.ShapeDtypeStruct
    share = shape((n_dp, D // n_dp, hidden), BF)
    dma = pltpu.SemaphoreType.DMA
    all_rows = 2 * half_rows
    results = pl.pallas_call(
        functools.partial(
            expert_kernel,
            plane,
            n_dp,
            half_steps,
            [index for _, index in pieces],
            [(index, flip) for _, index, flip in riders],
        ),
        grid=(2 * half_steps,),
        in_specs=pair(D) + pair(D) + pair(1) + [anywhere] * (len(pieces) + 4 + len(riders)),
        out_specs=pair(D) + pair(D) + pair(1) + [anywhere] * (7 + len(riders)),
        out_shape=[shape((half_rows, D), BF)] * 4
        + [shape((half_rows, 1), F32)] * 2
        + [share] * 3
        + [shape(array.shape, BF) for array in carried]
        + [shape(picked_shape(array, index), BF) for array, index, _ in riders],
        scratch_shapes=[
            pltpu.VMEM((D, hidden), BF),
            pltpu.VMEM((D, hidden), BF),
            pltpu.VMEM((hidden, D), BF),
            pltpu.VMEM((all_rows, D), BF),
            pltpu.VMEM((all_rows, D), BF),
            pltpu.VMEM((all_rows, hidden), BF),
            pltpu.VMEM((all_rows, hidden), BF),
            pltpu.VMEM((all_rows, hidden), BF),
            pltpu.VMEM((2, D // n_dp, hidden), BF),
            dma((len(pieces),)),
            dma((2,)),
            dma((4,)),
            dma((4, plane)),
            dma((4, plane)),
            dma((len(riders),)),
            dma((len(riders),)),
        ],
        compiler_params=pltpu.CompilerParams(
            vmem_limit_bytes=56 * 1024 * 1024, collective_id=number, has_side_effects=True
        ),
        name=name,
    )(*rows, *cots, *gates, *[a for a, _ in pieces], *carried, *[a for a, _, _ in riders])
    return results[:4], results[4:6], results[6:9], results[9:13], results[13:]


def plane_peer(index):
    n_context = lax.axis_size("context")
    return {"expert": index // n_context, "context": index % n_context}


def plane_here():
    return lax.axis_index("expert") * lax.axis_size("context") + lax.axis_index("context")


def greet(peers):
    barrier = pltpu.get_barrier_semaphore()
    for peer in peers:
        pl.semaphore_signal(barrier, inc=1, device_id=peer, device_id_type=MESH_ID)
    pl.semaphore_wait(barrier, len(peers))


def plane_and_partner(plane):
    here = plane_here()
    return [plane_peer(here ^ flip) for flip in range(1, plane)] + [{"dp": lax.axis_index("dp") ^ 1}]


def remote(source, target, send, receive, peer):
    return pltpu.make_async_remote_copy(
        src_ref=source,
        dst_ref=target,
        send_sem=send,
        recv_sem=receive,
        device_id=peer,
        device_id_type=MESH_ID,
    )


def gather_kernel(
    n_dp,
    in_ref,
    out_part_ref,
    routes_ref,
    whole_ref,
    out_ref,
    partner_routes_ref,
    local_sems,
    z_send,
    o_send,
    o_recv,
    sends,
    recvs,
    route_sems,
):
    here = plane_here()
    z_index = lax.axis_index("dp")
    z_peer = lambda flip: {"dp": z_index ^ flip}
    greet([z_peer(flip) for flip in range(1, n_dp)] + [plane_peer(here ^ flip) for flip in (1, 2, 4)])
    keep = [
        pltpu.make_async_copy(in_ref, whole_ref.at[z_index, here], local_sems.at[0]),
        pltpu.make_async_copy(out_part_ref, out_ref.at[z_index], local_sems.at[1]),
    ]
    for copy in keep:
        copy.start()
    routing = remote(routes_ref, partner_routes_ref, route_sems.at[0], route_sems.at[1], z_peer(1))
    routing.start()
    started = []
    for flip in range(1, n_dp):
        started.append(
            remote(in_ref, whole_ref.at[z_index, here], z_send.at[flip], recvs.at[z_index, here], z_peer(flip))
        )
        started[-1].start()
    for flip in range(1, n_dp):
        started.append(
            remote(out_part_ref, out_ref.at[z_index], o_send.at[flip], o_recv.at[z_index], z_peer(flip))
        )
        started[-1].start()

    def pass_on(lane, flip, z_from, place, source=None):
        block = whole_ref.at[z_from, place]
        move = remote(
            block if source is None else source,
            block,
            sends.at[lane, z_from, place],
            recvs.at[z_from, place],
            plane_peer(here ^ flip),
        )
        move.start()
        started.append(move)

    def landed(z_from, place):
        block = whole_ref.at[z_from, place]
        remote(block, block, z_send.at[0], recvs.at[z_from, place], z_peer(1)).wait_recv()

    froms = [z_index ^ flip for flip in range(n_dp)]
    for n, z_from in enumerate(froms):
        if n > 0:
            landed(z_from, here)
        source = in_ref if n == 0 else None
        pass_on(0, 2, z_from, here, source)
        pass_on(1, 4, z_from, here, source)
        pass_on(2, 1, z_from, here, source)
    for n, z_from in enumerate(froms):
        landed(z_from, here ^ 2)
        if n % 2 == 1:
            pass_on(1, 4, z_from, here ^ 2)
        pass_on(2, 1, z_from, here ^ 2)
        landed(z_from, here ^ 4)
        if n % 2 == 0:
            pass_on(0, 2, z_from, here ^ 4)
        pass_on(2, 1, z_from, here ^ 4)
    for z_from in froms:
        landed(z_from, here ^ 6)
        pass_on(2, 1, z_from, here ^ 6)
    for place in (1, 3, 5, 7):
        for z_from in froms:
            landed(z_from, here ^ place)
    for flip in range(1, n_dp):
        z_from = z_index ^ flip
        remote(out_part_ref, out_ref.at[z_from], o_send.at[0], o_recv.at[z_from], z_peer(1)).wait_recv()
    for move in started:
        move.wait_send()
    for copy in keep:
        copy.wait()
    routing.wait()


def gather_parts(part_in, part_out, routes, n_dp, plane):
    anywhere = pl.BlockSpec(memory_space=pl.ANY)
    return pl.pallas_call(
        functools.partial(gather_kernel, n_dp),
        in_specs=[anywhere] * 3,
        out_specs=[anywhere] * 3,
        out_shape=[
            jax.ShapeDtypeStruct((n_dp, plane) + part_in.shape, BF),
            jax.ShapeDtypeStruct((n_dp,) + part_out.shape, BF),
            jax.ShapeDtypeStruct(routes.shape, routes.dtype),
        ],
        scratch_shapes=[
            pltpu.SemaphoreType.DMA((2,)),
            pltpu.SemaphoreType.DMA((n_dp,)),
            pltpu.SemaphoreType.DMA((n_dp,)),
            pltpu.SemaphoreType.DMA((n_dp,)),
            pltpu.SemaphoreType.DMA((3, n_dp, plane)),
            pltpu.SemaphoreType.DMA((n_dp, plane)),
            pltpu.SemaphoreType.DMA((2,)),
        ],
        compiler_params=pltpu.CompilerParams(collective_id=3, has_side_effects=True),
        name="gather_parts",
    )(part_in, part_out, routes)


def dispatch_kernel(plane, n_dp, riders, *refs):
    (normed_ref, cot_ref, cot_partner_ref, own_rank_ref, partner_rank_ref), refs = refs[:5], refs[5:]
    sources, refs = refs[: len(riders)], refs[len(riders) :]
    landed, staged, targets = refs[:4], refs[4:8], refs[8 : 8 + len(riders)]
    refs = refs[8 + len(riders) :]
    stage, normed_partner, pair_sems, stage_sems, local_sems, send_sems, recv_sems, ride_send, ride_recv = refs
    here = plane_here()
    greet([plane_peer(here ^ flip) for flip in range(1, plane)] + dp_peers(n_dp))
    pair = remote(
        normed_ref, normed_partner, pair_sems.at[0], pair_sems.at[1], {"dp": lax.axis_index("dp") ^ 1}
    )
    pair.start()
    moves = dp_moves(sources, targets, riders, ride_send, ride_recv)
    for move in moves:
        move.start()
    plans = (
        (0, normed_ref, own_rank_ref),
        (1, cot_ref, own_rank_ref),
        (2, cot_partner_ref, partner_rank_ref),
        (3, normed_partner, partner_rank_ref),
    )
    exchanges = [
        plane_exchange(n, stage.at[n], landed[n], local_sems, send_sems, recv_sems) for n in range(4)
    ]
    copies = [pltpu.make_async_copy(stage.at[4 + n], staged[n], stage_sems.at[n]) for n in range(4)]
    for expert in range(2):
        for n, rows_ref, rank_ref in plans:
            if expert == 0 and n == 3:
                pair.wait()
            chooser = slot_matrix(rank_ref[expert], plane, True)
            stage[4 * expert + n] = mxu(chooser, rows_ref[...]).astype(BF).reshape(plane, SLOTS, D)
            if expert == 0:
                exchanges[n][0]()
            else:
                copies[n].start()
    for copy in copies:
        copy.wait()
    for _, finish in exchanges:
        finish()
    for move in moves:
        move.wait()


def dispatch_rows(normed, cot, cot_partner, own_ranks, partner_ranks, riders, n_dp):
    plane, tokens = own_ranks.shape[1:]
    vmem = pl.BlockSpec(memory_space=pltpu.VMEM)
    anywhere = pl.BlockSpec(memory_space=pl.ANY)
    shape = jax.ShapeDtypeStruct
    dma = pltpu.SemaphoreType.DMA
    results = pl.pallas_call(
        functools.partial(dispatch_kernel, plane, n_dp, [(index, flip) for _, index, flip in riders]),
        in_specs=[vmem] * 5 + [anywhere] * len(riders),
        out_specs=[anywhere] * (8 + len(riders)),
        out_shape=[shape((plane, SLOTS, D), BF)] * 8
        + [shape(picked_shape(array, index), BF) for array, index, _ in riders],
        scratch_shapes=[
            pltpu.VMEM((8, plane, SLOTS, D), BF),
            pltpu.VMEM((tokens, D), BF),
            dma((2,)),
            dma((4,)),
            dma((4,)),
            dma((4, plane)),
            dma((4, plane)),
            dma((len(riders),)),
            dma((len(riders),)),
        ],
        compiler_params=pltpu.CompilerParams(
            vmem_limit_bytes=VMEM_BYTES, collective_id=1, has_side_effects=True
        ),
        cost_estimate=pl.CostEstimate(flops=2 * 10**10, bytes_accessed=4 * 10**8, transcendentals=0),
        name="dispatch_rows",
    )(normed, cot, cot_partner, own_ranks, partner_ranks, *[array for array, _, _ in riders])
    return results[:4], results[4:8], results[8:]


def return_kernel(plane, n_dp, riders, own_rank_ref, partner_rank_ref, dots_ref, *refs):
    early, back, results = refs[0:2], refs[2:4], refs[4:6]
    sources, refs = refs[6 : 6 + len(riders)], refs[6 + len(riders) :]
    total_ref, dots_here_ref, dots_other_ref = refs[:3]
    results_back, targets = refs[3:5], refs[5 : 5 + len(riders)]
    (
        held,
        to_partner,
        of_partner,
        load_sems,
        pair_sems,
        local_sems,
        send_sems,
        recv_sems,
        ride_send,
        ride_recv,
        dot_sems,
        dot_send,
        dot_recv,
    ) = refs[5 + len(riders) :]
    here = plane_here()
    partner = {"dp": lax.axis_index("dp") ^ 1}
    greet([plane_peer(here ^ flip) for flip in range(1, plane)] + dp_peers(n_dp))
    own_dots = pltpu.make_async_copy(dots_ref.at[here], dots_here_ref.at[here], dot_sems.at[0])
    own_dots.start()
    dot_moves = [
        remote(
            dots_ref.at[here ^ flip],
            dots_here_ref.at[here],
            dot_send.at[flip],
            dot_recv.at[flip],
            plane_peer(here ^ flip),
        )
        for flip in range(1, plane)
    ]
    for move in dot_moves:
        move.start()
    loads, exchanges = {}, {}
    for side in (1, 0):
        loads[side] = pltpu.make_async_copy(early[side], held.at[2 * side], load_sems.at[side])
        loads[side].start()
        exchanges[side] = plane_exchange(
            side, back[side], held.at[2 * side + 1], local_sems, send_sems, recv_sems
        )
        exchanges[side][0]()
    later = [
        plane_exchange(2 + side, results[side], results_back[side], local_sems, send_sems, recv_sems)
        for side in range(2)
    ]
    for begin, _ in later:
        begin()
    moves = dp_moves(sources, targets, riders, ride_send, ride_recv)
    own_dots.wait()
    for move in dot_moves:
        move.wait()
    dots_pair = remote(dots_here_ref, dots_other_ref, dot_sems.at[1], dot_sems.at[2], partner)
    dots_pair.start()

    def collect(rank_ref, side, target, kind):
        loads[side].wait()
        exchanges[side][1]()

        def block(n, carry):
            rows = pl.ds(pl.multiple_of(n * PBLK, PBLK), PBLK)
            made = jnp.zeros((PBLK, D), F32)
            for expert in range(2):
                chooser = slot_matrix(rank_ref[expert, rows, :], plane, False)
                made = made + mxu(chooser, held[2 * side + expert].reshape(plane * SLOTS, D))
            target[rows, :] = made.astype(kind)
            return carry

        lax.fori_loop(0, total_ref.shape[0] // PBLK, block, 0)

    for move in moves[: len(moves) // 2]:
        move.start()
    collect(partner_rank_ref, 1, to_partner, BF)
    pair = remote(to_partner, of_partner, pair_sems.at[0], pair_sems.at[1], partner)
    pair.start()
    for move in moves[len(moves) // 2 :]:
        move.start()
    collect(own_rank_ref, 0, total_ref, F32)
    pair.wait()
    total_ref[...] += of_partner[...].astype(F32)
    dots_pair.wait()
    for _, finish in later:
        finish()
    for move in moves:
        move.wait()


def return_rows(own_ranks, partner_ranks, dots, early, back, results, riders, n_dp):
    tokens, plane = own_ranks.shape[1:]
    vmem = pl.BlockSpec(memory_space=pltpu.VMEM)
    anywhere = pl.BlockSpec(memory_space=pl.ANY)
    shape = jax.ShapeDtypeStruct
    dma = pltpu.SemaphoreType.DMA
    outcome = pl.pallas_call(
        functools.partial(return_kernel, plane, n_dp, [(index, flip) for _, index, flip in riders]),
        in_specs=[vmem, vmem, vmem] + [anywhere] * (6 + len(riders)),
        out_specs=[vmem, vmem, vmem] + [anywhere] * (2 + len(riders)),
        out_shape=[shape((tokens, D), F32)]
        + [shape(dots.shape, F32)] * 2
        + [shape(rows.shape, BF) for rows in results]
        + [shape(picked_shape(array, index), BF) for array, index, _ in riders],
        scratch_shapes=[
            pltpu.VMEM((4, plane, SLOTS, D), BF),
            pltpu.VMEM((tokens, D), BF),
            pltpu.VMEM((tokens, D), BF),
            dma((2,)),
            dma((2,)),
            dma((4,)),
            dma((4, plane)),
            dma((4, plane)),
            dma((len(riders),)),
            dma((len(riders),)),
            dma((3,)),
            dma((plane,)),
            dma((plane,)),
        ],
        compiler_params=pltpu.CompilerParams(
            vmem_limit_bytes=VMEM_BYTES, collective_id=2, has_side_effects=True
        ),
        cost_estimate=pl.CostEstimate(flops=3 * 10**10, bytes_accessed=4 * 10**8, transcendentals=0),
        name="return_rows",
    )(own_ranks, partner_ranks, dots, *early, *back, *results, *[array for array, _, _ in riders])
    return outcome[0], outcome[1], outcome[2], outcome[3:5], outcome[5:]


def normed_back(rows, gain, grads):
    scale = lax.rsqrt(jnp.mean(rows * rows, axis=-1, keepdims=True) + epsilon)
    weighted = grads * gain
    mean = jnp.mean(rows * weighted, axis=-1, keepdims=True)
    return scale * weighted - rows * (scale * scale * scale * mean), rows * scale * grads


def context_peer(flip):
    return {"context": lax.axis_index("context") ^ flip}


def share_context(part_ref, all_ref, sems, sends, recvs):
    here = lax.axis_index("context")
    own = pltpu.make_async_copy(part_ref, all_ref.at[here], sems)
    own.start()
    across = remote(part_ref, all_ref.at[here], sends.at[0], recvs.at[here], context_peer(2))
    across.start()
    beside = remote(part_ref, all_ref.at[here], sends.at[1], recvs.at[here], context_peer(1))
    beside.start()

    def pass_on():
        block = all_ref.at[here ^ 2]
        remote(part_ref, block, sends.at[0], recvs.at[here ^ 2], context_peer(2)).wait_recv()
        remote(block, block, sends.at[2], recvs.at[here ^ 2], context_peer(1)).start()

    def finish():
        block = all_ref.at[here ^ 2]
        for flip in (1, 3):
            remote(part_ref, all_ref.at[here ^ flip], sends.at[1], recvs.at[here ^ flip], context_peer(1)).wait_recv()
        across.wait_send()
        beside.wait_send()
        remote(block, block, sends.at[2], recvs.at[here ^ 2], context_peer(1)).wait_send()
        own.wait()

    return pass_on, finish


def backward_kernel(n_dp, prompt_len, riders, *refs):
    (
        dlog_ref,
        router_ref,
        cot_ref,
        x_ref,
        gain_one_ref,
        gain_two_ref,
        attended_ref,
        qkv_ref,
        kv_ref,
        log_ref,
        normed_ref,
        cos_ref,
        sin_ref,
        mid_ref,
        total_ref,
        w_out_ref,
        w_in_ref,
        four_ref,
    ) = refs[:18]
    late = len(riders)
    sources, refs = refs[18 : 18 + late], refs[18 + late :]
    grad_x_ref, gains_ref, grad_out_ref, grad_in_ref, all_ref = refs[:5]
    homes, refs = refs[5 : 5 + late], refs[5 + late :]
    (
        weights,
        grad_mid,
        grad_attn,
        mid_block,
        grad_qkv,
        grad_kv,
        kv_send,
        kv_recv,
        stage,
        load_sems,
        store_sems,
        kv_send_sems,
        kv_recv_sems,
        home_send,
        home_recv,
        own_sem,
        share_sends,
        share_recvs,
    ) = refs
    block_index = lax.axis_index("context")
    n_context = kv_send.shape[0]
    tokens = x_ref.shape[0]
    heads_width = HEADS * HD
    kv_width = KVH * HD
    greet([context_peer(flip) for flip in range(1, n_context)] + dp_peers(n_dp))
    load_total = pltpu.make_async_copy(total_ref, grad_mid, load_sems.at[0])
    load_out = pltpu.make_async_copy(w_out_ref, weights.at[:, pl.ds(0, D)], load_sems.at[1])
    load_in = pltpu.make_async_copy(w_in_ref.at[:, pl.ds(0, weights.shape[1])], weights, load_sems.at[2])
    load_total.start()
    load_out.start()
    homing = dp_moves(sources, homes, riders, home_send, home_recv)
    for move in homing:
        move.start()
    pass_on, finish = share_context(four_ref, all_ref, own_sem.at[0], share_sends, share_recvs)
    load_total.wait()
    load_out.wait()
    gains_ref[...] = jnp.zeros_like(gains_ref)

    def block_rows(n):
        return pl.ds(pl.multiple_of(n * PBLK, PBLK), PBLK)

    def through_norm(n, carry):
        rows = block_rows(n)
        load_mid = pltpu.make_async_copy(mid_ref.at[rows], mid_block, load_sems.at[3])
        load_mid.start()
        load_mid.wait()
        grads = grad_mid[rows, :] + mxu(dlog_ref[rows, :], router_ref[...], ((1,), (1,)))
        by_rows, by_gain = normed_back(mid_block[...], gain_two_ref[...], grads)
        gains_ref[1:2, :] += jnp.sum(by_gain, axis=0, keepdims=True)
        by_mid = cot_ref[rows, :].astype(F32) + by_rows
        grad_mid[rows, :] = by_mid
        low = by_mid.astype(BF)
        grad_attn[rows, :] = low
        grad_qkv[rows, :D] = mxu(low, weights[:, :D], ((1,), (1,))).astype(BF)
        return carry

    lax.fori_loop(0, tokens // PBLK, through_norm, 0)
    load_in.start()
    grad_kv[...] = jnp.zeros_like(grad_kv)

    def through_head(head, carry):
        columns = pl.ds(pl.multiple_of(head * HD, HD), HD)
        group = head // (HEADS // KVH)
        key_columns = pl.ds(pl.multiple_of(group * HD, HD), HD)
        value_columns = pl.ds(pl.multiple_of(kv_width + group * HD, HD), HD)
        for first_row, keys in row_blocks(prompt_len):
            rows = slice(first_row, first_row + PBLK)
            queries, grads = qkv_ref[rows, columns], grad_qkv[rows, columns]
            scores = mxu(queries, kv_ref[:keys, key_columns], ((1,), (1,)))
            scores = masked_scores(scores, first_row, prompt_len, block_index)
            lane = lax.broadcasted_iota(jnp.int32, (PBLK, log_ref.shape[1]), 1)
            logs = jnp.sum(jnp.where(lane == head, log_ref[rows, :], 0.0), axis=-1, keepdims=True)
            probs = jnp.exp(scores - logs)
            grad_probs = mxu(grads, kv_ref[:keys, value_columns], ((1,), (1,)))
            dots = jnp.sum(probs * grad_probs, axis=-1, keepdims=True)
            grad_scores = (probs * (grad_probs - dots)).astype(BF)
            grad_query = mxu(grad_scores, kv_ref[:keys, key_columns])
            grad_query = turn(grad_query, cos_ref[rows, :], -sin_ref[rows, :]) * (1.0 / math.sqrt(HD))
            grad_qkv[rows, columns] = grad_query.astype(BF)
            grad_kv[:keys, key_columns] += mxu(grad_scores, queries, ((0,), (0,)))
            grad_kv[:keys, value_columns] += mxu(probs.astype(BF), grads, ((0,), (0,)))
        return carry

    lax.fori_loop(0, HEADS, through_head, 0)

    for place in range(n_context):
        kv_send[place] = grad_kv[place * PBLK : (place + 1) * PBLK, :].astype(BF)
    kv_moves = [
        remote(
            kv_send.at[block_index ^ flip],
            kv_recv.at[flip],
            kv_send_sems.at[flip],
            kv_recv_sems.at[flip],
            context_peer(flip),
        )
        for flip in range(1, n_context)
    ]
    for move in kv_moves:
        move.start()
    pass_on()

    quarter = D // n_dp

    def quarter_rows(q):
        return pl.ds(pl.multiple_of(q * quarter, 128), quarter)

    def share_of_out(q, carry):
        made = mxu(attended_ref[:, quarter_rows(q)], grad_attn[...], ((0,), (0,)))
        stage[:, :D] = made.astype(BF)
        store = pltpu.make_async_copy(
            stage.at[:, pl.ds(0, D)], grad_out_ref.at[quarter_rows(q)], store_sems.at[0]
        )
        store.start()
        store.wait()
        return carry

    lax.fori_loop(0, n_dp, share_of_out, 0)

    for move in kv_moves:
        move.wait()
    own_rows = pl.ds(pl.multiple_of(block_index * PBLK, PBLK), PBLK)
    summed = grad_kv[own_rows, :]
    for flip in range(1, n_context):
        summed = summed + kv_recv[flip].astype(F32)
    pieces = [(0, PBLK, summed), (PBLK, tokens, grad_kv[prompt_len:, :])]
    for first, last, made in pieces:
        for group in range(KVH):
            turned = turn(
                made[:, group * HD : (group + 1) * HD], cos_ref[first:last, :], -sin_ref[first:last, :]
            )
            start = heads_width + group * HD
            grad_qkv[first:last, start : start + HD] = turned.astype(BF)
        grad_qkv[first:last, heads_width + kv_width :] = made[:, kv_width:].astype(BF)

    load_in.wait()

    def share_of_in(q, carry):
        stage[...] = mxu(normed_ref[:, quarter_rows(q)], grad_qkv[...], ((0,), (0,))).astype(BF)
        store = pltpu.make_async_copy(stage, grad_in_ref.at[quarter_rows(q)], store_sems.at[0])
        store.start()
        store.wait()
        return carry

    lax.fori_loop(0, n_dp, share_of_in, 0)

    def through_first(n, carry):
        rows = block_rows(n)
        grads = mxu(grad_qkv[rows, :], weights[...], ((1,), (1,)))
        by_rows, by_gain = normed_back(x_ref[rows, :].astype(F32), gain_one_ref[...], grads)
        gains_ref[0:1, :] += jnp.sum(by_gain, axis=0, keepdims=True)
        grad_x_ref[rows, :] = (grad_mid[rows, :] + by_rows).astype(BF)
        return carry

    lax.fori_loop(0, tokens // PBLK, through_first, 0)
    finish()
    for move in homing:
        move.wait()


def backward(prompt_len, n_dp, in_vmem, in_hbm, riders):
    tokens = in_vmem[0].shape[0]
    width = D + 2 * KVH * HD
    n_context = prompt_len // PBLK
    key_rows = prompt_len + CONT
    quarter = D // n_dp
    vmem = pl.BlockSpec(memory_space=pltpu.VMEM)
    anywhere = pl.BlockSpec(memory_space=pl.ANY)
    four = in_hbm[-1]
    shape = jax.ShapeDtypeStruct
    return pl.pallas_call(
        functools.partial(backward_kernel, n_dp, prompt_len, [(index, flip) for _, index, flip in riders]),
        in_specs=[vmem] * len(in_vmem) + [anywhere] * (len(in_hbm) + len(riders)),
        out_specs=[vmem] * 2 + [anywhere] * (3 + len(riders)),
        out_shape=[
            shape((tokens, D), BF),
            shape((8, D), F32),
            shape((D, D), BF),
            shape((D, width), BF),
            shape((n_context,) + four.shape, BF),
        ]
        + [shape(picked_shape(array, index), BF) for array, index, _ in riders],
        scratch_shapes=[
            pltpu.VMEM((D, width), BF),
            pltpu.VMEM((tokens, D), F32),
            pltpu.VMEM((tokens, D), BF),
            pltpu.VMEM((PBLK, D), F32),
            pltpu.VMEM((tokens, width), BF),
            pltpu.VMEM((key_rows, 2 * KVH * HD), F32),
            pltpu.VMEM((n_context, PBLK, 2 * KVH * HD), BF),
            pltpu.VMEM((n_context, PBLK, 2 * KVH * HD), BF),
            pltpu.VMEM((quarter, width), BF),
            pltpu.SemaphoreType.DMA((4,)),
            pltpu.SemaphoreType.DMA((1,)),
            pltpu.SemaphoreType.DMA((n_context,)),
            pltpu.SemaphoreType.DMA((n_context,)),
            pltpu.SemaphoreType.DMA((len(riders),)),
            pltpu.SemaphoreType.DMA((len(riders),)),
            pltpu.SemaphoreType.DMA((1,)),
            pltpu.SemaphoreType.DMA((3,)),
            pltpu.SemaphoreType.DMA((n_context,)),
        ],
        compiler_params=pltpu.CompilerParams(
            vmem_limit_bytes=56 * 1024 * 1024, collective_id=4, has_side_effects=True
        ),
        name="backward",
    )(*in_vmem, *in_hbm, *[array for array, _, _ in riders])


def reduce_kernel(n_dp, widths, *refs):
    count = len(widths)
    shares, refs = refs[:count], refs[count:]
    part_ref, for_partner_ref = refs[:2]
    refs = refs[2:]
    totals, refs = refs[:count], refs[count:]
    all_ref, of_partner_ref = refs[:2]
    refs = refs[2:]
    sums, core_in, first_in, second_in, z_in = (refs[n * count : (n + 1) * count] for n in range(5))
    (
        load_sems,
        core_send,
        core_recv,
        first_send,
        first_recv,
        second_send,
        second_recv,
        z_send,
        z_recv,
        out_send,
        out_recv,
        own_sems,
        share_sends,
        share_recvs,
        pair_sems,
    ) = refs[5 * count :]
    here = plane_here()
    z_index = lax.axis_index("dp")
    greet(
        [plane_peer(here ^ flip) for flip in (1, 2, 4)] + [{"dp": z_index ^ flip} for flip in range(1, n_dp)]
    )
    chips = (0, 2, 4, 6)
    order = [1, 2, 3, 0] if n_dp == 4 else list(range(1, n_dp)) + [0]
    loads, core_moves = {}, {}
    for n in order:
        z_to = z_index ^ n
        for a in range(count):
            for m, chip in enumerate(chips):
                loads[n, a, m] = pltpu.make_async_copy(
                    shares[a].at[z_to, here ^ chip], sums[a].at[n, m], load_sems.at[a, n, m]
                )
                loads[n, a, m].start()
                core_moves[n, a, m] = remote(
                    shares[a].at[z_to, here ^ 1 ^ chip],
                    core_in[a].at[n, m],
                    core_send.at[a, n, m],
                    core_recv.at[a, n, m],
                    plane_peer(here ^ 1),
                )
                core_moves[n, a, m].start()
    pair = remote(for_partner_ref, of_partner_ref, pair_sems.at[0], pair_sems.at[1], {"dp": z_index ^ 1})
    pair.start()
    all_on, all_done = share_context(part_ref, all_ref, own_sems.at[0], share_sends, share_recvs)

    def add(target, *others):
        total = target[...].astype(F32)
        for other in others:
            total = total + other[...].astype(F32)
        target[...] = total.astype(BF)

    first_moves, second_moves, z_moves = {}, {}, {}
    for n in order:
        toward = 2 if n % 2 == 0 else 4
        kept = 6 - toward
        for a in range(count):
            for m in range(4):
                loads[n, a, m].wait()
                core_moves[n, a, m].wait_recv()
                add(sums[a].at[n, m], core_in[a].at[n, m])
            for slot, chip in enumerate((toward, 6)):
                first_moves[n, a, slot] = remote(
                    sums[a].at[n, chip // 2],
                    first_in[a].at[n, slot],
                    first_send.at[a, n, slot],
                    first_recv.at[a, n, slot],
                    plane_peer(here ^ toward),
                )
                first_moves[n, a, slot].start()
    for n in order:
        toward = 2 if n % 2 == 0 else 4
        kept = 6 - toward
        for a in range(count):
            for slot, chip in enumerate((0, kept)):
                first_moves[n, a, slot].wait_recv()
                add(sums[a].at[n, chip // 2], first_in[a].at[n, slot])
            second_moves[n, a] = remote(
                sums[a].at[n, kept // 2],
                second_in[a].at[n],
                second_send.at[a, n],
                second_recv.at[a, n],
                plane_peer(here ^ kept),
            )
            second_moves[n, a].start()
    all_on()
    for n in order:
        for a in range(count):
            second_moves[n, a].wait_recv()
            add(sums[a].at[n, 0], second_in[a].at[n])
            if n > 0:
                z_moves[n, a] = remote(
                    sums[a].at[n, 0], z_in[a].at[n], z_send.at[a, n], z_recv.at[a, n], {"dp": z_index ^ n}
                )
                z_moves[n, a].start()
    started = list(core_moves.values()) + list(first_moves.values())
    started += list(second_moves.values()) + list(z_moves.values())

    def pass_on(a, lane, flip, place):
        block = totals[a].at[place]
        move = remote(
            block, block, out_send.at[a, lane, place], out_recv.at[a, place], plane_peer(here ^ flip)
        )
        move.start()
        started.append(move)

    def landed(a, place):
        block = totals[a].at[place]
        remote(block, block, out_send.at[a, 0, place], out_recv.at[a, place], plane_peer(here ^ 1)).wait_recv()

    for a in range(count):
        for n in range(1, n_dp):
            z_moves[n, a].wait_recv()
        add(sums[a].at[0, 0], *[z_in[a].at[n] for n in range(1, n_dp)])
        totals[a][here] = sums[a][0, 0]
        for lane, flip in enumerate((2, 4, 1)):
            pass_on(a, lane, flip, here)
    for a in range(count):
        landed(a, here ^ 2)
        if a % 2 == 1:
            pass_on(a, 1, 4, here ^ 2)
        pass_on(a, 2, 1, here ^ 2)
        landed(a, here ^ 4)
        if a % 2 == 0:
            pass_on(a, 0, 2, here ^ 4)
        pass_on(a, 2, 1, here ^ 4)
    for a in range(count):
        landed(a, here ^ 6)
        pass_on(a, 2, 1, here ^ 6)
    for a in range(count):
        for flip in (1, 3, 5, 7):
            landed(a, here ^ flip)
    for move in started:
        move.wait_send()
    all_done()
    pair.wait()


def reduce_shares(shares, part, for_partner, n_dp, n_context):
    plane, rows = shares[0].shape[1:3]
    widths = tuple(share.shape[3] for share in shares)
    count = len(widths)
    vmem = pl.BlockSpec(memory_space=pltpu.VMEM)
    anywhere = pl.BlockSpec(memory_space=pl.ANY)
    shape = jax.ShapeDtypeStruct
    dma = pltpu.SemaphoreType.DMA

    def buffers(*lead):
        return [pltpu.VMEM(lead + (rows, width), BF) for width in widths]

    return pl.pallas_call(
        functools.partial(reduce_kernel, n_dp, widths),
        in_specs=[anywhere] * (count + 2),
        out_specs=[vmem] * count + [anywhere] * 2,
        out_shape=[shape((plane, rows, width), BF) for width in widths]
        + [
            shape((n_context,) + part.shape, BF),
            shape(for_partner.shape, BF),
        ],
        scratch_shapes=buffers(n_dp, 4)
        + buffers(n_dp, 4)
        + buffers(n_dp, 2)
        + buffers(n_dp)
        + buffers(n_dp)
        + [
            dma((count, n_dp, 4)),
            dma((count, n_dp, 4)),
            dma((count, n_dp, 4)),
            dma((count, n_dp, 2)),
            dma((count, n_dp, 2)),
            dma((count, n_dp)),
            dma((count, n_dp)),
            dma((count, n_dp)),
            dma((count, n_dp)),
            dma((count, 3, plane)),
            dma((count, plane)),
            dma((1,)),
            dma((3,)),
            dma((n_context,)),
            dma((2,)),
        ],
        compiler_params=pltpu.CompilerParams(
            vmem_limit_bytes=VMEM_BYTES, collective_id=5, has_side_effects=True
        ),
        name="reduce_shares",
    )(*shares, part, for_partner)


def finish_kernel(down, first_ref, second_ref, out_ref):
    experts = out_ref.shape[1]
    both = [ref[:, :, 0].astype(F32) for ref in (first_ref, second_ref)]
    both = jnp.stack(both, axis=2).reshape((experts,) + both[0].shape[2:])
    if not down:
        out_ref[...] = jnp.swapaxes(both, 0, 1)
        return
    half = out_ref.shape[2] // 2
    for side in range(2):
        out_ref[:, :, side * half : (side + 1) * half] = jnp.swapaxes(both[:, side], 0, 1)


def finish_weight(which, first, second):
    n_context, pair, _, rows, width = first.shape
    experts = n_context * pair * 2
    step = 32
    down = which == 2
    if down:
        rows = rows // 2
        first, second = (part.reshape(part.shape[:3] + (2, rows, width)) for part in (first, second))
        spec = pl.BlockSpec((n_context, pair, 1, 2, step, width), lambda j: (0, 0, which, 0, j, 0))
        width = 2 * width
    else:
        spec = pl.BlockSpec((n_context, pair, 1, step, width), lambda j: (0, 0, which, j, 0))
    return pl.pallas_call(
        functools.partial(finish_kernel, down),
        grid=(rows // step,),
        in_specs=[spec, spec],
        out_specs=pl.BlockSpec((step, experts, width), lambda j: (j, 0, 0)),
        out_shape=jax.ShapeDtypeStruct((rows, experts, width), F32),
        compiler_params=grant(),
        name="finish_weight",
    )(first, second)


def tie(*values):
    return lax.optimization_barrier(values)


def flip_permute(value, axis, size, flip):
    return lax.ppermute(value, axis, [(i, i ^ flip) for i in range(size)])


def local_paired(
    inputs,
    cotangent,
    routes,
    attn_q,
    attn_k,
    attn_v,
    attn_o,
    norm_attn,
    norm_moe,
    router,
    expert_gate,
    expert_up,
    expert_down,
):
    n_context, n_expert, n_dp = lax.axis_size("context"), lax.axis_size("expert"), lax.axis_size("dp")
    plane = n_context * n_expert
    tokens = inputs.shape[1]
    block_index = lax.axis_index("context")
    z_index = lax.axis_index("dp")
    parity = z_index % 2
    prompt_len = PBLK * n_context
    x_low = inputs[0]
    cot_low = cotangent[0]
    route_rows = routes[0]

    small = jnp.concatenate(
        [router, norm_attn[:, None], norm_moe[:, None]], axis=1
    ).astype(BF)
    small = jnp.pad(small, ((0, 0), (0, 128 - small.shape[1])))
    shard_in = jnp.concatenate([attn_q.astype(BF), attn_k.astype(BF), attn_v.astype(BF), small], axis=1)
    here = lax.axis_index("expert") * n_context + block_index
    part_rows = attn_q.shape[0] // plane
    part_of = lambda shard: lax.dynamic_slice_in_dim(shard, here * part_rows, part_rows, 0)
    whole_in, out_parts, partner_routes = gather_parts(
        part_of(shard_in), part_of(attn_o).astype(BF), route_rows, n_dp, plane
    )
    whole_in = whole_in.reshape(-1, shard_in.shape[1])
    w_out = lax.all_gather(out_parts, PLANE, axis=1, tiled=False).reshape(-1, D)
    qkv_width = D + 2 * KVH * HD
    w_router = whole_in[:, qkv_width : qkv_width + EXPERTS]
    gain_one = whole_in[:, qkv_width + EXPERTS].astype(F32)
    gain_two = whole_in[:, qkv_width + EXPERTS + 1].astype(F32)

    per_device = expert_gate.shape[1] // n_context

    def weight_pieces(weight):
        mine = lax.dynamic_slice_in_dim(weight, block_index * per_device, per_device, 1)
        mine = mine.astype(BF).transpose(1, 0, 2)
        mine = mine.reshape(2, per_device // 2, mine.shape[1], mine.shape[2])
        same = lax.dynamic_index_in_dim(mine, parity, 0, keepdims=False)
        other = lax.dynamic_index_in_dim(mine, 1 - parity, 0, keepdims=False)
        return same, other

    weight_halves = [weight_pieces(weight) for weight in (expert_gate, expert_up, expert_down)]
    pieces = {(which, 0, i): (weight_halves[which][0], i) for which in range(3) for i in range(2)}
    moved_early = {flip: flip_permute(weight_halves[0][flip % 2], "dp", n_dp, flip) for flip in (2, 1)}

    def riding(names):
        return [(weight_halves[which][flip % 2], i, flip) for which, flip, i in names]

    def pieces_of(expert):
        return [pieces[which, flip, expert] for which in range(3) for flip in range(n_dp)]


    def ranks_of(rows):
        named = jnp.sum(
            (rows[:, :, None] == jnp.arange(EXPERTS, dtype=jnp.int32)[None, None, :]).astype(F32), axis=1
        )
        order = jnp.arange(tokens, dtype=jnp.int32)
        before = (order[None, :] < order[:, None]).astype(BF)
        count = mxu(before, named.astype(BF))
        return named > 0, jnp.where(named > 0, count, -1.0)

    named, own_ranks = ranks_of(route_rows)
    partner_ranks = ranks_of(partner_routes)[1]

    def mine_of(table):
        parted = table.reshape(tokens, plane, 2, 2)
        return lax.dynamic_index_in_dim(parted, parity, 2, keepdims=False)

    own_sel = mine_of(own_ranks)
    partner_sel = mine_of(partner_ranks)
    own_pair = [own_sel[:, :, i].astype(BF) for i in range(2)]
    partner_pair = [partner_sel[:, :, i].astype(BF) for i in range(2)]

    own_ranks_t = jnp.stack(own_pair, axis=0).transpose(0, 2, 1)
    partner_ranks_t = jnp.stack(partner_pair, axis=0).transpose(0, 2, 1)
    partner_cot = flip_permute(cot_low, "dp", n_dp, 1)

    positions = jnp.concatenate(
        [
            block_index * PBLK + jnp.arange(PBLK, dtype=jnp.int32),
            prompt_len + jnp.arange(CONT, dtype=jnp.int32),
        ]
    )
    angles = angle_table(positions)
    cos_half, sin_half = jnp.cos(angles), jnp.sin(angles)
    cosine = jnp.concatenate([cos_half, cos_half], axis=1)
    sine = jnp.concatenate([-sin_half, sin_half], axis=1)
    block_word = block_index.astype(jnp.int32).reshape(1)
    z_word = z_index.astype(jnp.int32).reshape(1)
    qkv, normed_one = project(x_low, gain_one[None, :], whole_in, qkv_width, cosine, sine)
    keys_own = qkv[:, D:]
    prompt_kv = lax.all_gather(keys_own[:PBLK], "context", axis=0, tiled=True)
    keys_values = jnp.concatenate([prompt_kv, keys_own[PBLK:]], axis=0)
    attended, logs = attend(block_word, qkv, keys_values, prompt_len)
    x_rows = x_low.astype(F32)
    mid_rows = x_rows + mxu(attended, w_out)
    normed_two = rms_scale(mid_rows, gain_two).astype(BF)

    normed_two, partner_cot, moved_early[1], moved_early[2] = tie(
        normed_two, partner_cot, moved_early[1], moved_early[2]
    )
    for flip, moved in moved_early.items():
        for i in range(2):
            pieces[0, flip, i] = (moved, i)
    landed, staged, arrived = dispatch_rows(
        normed_two, cot_low, partner_cot, own_ranks_t, partner_ranks_t, riding(RIDE_DISPATCH), n_dp
    )
    pieces.update({name: (piece, None) for name, piece in zip(RIDE_DISPATCH, arrived)})
    logits = mxu(normed_two, w_router)
    top_logit = jnp.max(jnp.where(named, logits, masked_score), axis=1, keepdims=True)
    raised = jnp.where(named, jnp.exp(jnp.where(named, logits - top_logit, 0.0)), 0.0)
    gates = raised / jnp.sum(raised, axis=1, keepdims=True)

    slot_ids = jnp.arange(SLOTS, dtype=F32)
    hits = own_ranks.T[:, None, :] == slot_ids[None, :, None]
    slot_gates = jnp.sum(jnp.where(hits, gates.T[:, None, :], 0.0), axis=-1)
    slot_gates = slot_gates.reshape(plane, 2, 2, SLOTS)
    own_gates = lax.dynamic_index_in_dim(slot_gates, parity, 1, keepdims=False)
    other_gates = lax.dynamic_index_in_dim(slot_gates, 1 - parity, 1, keepdims=False)
    partner_gates = flip_permute(other_gates, "dp", n_dp, 1)
    both_gates = jnp.stack([own_gates, partner_gates], axis=1)
    both_gates = lax.all_to_all(both_gates, PLANE, split_axis=0, concat_axis=0, tiled=True)

    def gates_of(expert):
        return [both_gates[:, side, expert].reshape(plane * SLOTS, 1) for side in range(2)]

    def slots_of(arrays):
        flat = [array.reshape(plane * SLOTS, D) for array in arrays]
        return (flat[0], flat[3]), (flat[1], flat[2])

    parted = lambda arrays: [array.reshape(plane, SLOTS, D) for array in arrays]
    rows, cots = slots_of(landed)
    first, first_dots, first_shares, landed, arrived = run_expert(
        "first_expert", 6, rows, cots, gates_of(0), pieces_of(0), staged, riding(RIDE_FIRST)
    )
    pieces.update({name: (piece, None) for name, piece in zip(RIDE_FIRST, arrived)})
    rows, cots = slots_of(landed)
    home_of = {}

    def homing(names, *shares):
        return [(shares[i][which], flip, flip) for which, flip, i in names]

    second, second_dots, second_shares, early, homes = run_expert(
        "second_expert",
        7,
        rows,
        cots,
        gates_of(1),
        pieces_of(1),
        parted(first),
        homing(HOME_SECOND, first_shares),
    )
    home_of.update(zip(HOME_SECOND, homes))

    dots = jnp.stack(
        [d[side].reshape(plane, SLOTS) for side in range(2) for d in (first_dots, second_dots)], axis=1
    )
    dots = jnp.pad(dots, ((0, 0), (0, 0), (0, 128 - SLOTS)))
    second = parted(second)
    grad_rows, dots_here, dots_other, late, homes = return_rows(
        jnp.stack(own_pair, axis=0),
        jnp.stack(partner_pair, axis=0),
        dots,
        early[2:4],
        second[2:4],
        second[0:2],
        homing(HOME_RETURN, first_shares, second_shares),
        n_dp,
    )
    home_of.update(zip(HOME_RETURN, homes))
    flat = lambda array: array.reshape(plane * SLOTS, D)
    out_own, out_partner = ([flat(early[side]), flat(late[side])] for side in range(2))
    own_dots = dots_here[:, 0:2, :SLOTS]
    other_dots = dots_other[:, 2:4, :SLOTS]
    all_dots = jnp.where(
        parity == 0,
        jnp.stack([own_dots, other_dots], axis=1),
        jnp.stack([other_dots, own_dots], axis=1),
    ).reshape(EXPERTS, SLOTS)
    grad_gates = jnp.sum(
        jnp.where(own_ranks[:, :, None] == slot_ids[None, None, :], all_dots[None], 0.0), axis=-1
    )
    grad_logits = gates * (grad_gates - jnp.sum(gates * grad_gates, axis=1, keepdims=True))
    grad_logits = grad_logits.astype(BF)
    grad_wrouter = mxu(normed_two, grad_logits, ((0,), (0,)))

    def part_of_expert(expert, shares):
        parts = []
        for which in range(3):
            got = [shares[which][0]] + [home_of[which, flip, expert] for flip in range(1, n_dp)]
            same = sum(got[flip].astype(F32) for flip in range(0, n_dp, 2)).astype(BF)
            other = sum(got[flip].astype(F32) for flip in range(1, n_dp, 2)).astype(BF)
            parts.append(
                jnp.stack([jnp.where(parity == 0, same, other), jnp.where(parity == 0, other, same)])
            )
        return jnp.stack(parts, axis=1)

    grad_inputs, grad_gains, grad_wout, grad_wqkv, all_first, *homes = backward(
        prompt_len,
        n_dp,
        (
            grad_logits,
            w_router,
            cot_low,
            x_low,
            gain_one[None, :],
            gain_two[None, :],
            attended,
            qkv,
            keys_values,
            logs,
            normed_one,
            cosine,
            sine,
        ),
        (mid_rows, grad_rows, w_out, whole_in, part_of_expert(0, first_shares)),
        homing(HOME_BACKWARD, first_shares, second_shares),
    )
    home_of.update(zip(HOME_BACKWARD, homes))

    out_for_partner = collect_rows(partner_pair[0], partner_pair[1], *out_partner, BF)
    grad_small = jnp.concatenate([grad_wrouter, grad_gains[0][:, None], grad_gains[1][:, None]], axis=1)
    grad_small = jnp.pad(grad_small, ((0, 0), (0, 128 - grad_small.shape[1]))).astype(BF)
    parts = lambda share: share.reshape(n_dp, plane, -1, share.shape[1])
    total_qkv, total_out, total_small, all_second, out_from_partner = reduce_shares(
        [parts(grad_wqkv), parts(grad_wout), parts(grad_small)],
        part_of_expert(1, second_shares),
        out_for_partner,
        n_dp,
        n_context,
    )
    moe_out = collect_rows(own_pair[0], own_pair[1], *out_own, F32)
    result = (mid_rows + moe_out + out_from_partner.astype(F32)).astype(BF)
    total_qkv = total_qkv.reshape(-1, qkv_width).astype(F32)
    total_out = total_out.reshape(-1, D).astype(F32)
    total_small = total_small.reshape(-1, 128).astype(F32)
    return (
        result[None],
        grad_inputs[None],
        total_qkv[:, :D],
        total_qkv[:, D : D + KVH * HD],
        total_qkv[:, D + KVH * HD :],
        total_out,
        total_small[:, EXPERTS],
        total_small[:, EXPERTS + 1],
        total_small[:, :EXPERTS],
        finish_weight(0, all_first, all_second),
        finish_weight(1, all_first, all_second),
        finish_weight(2, all_first, all_second),
    )


def paired_plan(mesh):
    n_expert, n_context, n_dp = mesh.shape["expert"], mesh.shape["context"], mesh.shape["dp"]
    owners = 2 * n_expert * n_context
    small_axes = all(size & (size - 1) == 0 for size in (n_expert, n_context, n_dp))
    return small_axes and n_dp % 2 == 0 and EXPERTS == 2 * owners


def solution(mesh):
    in_specs = (
        P(("expert", "dp"), "context", None),
        P(("expert", "dp"), "context", None),
        P(("expert", "dp"), "context", None),
        P("dp", None),
        P("dp", None),
        P("dp", None),
        P("dp", None),
        P("dp"),
        P("dp"),
        P("dp", None),
        P("dp", "expert", None),
        P("dp", "expert", None),
        P("dp", "expert", None),
    )
    out_specs = (
        P(("expert", "dp"), "context", None),
        P(("expert", "dp"), "context", None),
        P("dp", None),
        P("dp", None),
        P("dp", None),
        P("dp", None),
        P("dp"),
        P("dp"),
        P("dp", None),
        P("dp", "expert", None),
        P("dp", "expert", None),
        P("dp", "expert", None),
    )
    chosen = local_paired if paired_plan(mesh) else local
    return jax.shard_map(chosen, mesh=mesh, in_specs=in_specs, out_specs=out_specs, check_vma=False)
```

```python
import functools
import math

import jax
import jax.numpy as jnp
from jax import lax
from jax.experimental import pallas as pl
from jax.experimental.pallas import tpu as pltpu
from jax.sharding import PartitionSpec as P

D = 1536
HEADS = 12
KVH = 2
HD = 128
EXPERTS = 32
TOP = 4
PBLK = 256
CONT = 512
CAP = 103


epsilon = 1e-06
rope_base = 1000000.0
masked_score = -1e30


def rms_scale(values, gain):
    return values * lax.rsqrt(jnp.mean(values * values, axis=-1, keepdims=True) + epsilon) * gain


def angle_table(positions):
    steps_half = jnp.arange(HD // 2, dtype=jnp.float32)
    inverse = jnp.exp(steps_half * (-2.0 * math.log(rope_base) / HD))
    return positions.astype(jnp.float32)[..., None] * inverse


def rotary(values, angles, direction):
    halfway = values.shape[-1] // 2
    cosine = jnp.cos(angles)[..., None, :]
    sine_part = direction * jnp.sin(angles)[..., None, :]
    leading = values[..., :halfway]
    trailing = values[..., halfway:]
    return jnp.concatenate(
        [leading * cosine - trailing * sine_part, trailing * cosine + leading * sine_part], axis=-1
    )


def visible(query_pos, key_pos, prompt_len):
    query_cont = jnp.arange(query_pos.shape[0]) >= PBLK
    key_prompt = jnp.arange(key_pos.shape[0]) < prompt_len
    return (key_pos[None, :] <= query_pos[:, None]) & (key_prompt[None, :] | query_cont[:, None])


def gating(logit_rows, route_rows):
    picker = (route_rows[:, :, None] == jnp.arange(EXPERTS, dtype=jnp.int32)[None, None, :]).astype(
        logit_rows.dtype
    )
    chosen = jnp.sum(picker * logit_rows[:, None, :], axis=-1)
    return jax.nn.softmax(chosen, axis=-1)


def gated(gate_pre, up_pre):
    return jax.nn.silu(gate_pre) * up_pre


def expert_slots(flat_experts):
    picker = (flat_experts[:, None] == jnp.arange(EXPERTS, dtype=jnp.int32)[None, :]).astype(
        jnp.int32
    )
    earlier = jnp.cumsum(picker, axis=0) - picker
    return jnp.sum(earlier * picker, axis=1)


def local(
    inputs,
    cotangent,
    routes,
    attn_q,
    attn_k,
    attn_v,
    attn_o,
    norm_attn,
    norm_moe,
    router,
    expert_gate,
    expert_up,
    expert_down,
):
    low_type = jnp.bfloat16
    full_type = jnp.float32
    w_query, w_key, w_value, w_out, gain_first, gain_second, w_router, w_gate, w_up, w_down = (
        lax.all_gather(attn_q.astype(low_type), "dp", axis=0, tiled=True),
        lax.all_gather(attn_k.astype(low_type), "dp", axis=0, tiled=True),
        lax.all_gather(attn_v.astype(low_type), "dp", axis=0, tiled=True),
        lax.all_gather(attn_o.astype(low_type), "dp", axis=0, tiled=True),
        lax.all_gather(norm_attn.astype(low_type), "dp", axis=0, tiled=True),
        lax.all_gather(norm_moe.astype(low_type), "dp", axis=0, tiled=True),
        lax.all_gather(router.astype(low_type), "dp", axis=0, tiled=True),
        lax.all_gather(expert_gate.astype(low_type), "dp", axis=0, tiled=True),
        lax.all_gather(expert_up.astype(low_type), "dp", axis=0, tiled=True),
        lax.all_gather(expert_down.astype(low_type), "dp", axis=0, tiled=True),
    )
    n_context = lax.axis_size("context")
    n_expert = lax.axis_size("expert")
    block_index = lax.axis_index("context")
    prompt_len = PBLK * n_context
    tokens = inputs.shape[1]
    local_experts = w_gate.shape[1]
    group_width = HEADS // KVH
    score_scale = 1.0 / math.sqrt(HD)
    gain_one = gain_first.astype(full_type)
    gain_two = gain_second.astype(full_type)
    x_rows = inputs[0].astype(full_type)
    positions = jnp.concatenate(
        [
            block_index * PBLK + jnp.arange(PBLK, dtype=jnp.int32),
            prompt_len + jnp.arange(CONT, dtype=jnp.int32),
        ]
    )
    angles = angle_table(positions)
    normed_one = rms_scale(x_rows, gain_one).astype(low_type)
    q_proj = jnp.dot(normed_one, w_query, preferred_element_type=full_type)
    k_proj = jnp.dot(normed_one, w_key, preferred_element_type=full_type)
    v_proj = jnp.dot(normed_one, w_value, preferred_element_type=full_type)
    queries = (rotary(q_proj.reshape(tokens, HEADS, HD), angles, 1.0) * score_scale).astype(
        low_type
    )
    queries = queries.reshape(tokens, KVH, group_width, HD)
    keys_own = rotary(k_proj.reshape(tokens, KVH, HD), angles, 1.0).astype(low_type)
    values_own = v_proj.astype(low_type).reshape(tokens, KVH, HD)
    prompt_keys, prompt_values = (
        lax.all_gather(keys_own[:PBLK], "context", axis=0, tiled=True),
        lax.all_gather(values_own[:PBLK], "context", axis=0, tiled=True),
    )
    all_keys = jnp.concatenate([prompt_keys, keys_own[PBLK:]], axis=0)
    all_values = jnp.concatenate([prompt_values, values_own[PBLK:]], axis=0)
    key_pos = jnp.concatenate(
        [jnp.arange(prompt_len, dtype=jnp.int32), prompt_len + jnp.arange(CONT, dtype=jnp.int32)]
    )
    allowed = visible(positions, key_pos, prompt_len)
    head_outs = []
    log_totals = []
    for kv_head in range(KVH):
        scores = jnp.einsum(
            "tgn,kn->gtk",
            queries[:, kv_head],
            all_keys[:, kv_head],
            preferred_element_type=full_type,
        )
        scores = jnp.where(allowed[None], scores, masked_score)
        top_score = jnp.max(scores, axis=-1, keepdims=True)
        unnormed = jnp.exp(scores - top_score)
        totals = jnp.sum(unnormed, axis=-1, keepdims=True)
        attn_probs = (unnormed / totals).astype(low_type)
        head_outs.append(
            jnp.einsum(
                "gtk,kn->tgn", attn_probs, all_values[:, kv_head], preferred_element_type=full_type
            )
        )
        log_totals.append(top_score + jnp.log(totals))
    attended_low = jnp.stack(head_outs, axis=1).reshape(tokens, D).astype(low_type)
    mid_rows = x_rows + jnp.dot(attended_low, w_out, preferred_element_type=full_type)
    normed_two = rms_scale(mid_rows, gain_two).astype(low_type)
    logits = jnp.dot(normed_two, w_router, preferred_element_type=full_type)
    route_rows = routes[0]
    gate_weights = gating(logits, route_rows)
    flat_experts = route_rows.reshape(-1)
    slot_rank = expert_slots(flat_experts)
    destination = (
        flat_experts % local_experts * n_expert + flat_experts // local_experts
    ) * CAP + slot_rank
    capacity_rows = local_experts * n_expert * CAP
    assignments = tokens * TOP
    source = (
        jnp.full((capacity_rows,), assignments, dtype=jnp.int32)
        .at[destination]
        .set(jnp.arange(assignments, dtype=jnp.int32))
    )
    filled = source < assignments
    source_row = jnp.minimum(source, assignments - 1)
    send_rows = jnp.where(filled[:, None], normed_two[source_row // TOP], jnp.zeros((), low_type))
    received = lax.all_to_all(
        send_rows.reshape(local_experts, n_expert, CAP, D),
        "expert",
        split_axis=1,
        concat_axis=1,
        tiled=True,
    )
    received = received.reshape(local_experts, n_expert * CAP, D)
    gate_pre = jnp.einsum("lrd,dlf->lrf", received, w_gate, preferred_element_type=full_type)
    up_pre = jnp.einsum("lrd,dlf->lrf", received, w_up, preferred_element_type=full_type)
    activation = gated(gate_pre, up_pre).astype(low_type)
    expert_rows = jnp.einsum(
        "lrf,fld->lrd", activation, w_down, preferred_element_type=full_type
    ).astype(low_type)
    returned = lax.all_to_all(
        expert_rows.reshape(local_experts, n_expert, CAP, D),
        "expert",
        split_axis=1,
        concat_axis=1,
        tiled=True,
    )
    returned = returned.reshape(capacity_rows, D)
    picked = returned[destination].reshape(tokens, TOP, D)
    moe_out = jnp.sum(gate_weights[:, :, None] * picked.astype(full_type), axis=1)
    result = (mid_rows + moe_out).astype(low_type)
    grad_out = cotangent[0].astype(full_type)
    slot_grads = (
        (gate_weights[:, :, None] * grad_out[:, None, :]).reshape(assignments, D).astype(low_type)
    )
    send_grads = jnp.where(filled[:, None], slot_grads[source_row], jnp.zeros((), low_type))
    grad_rows = lax.all_to_all(
        send_grads.reshape(local_experts, n_expert, CAP, D),
        "expert",
        split_axis=1,
        concat_axis=1,
        tiled=True,
    )
    grad_rows = grad_rows.reshape(local_experts, n_expert * CAP, D)
    grad_gates = jnp.sum(picked.astype(full_type) * grad_out[:, None, :], axis=-1)
    grad_wdown = jnp.einsum("lrf,lrd->fld", activation, grad_rows, preferred_element_type=full_type)
    grad_act = jnp.einsum("lrd,fld->lrf", grad_rows, w_down, preferred_element_type=full_type)
    primal_gate, gated_back = jax.vjp(gated, gate_pre, up_pre)
    grad_gpre, grad_upre = gated_back(grad_act)
    grad_gpre = grad_gpre.astype(low_type)
    grad_upre = grad_upre.astype(low_type)
    grad_wgate = jnp.einsum("lrd,lrf->dlf", received, grad_gpre, preferred_element_type=full_type)
    grad_wup = jnp.einsum("lrd,lrf->dlf", received, grad_upre, preferred_element_type=full_type)
    grad_recv = jnp.einsum("lrf,dlf->lrd", grad_gpre, w_gate, preferred_element_type=full_type)
    grad_recv = (
        grad_recv + jnp.einsum("lrf,dlf->lrd", grad_upre, w_up, preferred_element_type=full_type)
    ).astype(low_type)
    back_rows = lax.all_to_all(
        grad_recv.reshape(local_experts, n_expert, CAP, D),
        "expert",
        split_axis=1,
        concat_axis=1,
        tiled=True,
    )
    back_rows = back_rows.reshape(capacity_rows, D)
    grad_normed_two = jnp.sum(
        back_rows[destination].reshape(tokens, TOP, D).astype(full_type), axis=1
    )

    def gate_of(logit_rows):
        return gating(logit_rows, route_rows)

    primal_gates, gate_back = jax.vjp(gate_of, logits)
    grad_logits = gate_back(grad_gates)[0].astype(low_type)
    grad_wrouter = jnp.einsum(
        "td,te->de", normed_two, grad_logits, preferred_element_type=full_type
    )
    grad_normed_two = grad_normed_two + jnp.einsum(
        "te,de->td", grad_logits, w_router, preferred_element_type=full_type
    )
    primal_two, norm_back_two = jax.vjp(rms_scale, mid_rows, gain_two)
    grad_mid_norm, grad_gain_two = norm_back_two(grad_normed_two)
    grad_mid = grad_out + grad_mid_norm
    grad_attn = grad_mid.astype(low_type)
    grad_wout = jnp.einsum("td,te->de", attended_low, grad_attn, preferred_element_type=full_type)
    grad_attended = jnp.einsum(
        "te,de->td", grad_attn, w_out, preferred_element_type=full_type
    ).astype(low_type)
    grad_attended = grad_attended.reshape(tokens, KVH, group_width, HD)
    query_grads = []
    key_grads = []
    value_grads = []
    for kv_head in range(KVH):
        scores = jnp.einsum(
            "tgn,kn->gtk",
            queries[:, kv_head],
            all_keys[:, kv_head],
            preferred_element_type=full_type,
        )
        scores = jnp.where(allowed[None], scores, masked_score)
        exact_probs = jnp.exp(scores - log_totals[kv_head])
        grad_probs = jnp.einsum(
            "tgn,kn->gtk",
            grad_attended[:, kv_head],
            all_values[:, kv_head],
            preferred_element_type=full_type,
        )
        row_dots = jnp.sum(exact_probs * grad_probs, axis=-1, keepdims=True)
        grad_scores = (exact_probs * (grad_probs - row_dots)).astype(low_type)
        query_grads.append(
            jnp.einsum(
                "gtk,kn->tgn", grad_scores, all_keys[:, kv_head], preferred_element_type=full_type
            )
        )
        key_grads.append(
            jnp.einsum(
                "gtk,tgn->kn", grad_scores, queries[:, kv_head], preferred_element_type=full_type
            )
        )
        value_grads.append(
            jnp.einsum(
                "gtk,tgn->kn",
                exact_probs.astype(low_type),
                grad_attended[:, kv_head],
                preferred_element_type=full_type,
            )
        )
    grad_queries = jnp.stack(query_grads, axis=1).reshape(tokens, HEADS, HD)
    grad_keys = jnp.stack(key_grads, axis=1)
    grad_values = jnp.stack(value_grads, axis=1)
    prompt_key_grad, prompt_value_grad = (
        lax.psum_scatter(
            grad_keys[:prompt_len].astype(jnp.bfloat16), "context", scatter_dimension=0, tiled=True
        ).astype(jnp.float32),
        lax.psum_scatter(
            grad_values[:prompt_len].astype(jnp.bfloat16),
            "context",
            scatter_dimension=0,
            tiled=True,
        ).astype(jnp.float32),
    )
    own_key_grad = jnp.concatenate([prompt_key_grad, grad_keys[prompt_len:]], axis=0)
    own_value_grad = jnp.concatenate([prompt_value_grad, grad_values[prompt_len:]], axis=0)
    grad_qproj = (
        rotary(grad_queries * score_scale, angles, -1.0).reshape(tokens, D).astype(low_type)
    )
    grad_kproj = rotary(own_key_grad, angles, -1.0).reshape(tokens, KVH * HD).astype(low_type)
    grad_vproj = own_value_grad.reshape(tokens, KVH * HD).astype(low_type)
    grad_wquery = jnp.einsum("td,te->de", normed_one, grad_qproj, preferred_element_type=full_type)
    grad_wkey = jnp.einsum("td,te->de", normed_one, grad_kproj, preferred_element_type=full_type)
    grad_wvalue = jnp.einsum("td,te->de", normed_one, grad_vproj, preferred_element_type=full_type)
    grad_normed_one = jnp.einsum("te,de->td", grad_qproj, w_query, preferred_element_type=full_type)
    grad_normed_one = grad_normed_one + jnp.einsum(
        "te,de->td", grad_kproj, w_key, preferred_element_type=full_type
    )
    grad_normed_one = grad_normed_one + jnp.einsum(
        "te,de->td", grad_vproj, w_value, preferred_element_type=full_type
    )
    primal_one, norm_back_one = jax.vjp(rms_scale, x_rows, gain_one)
    grad_x_norm, grad_gain_one = norm_back_one(grad_normed_one)
    grad_inputs = (grad_mid + grad_x_norm).astype(low_type)
    shares = (
        lax.psum_scatter(
            grad_wquery.astype(jnp.bfloat16), "dp", scatter_dimension=0, tiled=True
        ).astype(jnp.float32),
        lax.psum_scatter(
            grad_wkey.astype(jnp.bfloat16), "dp", scatter_dimension=0, tiled=True
        ).astype(jnp.float32),
        lax.psum_scatter(
            grad_wvalue.astype(jnp.bfloat16), "dp", scatter_dimension=0, tiled=True
        ).astype(jnp.float32),
        lax.psum_scatter(
            grad_wout.astype(jnp.bfloat16), "dp", scatter_dimension=0, tiled=True
        ).astype(jnp.float32),
        lax.psum_scatter(
            grad_gain_one.astype(jnp.bfloat16), "dp", scatter_dimension=0, tiled=True
        ).astype(jnp.float32),
        lax.psum_scatter(
            grad_gain_two.astype(jnp.bfloat16), "dp", scatter_dimension=0, tiled=True
        ).astype(jnp.float32),
        lax.psum_scatter(
            grad_wrouter.astype(jnp.bfloat16), "dp", scatter_dimension=0, tiled=True
        ).astype(jnp.float32),
        lax.psum_scatter(
            grad_wgate.astype(jnp.bfloat16), "dp", scatter_dimension=0, tiled=True
        ).astype(jnp.float32),
        lax.psum_scatter(
            grad_wup.astype(jnp.bfloat16), "dp", scatter_dimension=0, tiled=True
        ).astype(jnp.float32),
        lax.psum_scatter(
            grad_wdown.astype(jnp.bfloat16), "dp", scatter_dimension=0, tiled=True
        ).astype(jnp.float32),
    )
    dense_sum = lax.psum(
        (shares[0], shares[1], shares[2], shares[3], shares[4], shares[5], shares[6]),
        ("expert", "context"),
    )
    expert_sum = (
        lax.psum(shares[7].astype(jnp.bfloat16), "context").astype(jnp.float32),
        lax.psum(shares[8].astype(jnp.bfloat16), "context").astype(jnp.float32),
        lax.psum(shares[9].astype(jnp.bfloat16), "context").astype(jnp.float32),
    )
    totals_all = tuple(dense_sum) + tuple(expert_sum)
    return (
        result[None],
        grad_inputs[None],
        totals_all[0],
        totals_all[1],
        totals_all[2],
        totals_all[3],
        totals_all[4],
        totals_all[5],
        totals_all[6],
        totals_all[7],
        totals_all[8],
        totals_all[9],
    )


BF = jnp.bfloat16
F32 = jnp.float32
SLOTS = 112
MESH_ID = pl.DeviceIdType.MESH
PLANE = ("expert", "context")
VMEM_BYTES = 60 * 1024 * 1024


def mxu(lhs, rhs, contract=((1,), (0,))):
    return lax.dot_general(lhs, rhs, (contract, ((), ())), preferred_element_type=F32)


def grant(bytes_wanted=VMEM_BYTES):
    return pltpu.CompilerParams(vmem_limit_bytes=bytes_wanted)


def turn(values, cosine, sine):
    return values * cosine + pltpu.roll(values, HD // 2, 1) * sine


def row_blocks(prompt_len):
    blocks = [(0, prompt_len)]
    for start in range(0, CONT, PBLK):
        blocks.append((PBLK + start, prompt_len + start + PBLK))
    return blocks


def masked_scores(scores, first_row, prompt_len, block_index):
    row = lax.broadcasted_iota(jnp.int32, scores.shape, 0)
    column = lax.broadcasted_iota(jnp.int32, scores.shape, 1)
    if first_row == 0:
        limit = row + block_index * PBLK
    else:
        limit = row + (prompt_len + first_row - PBLK)
    return jnp.where(column <= limit, scores, masked_score)


def segment_matrix(parts, transposed):
    shape = (parts * SLOTS, parts) if transposed else (parts, parts * SLOTS)
    long = lax.broadcasted_iota(jnp.int32, shape, 0 if transposed else 1)
    short = lax.broadcasted_iota(jnp.int32, shape, 1 if transposed else 0)
    inside = (long >= short * SLOTS) & (long < (short + 1) * SLOTS)
    return jnp.where(inside, 1.0, 0.0).astype(BF)


def slot_matrix(ranks, parts, transposed):
    if transposed:
        spread = mxu(segment_matrix(parts, True), ranks)
        slot = lax.broadcasted_iota(jnp.int32, (parts * SLOTS, 1), 0)
    else:
        spread = mxu(ranks, segment_matrix(parts, False))
        slot = lax.broadcasted_iota(jnp.int32, (1, parts * SLOTS), 1)
    for part in range(parts - 1, 0, -1):
        slot = jnp.where(slot >= part * SLOTS, slot - SLOTS, slot)
    return jnp.where(spread == slot.astype(F32), 1.0, 0.0).astype(BF)


def collect_into(plane, rank_ref, held, base, target, finish):
    def block(n, carry):
        rows = pl.ds(pl.multiple_of(n * PBLK, PBLK), PBLK)
        made = jnp.zeros((PBLK, D), F32)
        for expert in range(2):
            chooser = slot_matrix(rank_ref[expert, rows, :], plane, False)
            made = made + mxu(chooser, held[base + expert].reshape(plane * SLOTS, D))
        target[rows, :] = finish(rows, made)
        return carry

    lax.fori_loop(0, target.shape[0] // PBLK, block, 0)


def plane_exchange(slot, source, target, local_sems, send_sems, recv_sems, bounce=None):
    here = plane_here()
    plane = source.shape[0]
    own_first = target.at[here] if bounce is None else bounce.at[slot]

    def begin():
        pltpu.make_async_copy(source.at[here], own_first, local_sems.at[slot]).start()

        def one(flip, carry):
            peer = here ^ flip
            remote(
                source.at[peer],
                target.at[here],
                send_sems.at[slot, peer],
                recv_sems.at[slot, here],
                plane_peer(peer),
            ).start()
            return carry

        lax.fori_loop(1, plane, one, 0)

    def finish():
        pltpu.make_async_copy(source.at[here], own_first, local_sems.at[slot]).wait()
        if bounce is not None:
            onward = pltpu.make_async_copy(own_first, target.at[here], local_sems.at[slot])
            onward.start()
            onward.wait()

        def one(flip, carry):
            peer = here ^ flip
            done = remote(
                source.at[peer],
                target.at[peer],
                send_sems.at[slot, peer],
                recv_sems.at[slot, peer],
                plane_peer(peer),
            )
            done.wait_send()
            done.wait_recv()
            return carry

        lax.fori_loop(1, plane, one, 0)

    return begin, finish


ALL_FLIPS = (2, 3, 1)
RIDE_FRONT = ((0, 2, None),)
RIDE_DISPATCH = ((0, 3, 0), (0, 1, 0)) + tuple((m, f, 0) for m in (1, 2) for f in ALL_FLIPS)
RIDE_FIRST = ((0, 3, 1), (0, 1, 1)) + tuple((m, f, 1) for m in (1, 2) for f in ALL_FLIPS)
HOME_SECOND = ((0, 2, 0), (0, 3, 0), (1, 2, 0), (1, 3, 0), (0, 1, 0))
HOME_RETURN = ((2, 2, 0), (1, 1, 0), (2, 1, 0), (2, 3, 0))
RETURN_FIRST = 3
HOME_BACKWARD = tuple((m, f, 1) for f in ALL_FLIPS for m in range(3))


def pick(array, index):
    return array if index is None else array.at[index]


def picked_shape(array, index):
    if index is None:
        return array.shape
    return array.shape[len(index) if isinstance(index, tuple) else 1 :]


def dp_moves(sources, targets, riders, sends, recvs):
    z_index = lax.axis_index("dp")
    return [
        remote(pick(source, index), target, sends.at[n], recvs.at[n], {"dp": z_index ^ flip})
        for n, (source, target, (index, flip)) in enumerate(zip(sources, targets, riders))
    ]


def dp_peers(n_dp):
    return [{"dp": lax.axis_index("dp") ^ flip} for flip in range(1, n_dp)]


def expert_kernel(plane, n_dp, half_steps, n_carried, picks, riders, *refs):
    (xo_ref, xp_ref, go_ref, gp_ref, so_ref, sp_ref), refs = refs[:6], refs[6:]
    pieces, refs = refs[: 3 * n_dp], refs[3 * n_dp :]
    carried, refs = refs[:n_carried], refs[n_carried:]
    sources, refs = refs[: len(riders)], refs[len(riders) :]
    (yo_ref, yp_ref, bo_ref, bp_ref, do_ref, dp_ref, gate_ref, up_ref, down_ref), refs = refs[:9], refs[9:]
    landed, refs = refs[:n_carried], refs[n_carried:]
    targets, refs = refs[: len(riders)], refs[len(riders) :]
    (wg_ref, wu_ref, wd_ref, x_all, de_all, a_all, dg_all, du_all, stage, bounce), sems = refs[:10], refs[10:]
    weight_sems, store_sems, local_sems, send_sems, recv_sems, ride_send, ride_recv = sems
    weights = (wg_ref, wu_ref, wd_ref)
    z_index = lax.axis_index("dp")
    step = pl.program_id(0)
    own = step < half_steps
    rows_of_step = xo_ref.shape[0]
    exchanges = [
        plane_exchange(n, source, target, local_sems, send_sems, recv_sems, bounce)
        for n, (source, target) in enumerate(zip(carried, landed))
    ]
    moves = dp_moves(sources, targets, riders, ride_send, ride_recv)

    @pl.when(step == 0)
    def _():
        here = plane_here()
        greet([plane_peer(here ^ flip) for flip in range(1, plane)] + dp_peers(n_dp))
        loads = []
        for n, piece in enumerate(pieces):
            source = pick(piece, picks[n])
            size = source.shape[0]
            start = pl.multiple_of((z_index ^ (n % n_dp)) * size, 64)
            loads.append(
                pltpu.make_async_copy(source, weights[n // n_dp].at[pl.ds(start, size)], weight_sems.at[n])
            )
            loads[-1].start()
        for begin, _ in exchanges:
            begin()
        for move in moves:
            move.start()
        for load in loads:
            load.wait()

    rows = jnp.where(own, xo_ref[...], xp_ref[...])
    cot = jnp.where(own, go_ref[...], gp_ref[...])
    share = jnp.where(own, so_ref[...], sp_ref[...])
    place = pl.ds(pl.multiple_of(step * rows_of_step, 32), rows_of_step)
    x_all[place, :] = rows
    gate_pre = mxu(rows, wg_ref[...])
    up_pre = mxu(rows, wu_ref[...])
    sigma = 1.0 / (1.0 + jnp.exp(-gate_pre))
    silu = gate_pre * sigma
    act = (silu * up_pre).astype(BF)
    a_all[place, :] = act
    cot_full = cot.astype(F32)
    weighted = (cot_full * share).astype(BF)
    de_all[place, :] = weighted
    result = mxu(act, wd_ref[...])
    dots = jnp.sum(result.astype(BF).astype(F32) * cot_full, axis=-1, keepdims=True)
    scaled = (result * share).astype(BF)
    grad_act = mxu(weighted, wd_ref[...], ((1,), (1,)))
    grad_gate = (grad_act * up_pre * sigma * (1.0 + gate_pre * (1.0 - sigma))).astype(BF)
    grad_up = (grad_act * silu).astype(BF)
    dg_all[place, :] = grad_gate
    du_all[place, :] = grad_up
    back = mxu(grad_gate, wg_ref[...], ((1,), (1,))) + mxu(grad_up, wu_ref[...], ((1,), (1,)))
    back = back.astype(BF)

    @pl.when(own)
    def _():
        yo_ref[...] = scaled
        bo_ref[...] = back
        do_ref[...] = dots

    @pl.when(jnp.logical_not(own))
    def _():
        yp_ref[...] = scaled
        bp_ref[...] = back
        dp_ref[...] = dots

    @pl.when(step == 2 * half_steps - 1)
    def _():
        quarter = D // n_dp
        hidden = a_all.shape[1]

        def of_rows(q, carry):
            columns = pl.ds(pl.multiple_of(q * quarter, 128), quarter)
            stores = []
            for n, (grads, out_ref) in enumerate(((dg_all, gate_ref), (du_all, up_ref))):
                stage[n] = mxu(x_all[:, columns], grads[...], ((0,), (0,))).astype(BF)
                stores.append(pltpu.make_async_copy(stage.at[n], out_ref.at[z_index ^ q], store_sems.at[n]))
                stores[-1].start()
            for store in stores:
                store.wait()
            return carry

        lax.fori_loop(0, n_dp, of_rows, 0)
        size = hidden // n_dp
        for q in range(0, n_dp, 2):
            made = mxu(a_all[:, q * size : (q + 2) * size], de_all[...], ((0,), (0,))).astype(BF)
            stores = []
            for half in range(2):
                part = made[half * size : (half + 1) * size]
                stage[half, :size] = part[:, :hidden]
                stage[half, size:] = part[:, hidden:]
                stores.append(
                    pltpu.make_async_copy(
                        stage.at[half], down_ref.at[z_index ^ (q + half)], store_sems.at[half]
                    )
                )
                stores[-1].start()
            for store in stores:
                store.wait()
        for _, finish in exchanges:
            finish()
        for move in moves:
            move.wait()


def run_expert(name, number, rows, cots, gates, pieces, carried, riders):
    half_rows = rows[0].shape[0]
    half_steps = 4
    step_rows = half_rows // half_steps
    plane = carried[0].shape[0]
    n_dp = lax.axis_size("dp")
    hidden = picked_shape(*pieces[0])[1]
    own_map = lambda j: (jnp.minimum(j, half_steps - 1), 0)
    par_map = lambda j: (jnp.maximum(j - half_steps, 0), 0)
    anywhere = pl.BlockSpec(memory_space=pl.ANY)

    def pair(width):
        return [pl.BlockSpec((step_rows, width), own_map), pl.BlockSpec((step_rows, width), par_map)]

    shape = jax.ShapeDtypeStruct
    share = shape((n_dp, D // n_dp, hidden), BF)
    dma = pltpu.SemaphoreType.DMA
    all_rows = 2 * half_rows
    results = pl.pallas_call(
        functools.partial(
            expert_kernel,
            plane,
            n_dp,
            half_steps,
            len(carried),
            [index for _, index in pieces],
            [(index, flip) for _, index, flip in riders],
        ),
        grid=(2 * half_steps,),
        in_specs=pair(D) + pair(D) + pair(1) + [anywhere] * (len(pieces) + len(carried) + len(riders)),
        out_specs=pair(D) + pair(D) + pair(1) + [anywhere] * (3 + len(carried) + len(riders)),
        out_shape=[shape((half_rows, D), BF)] * 4
        + [shape((half_rows, 1), F32)] * 2
        + [share] * 3
        + [shape(array.shape, BF) for array in carried]
        + [shape(picked_shape(array, index), BF) for array, index, _ in riders],
        scratch_shapes=[
            pltpu.VMEM((D, hidden), BF),
            pltpu.VMEM((D, hidden), BF),
            pltpu.VMEM((hidden, D), BF),
            pltpu.VMEM((all_rows, D), BF),
            pltpu.VMEM((all_rows, D), BF),
            pltpu.VMEM((all_rows, hidden), BF),
            pltpu.VMEM((all_rows, hidden), BF),
            pltpu.VMEM((all_rows, hidden), BF),
            pltpu.VMEM((2, D // n_dp, hidden), BF),
            pltpu.VMEM((len(carried), SLOTS, D), BF),
            dma((len(pieces),)),
            dma((2,)),
            dma((len(carried),)),
            dma((len(carried), plane)),
            dma((len(carried), plane)),
            dma((len(riders),)),
            dma((len(riders),)),
        ],
        compiler_params=pltpu.CompilerParams(
            vmem_limit_bytes=56 * 1024 * 1024, collective_id=number, has_side_effects=True
        ),
        name=name,
    )(*rows, *cots, *gates, *[a for a, _ in pieces], *carried, *[a for a, _, _ in riders])
    last = 9 + len(carried)
    return results[:4], results[4:6], results[6:9], results[9:last], results[last:]


def plane_peer(index):
    n_context = lax.axis_size("context")
    return {"expert": index // n_context, "context": index % n_context}


def plane_here():
    return lax.axis_index("expert") * lax.axis_size("context") + lax.axis_index("context")


def greet(peers):
    barrier = pltpu.get_barrier_semaphore()
    for peer in peers:
        pl.semaphore_signal(barrier, inc=1, device_id=peer, device_id_type=MESH_ID)
    pl.semaphore_wait(barrier, len(peers))


def remote(source, target, send, receive, peer):
    return pltpu.make_async_remote_copy(
        src_ref=source,
        dst_ref=target,
        send_sem=send,
        recv_sem=receive,
        device_id=peer,
        device_id_type=MESH_ID,
    )


def cast_halves(source_ref, halves_ref, loaded, made, load_sems, store_sems):
    rows, experts, width = source_ref.shape
    mine = experts // lax.axis_size("context")
    group = 8
    first = lax.axis_index("context") * mine
    start = pl.multiple_of(first // group * group, group)
    step = loaded.shape[1] * loaded.shape[3] // width
    lower = lax.rem(first, group) == 0
    even = lax.rem(lax.axis_index("dp"), 2) == 0
    steps = rows // step

    def load(n):
        slot = lax.rem(n, 2)
        block = source_ref.at[pl.ds(pl.multiple_of(n * step, step), step), pl.ds(start, group), :]
        return pltpu.make_async_copy(block, loaded.at[slot], load_sems.at[slot])

    def store(n, half):
        slot = lax.rem(n, 2)
        block = halves_ref.at[half, :, pl.ds(pl.multiple_of(n * step, step), step), :]
        return pltpu.make_async_copy(made.at[slot, half], block, store_sems.at[slot, half])

    load(0).start()

    def body(n, carry):
        @pl.when(n + 1 < steps)
        def _():
            load(n + 1).start()

        load(n).wait()

        @pl.when(n >= 2)
        def _():
            for half in range(2):
                store(n - 2, half).wait()

        slot = lax.rem(n, 2)
        block = loaded[slot]
        kept = jnp.where(lower, block[:, :mine, :], block[:, group - mine :, :])
        by_expert = jnp.swapaxes(kept, 0, 1).astype(BF)
        low, high = by_expert[: mine // 2], by_expert[mine // 2 :]
        made[slot, 0] = jnp.where(even, low, high)
        made[slot, 1] = jnp.where(even, high, low)
        for half in range(2):
            store(n, half).start()
        return carry

    lax.fori_loop(0, steps, body, 0)
    for n in (steps - 2, steps - 1):
        for half in range(2):
            store(n, half).wait()


def rank_tables(routes, plane, row_ref, column_ref):
    tokens = routes.shape[1]
    expert = lax.broadcasted_iota(jnp.int32, (EXPERTS, tokens), 0)
    named = jnp.zeros((EXPERTS, tokens), F32)
    for k in range(TOP):
        named = named + jnp.where(routes[k : k + 1, :] == expert, 1.0, 0.0)
    before = lax.broadcasted_iota(jnp.int32, (tokens, tokens), 0) < lax.broadcasted_iota(
        jnp.int32, (tokens, tokens), 1
    )
    count = mxu(named.astype(BF), jnp.where(before, 1.0, 0.0).astype(BF))
    ranks = jnp.where(named > 0, count, -1.0)
    low = ranks.astype(BF)
    owned = EXPERTS // plane
    parity = lax.rem(lax.axis_index("dp"), 2)
    for i in range(2):
        place = lax.broadcasted_iota(jnp.int32, (plane, EXPERTS), 0) * owned + parity * 2 + i
        column = lax.broadcasted_iota(jnp.int32, (plane, EXPERTS), 1)
        chosen = jnp.where(place == column, 1.0, 0.0).astype(BF)
        row_ref[i] = mxu(chosen, low).astype(BF)
        column_ref[i] = mxu(low, chosen, ((0,), (1,))).astype(BF)
    return ranks


def gather_kernel(
    n_dp,
    plane,
    routes_ref,
    in_ref,
    out_ref,
    gate_ref,
    up_ref,
    down_ref,
    cot_ref,
    ranks_ref,
    own_row_ref,
    own_column_ref,
    partner_row_ref,
    partner_column_ref,
    whole_in_ref,
    whole_out_ref,
    gate_halves_ref,
    up_halves_ref,
    down_halves_ref,
    cot_partner_ref,
    partner_routes,
    loaded,
    made,
    loaded_wide,
    made_wide,
    load_sems,
    store_sems,
    local_sems,
    z_send,
    sends,
    recvs,
    route_sems,
):
    here = plane_here()
    z_index = lax.axis_index("dp")
    parts, wholes = (in_ref, out_ref), (whole_in_ref, whole_out_ref)
    z_peer = lambda flip: {"dp": z_index ^ flip}
    greet([z_peer(flip) for flip in range(1, n_dp)] + [plane_peer(here ^ flip) for flip in (1, 2, 4)])
    routing = remote(routes_ref, partner_routes, route_sems.at[0], route_sems.at[1], z_peer(1))
    routing.start()
    keep = [
        pltpu.make_async_copy(part, whole.at[z_index, here], local_sems.at[a])
        for a, (part, whole) in enumerate(zip(parts, wholes))
    ]
    for copy in keep:
        copy.start()
    started = []
    for a in range(2):
        for flip in range(1, n_dp):
            started.append(
                remote(
                    parts[a],
                    wholes[a].at[z_index, here],
                    z_send.at[a, flip],
                    recvs.at[a, z_index, here],
                    z_peer(flip),
                )
            )
            started[-1].start()

    half = cot_partner_ref.shape[0]
    cot_pair = remote(
        cot_ref.at[pl.ds(0, half)], cot_partner_ref, route_sems.at[2], route_sems.at[3], z_peer(1)
    )
    cot_pair.start()

    def pass_on(a, lane, flip, z_from, place, source=None):
        block = wholes[a].at[z_from, place]
        move = remote(
            block if source is None else source,
            block,
            sends.at[a, lane, z_from, place],
            recvs.at[a, z_from, place],
            plane_peer(here ^ flip),
        )
        move.start()
        started.append(move)

    def landed(a, z_from, place):
        block = wholes[a].at[z_from, place]
        remote(block, block, z_send.at[a, 0], recvs.at[a, z_from, place], z_peer(1)).wait_recv()

    froms = [z_index ^ flip for flip in range(n_dp)]
    for a in range(2):
        for lane, flip in enumerate((2, 4, 1)):
            pass_on(a, lane, flip, z_index, here, parts[a])
    ranks_ref[...] = rank_tables(routes_ref[...], plane, own_row_ref, own_column_ref)
    cast_halves(gate_ref, gate_halves_ref, loaded, made, load_sems, store_sems)
    for a in range(2):
        for z_from in froms[1:]:
            landed(a, z_from, here)
            for lane, flip in enumerate((2, 4, 1)):
                pass_on(a, lane, flip, z_from, here)
    cast_halves(up_ref, up_halves_ref, loaded, made, load_sems, store_sems)
    for a in range(2):
        for n, z_from in enumerate(froms):
            landed(a, z_from, here ^ 2)
            if n % 2 == 1:
                pass_on(a, 1, 4, z_from, here ^ 2)
            pass_on(a, 2, 1, z_from, here ^ 2)
            landed(a, z_from, here ^ 4)
            if n % 2 == 0:
                pass_on(a, 0, 2, z_from, here ^ 4)
            pass_on(a, 2, 1, z_from, here ^ 4)
    routing.wait()
    rank_tables(partner_routes[...], plane, partner_row_ref, partner_column_ref)
    cast_halves(down_ref, down_halves_ref, loaded_wide, made_wide, load_sems, store_sems)
    for a in range(2):
        for z_from in froms:
            landed(a, z_from, here ^ 6)
            pass_on(a, 2, 1, z_from, here ^ 6)
    for a in range(2):
        for place in (1, 3, 5, 7):
            for z_from in froms:
                landed(a, z_from, here ^ place)
    for move in started:
        move.wait_send()
    for copy in keep:
        copy.wait()
    cot_pair.wait()


def gather_parts(routes, part_in, part_out, weights, cot, n_dp, n_context, plane):
    tokens = routes.shape[1]
    vmem = pl.BlockSpec(memory_space=pltpu.VMEM)
    anywhere = pl.BlockSpec(memory_space=pl.ANY)
    shape = jax.ShapeDtypeStruct
    dma = pltpu.SemaphoreType.DMA
    row, column = shape((2, plane, tokens), BF), shape((2, tokens, plane), BF)
    mine = weights[0].shape[1] // n_context
    rows, width = 64, weights[0].shape[2]
    return pl.pallas_call(
        functools.partial(gather_kernel, n_dp, plane),
        in_specs=[vmem] + [anywhere] * 6,
        out_specs=[vmem] * 5 + [anywhere] * 6,
        out_shape=[shape((EXPERTS, tokens), F32), row, column, row, column]
        + [shape((n_dp, plane) + part.shape, BF) for part in (part_in, part_out)]
        + [shape((2, mine // 2, w.shape[0], w.shape[2]), BF) for w in weights]
        + [shape((tokens // 2, D), BF)],
        scratch_shapes=[
            pltpu.VMEM(routes.shape, routes.dtype),
            pltpu.VMEM((2, rows, 8, width), F32),
            pltpu.VMEM((2, 2, mine // 2, rows, width), BF),
            pltpu.VMEM((2, rows // 2, 8, 2 * width), F32),
            pltpu.VMEM((2, 2, mine // 2, rows // 2, 2 * width), BF),
            dma((2,)),
            dma((2, 2)),
            dma((2,)),
            dma((2, n_dp)),
            dma((2, 3, n_dp, plane)),
            dma((2, n_dp, plane)),
            dma((4,)),
        ],
        compiler_params=pltpu.CompilerParams(
            vmem_limit_bytes=60 * 1024 * 1024, collective_id=3, has_side_effects=True
        ),
        name="gather_parts",
    )(routes, part_in, part_out, *weights, cot)


def front_kernel(n_dp, prompt_len, riders, *refs):
    (x_ref, cos_ref, sin_ref, w_in_ref, w_out_ref, cot_ref), refs = refs[:6], refs[6:]
    sources, refs = refs[: len(riders)], refs[len(riders) :]
    (
        gains_ref,
        normed_one_ref,
        qkv_ref,
        kv_ref,
        attended_ref,
        log_ref,
        normed_two_ref,
        logits_ref,
        mid_ref,
        cot_partner_ref,
    ), refs = refs[:10], refs[10:]
    targets, refs = refs[: len(riders)], refs[len(riders) :]
    (
        columns_buf,
        small,
        w_out,
        mid_block,
        load_sems,
        column_sems,
        pair_sems,
        kv_send,
        kv_recv,
        ride_send,
        ride_recv,
    ) = refs
    block_index = lax.axis_index("context")
    n_context = prompt_len // PBLK
    tokens = x_ref.shape[0]
    width = qkv_ref.shape[1]
    greet([context_peer(flip) for flip in range(1, n_context)] + dp_peers(n_dp))
    load_small = pltpu.make_async_copy(w_in_ref.at[:, pl.ds(width, 128)], small, load_sems.at[0])
    load_out = pltpu.make_async_copy(w_out_ref, w_out, load_sems.at[1])
    step_width = columns_buf.shape[2]
    steps = width // step_width
    kv_steps = (width - D) // step_width

    def place_of(n):
        return lax.rem(n + steps - kv_steps, steps)

    def load_columns(n):
        slot = lax.rem(n, 2)
        start = pl.multiple_of(place_of(n) * step_width, step_width)
        return pltpu.make_async_copy(
            w_in_ref.at[:, pl.ds(start, step_width)], columns_buf.at[slot], column_sems.at[slot]
        )

    load_small.start()
    load_columns(0).start()
    load_out.start()
    half = cot_partner_ref.shape[0]
    pair = remote(
        cot_ref.at[pl.ds(half, half)],
        cot_partner_ref,
        pair_sems.at[0],
        pair_sems.at[1],
        {"dp": lax.axis_index("dp") ^ 1},
    )
    pair.start()
    moves = dp_moves(sources, targets, riders, ride_send, ride_recv)
    for move in moves:
        move.start()
    load_small.wait()
    picked = lax.broadcasted_iota(jnp.int32, (8, 128), 1) - lax.broadcasted_iota(jnp.int32, (8, 128), 0)
    gains_ref[...] = mxu(jnp.where(picked == EXPERTS, 1.0, 0.0).astype(BF), small[...], ((1,), (1,)))

    def normed(rows, gain):
        scale = lax.rsqrt(jnp.mean(rows * rows, axis=-1, keepdims=True) + epsilon)
        return (rows * scale * gain).astype(BF)

    def block_rows(n):
        return pl.ds(pl.multiple_of(n * PBLK, PBLK), PBLK)

    def first_norm(n, carry):
        rows = block_rows(n)
        normed_one_ref[rows, :] = normed(x_ref[rows, :].astype(F32), gains_ref[0:1, :])
        return carry

    lax.fori_loop(0, tokens // PBLK, first_norm, 0)

    def project(n, carry):
        @pl.when(n + 1 < steps)
        def _():
            load_columns(n + 1).start()

        load_columns(n).wait()
        place = place_of(n)
        product = mxu(normed_one_ref[...], columns_buf[lax.rem(n, 2)])
        is_value = place == steps - kv_steps // 2
        cosine = jnp.where(is_value, 1.0, cos_ref[...])
        sine = jnp.where(is_value, 0.0, sin_ref[...])
        factor = jnp.where(place < steps - kv_steps, 1.0 / math.sqrt(HD), 1.0)
        for half in range(step_width // HD):
            part = product[:, half * HD : (half + 1) * HD]
            start = pl.multiple_of(place * step_width + half * HD, HD)
            qkv_ref[:, pl.ds(start, HD)] = (turn(part, cosine, sine) * factor).astype(BF)
        return carry

    lax.fori_loop(0, kv_steps, project, 0)
    own_keys = pl.ds(pl.multiple_of(block_index * PBLK, PBLK), PBLK)
    kv_ref[own_keys, :] = qkv_ref[:PBLK, D:]
    kv_ref[prompt_len:, :] = qkv_ref[PBLK:, D:]
    kv_moves = [
        remote(
            kv_ref.at[own_keys],
            kv_ref.at[own_keys],
            kv_send.at[flip],
            kv_recv.at[flip],
            context_peer(flip),
        )
        for flip in range(1, n_context)
    ]
    for move in kv_moves:
        move.start()
    lax.fori_loop(kv_steps, steps, project, 0)
    for move in kv_moves:
        move.wait()
    log_ref[...] = jnp.zeros_like(log_ref)

    def through_head(head, carry):
        columns = pl.ds(pl.multiple_of(head * HD, HD), HD)
        group = head // (HEADS // KVH)
        key_columns = pl.ds(pl.multiple_of(group * HD, HD), HD)
        value_columns = pl.ds(pl.multiple_of(KVH * HD + group * HD, HD), HD)
        for first_row, keys in row_blocks(prompt_len):
            rows = slice(first_row, first_row + PBLK)
            scores = mxu(qkv_ref[rows, columns], kv_ref[:keys, key_columns], ((1,), (1,)))
            scores = masked_scores(scores, first_row, prompt_len, block_index)
            top = jnp.max(scores, axis=-1, keepdims=True)
            unnormed = jnp.exp(scores - top)
            total = jnp.sum(unnormed, axis=-1, keepdims=True)
            mixed = mxu(unnormed.astype(BF), kv_ref[:keys, value_columns]) / total
            attended_ref[rows, columns] = mixed.astype(BF)
            lane = lax.broadcasted_iota(jnp.int32, (PBLK, log_ref.shape[1]), 1)
            log_ref[rows, :] = jnp.where(lane == head, top + jnp.log(total), log_ref[rows, :])
        return carry

    lax.fori_loop(0, HEADS, through_head, 0)
    load_out.wait()

    def second_norm(n, carry):
        rows = block_rows(n)
        mid = x_ref[rows, :].astype(F32) + mxu(attended_ref[rows, :], w_out[...])
        mid_block[...] = mid
        store = pltpu.make_async_copy(mid_block, mid_ref.at[rows], load_sems.at[2])
        store.start()
        low = normed(mid, gains_ref[1:2, :])
        normed_two_ref[rows, :] = low
        logits_ref[rows, :] = mxu(low, small[...])
        store.wait()
        return carry

    lax.fori_loop(0, tokens // PBLK, second_norm, 0)
    pair.wait()
    for move in moves:
        move.wait()


def front(prompt_len, n_dp, x_low, cosine, sine, w_in, w_out, cot, riders):
    tokens = x_low.shape[0]
    width = D + 2 * KVH * HD
    key_rows = prompt_len + CONT
    n_context = prompt_len // PBLK
    vmem = pl.BlockSpec(memory_space=pltpu.VMEM)
    anywhere = pl.BlockSpec(memory_space=pl.ANY)
    shape = jax.ShapeDtypeStruct
    dma = pltpu.SemaphoreType.DMA
    return pl.pallas_call(
        functools.partial(front_kernel, n_dp, prompt_len, [(index, flip) for _, index, flip in riders]),
        in_specs=[vmem] * 3 + [anywhere] * (3 + len(riders)),
        out_specs=[vmem] * 8 + [anywhere] * (2 + len(riders)),
        out_shape=[
            shape((8, D), F32),
            shape((tokens, D), BF),
            shape((tokens, width), BF),
            shape((key_rows, 2 * KVH * HD), BF),
            shape((tokens, D), BF),
            shape((tokens, 128), F32),
            shape((tokens, D), BF),
            shape((tokens, 128), F32),
            shape((tokens, D), F32),
            shape((tokens // 2, D), BF),
        ]
        + [shape(picked_shape(array, index), BF) for array, index, _ in riders],
        scratch_shapes=[
            pltpu.VMEM((2, D, 2 * HD), BF),
            pltpu.VMEM((D, 128), BF),
            pltpu.VMEM((D, D), BF),
            pltpu.VMEM((PBLK, D), F32),
            dma((3,)),
            dma((2,)),
            dma((2,)),
            dma((n_context,)),
            dma((n_context,)),
            dma((len(riders),)),
            dma((len(riders),)),
        ],
        compiler_params=pltpu.CompilerParams(
            vmem_limit_bytes=56 * 1024 * 1024, collective_id=8, has_side_effects=True
        ),
        name="front",
    )(x_low, cosine, sine, w_in, w_out, cot, *[array for array, _, _ in riders])


def dispatch_kernel(plane, n_dp, riders, *refs):
    normed_ref, cot_ref, own_rank_ref, partner_rank_ref, gates_ref, other_gates_ref = refs[:6]
    cot_halves, refs = refs[6:8], refs[8:]
    sources, refs = refs[: len(riders)], refs[len(riders) :]
    gates_here_ref, refs = refs[0], refs[1:]
    landed, staged, targets = refs[:4], refs[4:8], refs[8 : 8 + len(riders)]
    (
        stage,
        normed_partner,
        pair_sems,
        stage_sems,
        local_sems,
        send_sems,
        recv_sems,
        ride_send,
        ride_recv,
        all_gates,
        partner_gates,
        gate_sems,
        gate_send,
        gate_recv,
        cot_partner,
        cot_sems,
    ) = refs[8 + len(riders) :]
    here = plane_here()
    greet([plane_peer(here ^ flip) for flip in range(1, plane)] + dp_peers(n_dp))
    partner = {"dp": lax.axis_index("dp") ^ 1}
    gate_pair = remote(other_gates_ref, partner_gates, gate_sems.at[0], gate_sems.at[1], partner)
    gate_pair.start()
    pair = remote(normed_ref, normed_partner, pair_sems.at[0], pair_sems.at[1], partner)
    pair.start()
    moves = dp_moves(sources, targets, riders, ride_send, ride_recv)
    for move in moves:
        move.start()
    half = cot_halves[0].shape[0]
    cot_loads = [
        pltpu.make_async_copy(part, cot_partner.at[pl.ds(n * half, half)], cot_sems.at[n])
        for n, part in enumerate(cot_halves)
    ]
    for load in cot_loads:
        load.start()
    plans = (
        (0, normed_ref, own_rank_ref),
        (1, cot_ref, own_rank_ref),
        (2, cot_partner, partner_rank_ref),
        (3, normed_partner, partner_rank_ref),
    )
    exchanges = [
        plane_exchange(n, stage.at[n], landed[n], local_sems, send_sems, recv_sems) for n in range(4)
    ]
    copies = [pltpu.make_async_copy(stage.at[4 + n], staged[n], stage_sems.at[n]) for n in range(4)]
    for expert in range(2):
        for n, rows_ref, rank_ref in plans:
            if expert == 0 and n == 2:
                for load in cot_loads:
                    load.wait()
            if expert == 0 and n == 3:
                pair.wait()
            chooser = slot_matrix(rank_ref[expert], plane, True)
            stage[4 * expert + n] = mxu(chooser, rows_ref[...]).astype(BF).reshape(plane, SLOTS, D)
            if expert == 0:
                exchanges[n][0]()
            else:
                copies[n].start()
    gate_pair.wait()
    all_gates[:, 0:2, :] = gates_ref[...]
    all_gates[:, 2:4, :] = partner_gates[...]
    gates_here_ref[here] = all_gates[here]
    gate_moves = [
        remote(
            all_gates.at[here ^ flip],
            gates_here_ref.at[here],
            gate_send.at[flip],
            gate_recv.at[flip],
            plane_peer(here ^ flip),
        )
        for flip in range(1, plane)
    ]
    for move in gate_moves:
        move.start()
    for copy in copies:
        copy.wait()
    for _, finish in exchanges:
        finish()
    for move in gate_moves + moves:
        move.wait()


def dispatch_rows(normed, cot, cot_halves, own_ranks, partner_ranks, gates, other_gates, riders, n_dp):
    plane, tokens = own_ranks.shape[1:]
    vmem = pl.BlockSpec(memory_space=pltpu.VMEM)
    anywhere = pl.BlockSpec(memory_space=pl.ANY)
    shape = jax.ShapeDtypeStruct
    dma = pltpu.SemaphoreType.DMA
    results = pl.pallas_call(
        functools.partial(dispatch_kernel, plane, n_dp, [(index, flip) for _, index, flip in riders]),
        in_specs=[vmem] * 6 + [anywhere] * (2 + len(riders)),
        out_specs=[vmem] + [anywhere] * (8 + len(riders)),
        out_shape=[shape((plane, 4, gates.shape[2]), F32)]
        + [shape((plane, SLOTS, D), BF)] * 8
        + [shape(picked_shape(array, index), BF) for array, index, _ in riders],
        scratch_shapes=[
            pltpu.VMEM((8, plane, SLOTS, D), BF),
            pltpu.VMEM((tokens, D), BF),
            dma((2,)),
            dma((4,)),
            dma((4,)),
            dma((4, plane)),
            dma((4, plane)),
            dma((len(riders),)),
            dma((len(riders),)),
            pltpu.VMEM((plane, 4, gates.shape[2]), F32),
            pltpu.VMEM(gates.shape, F32),
            dma((2,)),
            dma((plane,)),
            dma((plane,)),
            pltpu.VMEM((tokens, D), BF),
            dma((2,)),
        ],
        compiler_params=pltpu.CompilerParams(
            vmem_limit_bytes=56 * 1024 * 1024, collective_id=1, has_side_effects=True
        ),
        cost_estimate=pl.CostEstimate(flops=2 * 10**10, bytes_accessed=4 * 10**8, transcendentals=0),
        name="dispatch_rows",
    )(
        normed, cot, own_ranks, partner_ranks, gates, other_gates, *cot_halves, *[a for a, _, _ in riders]
    )
    return results[0], results[1:5], results[5:9], results[9:]


def return_kernel(
    plane, n_dp, n_results, riders, names, own_rank_ref, partner_rank_ref, dots_ref, ranks_ref, gates_ref, *refs
):
    early, back = refs[0:2], refs[2:4]
    results, refs = refs[4 : 4 + n_results], refs[4 + n_results :]
    sources, refs = refs[: len(riders)], refs[len(riders) :]
    mine, refs = refs[:3], refs[3:]
    arrived, refs = refs[: len(HOME_SECOND)], refs[len(HOME_SECOND) :]
    total_ref, dlog_ref, part_ref = refs[:3]
    results_back, refs = refs[3 : 3 + n_results], refs[3 + n_results :]
    targets = refs[: len(riders)]
    homes = dict(zip(HOME_SECOND, arrived))
    homes.update(zip(names, targets))
    (
        held,
        to_partner,
        of_partner,
        load_sems,
        pair_sems,
        local_sems,
        send_sems,
        recv_sems,
        ride_send,
        ride_recv,
        dot_sems,
        dot_send,
        dot_recv,
        dots_here_ref,
        dots_other_ref,
        bounce,
        summed,
        sums,
        piece_sems,
        sum_sems,
    ) = refs[len(riders) :]
    here = plane_here()
    partner = {"dp": lax.axis_index("dp") ^ 1}
    greet([plane_peer(here ^ flip) for flip in range(1, plane)] + dp_peers(n_dp))
    own_dots = pltpu.make_async_copy(dots_ref.at[here], dots_here_ref.at[here], dot_sems.at[0])
    own_dots.start()
    dot_moves = [
        remote(
            dots_ref.at[here ^ flip],
            dots_here_ref.at[here],
            dot_send.at[flip],
            dot_recv.at[flip],
            plane_peer(here ^ flip),
        )
        for flip in range(1, plane)
    ]
    for move in dot_moves:
        move.start()
    loads, exchanges = {}, {}
    for side in (1, 0):
        loads[side] = pltpu.make_async_copy(early[side], held.at[2 * side], load_sems.at[side])
        loads[side].start()
        exchanges[side] = plane_exchange(
            side, back[side], held.at[2 * side + 1], local_sems, send_sems, recv_sems
        )
    exchanges[1][0]()
    later = [
        plane_exchange(2 + n, results[n], results_back[n], local_sems, send_sems, recv_sems, bounce)
        for n in range(n_results)
    ]
    moves = dp_moves(sources, targets, riders, ride_send, ride_recv)
    own_dots.wait()
    for move in dot_moves:
        move.wait()
    dots_pair = remote(dots_here_ref, dots_other_ref, dot_sems.at[1], dot_sems.at[2], partner)
    dots_pair.start()

    def sum_matrix(which):
        sources = [mine[which].at[0]] + [homes[which, flip, 0] for flip in range(1, n_dp)]
        copies = [
            pltpu.make_async_copy(source, summed.at[n], piece_sems.at[n]) for n, source in enumerate(sources)
        ]
        for copy in copies:
            copy.start()
        for copy in copies:
            copy.wait()
        parity = lax.rem(lax.axis_index("dp"), 2)
        stores = []
        for side in range(2):
            total = summed[side].astype(F32)
            for n in range(side + 2, n_dp, 2):
                total = total + summed[n].astype(F32)
            sums[side] = total.astype(BF)
            place = parity if side == 0 else 1 - parity
            stores.append(pltpu.make_async_copy(sums.at[side], part_ref.at[place, which], sum_sems.at[side]))
            stores[-1].start()
        for store in stores:
            store.wait()

    def of_gates():
        tokens = ranks_ref.shape[0]
        parity = lax.rem(lax.axis_index("dp"), 2)
        owned = EXPERTS // plane
        slot = lax.broadcasted_iota(jnp.int32, (tokens, 128), 1).astype(F32)
        lane = lax.broadcasted_iota(jnp.int32, (tokens, EXPERTS), 1)
        made = jnp.zeros((tokens, EXPERTS), F32)
        for expert in range(EXPERTS):
            place, side, i = expert // owned, expert % owned // 2, expert % 2
            row = jnp.where(
                parity == side,
                dots_here_ref[place, i : i + 1, :],
                dots_other_ref[place, 2 + i : 3 + i, :],
            )
            hit = ranks_ref[:, expert : expert + 1] == slot
            value = jnp.sum(jnp.where(hit, row, 0.0), axis=-1, keepdims=True)
            made = jnp.where(lane == expert, value, made)
        gates = gates_ref[...]
        mean = jnp.sum(gates * made, axis=-1, keepdims=True)
        dlog_ref[...] = jnp.zeros_like(dlog_ref)
        dlog_ref[:, :EXPERTS] = (gates * (made - mean)).astype(BF)

    for move in moves[:RETURN_FIRST]:
        move.start()
    sum_matrix(0)
    loads[1].wait()
    exchanges[1][1]()
    exchanges[0][0]()
    collect_into(plane, partner_rank_ref, held, 2, to_partner, lambda rows, made: made.astype(BF))
    pair = remote(to_partner, of_partner, pair_sems.at[0], pair_sems.at[1], partner)
    pair.start()
    for move in moves[RETURN_FIRST:]:
        move.start()
    for begin, _ in later:
        begin()
    loads[0].wait()
    exchanges[0][1]()
    collect_into(plane, own_rank_ref, held, 0, total_ref, lambda rows, made: made)
    dots_pair.wait()
    of_gates()
    pair.wait()
    total_ref[...] += of_partner[...].astype(F32)
    for _, finish in later:
        finish()
    for move in moves:
        move.wait()
    sum_matrix(1)
    sum_matrix(2)


def return_rows(
    own_ranks, partner_ranks, dots, ranks, gates, early, back, results, riders, names, shares, arrived, n_dp
):
    tokens, plane = own_ranks.shape[1:]
    vmem = pl.BlockSpec(memory_space=pltpu.VMEM)
    anywhere = pl.BlockSpec(memory_space=pl.ANY)
    shape = jax.ShapeDtypeStruct
    dma = pltpu.SemaphoreType.DMA
    outcome = pl.pallas_call(
        functools.partial(
            return_kernel, plane, n_dp, len(results), [(index, flip) for _, index, flip in riders], names
        ),
        in_specs=[vmem] * 5 + [anywhere] * (7 + len(results) + len(riders) + len(arrived)),
        out_specs=[vmem] * 2 + [anywhere] * (1 + len(results) + len(riders)),
        out_shape=[shape((tokens, D), F32), shape((tokens, 128), BF), shape((2, 3) + shares[0].shape[1:], BF)]
        + [shape(rows.shape, BF) for rows in results]
        + [shape(picked_shape(array, index), BF) for array, index, _ in riders],
        scratch_shapes=[
            pltpu.VMEM((4, plane, SLOTS, D), BF),
            pltpu.VMEM((tokens, D), BF),
            pltpu.VMEM((tokens, D), BF),
            dma((2,)),
            dma((2,)),
            dma((4,)),
            dma((4, plane)),
            dma((4, plane)),
            dma((len(riders),)),
            dma((len(riders),)),
            dma((3,)),
            dma((plane,)),
            dma((plane,)),
            pltpu.VMEM(dots.shape, F32),
            pltpu.VMEM(dots.shape, F32),
            pltpu.VMEM((2 + len(results), SLOTS, D), BF),
            pltpu.VMEM(shares[0].shape, BF),
            pltpu.VMEM((2,) + shares[0].shape[1:], BF),
            dma((n_dp,)),
            dma((2,)),
        ],
        compiler_params=pltpu.CompilerParams(
            vmem_limit_bytes=56 * 1024 * 1024, collective_id=2, has_side_effects=True
        ),
        cost_estimate=pl.CostEstimate(flops=3 * 10**10, bytes_accessed=4 * 10**8, transcendentals=0),
        name="return_rows",
    )(
        own_ranks,
        partner_ranks,
        dots,
        ranks,
        gates,
        *early,
        *back,
        *results,
        *[array for array, _, _ in riders],
        *shares,
        *arrived,
    )
    last = 3 + len(results)
    return outcome[0], outcome[1], outcome[2], outcome[3:last], outcome[last:]


def normed_back(rows, gain, grads):
    scale = lax.rsqrt(jnp.mean(rows * rows, axis=-1, keepdims=True) + epsilon)
    weighted = grads * gain
    mean = jnp.mean(rows * weighted, axis=-1, keepdims=True)
    return scale * weighted - rows * (scale * scale * scale * mean), rows * scale * grads


def context_peer(flip):
    return {"context": lax.axis_index("context") ^ flip}


def share_context(part, place_of, sends, recvs):
    here = lax.axis_index("context")
    across = remote(part, place_of(here), sends.at[0], recvs.at[here], context_peer(2))
    beside = remote(part, place_of(here), sends.at[1], recvs.at[here], context_peer(1))
    block = place_of(here ^ 2)
    onward = remote(block, block, sends.at[2], recvs.at[here ^ 2], context_peer(1))

    def begin():
        across.start()
        beside.start()

    def pass_on():
        remote(part, block, sends.at[0], recvs.at[here ^ 2], context_peer(2)).wait_recv()
        onward.start()

    def finish():
        for flip in (1, 3):
            remote(part, place_of(here ^ flip), sends.at[1], recvs.at[here ^ flip], context_peer(1)).wait_recv()
        across.wait_send()
        beside.wait_send()
        onward.wait_send()

    return begin, pass_on, finish


def backward_kernel(n_dp, prompt_len, riders, *refs):
    (
        dlog_ref,
        cot_ref,
        x_ref,
        gains_in_ref,
        attended_ref,
        qkv_ref,
        kv_ref,
        log_ref,
        normed_ref,
        cos_ref,
        sin_ref,
        mid_ref,
        total_ref,
        w_out_ref,
        w_in_ref,
        part_ref,
    ) = refs[:16]
    results, refs = refs[16:18], refs[18:]
    late = len(riders)
    sources, refs = refs[:late], refs[late:]
    grad_x_ref, gains_ref, grad_out_ref, grad_in_ref, all_ref = refs[:5]
    results_back, refs = refs[5:7], refs[7:]
    homes, refs = refs[:late], refs[late:]
    (
        weights,
        grad_mid,
        grad_attn,
        mid_block,
        grad_qkv,
        grad_kv,
        kv_send,
        kv_recv,
        stage,
        load_sems,
        store_sems,
        kv_send_sems,
        kv_recv_sems,
        home_send,
        home_recv,
        share_sends,
        share_recvs,
        small,
        bounce,
        local_sems,
        send_sems,
        recv_sems,
    ) = refs
    block_index = lax.axis_index("context")
    n_context = kv_send.shape[0]
    tokens = x_ref.shape[0]
    heads_width = HEADS * HD
    kv_width = KVH * HD
    here = plane_here()
    plane = results[0].shape[0]
    greet([plane_peer(here ^ flip) for flip in range(1, plane)] + dp_peers(n_dp))
    load_small = pltpu.make_async_copy(
        w_in_ref.at[:, pl.ds(weights.shape[1], 128)], small, load_sems.at[4]
    )
    load_small.start()
    load_total = pltpu.make_async_copy(total_ref, grad_mid, load_sems.at[0])
    load_out = pltpu.make_async_copy(w_out_ref, weights.at[:, pl.ds(0, D)], load_sems.at[1])
    load_in = pltpu.make_async_copy(w_in_ref.at[:, pl.ds(0, weights.shape[1])], weights, load_sems.at[2])
    load_total.start()
    load_out.start()
    homing = dp_moves(sources, homes, riders, home_send, home_recv)
    for move in homing:
        move.start()
    begin_all, pass_on, finish = share_context(
        part_ref, lambda place: all_ref.at[place], share_sends, share_recvs
    )
    begin_all()
    exchanges = [
        plane_exchange(side, results[side], results_back[side], local_sems, send_sems, recv_sems, bounce)
        for side in range(2)
    ]
    load_small.wait()
    load_total.wait()
    load_out.wait()
    gains_ref[...] = jnp.zeros_like(gains_ref)

    def block_rows(n):
        return pl.ds(pl.multiple_of(n * PBLK, PBLK), PBLK)

    def through_norm(n, carry):
        rows = block_rows(n)
        load_mid = pltpu.make_async_copy(mid_ref.at[rows], mid_block, load_sems.at[3])
        load_mid.start()
        load_mid.wait()
        grads = grad_mid[rows, :] + mxu(dlog_ref[rows, :], small[...], ((1,), (1,)))
        by_rows, by_gain = normed_back(mid_block[...], gains_in_ref[1:2, :], grads)
        gains_ref[1:2, :] += jnp.sum(by_gain, axis=0, keepdims=True)
        by_mid = cot_ref[rows, :].astype(F32) + by_rows
        grad_mid[rows, :] = by_mid
        low = by_mid.astype(BF)
        grad_attn[rows, :] = low
        grad_qkv[rows, :D] = mxu(low, weights[:, :D], ((1,), (1,))).astype(BF)
        return carry

    lax.fori_loop(0, tokens // PBLK, through_norm, 0)
    load_in.start()
    grad_kv[...] = jnp.zeros_like(grad_kv)

    def through_head(head, carry):
        columns = pl.ds(pl.multiple_of(head * HD, HD), HD)
        group = head // (HEADS // KVH)
        key_columns = pl.ds(pl.multiple_of(group * HD, HD), HD)
        value_columns = pl.ds(pl.multiple_of(kv_width + group * HD, HD), HD)
        for first_row, keys in row_blocks(prompt_len):
            rows = slice(first_row, first_row + PBLK)
            queries, grads = qkv_ref[rows, columns], grad_qkv[rows, columns]
            scores = mxu(queries, kv_ref[:keys, key_columns], ((1,), (1,)))
            scores = masked_scores(scores, first_row, prompt_len, block_index)
            lane = lax.broadcasted_iota(jnp.int32, (PBLK, log_ref.shape[1]), 1)
            logs = jnp.sum(jnp.where(lane == head, log_ref[rows, :], 0.0), axis=-1, keepdims=True)
            probs = jnp.exp(scores - logs)
            grad_probs = mxu(grads, kv_ref[:keys, value_columns], ((1,), (1,)))
            dots = jnp.sum(probs * grad_probs, axis=-1, keepdims=True)
            grad_scores = (probs * (grad_probs - dots)).astype(BF)
            grad_query = mxu(grad_scores, kv_ref[:keys, key_columns])
            grad_query = turn(grad_query, cos_ref[rows, :], -sin_ref[rows, :]) * (1.0 / math.sqrt(HD))
            grad_qkv[rows, columns] = grad_query.astype(BF)
            grad_kv[:keys, key_columns] += mxu(grad_scores, queries, ((0,), (0,)))
            grad_kv[:keys, value_columns] += mxu(probs.astype(BF), grads, ((0,), (0,)))
        return carry

    lax.fori_loop(0, HEADS, through_head, 0)

    for place in range(n_context):
        kv_send[place] = grad_kv[place * PBLK : (place + 1) * PBLK, :].astype(BF)
    kv_moves = [
        remote(
            kv_send.at[block_index ^ flip],
            kv_recv.at[flip],
            kv_send_sems.at[flip],
            kv_recv_sems.at[flip],
            context_peer(flip),
        )
        for flip in range(1, n_context)
    ]
    for move in kv_moves:
        move.start()
    for begin, _ in exchanges:
        begin()

    quarter = D // n_dp

    def quarter_rows(q):
        return pl.ds(pl.multiple_of(q * quarter, 128), quarter)

    def share_of_out(q, carry):
        made = mxu(attended_ref[:, quarter_rows(q)], grad_attn[...], ((0,), (0,)))
        stage[:, :D] = made.astype(BF)
        store = pltpu.make_async_copy(
            stage.at[:, pl.ds(0, D)], grad_out_ref.at[quarter_rows(q)], store_sems.at[0]
        )
        store.start()
        store.wait()
        return carry

    lax.fori_loop(0, n_dp, share_of_out, 0)

    for move in kv_moves:
        move.wait()
    own_rows = pl.ds(pl.multiple_of(block_index * PBLK, PBLK), PBLK)
    summed = grad_kv[own_rows, :]
    for flip in range(1, n_context):
        summed = summed + kv_recv[flip].astype(F32)
    pieces = [(0, PBLK, summed), (PBLK, tokens, grad_kv[prompt_len:, :])]
    for first, last, made in pieces:
        for group in range(KVH):
            turned = turn(
                made[:, group * HD : (group + 1) * HD], cos_ref[first:last, :], -sin_ref[first:last, :]
            )
            start = heads_width + group * HD
            grad_qkv[first:last, start : start + HD] = turned.astype(BF)
        grad_qkv[first:last, heads_width + kv_width :] = made[:, kv_width:].astype(BF)

    load_in.wait()

    def share_of_in(q, carry):
        stage[...] = mxu(normed_ref[:, quarter_rows(q)], grad_qkv[...], ((0,), (0,))).astype(BF)
        store = pltpu.make_async_copy(stage, grad_in_ref.at[quarter_rows(q)], store_sems.at[0])
        store.start()
        store.wait()
        return carry

    lax.fori_loop(0, n_dp, share_of_in, 0)

    def through_first(n, carry):
        rows = block_rows(n)
        grads = mxu(grad_qkv[rows, :], weights[...], ((1,), (1,)))
        by_rows, by_gain = normed_back(x_ref[rows, :].astype(F32), gains_in_ref[0:1, :], grads)
        gains_ref[0:1, :] += jnp.sum(by_gain, axis=0, keepdims=True)
        grad_x_ref[rows, :] = (grad_mid[rows, :] + by_rows).astype(BF)
        return carry

    lax.fori_loop(0, tokens // PBLK, through_first, 0)
    pass_on()
    finish()
    for _, end in exchanges:
        end()
    for move in homing:
        move.wait()


def backward(prompt_len, n_dp, in_vmem, in_hbm, results, riders):
    tokens = in_vmem[0].shape[0]
    width = D + 2 * KVH * HD
    n_context = prompt_len // PBLK
    key_rows = prompt_len + CONT
    quarter = D // n_dp
    vmem = pl.BlockSpec(memory_space=pltpu.VMEM)
    anywhere = pl.BlockSpec(memory_space=pl.ANY)
    part = in_hbm[-1]
    plane = results[0].shape[0]
    shape = jax.ShapeDtypeStruct
    return pl.pallas_call(
        functools.partial(backward_kernel, n_dp, prompt_len, [(index, flip) for _, index, flip in riders]),
        in_specs=[vmem] * len(in_vmem) + [anywhere] * (len(in_hbm) + 2 + len(riders)),
        out_specs=[vmem] * 2 + [anywhere] * (5 + len(riders)),
        out_shape=[
            shape((tokens, D), BF),
            shape((8, D), F32),
            shape((D, D), BF),
            shape((D, width), BF),
            shape((n_context,) + part.shape, BF),
        ]
        + [shape(rows.shape, BF) for rows in results]
        + [shape(picked_shape(array, index), BF) for array, index, _ in riders],
        scratch_shapes=[
            pltpu.VMEM((D, width), BF),
            pltpu.VMEM((tokens, D), F32),
            pltpu.VMEM((tokens, D), BF),
            pltpu.VMEM((PBLK, D), F32),
            pltpu.VMEM((tokens, width), BF),
            pltpu.VMEM((key_rows, 2 * KVH * HD), F32),
            pltpu.VMEM((n_context, PBLK, 2 * KVH * HD), BF),
            pltpu.VMEM((n_context, PBLK, 2 * KVH * HD), BF),
            pltpu.VMEM((quarter, width), BF),
            pltpu.SemaphoreType.DMA((5,)),
            pltpu.SemaphoreType.DMA((1,)),
            pltpu.SemaphoreType.DMA((n_context,)),
            pltpu.SemaphoreType.DMA((n_context,)),
            pltpu.SemaphoreType.DMA((len(riders),)),
            pltpu.SemaphoreType.DMA((len(riders),)),
            pltpu.SemaphoreType.DMA((3,)),
            pltpu.SemaphoreType.DMA((n_context,)),
            pltpu.VMEM((D, 128), BF),
            pltpu.VMEM((2, SLOTS, D), BF),
            pltpu.SemaphoreType.DMA((2,)),
            pltpu.SemaphoreType.DMA((2, plane)),
            pltpu.SemaphoreType.DMA((2, plane)),
        ],
        compiler_params=pltpu.CompilerParams(
            vmem_limit_bytes=56 * 1024 * 1024, collective_id=4, has_side_effects=True
        ),
        name="backward",
    )(*in_vmem, *in_hbm, *results, *[array for array, _, _ in riders])


def reduce_kernel(n_dp, widths, *refs):
    count = len(widths)
    shares, refs = refs[:count], refs[count:]
    part_ref, own_rank_ref, partner_rank_ref, mid_ref = refs[:4]
    rows_of, refs = (refs[4:6], refs[6:8]), refs[8:]
    totals, refs = refs[:count], refs[count:]
    result_ref, all_ref = refs[:2]
    refs = refs[2:]
    sums, core_in, first_in, second_in, z_in = (refs[n * count : (n + 1) * count] for n in range(5))
    (
        load_sems,
        core_send,
        core_recv,
        first_send,
        first_recv,
        second_send,
        second_recv,
        z_send,
        z_recv,
        out_send,
        out_recv,
        share_sends,
        share_recvs,
        pair_sems,
        held,
        to_partner,
        of_partner,
        mixed,
        mid_block,
        held_sems,
    ) = refs[5 * count :]
    here = plane_here()
    plane = held.shape[1]
    z_index = lax.axis_index("dp")
    greet(
        [plane_peer(here ^ flip) for flip in (1, 2, 4)] + [{"dp": z_index ^ flip} for flip in range(1, n_dp)]
    )
    chips = (0, 2, 4, 6)
    order = [1, 2, 3, 0] if n_dp == 4 else list(range(1, n_dp)) + [0]
    loads, core_moves = {}, {}
    for n in order:
        z_to = z_index ^ n
        for a in range(count):
            for m, chip in enumerate(chips):
                loads[n, a, m] = pltpu.make_async_copy(
                    shares[a].at[z_to, here ^ chip], sums[a].at[n, m], load_sems.at[a, n, m]
                )
                loads[n, a, m].start()
                core_moves[n, a, m] = remote(
                    shares[a].at[z_to, here ^ 1 ^ chip],
                    core_in[a].at[n, m],
                    core_send.at[a, n, m],
                    core_recv.at[a, n, m],
                    plane_peer(here ^ 1),
                )
                core_moves[n, a, m].start()

    def load_rows(side):
        copies = [
            pltpu.make_async_copy(rows_of[side][expert], held.at[expert], held_sems.at[expert])
            for expert in range(2)
        ]
        for copy in copies:
            copy.start()
        return copies

    rows_here = load_rows(1)
    gathers = [
        share_context(
            part_ref.at[:, m],
            lambda place, m=m: all_ref.at[place, :, m],
            share_sends.at[m],
            share_recvs.at[m],
        )
        for m in range(3)
    ]
    gathers[0][0]()

    for copy in rows_here:
        copy.wait()
    collect_into(plane, partner_rank_ref, held, 0, to_partner, lambda rows, made: made.astype(BF))
    pair = remote(to_partner, of_partner, pair_sems.at[0], pair_sems.at[1], {"dp": z_index ^ 1})
    pair.start()
    rows_here = load_rows(0)

    def add(target, *others):
        total = target[...].astype(F32)
        for other in others:
            total = total + other[...].astype(F32)
        target[...] = total.astype(BF)

    first_moves, second_moves, z_moves = {}, {}, {}
    for n in order:
        toward = 2 if n % 2 == 0 else 4
        kept = 6 - toward
        for a in range(count):
            for m in range(4):
                loads[n, a, m].wait()
                core_moves[n, a, m].wait_recv()
                add(sums[a].at[n, m], core_in[a].at[n, m])
            for slot, chip in enumerate((toward, 6)):
                first_moves[n, a, slot] = remote(
                    sums[a].at[n, chip // 2],
                    first_in[a].at[n, slot],
                    first_send.at[a, n, slot],
                    first_recv.at[a, n, slot],
                    plane_peer(here ^ toward),
                )
                first_moves[n, a, slot].start()
    for copy in rows_here:
        copy.wait()

    def with_mid(rows, made):
        load = pltpu.make_async_copy(mid_ref.at[rows], mid_block, held_sems.at[2])
        load.start()
        load.wait()
        return mid_block[...] + made

    collect_into(plane, own_rank_ref, held, 0, mixed, with_mid)
    for n in order:
        toward = 2 if n % 2 == 0 else 4
        kept = 6 - toward
        for a in range(count):
            for slot, chip in enumerate((0, kept)):
                first_moves[n, a, slot].wait_recv()
                add(sums[a].at[n, chip // 2], first_in[a].at[n, slot])
            second_moves[n, a] = remote(
                sums[a].at[n, kept // 2],
                second_in[a].at[n],
                second_send.at[a, n],
                second_recv.at[a, n],
                plane_peer(here ^ kept),
            )
            second_moves[n, a].start()
    gathers[1][0]()
    gathers[2][0]()
    gathers[0][1]()
    for n in order:
        for a in range(count):
            second_moves[n, a].wait_recv()
            add(sums[a].at[n, 0], second_in[a].at[n])
            if n > 0:
                z_moves[n, a] = remote(
                    sums[a].at[n, 0], z_in[a].at[n], z_send.at[a, n], z_recv.at[a, n], {"dp": z_index ^ n}
                )
                z_moves[n, a].start()
    started = list(core_moves.values()) + list(first_moves.values())
    started += list(second_moves.values()) + list(z_moves.values())

    def pass_on(a, lane, flip, place):
        block = totals[a].at[place]
        move = remote(
            block, block, out_send.at[a, lane, place], out_recv.at[a, place], plane_peer(here ^ flip)
        )
        move.start()
        started.append(move)

    def landed(a, place):
        block = totals[a].at[place]
        remote(block, block, out_send.at[a, 0, place], out_recv.at[a, place], plane_peer(here ^ 1)).wait_recv()

    for a in range(count):
        for n in range(1, n_dp):
            z_moves[n, a].wait_recv()
        add(sums[a].at[0, 0], *[z_in[a].at[n] for n in range(1, n_dp)])
        totals[a][here] = sums[a][0, 0]
        for lane, flip in enumerate((2, 4, 1)):
            pass_on(a, lane, flip, here)
    for a in range(count):
        landed(a, here ^ 2)
        if a % 2 == 1:
            pass_on(a, 1, 4, here ^ 2)
        pass_on(a, 2, 1, here ^ 2)
        landed(a, here ^ 4)
        if a % 2 == 0:
            pass_on(a, 0, 2, here ^ 4)
        pass_on(a, 2, 1, here ^ 4)
    for a in range(count):
        landed(a, here ^ 6)
        pass_on(a, 2, 1, here ^ 6)
    gathers[1][1]()
    gathers[2][1]()
    pair.wait()
    result_ref[...] = (mixed[...] + of_partner[...].astype(F32)).astype(BF)
    for a in range(count):
        for flip in (1, 3, 5, 7):
            landed(a, here ^ flip)
    for move in started:
        move.wait_send()
    for _, _, finish in gathers:
        finish()


def reduce_shares(shares, part, ranks, mid, slot_rows, n_dp, n_context):
    plane, rows = shares[0].shape[1:3]
    widths = tuple(share.shape[3] for share in shares)
    count = len(widths)
    vmem = pl.BlockSpec(memory_space=pltpu.VMEM)
    anywhere = pl.BlockSpec(memory_space=pl.ANY)
    shape = jax.ShapeDtypeStruct
    dma = pltpu.SemaphoreType.DMA

    def buffers(*lead):
        return [pltpu.VMEM(lead + (rows, width), BF) for width in widths]

    return pl.pallas_call(
        functools.partial(reduce_kernel, n_dp, widths),
        in_specs=[anywhere] * (count + 1) + [vmem] * 2 + [anywhere] * 5,
        out_specs=[vmem] * (count + 1) + [anywhere],
        out_shape=[shape((plane, rows, width), BF) for width in widths]
        + [
            shape(mid.shape, BF),
            shape((n_context,) + part.shape, BF),
        ],
        scratch_shapes=buffers(n_dp, 4)
        + buffers(n_dp, 4)
        + buffers(n_dp, 2)
        + buffers(n_dp)
        + buffers(n_dp)
        + [
            dma((count, n_dp, 4)),
            dma((count, n_dp, 4)),
            dma((count, n_dp, 4)),
            dma((count, n_dp, 2)),
            dma((count, n_dp, 2)),
            dma((count, n_dp)),
            dma((count, n_dp)),
            dma((count, n_dp)),
            dma((count, n_dp)),
            dma((count, 3, plane)),
            dma((count, plane)),
            dma((3, 3)),
            dma((3, n_context)),
            dma((2,)),
            pltpu.VMEM((2, plane, SLOTS, D), BF),
            pltpu.VMEM(mid.shape, BF),
            pltpu.VMEM(mid.shape, BF),
            pltpu.VMEM(mid.shape, F32),
            pltpu.VMEM((PBLK, D), F32),
            dma((3,)),
        ],
        compiler_params=pltpu.CompilerParams(
            vmem_limit_bytes=56 * 1024 * 1024, collective_id=5, has_side_effects=True
        ),
        name="reduce_shares",
    )(*shares, part, *ranks, mid, *slot_rows[0], *slot_rows[1])


def finish_kernel(down, first_ref, second_ref, own_first_ref, own_second_ref, out_ref):
    n_context = first_ref.shape[0]
    experts = out_ref.shape[1]
    here = lax.axis_index("context")

    def of_expert(all_ref, own_ref):
        own = own_ref[:, 0].astype(F32)
        return jnp.stack(
            [jnp.where(here == place, own, all_ref[place, :, 0].astype(F32)) for place in range(n_context)]
        )

    both = [of_expert(first_ref, own_first_ref), of_expert(second_ref, own_second_ref)]
    both = jnp.stack(both, axis=2).reshape((experts,) + both[0].shape[2:])
    if not down:
        out_ref[...] = jnp.swapaxes(both, 0, 1)
        return
    half = out_ref.shape[2] // 2
    for side in range(2):
        out_ref[:, :, side * half : (side + 1) * half] = jnp.swapaxes(both[:, side], 0, 1)


def finish_weight(which, first, second, own_first, own_second):
    n_context, pair, _, rows, width = first.shape
    experts = n_context * pair * 2
    step = 32
    down = which == 2
    parts = (first, second, own_first, own_second)
    if down:
        rows = rows // 2
        parts = [part.reshape(part.shape[:-2] + (2, rows, width)) for part in parts]
        spec = pl.BlockSpec((n_context, pair, 1, 2, step, width), lambda j: (0, 0, which, 0, j, 0))
        own = pl.BlockSpec((pair, 1, 2, step, width), lambda j: (0, which, 0, j, 0))
        width = 2 * width
    else:
        spec = pl.BlockSpec((n_context, pair, 1, step, width), lambda j: (0, 0, which, j, 0))
        own = pl.BlockSpec((pair, 1, step, width), lambda j: (0, which, j, 0))
    return pl.pallas_call(
        functools.partial(finish_kernel, down),
        grid=(rows // step,),
        in_specs=[spec, spec, own, own],
        out_specs=pl.BlockSpec((step, experts, width), lambda j: (j, 0, 0)),
        out_shape=jax.ShapeDtypeStruct((rows, experts, width), F32),
        compiler_params=grant(),
        name="finish_weight",
    )(*parts)


def local_paired(
    inputs,
    cotangent,
    routes,
    attn_q,
    attn_k,
    attn_v,
    attn_o,
    norm_attn,
    norm_moe,
    router,
    expert_gate,
    expert_up,
    expert_down,
):
    n_context, n_expert, n_dp = lax.axis_size("context"), lax.axis_size("expert"), lax.axis_size("dp")
    plane = n_context * n_expert
    tokens = inputs.shape[1]
    block_index = lax.axis_index("context")
    z_index = lax.axis_index("dp")
    parity = z_index % 2
    prompt_len = PBLK * n_context
    x_low = inputs[0]
    cot_low = cotangent[0]
    route_rows = routes[0]

    here = lax.axis_index("expert") * n_context + block_index
    part_rows = attn_q.shape[0] // plane

    def part_of(shard):
        return lax.dynamic_slice_in_dim(shard, here * part_rows, part_rows, 0).astype(BF)

    part_in = jnp.concatenate(
        [part_of(attn_q), part_of(attn_k), part_of(attn_v), part_of(router)]
        + [part_of(norm_attn)[:, None], part_of(norm_moe)[:, None]]
        + [jnp.zeros((part_rows, 128 - EXPERTS - 2), BF)],
        axis=1,
    )
    qkv_width = D + 2 * KVH * HD
    weights = (expert_gate, expert_up, expert_down)
    own_ranks_t, own_rows, own_columns, partner_rows, partner_columns, whole_in, w_out, *weight_halves = (
        gather_parts(route_rows.T, part_in, part_of(attn_o), weights, cot_low, n_dp, n_context, plane)
    )
    partner_cot = [weight_halves.pop()]
    whole_in = whole_in.reshape(-1, part_in.shape[1])
    w_out = w_out.reshape(-1, D)
    own_ranks = own_ranks_t.T
    named = own_ranks >= 0
    pieces = {(which, 0, i): (weight_halves[which], (0, i)) for which in range(3) for i in range(2)}

    def riding(names):
        return [
            (weight_halves[which], flip % 2 if i is None else (flip % 2, i), flip) for which, flip, i in names
        ]

    def pieces_of(expert):
        return [pieces[which, flip, expert] for which in range(3) for flip in range(n_dp)]

    positions = jnp.concatenate(
        [
            block_index * PBLK + jnp.arange(PBLK, dtype=jnp.int32),
            prompt_len + jnp.arange(CONT, dtype=jnp.int32),
        ]
    )
    angles = angle_table(positions)
    cos_half, sin_half = jnp.cos(angles), jnp.sin(angles)
    cosine = jnp.concatenate([cos_half, cos_half], axis=1)
    sine = jnp.concatenate([-sin_half, sin_half], axis=1)
    gains, normed_one, qkv, keys_values, attended, logs, normed_two, logits, mid_rows, cot_half, *moved = (
        front(prompt_len, n_dp, x_low, cosine, sine, whole_in, w_out, cot_low, riding(RIDE_FRONT))
    )
    partner_cot.append(cot_half)
    for (which, flip, _), piece in zip(RIDE_FRONT, moved):
        for i in range(2):
            pieces[which, flip, i] = (piece, i)

    logits = logits[:, :EXPERTS]
    top_logit = jnp.max(jnp.where(named, logits, masked_score), axis=1, keepdims=True)
    raised = jnp.where(named, jnp.exp(jnp.where(named, logits - top_logit, 0.0)), 0.0)
    gates = raised / jnp.sum(raised, axis=1, keepdims=True)

    slot_ids = jnp.arange(SLOTS, dtype=F32)
    hits = own_ranks_t[:, None, :] == slot_ids[None, :, None]
    slot_gates = jnp.sum(jnp.where(hits, gates.T[:, None, :], 0.0), axis=-1)
    slot_gates = jnp.pad(slot_gates, ((0, 0), (0, 128 - SLOTS))).reshape(plane, 2, 2, 128)
    own_gates = lax.dynamic_index_in_dim(slot_gates, parity, 1, keepdims=False)
    other_gates = lax.dynamic_index_in_dim(slot_gates, 1 - parity, 1, keepdims=False)
    gates_here, landed, staged, arrived = dispatch_rows(
        normed_two, cot_low, partner_cot, own_rows, partner_rows, own_gates, other_gates, riding(RIDE_DISPATCH), n_dp
    )
    pieces.update({name: (piece, None) for name, piece in zip(RIDE_DISPATCH, arrived)})
    def gates_of(expert):
        return [gates_here[:, 2 * side + expert, :SLOTS].reshape(plane * SLOTS, 1) for side in range(2)]

    def slots_of(arrays):
        flat = [array.reshape(plane * SLOTS, D) for array in arrays]
        return (flat[0], flat[3]), (flat[1], flat[2])

    parted = lambda arrays: [array.reshape(plane, SLOTS, D) for array in arrays]
    rows, cots = slots_of(landed)
    first, first_dots, first_shares, landed, arrived = run_expert(
        "first_expert", 6, rows, cots, gates_of(0), pieces_of(0), staged, riding(RIDE_FIRST)
    )
    pieces.update({name: (piece, None) for name, piece in zip(RIDE_FIRST, arrived)})
    rows, cots = slots_of(landed)
    home_of = {}

    def homing(names, *shares):
        return [(shares[i][which], flip, flip) for which, flip, i in names]

    second, second_dots, second_shares, early, homes = run_expert(
        "second_expert",
        7,
        rows,
        cots,
        gates_of(1),
        pieces_of(1),
        parted(first)[1:4],
        homing(HOME_SECOND, first_shares),
    )

    dots = jnp.stack(
        [d[side].reshape(plane, SLOTS) for side in range(2) for d in (first_dots, second_dots)], axis=1
    )
    dots = jnp.pad(dots, ((0, 0), (0, 0), (0, 128 - SLOTS)))
    second = parted(second)
    grad_rows, grad_logits, part_first, late, _ = return_rows(
        own_columns,
        partner_columns,
        dots,
        own_ranks,
        gates,
        early[1:3],
        second[2:4],
        parted(first)[0:1],
        homing(HOME_RETURN, first_shares, second_shares),
        HOME_RETURN,
        first_shares,
        homes,
        n_dp,
    )
    grad_wrouter = mxu(normed_two, grad_logits, ((0,), (0,)))[:, :EXPERTS]

    def part_of_expert(expert, shares):
        parts = []
        for which in range(3):
            got = [shares[which][0]] + [home_of[which, flip, expert] for flip in range(1, n_dp)]
            same = sum(got[flip].astype(F32) for flip in range(0, n_dp, 2)).astype(BF)
            other = sum(got[flip].astype(F32) for flip in range(1, n_dp, 2)).astype(BF)
            parts.append(
                jnp.stack([jnp.where(parity == 0, same, other), jnp.where(parity == 0, other, same)])
            )
        return jnp.stack(parts, axis=1)

    grad_inputs, grad_gains, grad_wout, grad_wqkv, all_first, *homes = backward(
        prompt_len,
        n_dp,
        (
            grad_logits,
            cot_low,
            x_low,
            gains,
            attended,
            qkv,
            keys_values,
            logs,
            normed_one,
            cosine,
            sine,
        ),
        (mid_rows, grad_rows, w_out, whole_in, part_first),
        second[0:2],
        homing(HOME_BACKWARD, first_shares, second_shares),
    )
    last, homes = homes[:2], homes[2:]
    out_own, out_partner = [late[0], last[0]], [early[0], last[1]]
    home_of.update(zip(HOME_BACKWARD, homes))

    grad_small = jnp.concatenate([grad_wrouter, grad_gains[0][:, None], grad_gains[1][:, None]], axis=1)
    grad_small = jnp.pad(grad_small, ((0, 0), (0, 128 - grad_small.shape[1]))).astype(BF)
    parts = lambda share: share.reshape(n_dp, plane, -1, share.shape[1])
    part_second = part_of_expert(1, second_shares)
    total_qkv, total_out, total_small, result, all_second = reduce_shares(
        [parts(grad_wqkv), parts(grad_wout), parts(grad_small)],
        part_second,
        (own_columns, partner_columns),
        mid_rows,
        (out_own, out_partner),
        n_dp,
        n_context,
    )
    total_qkv = total_qkv.reshape(-1, qkv_width).astype(F32)
    total_out = total_out.reshape(-1, D).astype(F32)
    total_small = total_small.reshape(-1, 128).astype(F32)
    return (
        result[None],
        grad_inputs[None],
        total_qkv[:, :D],
        total_qkv[:, D : D + KVH * HD],
        total_qkv[:, D + KVH * HD :],
        total_out,
        total_small[:, EXPERTS],
        total_small[:, EXPERTS + 1],
        total_small[:, :EXPERTS],
        finish_weight(0, all_first, all_second, part_first, part_second),
        finish_weight(1, all_first, all_second, part_first, part_second),
        finish_weight(2, all_first, all_second, part_first, part_second),
    )


def paired_plan(mesh):
    n_expert, n_context, n_dp = mesh.shape["expert"], mesh.shape["context"], mesh.shape["dp"]
    owners = 2 * n_expert * n_context
    small_axes = all(size & (size - 1) == 0 for size in (n_expert, n_context, n_dp))
    return small_axes and n_dp % 2 == 0 and EXPERTS == 2 * owners


def solution(mesh):
    in_specs = (
        P(("expert", "dp"), "context", None),
        P(("expert", "dp"), "context", None),
        P(("expert", "dp"), "context", None),
        P("dp", None),
        P("dp", None),
        P("dp", None),
        P("dp", None),
        P("dp"),
        P("dp"),
        P("dp", None),
        P("dp", "expert", None),
        P("dp", "expert", None),
        P("dp", "expert", None),
    )
    out_specs = (
        P(("expert", "dp"), "context", None),
        P(("expert", "dp"), "context", None),
        P("dp", None),
        P("dp", None),
        P("dp", None),
        P("dp", None),
        P("dp"),
        P("dp"),
        P("dp", None),
        P("dp", "expert", None),
        P("dp", "expert", None),
        P("dp", "expert", None),
    )
    chosen = local_paired if paired_plan(mesh) else local
    return jax.shard_map(chosen, mesh=mesh, in_specs=in_specs, out_specs=out_specs, check_vma=False)
```

```python
import functools
import math

import jax
import jax.numpy as jnp
from jax import lax
from jax.experimental import pallas as pl
from jax.experimental.pallas import tpu as pltpu
from jax.sharding import PartitionSpec as P

D = 1536
HEADS = 12
KVH = 2
HD = 128
EXPERTS = 32
TOP = 4
PBLK = 256
CONT = 512
CAP = 103


epsilon = 1e-06
rope_base = 1000000.0
masked_score = -1e30


def rms_scale(values, gain):
    return values * lax.rsqrt(jnp.mean(values * values, axis=-1, keepdims=True) + epsilon) * gain


def angle_table(positions):
    steps_half = jnp.arange(HD // 2, dtype=jnp.float32)
    inverse = jnp.exp(steps_half * (-2.0 * math.log(rope_base) / HD))
    return positions.astype(jnp.float32)[..., None] * inverse


def rotary(values, angles, direction):
    halfway = values.shape[-1] // 2
    cosine = jnp.cos(angles)[..., None, :]
    sine_part = direction * jnp.sin(angles)[..., None, :]
    leading = values[..., :halfway]
    trailing = values[..., halfway:]
    return jnp.concatenate(
        [leading * cosine - trailing * sine_part, trailing * cosine + leading * sine_part], axis=-1
    )


def visible(query_pos, key_pos, prompt_len):
    query_cont = jnp.arange(query_pos.shape[0]) >= PBLK
    key_prompt = jnp.arange(key_pos.shape[0]) < prompt_len
    return (key_pos[None, :] <= query_pos[:, None]) & (key_prompt[None, :] | query_cont[:, None])


def gating(logit_rows, route_rows):
    picker = (route_rows[:, :, None] == jnp.arange(EXPERTS, dtype=jnp.int32)[None, None, :]).astype(
        logit_rows.dtype
    )
    chosen = jnp.sum(picker * logit_rows[:, None, :], axis=-1)
    return jax.nn.softmax(chosen, axis=-1)


def gated(gate_pre, up_pre):
    return jax.nn.silu(gate_pre) * up_pre


def expert_slots(flat_experts):
    picker = (flat_experts[:, None] == jnp.arange(EXPERTS, dtype=jnp.int32)[None, :]).astype(
        jnp.int32
    )
    earlier = jnp.cumsum(picker, axis=0) - picker
    return jnp.sum(earlier * picker, axis=1)


def local(
    inputs,
    cotangent,
    routes,
    attn_q,
    attn_k,
    attn_v,
    attn_o,
    norm_attn,
    norm_moe,
    router,
    expert_gate,
    expert_up,
    expert_down,
):
    low_type = jnp.bfloat16
    full_type = jnp.float32
    w_query, w_key, w_value, w_out, gain_first, gain_second, w_router, w_gate, w_up, w_down = (
        lax.all_gather(attn_q.astype(low_type), "dp", axis=0, tiled=True),
        lax.all_gather(attn_k.astype(low_type), "dp", axis=0, tiled=True),
        lax.all_gather(attn_v.astype(low_type), "dp", axis=0, tiled=True),
        lax.all_gather(attn_o.astype(low_type), "dp", axis=0, tiled=True),
        lax.all_gather(norm_attn.astype(low_type), "dp", axis=0, tiled=True),
        lax.all_gather(norm_moe.astype(low_type), "dp", axis=0, tiled=True),
        lax.all_gather(router.astype(low_type), "dp", axis=0, tiled=True),
        lax.all_gather(expert_gate.astype(low_type), "dp", axis=0, tiled=True),
        lax.all_gather(expert_up.astype(low_type), "dp", axis=0, tiled=True),
        lax.all_gather(expert_down.astype(low_type), "dp", axis=0, tiled=True),
    )
    n_context = lax.axis_size("context")
    n_expert = lax.axis_size("expert")
    block_index = lax.axis_index("context")
    prompt_len = PBLK * n_context
    tokens = inputs.shape[1]
    local_experts = w_gate.shape[1]
    group_width = HEADS // KVH
    score_scale = 1.0 / math.sqrt(HD)
    gain_one = gain_first.astype(full_type)
    gain_two = gain_second.astype(full_type)
    x_rows = inputs[0].astype(full_type)
    positions = jnp.concatenate(
        [
            block_index * PBLK + jnp.arange(PBLK, dtype=jnp.int32),
            prompt_len + jnp.arange(CONT, dtype=jnp.int32),
        ]
    )
    angles = angle_table(positions)
    normed_one = rms_scale(x_rows, gain_one).astype(low_type)
    q_proj = jnp.dot(normed_one, w_query, preferred_element_type=full_type)
    k_proj = jnp.dot(normed_one, w_key, preferred_element_type=full_type)
    v_proj = jnp.dot(normed_one, w_value, preferred_element_type=full_type)
    queries = (rotary(q_proj.reshape(tokens, HEADS, HD), angles, 1.0) * score_scale).astype(
        low_type
    )
    queries = queries.reshape(tokens, KVH, group_width, HD)
    keys_own = rotary(k_proj.reshape(tokens, KVH, HD), angles, 1.0).astype(low_type)
    values_own = v_proj.astype(low_type).reshape(tokens, KVH, HD)
    prompt_keys, prompt_values = (
        lax.all_gather(keys_own[:PBLK], "context", axis=0, tiled=True),
        lax.all_gather(values_own[:PBLK], "context", axis=0, tiled=True),
    )
    all_keys = jnp.concatenate([prompt_keys, keys_own[PBLK:]], axis=0)
    all_values = jnp.concatenate([prompt_values, values_own[PBLK:]], axis=0)
    key_pos = jnp.concatenate(
        [jnp.arange(prompt_len, dtype=jnp.int32), prompt_len + jnp.arange(CONT, dtype=jnp.int32)]
    )
    allowed = visible(positions, key_pos, prompt_len)
    head_outs = []
    log_totals = []
    for kv_head in range(KVH):
        scores = jnp.einsum(
            "tgn,kn->gtk",
            queries[:, kv_head],
            all_keys[:, kv_head],
            preferred_element_type=full_type,
        )
        scores = jnp.where(allowed[None], scores, masked_score)
        top_score = jnp.max(scores, axis=-1, keepdims=True)
        unnormed = jnp.exp(scores - top_score)
        totals = jnp.sum(unnormed, axis=-1, keepdims=True)
        attn_probs = (unnormed / totals).astype(low_type)
        head_outs.append(
            jnp.einsum(
                "gtk,kn->tgn", attn_probs, all_values[:, kv_head], preferred_element_type=full_type
            )
        )
        log_totals.append(top_score + jnp.log(totals))
    attended_low = jnp.stack(head_outs, axis=1).reshape(tokens, D).astype(low_type)
    mid_rows = x_rows + jnp.dot(attended_low, w_out, preferred_element_type=full_type)
    normed_two = rms_scale(mid_rows, gain_two).astype(low_type)
    logits = jnp.dot(normed_two, w_router, preferred_element_type=full_type)
    route_rows = routes[0]
    gate_weights = gating(logits, route_rows)
    flat_experts = route_rows.reshape(-1)
    slot_rank = expert_slots(flat_experts)
    destination = (
        flat_experts % local_experts * n_expert + flat_experts // local_experts
    ) * CAP + slot_rank
    capacity_rows = local_experts * n_expert * CAP
    assignments = tokens * TOP
    source = (
        jnp.full((capacity_rows,), assignments, dtype=jnp.int32)
        .at[destination]
        .set(jnp.arange(assignments, dtype=jnp.int32))
    )
    filled = source < assignments
    source_row = jnp.minimum(source, assignments - 1)
    send_rows = jnp.where(filled[:, None], normed_two[source_row // TOP], jnp.zeros((), low_type))
    received = lax.all_to_all(
        send_rows.reshape(local_experts, n_expert, CAP, D),
        "expert",
        split_axis=1,
        concat_axis=1,
        tiled=True,
    )
    received = received.reshape(local_experts, n_expert * CAP, D)
    gate_pre = jnp.einsum("lrd,dlf->lrf", received, w_gate, preferred_element_type=full_type)
    up_pre = jnp.einsum("lrd,dlf->lrf", received, w_up, preferred_element_type=full_type)
    activation = gated(gate_pre, up_pre).astype(low_type)
    expert_rows = jnp.einsum(
        "lrf,fld->lrd", activation, w_down, preferred_element_type=full_type
    ).astype(low_type)
    returned = lax.all_to_all(
        expert_rows.reshape(local_experts, n_expert, CAP, D),
        "expert",
        split_axis=1,
        concat_axis=1,
        tiled=True,
    )
    returned = returned.reshape(capacity_rows, D)
    picked = returned[destination].reshape(tokens, TOP, D)
    moe_out = jnp.sum(gate_weights[:, :, None] * picked.astype(full_type), axis=1)
    result = (mid_rows + moe_out).astype(low_type)
    grad_out = cotangent[0].astype(full_type)
    slot_grads = (
        (gate_weights[:, :, None] * grad_out[:, None, :]).reshape(assignments, D).astype(low_type)
    )
    send_grads = jnp.where(filled[:, None], slot_grads[source_row], jnp.zeros((), low_type))
    grad_rows = lax.all_to_all(
        send_grads.reshape(local_experts, n_expert, CAP, D),
        "expert",
        split_axis=1,
        concat_axis=1,
        tiled=True,
    )
    grad_rows = grad_rows.reshape(local_experts, n_expert * CAP, D)
    grad_gates = jnp.sum(picked.astype(full_type) * grad_out[:, None, :], axis=-1)
    grad_wdown = jnp.einsum("lrf,lrd->fld", activation, grad_rows, preferred_element_type=full_type)
    grad_act = jnp.einsum("lrd,fld->lrf", grad_rows, w_down, preferred_element_type=full_type)
    primal_gate, gated_back = jax.vjp(gated, gate_pre, up_pre)
    grad_gpre, grad_upre = gated_back(grad_act)
    grad_gpre = grad_gpre.astype(low_type)
    grad_upre = grad_upre.astype(low_type)
    grad_wgate = jnp.einsum("lrd,lrf->dlf", received, grad_gpre, preferred_element_type=full_type)
    grad_wup = jnp.einsum("lrd,lrf->dlf", received, grad_upre, preferred_element_type=full_type)
    grad_recv = jnp.einsum("lrf,dlf->lrd", grad_gpre, w_gate, preferred_element_type=full_type)
    grad_recv = (
        grad_recv + jnp.einsum("lrf,dlf->lrd", grad_upre, w_up, preferred_element_type=full_type)
    ).astype(low_type)
    back_rows = lax.all_to_all(
        grad_recv.reshape(local_experts, n_expert, CAP, D),
        "expert",
        split_axis=1,
        concat_axis=1,
        tiled=True,
    )
    back_rows = back_rows.reshape(capacity_rows, D)
    grad_normed_two = jnp.sum(
        back_rows[destination].reshape(tokens, TOP, D).astype(full_type), axis=1
    )

    def gate_of(logit_rows):
        return gating(logit_rows, route_rows)

    primal_gates, gate_back = jax.vjp(gate_of, logits)
    grad_logits = gate_back(grad_gates)[0].astype(low_type)
    grad_wrouter = jnp.einsum(
        "td,te->de", normed_two, grad_logits, preferred_element_type=full_type
    )
    grad_normed_two = grad_normed_two + jnp.einsum(
        "te,de->td", grad_logits, w_router, preferred_element_type=full_type
    )
    primal_two, norm_back_two = jax.vjp(rms_scale, mid_rows, gain_two)
    grad_mid_norm, grad_gain_two = norm_back_two(grad_normed_two)
    grad_mid = grad_out + grad_mid_norm
    grad_attn = grad_mid.astype(low_type)
    grad_wout = jnp.einsum("td,te->de", attended_low, grad_attn, preferred_element_type=full_type)
    grad_attended = jnp.einsum(
        "te,de->td", grad_attn, w_out, preferred_element_type=full_type
    ).astype(low_type)
    grad_attended = grad_attended.reshape(tokens, KVH, group_width, HD)
    query_grads = []
    key_grads = []
    value_grads = []
    for kv_head in range(KVH):
        scores = jnp.einsum(
            "tgn,kn->gtk",
            queries[:, kv_head],
            all_keys[:, kv_head],
            preferred_element_type=full_type,
        )
        scores = jnp.where(allowed[None], scores, masked_score)
        exact_probs = jnp.exp(scores - log_totals[kv_head])
        grad_probs = jnp.einsum(
            "tgn,kn->gtk",
            grad_attended[:, kv_head],
            all_values[:, kv_head],
            preferred_element_type=full_type,
        )
        row_dots = jnp.sum(exact_probs * grad_probs, axis=-1, keepdims=True)
        grad_scores = (exact_probs * (grad_probs - row_dots)).astype(low_type)
        query_grads.append(
            jnp.einsum(
                "gtk,kn->tgn", grad_scores, all_keys[:, kv_head], preferred_element_type=full_type
            )
        )
        key_grads.append(
            jnp.einsum(
                "gtk,tgn->kn", grad_scores, queries[:, kv_head], preferred_element_type=full_type
            )
        )
        value_grads.append(
            jnp.einsum(
                "gtk,tgn->kn",
                exact_probs.astype(low_type),
                grad_attended[:, kv_head],
                preferred_element_type=full_type,
            )
        )
    grad_queries = jnp.stack(query_grads, axis=1).reshape(tokens, HEADS, HD)
    grad_keys = jnp.stack(key_grads, axis=1)
    grad_values = jnp.stack(value_grads, axis=1)
    prompt_key_grad, prompt_value_grad = (
        lax.psum_scatter(
            grad_keys[:prompt_len].astype(jnp.bfloat16), "context", scatter_dimension=0, tiled=True
        ).astype(jnp.float32),
        lax.psum_scatter(
            grad_values[:prompt_len].astype(jnp.bfloat16),
            "context",
            scatter_dimension=0,
            tiled=True,
        ).astype(jnp.float32),
    )
    own_key_grad = jnp.concatenate([prompt_key_grad, grad_keys[prompt_len:]], axis=0)
    own_value_grad = jnp.concatenate([prompt_value_grad, grad_values[prompt_len:]], axis=0)
    grad_qproj = (
        rotary(grad_queries * score_scale, angles, -1.0).reshape(tokens, D).astype(low_type)
    )
    grad_kproj = rotary(own_key_grad, angles, -1.0).reshape(tokens, KVH * HD).astype(low_type)
    grad_vproj = own_value_grad.reshape(tokens, KVH * HD).astype(low_type)
    grad_wquery = jnp.einsum("td,te->de", normed_one, grad_qproj, preferred_element_type=full_type)
    grad_wkey = jnp.einsum("td,te->de", normed_one, grad_kproj, preferred_element_type=full_type)
    grad_wvalue = jnp.einsum("td,te->de", normed_one, grad_vproj, preferred_element_type=full_type)
    grad_normed_one = jnp.einsum("te,de->td", grad_qproj, w_query, preferred_element_type=full_type)
    grad_normed_one = grad_normed_one + jnp.einsum(
        "te,de->td", grad_kproj, w_key, preferred_element_type=full_type
    )
    grad_normed_one = grad_normed_one + jnp.einsum(
        "te,de->td", grad_vproj, w_value, preferred_element_type=full_type
    )
    primal_one, norm_back_one = jax.vjp(rms_scale, x_rows, gain_one)
    grad_x_norm, grad_gain_one = norm_back_one(grad_normed_one)
    grad_inputs = (grad_mid + grad_x_norm).astype(low_type)
    shares = (
        lax.psum_scatter(
            grad_wquery.astype(jnp.bfloat16), "dp", scatter_dimension=0, tiled=True
        ).astype(jnp.float32),
        lax.psum_scatter(
            grad_wkey.astype(jnp.bfloat16), "dp", scatter_dimension=0, tiled=True
        ).astype(jnp.float32),
        lax.psum_scatter(
            grad_wvalue.astype(jnp.bfloat16), "dp", scatter_dimension=0, tiled=True
        ).astype(jnp.float32),
        lax.psum_scatter(
            grad_wout.astype(jnp.bfloat16), "dp", scatter_dimension=0, tiled=True
        ).astype(jnp.float32),
        lax.psum_scatter(
            grad_gain_one.astype(jnp.bfloat16), "dp", scatter_dimension=0, tiled=True
        ).astype(jnp.float32),
        lax.psum_scatter(
            grad_gain_two.astype(jnp.bfloat16), "dp", scatter_dimension=0, tiled=True
        ).astype(jnp.float32),
        lax.psum_scatter(
            grad_wrouter.astype(jnp.bfloat16), "dp", scatter_dimension=0, tiled=True
        ).astype(jnp.float32),
        lax.psum_scatter(
            grad_wgate.astype(jnp.bfloat16), "dp", scatter_dimension=0, tiled=True
        ).astype(jnp.float32),
        lax.psum_scatter(
            grad_wup.astype(jnp.bfloat16), "dp", scatter_dimension=0, tiled=True
        ).astype(jnp.float32),
        lax.psum_scatter(
            grad_wdown.astype(jnp.bfloat16), "dp", scatter_dimension=0, tiled=True
        ).astype(jnp.float32),
    )
    dense_sum = lax.psum(
        (shares[0], shares[1], shares[2], shares[3], shares[4], shares[5], shares[6]),
        ("expert", "context"),
    )
    expert_sum = (
        lax.psum(shares[7].astype(jnp.bfloat16), "context").astype(jnp.float32),
        lax.psum(shares[8].astype(jnp.bfloat16), "context").astype(jnp.float32),
        lax.psum(shares[9].astype(jnp.bfloat16), "context").astype(jnp.float32),
    )
    totals_all = tuple(dense_sum) + tuple(expert_sum)
    return (
        result[None],
        grad_inputs[None],
        totals_all[0],
        totals_all[1],
        totals_all[2],
        totals_all[3],
        totals_all[4],
        totals_all[5],
        totals_all[6],
        totals_all[7],
        totals_all[8],
        totals_all[9],
    )


BF = jnp.bfloat16
F32 = jnp.float32
SLOTS = 112
MESH_ID = pl.DeviceIdType.MESH
PLANE = ("expert", "context")
VMEM_BYTES = 60 * 1024 * 1024


def mxu(lhs, rhs, contract=((1,), (0,))):
    return lax.dot_general(lhs, rhs, (contract, ((), ())), preferred_element_type=F32)


def grant(bytes_wanted=VMEM_BYTES):
    return pltpu.CompilerParams(vmem_limit_bytes=bytes_wanted)


def turn(values, cosine, sine):
    return values * cosine + pltpu.roll(values, HD // 2, 1) * sine


def row_blocks(prompt_len):
    blocks = [(0, prompt_len)]
    for start in range(0, CONT, PBLK):
        blocks.append((PBLK + start, prompt_len + start + PBLK))
    return blocks


def masked_scores(scores, first_row, block_index):
    tail = scores if first_row == 0 else scores[:, -PBLK:]
    row = lax.broadcasted_iota(jnp.int32, tail.shape, 0)
    column = lax.broadcasted_iota(jnp.int32, tail.shape, 1)
    limit = row + block_index * PBLK if first_row == 0 else row
    tail = jnp.where(column <= limit, tail, masked_score)
    return tail if first_row == 0 else jnp.concatenate([scores[:, :-PBLK], tail], axis=1)


def segment_matrix(parts, transposed):
    shape = (parts * SLOTS, parts) if transposed else (parts, parts * SLOTS)
    long = lax.broadcasted_iota(jnp.int32, shape, 0 if transposed else 1)
    short = lax.broadcasted_iota(jnp.int32, shape, 1 if transposed else 0)
    inside = (long >= short * SLOTS) & (long < (short + 1) * SLOTS)
    return jnp.where(inside, 1.0, 0.0).astype(BF)


def slot_matrix(ranks, parts, transposed):
    if transposed:
        spread = mxu(segment_matrix(parts, True), ranks)
        slot = lax.broadcasted_iota(jnp.int32, (parts * SLOTS, 1), 0)
    else:
        spread = mxu(ranks, segment_matrix(parts, False))
        slot = lax.broadcasted_iota(jnp.int32, (1, parts * SLOTS), 1)
    for part in range(parts - 1, 0, -1):
        slot = jnp.where(slot >= part * SLOTS, slot - SLOTS, slot)
    return jnp.where(spread == slot.astype(F32), 1.0, 0.0).astype(BF)


def collect_into(plane, rank_ref, held, base, target, finish):
    def block(n, carry):
        rows = pl.ds(pl.multiple_of(n * PBLK, PBLK), PBLK)
        made = jnp.zeros((PBLK, D), F32)
        for expert in range(2):
            chooser = slot_matrix(rank_ref[expert, rows, :], plane, False)
            made = made + mxu(chooser, held[base + expert].reshape(plane * SLOTS, D))
        target[rows, :] = finish(rows, made)
        return carry

    lax.fori_loop(0, target.shape[0] // PBLK, block, 0)


def plane_exchange(slot, source, target, local_sems, send_sems, recv_sems, bounce=None):
    here = plane_here()
    plane = source.shape[0]
    own_first = target.at[here] if bounce is None else bounce.at[slot]

    def begin():
        pltpu.make_async_copy(source.at[here], own_first, local_sems.at[slot]).start()

        def one(flip, carry):
            peer = here ^ flip
            remote(
                source.at[peer],
                target.at[here],
                send_sems.at[slot, peer],
                recv_sems.at[slot, here],
                plane_peer(peer),
            ).start()
            return carry

        lax.fori_loop(1, plane, one, 0)

    def finish():
        pltpu.make_async_copy(source.at[here], own_first, local_sems.at[slot]).wait()
        if bounce is not None:
            onward = pltpu.make_async_copy(own_first, target.at[here], local_sems.at[slot])
            onward.start()
            onward.wait()

        def one(flip, carry):
            peer = here ^ flip
            done = remote(
                source.at[peer],
                target.at[peer],
                send_sems.at[slot, peer],
                recv_sems.at[slot, peer],
                plane_peer(peer),
            )
            done.wait_send()
            done.wait_recv()
            return carry

        lax.fori_loop(1, plane, one, 0)

    return begin, finish


ALL_FLIPS = (2, 3, 1)
RIDE_FRONT = ((0, 2, None), (0, 1, 0), (1, 1, 0))
RIDE_DISPATCH = ((0, 3, 0), (1, 2, 0), (1, 3, 0), (2, 2, 0), (2, 3, 0), (2, 1, 0))
RIDE_FIRST = ((0, 3, 1), (0, 1, 1)) + tuple((m, f, 1) for m in (1, 2) for f in ALL_FLIPS)
HOME_SECOND = tuple((m, f, 0) for m in (0, 1) for f in (2, 3)) + tuple((m, 1, 0) for m in range(3))
HOME_RETURN = ((2, 2, 0), (2, 3, 0), (0, 2, 1), (0, 3, 1))
RETURN_FIRST = 2
HOME_BACKWARD = tuple((m, f, 1) for m in (1, 2) for f in (2, 3)) + tuple((m, 1, 1) for m in range(3))


def pick(array, index):
    return array if index is None else array.at[index]


def picked_shape(array, index):
    if index is None:
        return array.shape
    return array.shape[len(index) if isinstance(index, tuple) else 1 :]


def dp_moves(sources, targets, riders, sends, recvs):
    z_index = lax.axis_index("dp")
    return [
        remote(pick(source, index), target, sends.at[n], recvs.at[n], {"dp": z_index ^ flip})
        for n, (source, target, (index, flip)) in enumerate(zip(sources, targets, riders))
    ]


def dp_peers(n_dp):
    return [{"dp": lax.axis_index("dp") ^ flip} for flip in range(1, n_dp)]


def expert_kernel(plane, n_dp, half_steps, number, n_carried, picks, riders, *refs):
    (xo_ref, xp_ref, go_ref, gp_ref, gates_ref), refs = refs[:5], refs[5:]
    pieces, refs = refs[: 3 * n_dp], refs[3 * n_dp :]
    carried, refs = refs[:n_carried], refs[n_carried:]
    sources, refs = refs[: len(riders)], refs[len(riders) :]
    (yo_ref, yp_ref, bo_ref, bp_ref, dots_ref, gate_ref, up_ref, down_ref), refs = refs[:8], refs[8:]
    landed, refs = refs[:n_carried], refs[n_carried:]
    targets, refs = refs[: len(riders)], refs[len(riders) :]
    (wg_ref, wu_ref, wd_ref, x_all, de_all, a_all, dg_all, du_all, stage, bounce), sems = refs[:10], refs[10:]
    weight_sems, store_sems, local_sems, send_sems, recv_sems, ride_send, ride_recv = sems
    weights = (wg_ref, wu_ref, wd_ref)
    z_index = lax.axis_index("dp")
    step = pl.program_id(0)
    own = step < half_steps
    rows_of_step = xo_ref.shape[0]
    exchanges = [
        plane_exchange(n, source, target, local_sems, send_sems, recv_sems, bounce)
        for n, (source, target) in enumerate(zip(carried, landed))
    ]
    moves = dp_moves(sources, targets, riders, ride_send, ride_recv)

    @pl.when(step == 0)
    def _():
        here = plane_here()
        greet([plane_peer(here ^ flip) for flip in range(1, plane)] + dp_peers(n_dp))
        loads = []
        for n, piece in enumerate(pieces):
            source = pick(piece, picks[n])
            size = source.shape[0]
            start = pl.multiple_of((z_index ^ (n % n_dp)) * size, 64)
            loads.append(
                pltpu.make_async_copy(source, weights[n // n_dp].at[pl.ds(start, size)], weight_sems.at[n])
            )
            loads[-1].start()
        for begin, _ in exchanges:
            begin()
        for move in moves:
            move.start()
        for load in loads:
            load.wait()

    rows = jnp.where(own, xo_ref[...], xp_ref[...])
    cot = jnp.where(own, go_ref[...], gp_ref[...])
    places = rows_of_step // SLOTS
    first_place = lax.rem(step, half_steps) * places
    at = (SLOTS, 128)
    diagonal = lax.broadcasted_iota(jnp.int32, at, 0) == lax.broadcasted_iota(jnp.int32, at, 1)
    columns = []
    for n in range(places):
        own_row = gates_ref[first_place + n, number : number + 1, :]
        row = jnp.where(own, own_row, gates_ref[first_place + n, 2 + number : 3 + number, :])
        columns.append(jnp.sum(jnp.where(diagonal, row, 0.0), axis=-1, keepdims=True))
    share = jnp.concatenate(columns, axis=0)
    place = pl.ds(pl.multiple_of(step * rows_of_step, 32), rows_of_step)
    x_all[place, :] = rows
    gate_pre = mxu(rows, wg_ref[...])
    up_pre = mxu(rows, wu_ref[...])
    sigma = 1.0 / (1.0 + jnp.exp(-gate_pre))
    silu = gate_pre * sigma
    act = (silu * up_pre).astype(BF)
    a_all[place, :] = act
    cot_full = cot.astype(F32)
    weighted = (cot_full * share).astype(BF)
    de_all[place, :] = weighted
    result = mxu(act, wd_ref[...])
    dots = jnp.sum(result.astype(BF).astype(F32) * cot_full, axis=-1, keepdims=True)
    scaled = (result * share).astype(BF)
    grad_act = mxu(weighted, wd_ref[...], ((1,), (1,)))
    grad_gate = (grad_act * up_pre * sigma * (1.0 + gate_pre * (1.0 - sigma))).astype(BF)
    grad_up = (grad_act * silu).astype(BF)
    dg_all[place, :] = grad_gate
    du_all[place, :] = grad_up
    back = mxu(grad_gate, wg_ref[...], ((1,), (1,))) + mxu(grad_up, wu_ref[...], ((1,), (1,)))
    back = back.astype(BF)

    @pl.when(own)
    def _():
        yo_ref[...] = scaled
        bo_ref[...] = back

    @pl.when(jnp.logical_not(own))
    def _():
        yp_ref[...] = scaled
        bp_ref[...] = back

    for n in range(places):
        column = dots[n * SLOTS : (n + 1) * SLOTS]
        dots_ref[step // half_steps, first_place + n] = jnp.sum(
            jnp.where(diagonal, column, 0.0), axis=0, keepdims=True
        )

    @pl.when(step == 2 * half_steps - 1)
    def _():
        quarter = D // n_dp
        hidden = a_all.shape[1]

        def of_rows(q, carry):
            columns = pl.ds(pl.multiple_of(q * quarter, 128), quarter)
            stores = []
            for n, (grads, out_ref) in enumerate(((dg_all, gate_ref), (du_all, up_ref))):
                stage[n] = mxu(x_all[:, columns], grads[...], ((0,), (0,))).astype(BF)
                stores.append(pltpu.make_async_copy(stage.at[n], out_ref.at[z_index ^ q], store_sems.at[n]))
                stores[-1].start()
            for store in stores:
                store.wait()
            return carry

        lax.fori_loop(0, n_dp, of_rows, 0)
        size = hidden // n_dp
        for q in range(0, n_dp, 2):
            made = mxu(a_all[:, q * size : (q + 2) * size], de_all[...], ((0,), (0,))).astype(BF)
            stores = []
            for half in range(2):
                part = made[half * size : (half + 1) * size]
                stage[half, :size] = part[:, :hidden]
                stage[half, size:] = part[:, hidden:]
                stores.append(
                    pltpu.make_async_copy(
                        stage.at[half], down_ref.at[z_index ^ (q + half)], store_sems.at[half]
                    )
                )
                stores[-1].start()
            for store in stores:
                store.wait()
        for _, finish in exchanges:
            finish()
        for move in moves:
            move.wait()


def run_expert(name, which, number, rows, cots, gates, pieces, carried, riders):
    half_rows = rows[0].shape[0]
    half_steps = 4
    step_rows = half_rows // half_steps
    plane = carried[0].shape[0]
    n_dp = lax.axis_size("dp")
    hidden = picked_shape(*pieces[0])[1]
    own_map = lambda j: (jnp.minimum(j, half_steps - 1), 0)
    par_map = lambda j: (jnp.maximum(j - half_steps, 0), 0)
    anywhere = pl.BlockSpec(memory_space=pl.ANY)

    def pair(width):
        return [pl.BlockSpec((step_rows, width), own_map), pl.BlockSpec((step_rows, width), par_map)]

    shape = jax.ShapeDtypeStruct
    share = shape((n_dp, D // n_dp, hidden), BF)
    dma = pltpu.SemaphoreType.DMA
    all_rows = 2 * half_rows
    results = pl.pallas_call(
        functools.partial(
            expert_kernel,
            plane,
            n_dp,
            half_steps,
            which,
            len(carried),
            [index for _, index in pieces],
            [(index, flip) for _, index, flip in riders],
        ),
        grid=(2 * half_steps,),
        in_specs=pair(D)
        + pair(D)
        + [pl.BlockSpec(gates.shape, lambda j: (0, 0, 0))]
        + [anywhere] * (len(pieces) + len(carried) + len(riders)),
        out_specs=pair(D)
        + pair(D)
        + [pl.BlockSpec((2, plane, 1, 128), lambda j: (0, 0, 0, 0))]
        + [anywhere] * (3 + len(carried) + len(riders)),
        out_shape=[shape((half_rows, D), BF)] * 4
        + [shape((2, plane, 1, 128), F32)]
        + [share] * 3
        + [shape(array.shape, BF) for array in carried]
        + [shape(picked_shape(array, index), BF) for array, index, _ in riders],
        scratch_shapes=[
            pltpu.VMEM((D, hidden), BF),
            pltpu.VMEM((D, hidden), BF),
            pltpu.VMEM((hidden, D), BF),
            pltpu.VMEM((all_rows, D), BF),
            pltpu.VMEM((all_rows, D), BF),
            pltpu.VMEM((all_rows, hidden), BF),
            pltpu.VMEM((all_rows, hidden), BF),
            pltpu.VMEM((all_rows, hidden), BF),
            pltpu.VMEM((2, D // n_dp, hidden), BF),
            pltpu.VMEM((len(carried), SLOTS, D), BF),
            dma((len(pieces),)),
            dma((2,)),
            dma((len(carried),)),
            dma((len(carried), plane)),
            dma((len(carried), plane)),
            dma((len(riders),)),
            dma((len(riders),)),
        ],
        compiler_params=pltpu.CompilerParams(
            vmem_limit_bytes=56 * 1024 * 1024, collective_id=number, has_side_effects=True
        ),
        name=name,
    )(*rows, *cots, gates, *[a for a, _ in pieces], *carried, *[a for a, _, _ in riders])
    last = 8 + len(carried)
    return results[:4], results[4], results[5:8], results[8:last], results[last:]


def plane_peer(index):
    n_context = lax.axis_size("context")
    return {"expert": index // n_context, "context": index % n_context}


def plane_here():
    return lax.axis_index("expert") * lax.axis_size("context") + lax.axis_index("context")


def greet(peers):
    barrier = pltpu.get_barrier_semaphore()
    for peer in peers:
        pl.semaphore_signal(barrier, inc=1, device_id=peer, device_id_type=MESH_ID)
    pl.semaphore_wait(barrier, len(peers))


def remote(source, target, send, receive, peer):
    return pltpu.make_async_remote_copy(
        src_ref=source,
        dst_ref=target,
        send_sem=send,
        recv_sem=receive,
        device_id=peer,
        device_id_type=MESH_ID,
    )


def cast_halves(source_ref, halves_ref, loaded, made, load_sems, store_sems):
    rows, experts, width = source_ref.shape
    mine = experts // lax.axis_size("context")
    group = 8
    first = lax.axis_index("context") * mine
    start = pl.multiple_of(first // group * group, group)
    step = loaded.shape[1] * loaded.shape[3] // width
    lower = lax.rem(first, group) == 0
    even = lax.rem(lax.axis_index("dp"), 2) == 0
    steps = rows // step

    def load(n):
        slot = lax.rem(n, 2)
        block = source_ref.at[pl.ds(pl.multiple_of(n * step, step), step), pl.ds(start, group), :]
        return pltpu.make_async_copy(block, loaded.at[slot], load_sems.at[slot])

    def store(n, half):
        slot = lax.rem(n, 2)
        block = halves_ref.at[half, :, pl.ds(pl.multiple_of(n * step, step), step), :]
        return pltpu.make_async_copy(made.at[slot, half], block, store_sems.at[slot, half])

    load(0).start()

    def body(n, carry):
        @pl.when(n + 1 < steps)
        def _():
            load(n + 1).start()

        load(n).wait()

        @pl.when(n >= 2)
        def _():
            for half in range(2):
                store(n - 2, half).wait()

        slot = lax.rem(n, 2)
        block = loaded[slot]
        kept = jnp.where(lower, block[:, :mine, :], block[:, group - mine :, :])
        by_expert = jnp.swapaxes(kept, 0, 1).astype(BF)
        low, high = by_expert[: mine // 2], by_expert[mine // 2 :]
        made[slot, 0] = jnp.where(even, low, high)
        made[slot, 1] = jnp.where(even, high, low)
        for half in range(2):
            store(n, half).start()
        return carry

    lax.fori_loop(0, steps, body, 0)
    for n in (steps - 2, steps - 1):
        for half in range(2):
            store(n, half).wait()


def rank_tables(routes, plane, row_ref, column_ref):
    tokens = routes.shape[1]
    expert = lax.broadcasted_iota(jnp.int32, (EXPERTS, tokens), 0)
    named = jnp.zeros((EXPERTS, tokens), F32)
    for k in range(TOP):
        named = named + jnp.where(routes[k : k + 1, :] == expert, 1.0, 0.0)
    before = lax.broadcasted_iota(jnp.int32, (tokens, tokens), 0) < lax.broadcasted_iota(
        jnp.int32, (tokens, tokens), 1
    )
    count = mxu(named.astype(BF), jnp.where(before, 1.0, 0.0).astype(BF))
    ranks = jnp.where(named > 0, count, -1.0)
    low = ranks.astype(BF)
    owned = EXPERTS // plane
    parity = lax.rem(lax.axis_index("dp"), 2)
    for i in range(2):
        place = lax.broadcasted_iota(jnp.int32, (plane, EXPERTS), 0) * owned + parity * 2 + i
        column = lax.broadcasted_iota(jnp.int32, (plane, EXPERTS), 1)
        chosen = jnp.where(place == column, 1.0, 0.0).astype(BF)
        row_ref[i] = mxu(chosen, low).astype(BF)
        column_ref[i] = mxu(low, chosen, ((0,), (1,))).astype(BF)
    one = lax.broadcasted_iota(jnp.int32, (EXPERTS, EXPERTS), 0) == lax.broadcasted_iota(
        jnp.int32, (EXPERTS, EXPERTS), 1
    )
    return mxu(low, jnp.where(one, 1.0, 0.0).astype(BF), ((0,), (0,)))


def gather_kernel(
    n_dp,
    plane,
    routes_ref,
    in_ref,
    out_ref,
    gate_ref,
    up_ref,
    down_ref,
    cot_ref,
    ranks_ref,
    own_row_ref,
    own_column_ref,
    partner_row_ref,
    partner_column_ref,
    whole_in_ref,
    whole_out_ref,
    gate_halves_ref,
    up_halves_ref,
    down_halves_ref,
    cot_partner_ref,
    partner_routes,
    loaded,
    made,
    loaded_wide,
    made_wide,
    load_sems,
    store_sems,
    local_sems,
    z_send,
    sends,
    recvs,
    route_sems,
):
    here = plane_here()
    z_index = lax.axis_index("dp")
    parts, wholes = (in_ref, out_ref), (whole_in_ref, whole_out_ref)
    z_peer = lambda flip: {"dp": z_index ^ flip}
    greet([z_peer(flip) for flip in range(1, n_dp)] + [plane_peer(here ^ flip) for flip in (1, 2, 4)])
    routing = remote(routes_ref, partner_routes, route_sems.at[0], route_sems.at[1], z_peer(1))
    routing.start()
    keep = [
        pltpu.make_async_copy(part, whole.at[z_index, here], local_sems.at[a])
        for a, (part, whole) in enumerate(zip(parts, wholes))
    ]
    for copy in keep:
        copy.start()
    started = []
    for a in range(2):
        for flip in range(1, n_dp):
            started.append(
                remote(
                    parts[a],
                    wholes[a].at[z_index, here],
                    z_send.at[a, flip],
                    recvs.at[a, z_index, here],
                    z_peer(flip),
                )
            )
            started[-1].start()

    half = cot_partner_ref.shape[0]
    cot_pair = remote(
        cot_ref.at[pl.ds(0, half)], cot_partner_ref, route_sems.at[2], route_sems.at[3], z_peer(1)
    )
    cot_pair.start()

    def pass_on(a, lane, flip, z_from, place, source=None):
        block = wholes[a].at[z_from, place]
        move = remote(
            block if source is None else source,
            block,
            sends.at[a, lane, z_from, place],
            recvs.at[a, z_from, place],
            plane_peer(here ^ flip),
        )
        move.start()
        started.append(move)

    def landed(a, z_from, place):
        block = wholes[a].at[z_from, place]
        remote(block, block, z_send.at[a, 0], recvs.at[a, z_from, place], z_peer(1)).wait_recv()

    froms = [z_index ^ flip for flip in range(n_dp)]
    for a in range(2):
        for lane, flip in enumerate((2, 4, 1)):
            pass_on(a, lane, flip, z_index, here, parts[a])
    ranks_ref[...] = rank_tables(routes_ref[...], plane, own_row_ref, own_column_ref)
    cast_halves(gate_ref, gate_halves_ref, loaded, made, load_sems, store_sems)
    for a in range(2):
        for z_from in froms[1:]:
            landed(a, z_from, here)
            for lane, flip in enumerate((2, 4, 1)):
                pass_on(a, lane, flip, z_from, here)
    cast_halves(up_ref, up_halves_ref, loaded, made, load_sems, store_sems)
    for a in range(2):
        for n, z_from in enumerate(froms):
            landed(a, z_from, here ^ 2)
            if n % 2 == 1:
                pass_on(a, 1, 4, z_from, here ^ 2)
            pass_on(a, 2, 1, z_from, here ^ 2)
            landed(a, z_from, here ^ 4)
            if n % 2 == 0:
                pass_on(a, 0, 2, z_from, here ^ 4)
            pass_on(a, 2, 1, z_from, here ^ 4)
    routing.wait()
    rank_tables(partner_routes[...], plane, partner_row_ref, partner_column_ref)
    cast_halves(down_ref, down_halves_ref, loaded_wide, made_wide, load_sems, store_sems)
    for a in range(2):
        for z_from in froms:
            landed(a, z_from, here ^ 6)
            pass_on(a, 2, 1, z_from, here ^ 6)
    for a in range(2):
        for place in (1, 3, 5, 7):
            for z_from in froms:
                landed(a, z_from, here ^ place)
    for move in started:
        move.wait_send()
    for copy in keep:
        copy.wait()
    cot_pair.wait()


def gather_parts(routes, part_in, part_out, weights, cot, n_dp, n_context, plane):
    tokens = routes.shape[1]
    vmem = pl.BlockSpec(memory_space=pltpu.VMEM)
    anywhere = pl.BlockSpec(memory_space=pl.ANY)
    shape = jax.ShapeDtypeStruct
    dma = pltpu.SemaphoreType.DMA
    row, column = shape((2, plane, tokens), BF), shape((2, tokens, plane), BF)
    mine = weights[0].shape[1] // n_context
    rows, width = 64, weights[0].shape[2]
    return pl.pallas_call(
        functools.partial(gather_kernel, n_dp, plane),
        in_specs=[vmem] + [anywhere] * 6,
        out_specs=[vmem] * 5 + [anywhere] * 6,
        out_shape=[shape((tokens, EXPERTS), F32), row, column, row, column]
        + [shape((n_dp, plane) + part.shape, BF) for part in (part_in, part_out)]
        + [shape((2, mine // 2, w.shape[0], w.shape[2]), BF) for w in weights]
        + [shape((tokens * 3 // 4, D), BF)],
        scratch_shapes=[
            pltpu.VMEM(routes.shape, routes.dtype),
            pltpu.VMEM((2, rows, 8, width), F32),
            pltpu.VMEM((2, 2, mine // 2, rows, width), BF),
            pltpu.VMEM((2, rows // 2, 8, 2 * width), F32),
            pltpu.VMEM((2, 2, mine // 2, rows // 2, 2 * width), BF),
            dma((2,)),
            dma((2, 2)),
            dma((2,)),
            dma((2, n_dp)),
            dma((2, 3, n_dp, plane)),
            dma((2, n_dp, plane)),
            dma((4,)),
        ],
        compiler_params=pltpu.CompilerParams(
            vmem_limit_bytes=60 * 1024 * 1024, collective_id=3, has_side_effects=True
        ),
        name="gather_parts",
    )(routes, part_in, part_out, *weights, cot)


def front_kernel(n_dp, prompt_len, riders, *refs):
    (x_ref, cos_ref, sin_ref, w_in_ref, w_out_ref, cot_ref), refs = refs[:6], refs[6:]
    sources, refs = refs[: len(riders)], refs[len(riders) :]
    (
        gains_ref,
        normed_one_ref,
        qkv_ref,
        kv_ref,
        attended_ref,
        log_ref,
        normed_two_ref,
        logits_ref,
        mid_ref,
        cot_partner_ref,
    ), refs = refs[:10], refs[10:]
    targets, refs = refs[: len(riders)], refs[len(riders) :]
    (
        columns_buf,
        small,
        w_out,
        mid_block,
        load_sems,
        column_sems,
        pair_sems,
        kv_send,
        kv_recv,
        ride_send,
        ride_recv,
    ) = refs
    block_index = lax.axis_index("context")
    n_context = prompt_len // PBLK
    tokens = x_ref.shape[0]
    width = qkv_ref.shape[1]
    greet([context_peer(flip) for flip in range(1, n_context)] + dp_peers(n_dp))
    load_small = pltpu.make_async_copy(w_in_ref.at[:, pl.ds(width, 128)], small, load_sems.at[0])
    load_out = pltpu.make_async_copy(w_out_ref, w_out, load_sems.at[1])
    step_width = columns_buf.shape[2]
    steps = width // step_width
    kv_steps = (width - D) // step_width

    def place_of(n):
        return lax.rem(n + steps - kv_steps, steps)

    def load_columns(n):
        slot = lax.rem(n, 2)
        start = pl.multiple_of(place_of(n) * step_width, step_width)
        return pltpu.make_async_copy(
            w_in_ref.at[:, pl.ds(start, step_width)], columns_buf.at[slot], column_sems.at[slot]
        )

    load_small.start()
    load_columns(0).start()
    load_out.start()
    rest = cot_partner_ref.shape[0]
    pair = remote(
        cot_ref.at[pl.ds(tokens - rest, rest)],
        cot_partner_ref,
        pair_sems.at[0],
        pair_sems.at[1],
        {"dp": lax.axis_index("dp") ^ 1},
    )
    pair.start()
    moves = dp_moves(sources, targets, riders, ride_send, ride_recv)
    for move in moves:
        move.start()
    load_small.wait()
    picked = lax.broadcasted_iota(jnp.int32, (8, 128), 1) - lax.broadcasted_iota(jnp.int32, (8, 128), 0)
    gains_ref[...] = mxu(jnp.where(picked == EXPERTS, 1.0, 0.0).astype(BF), small[...], ((1,), (1,)))

    def normed(rows, gain):
        scale = lax.rsqrt(jnp.mean(rows * rows, axis=-1, keepdims=True) + epsilon)
        return (rows * scale * gain).astype(BF)

    def block_rows(n):
        return pl.ds(pl.multiple_of(n * PBLK, PBLK), PBLK)

    def first_norm(n, carry):
        rows = block_rows(n)
        normed_one_ref[rows, :] = normed(x_ref[rows, :].astype(F32), gains_ref[0:1, :])
        return carry

    lax.fori_loop(0, tokens // PBLK, first_norm, 0)

    def project(n, carry):
        @pl.when(n + 1 < steps)
        def _():
            load_columns(n + 1).start()

        load_columns(n).wait()
        place = place_of(n)
        product = mxu(normed_one_ref[...], columns_buf[lax.rem(n, 2)])
        is_value = place == steps - kv_steps // 2
        cosine = jnp.where(is_value, 1.0, cos_ref[...])
        sine = jnp.where(is_value, 0.0, sin_ref[...])
        factor = jnp.where(place < steps - kv_steps, 1.0 / math.sqrt(HD), 1.0)
        for half in range(step_width // HD):
            part = product[:, half * HD : (half + 1) * HD]
            start = pl.multiple_of(place * step_width + half * HD, HD)
            qkv_ref[:, pl.ds(start, HD)] = (turn(part, cosine, sine) * factor).astype(BF)
        return carry

    lax.fori_loop(0, kv_steps, project, 0)
    own_keys = pl.ds(pl.multiple_of(block_index * PBLK, PBLK), PBLK)
    kv_ref[own_keys, :] = qkv_ref[:PBLK, D:]
    kv_ref[prompt_len:, :] = qkv_ref[PBLK:, D:]
    kv_moves = [
        remote(
            kv_ref.at[own_keys],
            kv_ref.at[own_keys],
            kv_send.at[flip],
            kv_recv.at[flip],
            context_peer(flip),
        )
        for flip in range(1, n_context)
    ]
    for move in kv_moves:
        move.start()
    lax.fori_loop(kv_steps, steps, project, 0)
    for move in kv_moves:
        move.wait()
    log_ref[...] = jnp.zeros_like(log_ref)

    def through_head(head, carry):
        columns = pl.ds(pl.multiple_of(head * HD, HD), HD)
        group = head // (HEADS // KVH)
        key_columns = pl.ds(pl.multiple_of(group * HD, HD), HD)
        value_columns = pl.ds(pl.multiple_of(KVH * HD + group * HD, HD), HD)
        for first_row, keys in row_blocks(prompt_len):
            rows = slice(first_row, first_row + PBLK)
            scores = mxu(qkv_ref[rows, columns], kv_ref[:keys, key_columns], ((1,), (1,)))
            scores = masked_scores(scores, first_row, block_index)
            top = jnp.max(scores, axis=-1, keepdims=True)
            unnormed = jnp.exp(scores - top)
            total = jnp.sum(unnormed, axis=-1, keepdims=True)
            mixed = mxu(unnormed.astype(BF), kv_ref[:keys, value_columns]) / total
            attended_ref[rows, columns] = mixed.astype(BF)
            lane = lax.broadcasted_iota(jnp.int32, (PBLK, log_ref.shape[1]), 1)
            log_ref[rows, :] = jnp.where(lane == head, top + jnp.log(total), log_ref[rows, :])
        return carry

    lax.fori_loop(0, HEADS, through_head, 0)
    load_out.wait()

    def second_norm(n, carry):
        rows = block_rows(n)
        mid = x_ref[rows, :].astype(F32) + mxu(attended_ref[rows, :], w_out[...])
        mid_block[...] = mid
        store = pltpu.make_async_copy(mid_block, mid_ref.at[rows], load_sems.at[2])
        store.start()
        low = normed(mid, gains_ref[1:2, :])
        normed_two_ref[rows, :] = low
        logits_ref[rows, :] = mxu(low, small[...])
        store.wait()
        return carry

    lax.fori_loop(0, tokens // PBLK, second_norm, 0)
    pair.wait()
    for move in moves:
        move.wait()


def front(prompt_len, n_dp, x_low, cosine, sine, w_in, w_out, cot, riders):
    tokens = x_low.shape[0]
    width = D + 2 * KVH * HD
    key_rows = prompt_len + CONT
    n_context = prompt_len // PBLK
    vmem = pl.BlockSpec(memory_space=pltpu.VMEM)
    anywhere = pl.BlockSpec(memory_space=pl.ANY)
    shape = jax.ShapeDtypeStruct
    dma = pltpu.SemaphoreType.DMA
    return pl.pallas_call(
        functools.partial(front_kernel, n_dp, prompt_len, [(index, flip) for _, index, flip in riders]),
        in_specs=[vmem] * 3 + [anywhere] * (3 + len(riders)),
        out_specs=[vmem] * 8 + [anywhere] * (2 + len(riders)),
        out_shape=[
            shape((8, D), F32),
            shape((tokens, D), BF),
            shape((tokens, width), BF),
            shape((key_rows, 2 * KVH * HD), BF),
            shape((tokens, D), BF),
            shape((tokens, 128), F32),
            shape((tokens, D), BF),
            shape((tokens, 128), F32),
            shape((tokens, D), F32),
            shape((tokens // 4, D), BF),
        ]
        + [shape(picked_shape(array, index), BF) for array, index, _ in riders],
        scratch_shapes=[
            pltpu.VMEM((2, D, 2 * HD), BF),
            pltpu.VMEM((D, 128), BF),
            pltpu.VMEM((D, D), BF),
            pltpu.VMEM((PBLK, D), F32),
            dma((3,)),
            dma((2,)),
            dma((2,)),
            dma((n_context,)),
            dma((n_context,)),
            dma((len(riders),)),
            dma((len(riders),)),
        ],
        compiler_params=pltpu.CompilerParams(
            vmem_limit_bytes=56 * 1024 * 1024, collective_id=8, has_side_effects=True
        ),
        name="front",
    )(x_low, cosine, sine, w_in, w_out, cot, *[array for array, _, _ in riders])


def dispatch_kernel(plane, n_dp, riders, *refs):
    normed_ref, cot_ref, own_rank_ref, partner_rank_ref, logits_ref, ranks_ref = refs[:6]
    cot_halves, refs = refs[6:8], refs[8:]
    sources, refs = refs[: len(riders)], refs[len(riders) :]
    gates_ref, gates_here_ref, refs = refs[0], refs[1], refs[2:]
    landed, staged, targets = refs[:4], refs[4:8], refs[8 : 8 + len(riders)]
    (
        stage,
        normed_partner,
        pair_sems,
        stage_sems,
        local_sems,
        send_sems,
        recv_sems,
        ride_send,
        ride_recv,
        all_gates,
        other_gates,
        partner_gates,
        gate_sems,
        gate_send,
        gate_recv,
        cot_partner,
        cot_sems,
    ) = refs[8 + len(riders) :]
    here = plane_here()
    greet([plane_peer(here ^ flip) for flip in range(1, plane)] + dp_peers(n_dp))
    partner = {"dp": lax.axis_index("dp") ^ 1}
    gate_pair = remote(other_gates, partner_gates, gate_sems.at[0], gate_sems.at[1], partner)
    pair = remote(normed_ref, normed_partner, pair_sems.at[0], pair_sems.at[1], partner)
    pair.start()
    moves = dp_moves(sources, targets, riders, ride_send, ride_recv)
    for move in moves:
        move.start()
    first = cot_halves[0].shape[0]
    places = (pl.ds(0, first), pl.ds(first, cot_halves[1].shape[0]))
    cot_loads = [
        pltpu.make_async_copy(part, cot_partner.at[place], cot_sems.at[n])
        for n, (part, place) in enumerate(zip(cot_halves, places))
    ]
    for load in cot_loads:
        load.start()
    plans = (
        (0, normed_ref, own_rank_ref),
        (1, cot_ref, own_rank_ref),
        (2, cot_partner, partner_rank_ref),
        (3, normed_partner, partner_rank_ref),
    )
    exchanges = [
        plane_exchange(n, stage.at[n], landed[n], local_sems, send_sems, recv_sems) for n in range(4)
    ]
    copies = [pltpu.make_async_copy(stage.at[4 + n], staged[n], stage_sems.at[n]) for n in range(4)]

    def slot_gates():
        ranks = ranks_ref[...]
        parity = lax.rem(lax.axis_index("dp"), 2)
        named = ranks >= 0
        logits = jnp.where(named, logits_ref[:, :EXPERTS], masked_score)
        top = jnp.max(logits, axis=-1, keepdims=True)
        raised = jnp.where(named, jnp.exp(logits - top), 0.0)
        gates = raised / jnp.sum(raised, axis=-1, keepdims=True)
        gates_ref[...] = gates
        slot = lax.broadcasted_iota(jnp.int32, (ranks.shape[0], 128), 1).astype(F32)
        owned = EXPERTS // plane
        for place in range(plane):
            for i in range(2):
                rows = []
                for expert in (place * owned + i, place * owned + 2 + i):
                    hit = ranks[:, expert : expert + 1] == slot
                    rows.append(
                        jnp.sum(jnp.where(hit, gates[:, expert : expert + 1], 0.0), axis=0, keepdims=True)
                    )
                all_gates[place, i : i + 1, :] = jnp.where(parity == 0, rows[0], rows[1])
                other_gates[place, i : i + 1, :] = jnp.where(parity == 0, rows[1], rows[0])

    for expert in range(2):
        for n, rows_ref, rank_ref in plans:
            if expert == 0 and n == 2:
                for load in cot_loads:
                    load.wait()
            if expert == 0 and n == 3:
                slot_gates()
                gate_pair.start()
                pair.wait()
            chooser = slot_matrix(rank_ref[expert], plane, True)
            stage[4 * expert + n] = mxu(chooser, rows_ref[...]).astype(BF).reshape(plane, SLOTS, D)
            if expert == 0:
                exchanges[n][0]()
            else:
                copies[n].start()
    gate_pair.wait()
    all_gates[:, 2:4, :] = partner_gates[...]
    gates_here_ref[here] = all_gates[here]
    gate_moves = [
        remote(
            all_gates.at[here ^ flip],
            gates_here_ref.at[here],
            gate_send.at[flip],
            gate_recv.at[flip],
            plane_peer(here ^ flip),
        )
        for flip in range(1, plane)
    ]
    for move in gate_moves:
        move.start()
    for copy in copies:
        copy.wait()
    for _, finish in exchanges:
        finish()
    for move in gate_moves + moves:
        move.wait()


def dispatch_rows(normed, cot, cot_halves, own_ranks, partner_ranks, logits, ranks, riders, n_dp):
    plane, tokens = own_ranks.shape[1:]
    vmem = pl.BlockSpec(memory_space=pltpu.VMEM)
    anywhere = pl.BlockSpec(memory_space=pl.ANY)
    shape = jax.ShapeDtypeStruct
    dma = pltpu.SemaphoreType.DMA
    results = pl.pallas_call(
        functools.partial(dispatch_kernel, plane, n_dp, [(index, flip) for _, index, flip in riders]),
        in_specs=[vmem] * 6 + [anywhere] * (2 + len(riders)),
        out_specs=[vmem] * 2 + [anywhere] * (8 + len(riders)),
        out_shape=[shape(ranks.shape, F32), shape((plane, 4, 128), F32)]
        + [shape((plane, SLOTS, D), BF)] * 8
        + [shape(picked_shape(array, index), BF) for array, index, _ in riders],
        scratch_shapes=[
            pltpu.VMEM((8, plane, SLOTS, D), BF),
            pltpu.VMEM((tokens, D), BF),
            dma((2,)),
            dma((4,)),
            dma((4,)),
            dma((4, plane)),
            dma((4, plane)),
            dma((len(riders),)),
            dma((len(riders),)),
            pltpu.VMEM((plane, 4, 128), F32),
            pltpu.VMEM((plane, 2, 128), F32),
            pltpu.VMEM((plane, 2, 128), F32),
            dma((2,)),
            dma((plane,)),
            dma((plane,)),
            pltpu.VMEM((tokens, D), BF),
            dma((2,)),
        ],
        compiler_params=pltpu.CompilerParams(
            vmem_limit_bytes=56 * 1024 * 1024, collective_id=1, has_side_effects=True
        ),
        cost_estimate=pl.CostEstimate(flops=2 * 10**10, bytes_accessed=4 * 10**8, transcendentals=0),
        name="dispatch_rows",
    )(
        normed, cot, own_ranks, partner_ranks, logits, ranks, *cot_halves, *[a for a, _, _ in riders]
    )
    return results[0], results[1], results[2:6], results[6:10], results[10:]


def sum_matrix(which, sources, summed, sums, part_ref, piece_sems, sum_sems):
    copies = [pltpu.make_async_copy(source, summed.at[n], piece_sems.at[n]) for n, source in enumerate(sources)]
    for copy in copies:
        copy.start()
    for copy in copies:
        copy.wait()
    parity = lax.rem(lax.axis_index("dp"), 2)
    stores = []
    for side in range(2):
        total = summed[side].astype(F32)
        for n in range(side + 2, len(sources), 2):
            total = total + summed[n].astype(F32)
        sums[side] = total.astype(BF)
        place = parity if side == 0 else 1 - parity
        stores.append(pltpu.make_async_copy(sums.at[side], part_ref.at[place, which], sum_sems.at[side]))
        stores[-1].start()
    for store in stores:
        store.wait()


def return_kernel(
    plane,
    n_dp,
    n_results,
    riders,
    names,
    own_rank_ref,
    partner_rank_ref,
    first_dots_ref,
    second_dots_ref,
    ranks_ref,
    gates_ref,
    *refs,
):
    early, back = refs[0:2], refs[2:4]
    results, refs = refs[4 : 4 + n_results], refs[4 + n_results :]
    sources, refs = refs[: len(riders)], refs[len(riders) :]
    mine, refs = refs[:3], refs[3:]
    arrived, refs = refs[: len(HOME_SECOND)], refs[len(HOME_SECOND) :]
    total_ref, dlog_ref, part_ref = refs[:3]
    results_back, refs = refs[3 : 3 + n_results], refs[3 + n_results :]
    targets = refs[: len(riders)]
    homes = dict(zip(HOME_SECOND, arrived))
    homes.update(zip(names, targets))
    (
        held,
        to_partner,
        of_partner,
        load_sems,
        pair_sems,
        local_sems,
        send_sems,
        recv_sems,
        ride_send,
        ride_recv,
        dot_sems,
        dot_send,
        dot_recv,
        dots_ref,
        dots_here_ref,
        dots_other_ref,
        bounce,
        summed,
        sums,
        partial,
        piece_sems,
        sum_sems,
    ) = refs[len(riders) :]
    here = plane_here()
    partner = {"dp": lax.axis_index("dp") ^ 1}
    greet([plane_peer(here ^ flip) for flip in range(1, plane)] + dp_peers(n_dp))
    for n, by_side in enumerate((first_dots_ref, second_dots_ref)):
        for side in range(2):
            dots_ref[:, 2 * side + n : 2 * side + n + 1, :] = by_side[side]
    own_dots = pltpu.make_async_copy(dots_ref.at[here], dots_here_ref.at[here], dot_sems.at[0])
    own_dots.start()
    dot_moves = [
        remote(
            dots_ref.at[here ^ flip],
            dots_here_ref.at[here],
            dot_send.at[flip],
            dot_recv.at[flip],
            plane_peer(here ^ flip),
        )
        for flip in range(1, plane)
    ]
    for move in dot_moves:
        move.start()
    loads, exchanges = {}, {}
    for side in (1, 0):
        loads[side] = pltpu.make_async_copy(early[side], held.at[2 * side], load_sems.at[side])
        loads[side].start()
        exchanges[side] = plane_exchange(
            side, back[side], held.at[2 * side + 1], local_sems, send_sems, recv_sems
        )
    exchanges[1][0]()
    later = [
        plane_exchange(2 + n, results[n], results_back[n], local_sems, send_sems, recv_sems, bounce)
        for n in range(n_results)
    ]
    moves = dp_moves(sources, targets, riders, ride_send, ride_recv)
    own_dots.wait()
    for move in dot_moves:
        move.wait()
    dots_pair = remote(dots_here_ref, dots_other_ref, dot_sems.at[1], dot_sems.at[2], partner)
    dots_pair.start()

    def of_gates():
        tokens = ranks_ref.shape[0]
        parity = lax.rem(lax.axis_index("dp"), 2)
        owned = EXPERTS // plane
        slot = lax.broadcasted_iota(jnp.int32, (tokens, 128), 1).astype(F32)
        lane = lax.broadcasted_iota(jnp.int32, (tokens, EXPERTS), 1)
        made = jnp.zeros((tokens, EXPERTS), F32)
        for expert in range(EXPERTS):
            place, side, i = expert // owned, expert % owned // 2, expert % 2
            row = jnp.where(
                parity == side,
                dots_here_ref[place, i : i + 1, :],
                dots_other_ref[place, 2 + i : 3 + i, :],
            )
            hit = ranks_ref[:, expert : expert + 1] == slot
            value = jnp.sum(jnp.where(hit, row, 0.0), axis=-1, keepdims=True)
            made = jnp.where(lane == expert, value, made)
        gates = gates_ref[...]
        mean = jnp.sum(gates * made, axis=-1, keepdims=True)
        dlog_ref[...] = jnp.zeros_like(dlog_ref)
        dlog_ref[:, :EXPERTS] = (gates * (made - mean)).astype(BF)

    def sum_of(which):
        sources = [mine[which].at[0]] + [homes[which, flip, 0] for flip in range(1, n_dp)]
        sum_matrix(which, sources, summed, sums, part_ref, piece_sems, sum_sems)

    blocks = [slice(start, start + PBLK) for start in range(0, total_ref.shape[0], PBLK)]

    def collected(rank_ref, rows, side, expert):
        chooser = slot_matrix(rank_ref[expert, rows, :], plane, False)
        return mxu(chooser, held[2 * side + expert].reshape(plane * SLOTS, D))

    for move in moves[:RETURN_FIRST]:
        move.start()
    loads[1].wait()
    for rows in blocks:
        partial[rows, :] = collected(partner_rank_ref, rows, 1, 0)
    loads[0].wait()
    for rows in blocks:
        total_ref[rows, :] = collected(own_rank_ref, rows, 0, 0)
    sum_of(0)
    sum_of(1)
    exchanges[1][1]()
    exchanges[0][0]()
    pairs = []
    for n, rows in enumerate(blocks):
        to_partner[rows, :] = (partial[rows, :] + collected(partner_rank_ref, rows, 1, 1)).astype(BF)
        block = pl.ds(n * PBLK, PBLK)
        pairs.append(
            remote(to_partner.at[block], of_partner.at[block], pair_sems.at[0, n], pair_sems.at[1, n], partner)
        )
        pairs[-1].start()
    for move in moves[RETURN_FIRST:]:
        move.start()
    for begin, _ in later:
        begin()
    dots_pair.wait()
    of_gates()
    for move in moves[:RETURN_FIRST]:
        move.wait()
    sum_of(2)
    exchanges[0][1]()
    for rows in blocks:
        total_ref[rows, :] += collected(own_rank_ref, rows, 0, 1)
    for pair, rows in zip(pairs, blocks):
        pair.wait()
        total_ref[rows, :] += of_partner[rows, :].astype(F32)
    for move in moves[RETURN_FIRST:]:
        move.wait()
    for _, finish in later:
        finish()


def return_rows(
    own_ranks, partner_ranks, first_dots, second_dots, ranks, gates, early, back, results, riders, names, shares, arrived, n_dp
):
    tokens, plane = own_ranks.shape[1:]
    vmem = pl.BlockSpec(memory_space=pltpu.VMEM)
    anywhere = pl.BlockSpec(memory_space=pl.ANY)
    shape = jax.ShapeDtypeStruct
    dma = pltpu.SemaphoreType.DMA
    outcome = pl.pallas_call(
        functools.partial(
            return_kernel, plane, n_dp, len(results), [(index, flip) for _, index, flip in riders], names
        ),
        in_specs=[vmem] * 6 + [anywhere] * (7 + len(results) + len(riders) + len(arrived)),
        out_specs=[vmem] * 2 + [anywhere] * (1 + len(results) + len(riders)),
        out_shape=[shape((tokens, D), F32), shape((tokens, 128), BF), shape((2, 3) + shares[0].shape[1:], BF)]
        + [shape(rows.shape, BF) for rows in results]
        + [shape(picked_shape(array, index), BF) for array, index, _ in riders],
        scratch_shapes=[
            pltpu.VMEM((4, plane, SLOTS, D), BF),
            pltpu.VMEM((tokens, D), BF),
            pltpu.VMEM((tokens, D), BF),
            dma((2,)),
            dma((2, tokens // PBLK)),
            dma((4,)),
            dma((4, plane)),
            dma((4, plane)),
            dma((len(riders),)),
            dma((len(riders),)),
            dma((3,)),
            dma((plane,)),
            dma((plane,)),
            pltpu.VMEM((plane, 4, 128), F32),
            pltpu.VMEM((plane, 4, 128), F32),
            pltpu.VMEM((plane, 4, 128), F32),
            pltpu.VMEM((2 + len(results), SLOTS, D), BF),
            pltpu.VMEM(shares[0].shape, BF),
            pltpu.VMEM((2,) + shares[0].shape[1:], BF),
            pltpu.VMEM((tokens, D), F32),
            dma((n_dp,)),
            dma((2,)),
        ],
        compiler_params=pltpu.CompilerParams(
            vmem_limit_bytes=56 * 1024 * 1024, collective_id=2, has_side_effects=True
        ),
        cost_estimate=pl.CostEstimate(flops=3 * 10**10, bytes_accessed=4 * 10**8, transcendentals=0),
        name="return_rows",
    )(
        own_ranks,
        partner_ranks,
        first_dots,
        second_dots,
        ranks,
        gates,
        *early,
        *back,
        *results,
        *[array for array, _, _ in riders],
        *shares,
        *arrived,
    )
    last = 3 + len(results)
    return outcome[0], outcome[1], outcome[2], outcome[3:last], outcome[last:]


def normed_back(rows, gain, grads):
    scale = lax.rsqrt(jnp.mean(rows * rows, axis=-1, keepdims=True) + epsilon)
    weighted = grads * gain
    mean = jnp.mean(rows * weighted, axis=-1, keepdims=True)
    return scale * weighted - rows * (scale * scale * scale * mean), rows * scale * grads


def context_peer(flip):
    return {"context": lax.axis_index("context") ^ flip}


def share_context(part, place_of, sends, recvs):
    here = lax.axis_index("context")
    across = remote(part, place_of(here), sends.at[0], recvs.at[here], context_peer(2))
    beside = remote(part, place_of(here), sends.at[1], recvs.at[here], context_peer(1))
    block = place_of(here ^ 2)
    onward = remote(block, block, sends.at[2], recvs.at[here ^ 2], context_peer(1))

    def begin():
        across.start()
        beside.start()

    def pass_on():
        remote(part, block, sends.at[0], recvs.at[here ^ 2], context_peer(2)).wait_recv()
        onward.start()

    def finish():
        for flip in (1, 3):
            remote(part, place_of(here ^ flip), sends.at[1], recvs.at[here ^ flip], context_peer(1)).wait_recv()
        across.wait_send()
        beside.wait_send()
        onward.wait_send()

    return begin, pass_on, finish


def backward_kernel(n_dp, prompt_len, n_results, riders, *refs):
    (
        dlog_ref,
        cot_ref,
        x_ref,
        gains_in_ref,
        attended_ref,
        qkv_ref,
        kv_ref,
        log_ref,
        normed_ref,
        cos_ref,
        sin_ref,
        mid_ref,
        total_ref,
        w_out_ref,
        w_in_ref,
        normed_two_ref,
        part_ref,
    ) = refs[:17]
    results, refs = refs[17 : 17 + n_results], refs[17 + n_results :]
    late = len(riders)
    sources, refs = refs[:late], refs[late:]
    grad_x_ref, grad_out_ref, grad_in_ref, grad_small_ref, all_ref = refs[:5]
    results_back, refs = refs[5 : 5 + n_results], refs[5 + n_results :]
    homes, refs = refs[:late], refs[late:]
    (
        weights,
        grad_mid,
        grad_attn,
        mid_block,
        grad_qkv,
        grad_kv,
        kv_send,
        kv_recv,
        stage,
        load_sems,
        store_sems,
        kv_send_sems,
        kv_recv_sems,
        home_send,
        home_recv,
        share_sends,
        share_recvs,
        small,
        gains_ref,
        bounce,
        local_sems,
        send_sems,
        recv_sems,
    ) = refs
    block_index = lax.axis_index("context")
    n_context = kv_send.shape[0]
    tokens = x_ref.shape[0]
    heads_width = HEADS * HD
    kv_width = KVH * HD
    here = plane_here()
    plane = results[0].shape[0]
    greet([plane_peer(here ^ flip) for flip in range(1, plane)] + dp_peers(n_dp))
    load_small = pltpu.make_async_copy(
        w_in_ref.at[:, pl.ds(weights.shape[1], 128)], small, load_sems.at[4]
    )
    load_small.start()
    load_total = pltpu.make_async_copy(total_ref, grad_mid, load_sems.at[0])
    load_out = pltpu.make_async_copy(w_out_ref, weights.at[:, pl.ds(0, D)], load_sems.at[1])
    load_in = pltpu.make_async_copy(w_in_ref.at[:, pl.ds(0, weights.shape[1])], weights, load_sems.at[2])
    load_total.start()
    load_out.start()
    homing = dp_moves(sources, homes, riders, home_send, home_recv)
    for move in homing:
        move.start()
    begin_all, pass_on, finish = share_context(
        part_ref, lambda place: all_ref.at[place], share_sends, share_recvs
    )
    begin_all()
    exchanges = [
        plane_exchange(side, results[side], results_back[side], local_sems, send_sems, recv_sems, bounce)
        for side in range(n_results)
    ]
    load_small.wait()
    load_total.wait()
    load_out.wait()
    gains_ref[...] = jnp.zeros_like(gains_ref)

    def block_rows(n):
        return pl.ds(pl.multiple_of(n * PBLK, PBLK), PBLK)

    def through_norm(n, carry):
        rows = block_rows(n)
        load_mid = pltpu.make_async_copy(mid_ref.at[rows], mid_block, load_sems.at[3])
        load_mid.start()
        load_mid.wait()
        grads = grad_mid[rows, :] + mxu(dlog_ref[rows, :], small[...], ((1,), (1,)))
        by_rows, by_gain = normed_back(mid_block[...], gains_in_ref[1:2, :], grads)
        gains_ref[1:2, :] += jnp.sum(by_gain, axis=0, keepdims=True)
        by_mid = cot_ref[rows, :].astype(F32) + by_rows
        grad_mid[rows, :] = by_mid
        low = by_mid.astype(BF)
        grad_attn[rows, :] = low
        grad_qkv[rows, :D] = mxu(low, weights[:, :D], ((1,), (1,))).astype(BF)
        return carry

    lax.fori_loop(0, tokens // PBLK, through_norm, 0)
    load_in.start()
    grad_kv[...] = jnp.zeros_like(grad_kv)

    def through_head(head, carry):
        columns = pl.ds(pl.multiple_of(head * HD, HD), HD)
        group = head // (HEADS // KVH)
        key_columns = pl.ds(pl.multiple_of(group * HD, HD), HD)
        value_columns = pl.ds(pl.multiple_of(kv_width + group * HD, HD), HD)
        for first_row, keys in row_blocks(prompt_len):
            rows = slice(first_row, first_row + PBLK)
            queries, grads = qkv_ref[rows, columns], grad_qkv[rows, columns]
            scores = mxu(queries, kv_ref[:keys, key_columns], ((1,), (1,)))
            scores = masked_scores(scores, first_row, block_index)
            lane = lax.broadcasted_iota(jnp.int32, (PBLK, log_ref.shape[1]), 1)
            logs = jnp.sum(jnp.where(lane == head, log_ref[rows, :], 0.0), axis=-1, keepdims=True)
            probs = jnp.exp(scores - logs)
            grad_probs = mxu(grads, kv_ref[:keys, value_columns], ((1,), (1,)))
            dots = jnp.sum(probs * grad_probs, axis=-1, keepdims=True)
            grad_scores = (probs * (grad_probs - dots)).astype(BF)
            grad_query = mxu(grad_scores, kv_ref[:keys, key_columns])
            grad_query = turn(grad_query, cos_ref[rows, :], -sin_ref[rows, :]) * (1.0 / math.sqrt(HD))
            grad_qkv[rows, columns] = grad_query.astype(BF)
            grad_kv[:keys, key_columns] += mxu(grad_scores, queries, ((0,), (0,)))
            grad_kv[:keys, value_columns] += mxu(probs.astype(BF), grads, ((0,), (0,)))
        return carry

    lax.fori_loop(0, HEADS, through_head, 0)

    for place in range(n_context):
        kv_send[place] = grad_kv[place * PBLK : (place + 1) * PBLK, :].astype(BF)
    kv_moves = [
        remote(
            kv_send.at[block_index ^ flip],
            kv_recv.at[flip],
            kv_send_sems.at[flip],
            kv_recv_sems.at[flip],
            context_peer(flip),
        )
        for flip in range(1, n_context)
    ]
    for move in kv_moves:
        move.start()
    for begin, _ in exchanges:
        begin()

    quarter = D // n_dp

    def quarter_rows(q):
        return pl.ds(pl.multiple_of(q * quarter, 128), quarter)

    def share_of_out(q, carry):
        made = mxu(attended_ref[:, quarter_rows(q)], grad_attn[...], ((0,), (0,)))
        stage[:, :D] = made.astype(BF)
        store = pltpu.make_async_copy(
            stage.at[:, pl.ds(0, D)], grad_out_ref.at[quarter_rows(q)], store_sems.at[0]
        )
        store.start()
        store.wait()
        return carry

    lax.fori_loop(0, n_dp, share_of_out, 0)
    load_normed = pltpu.make_async_copy(normed_two_ref, grad_attn, load_sems.at[0])
    load_normed.start()

    for move in kv_moves:
        move.wait()
    own_rows = pl.ds(pl.multiple_of(block_index * PBLK, PBLK), PBLK)
    summed = grad_kv[own_rows, :]
    for flip in range(1, n_context):
        summed = summed + kv_recv[flip].astype(F32)
    pieces = [(0, PBLK, summed), (PBLK, tokens, grad_kv[prompt_len:, :])]
    for first, last, made in pieces:
        for group in range(KVH):
            turned = turn(
                made[:, group * HD : (group + 1) * HD], cos_ref[first:last, :], -sin_ref[first:last, :]
            )
            start = heads_width + group * HD
            grad_qkv[first:last, start : start + HD] = turned.astype(BF)
        grad_qkv[first:last, heads_width + kv_width :] = made[:, kv_width:].astype(BF)

    load_in.wait()

    def share_of_in(q, carry):
        stage[...] = mxu(normed_ref[:, quarter_rows(q)], grad_qkv[...], ((0,), (0,))).astype(BF)
        store = pltpu.make_async_copy(stage, grad_in_ref.at[quarter_rows(q)], store_sems.at[0])
        store.start()
        store.wait()
        return carry

    lax.fori_loop(0, n_dp, share_of_in, 0)

    def through_first(n, carry):
        rows = block_rows(n)
        grads = mxu(grad_qkv[rows, :], weights[...], ((1,), (1,)))
        by_rows, by_gain = normed_back(x_ref[rows, :].astype(F32), gains_in_ref[0:1, :], grads)
        gains_ref[0:1, :] += jnp.sum(by_gain, axis=0, keepdims=True)
        grad_x_ref[rows, :] = (grad_mid[rows, :] + by_rows).astype(BF)
        return carry

    pass_on()
    lax.fori_loop(0, tokens // PBLK, through_first, 0)
    load_normed.wait()
    lane = lax.broadcasted_iota(jnp.int32, (8, 128), 1)
    column = lax.broadcasted_iota(jnp.int32, (8, 128), 0) + EXPERTS
    place = jnp.where((lane == column) & (column < EXPERTS + 2), 1.0, 0.0).astype(BF)
    of_router = mxu(grad_attn[...], dlog_ref[...], ((0,), (0,)))
    small[...] = (of_router + mxu(gains_ref[...].astype(BF), place, ((0,), (0,)))).astype(BF)
    store_small = pltpu.make_async_copy(small, grad_small_ref, store_sems.at[0])
    store_small.start()
    finish()
    store_small.wait()
    for _, end in exchanges:
        end()
    for move in homing:
        move.wait()


def backward(prompt_len, n_dp, in_vmem, in_hbm, results, riders):
    tokens = in_vmem[0].shape[0]
    width = D + 2 * KVH * HD
    n_context = prompt_len // PBLK
    key_rows = prompt_len + CONT
    quarter = D // n_dp
    vmem = pl.BlockSpec(memory_space=pltpu.VMEM)
    anywhere = pl.BlockSpec(memory_space=pl.ANY)
    part = in_hbm[-1]
    plane = results[0].shape[0]
    shape = jax.ShapeDtypeStruct
    return pl.pallas_call(
        functools.partial(
            backward_kernel, n_dp, prompt_len, len(results), [(index, flip) for _, index, flip in riders]
        ),
        in_specs=[vmem] * len(in_vmem) + [anywhere] * (len(in_hbm) + len(results) + len(riders)),
        out_specs=[vmem] + [anywhere] * (4 + len(results) + len(riders)),
        out_shape=[
            shape((tokens, D), BF),
            shape((D, D), BF),
            shape((D, width), BF),
            shape((D, 128), BF),
            shape((n_context,) + part.shape, BF),
        ]
        + [shape(rows.shape, BF) for rows in results]
        + [shape(picked_shape(array, index), BF) for array, index, _ in riders],
        scratch_shapes=[
            pltpu.VMEM((D, width), BF),
            pltpu.VMEM((tokens, D), F32),
            pltpu.VMEM((tokens, D), BF),
            pltpu.VMEM((PBLK, D), F32),
            pltpu.VMEM((tokens, width), BF),
            pltpu.VMEM((key_rows, 2 * KVH * HD), F32),
            pltpu.VMEM((n_context, PBLK, 2 * KVH * HD), BF),
            pltpu.VMEM((n_context, PBLK, 2 * KVH * HD), BF),
            pltpu.VMEM((quarter, width), BF),
            pltpu.SemaphoreType.DMA((5,)),
            pltpu.SemaphoreType.DMA((1,)),
            pltpu.SemaphoreType.DMA((n_context,)),
            pltpu.SemaphoreType.DMA((n_context,)),
            pltpu.SemaphoreType.DMA((len(riders),)),
            pltpu.SemaphoreType.DMA((len(riders),)),
            pltpu.SemaphoreType.DMA((3,)),
            pltpu.SemaphoreType.DMA((n_context,)),
            pltpu.VMEM((D, 128), BF),
            pltpu.VMEM((8, D), F32),
            pltpu.VMEM((len(results), SLOTS, D), BF),
            pltpu.SemaphoreType.DMA((len(results),)),
            pltpu.SemaphoreType.DMA((len(results), plane)),
            pltpu.SemaphoreType.DMA((len(results), plane)),
        ],
        compiler_params=pltpu.CompilerParams(
            vmem_limit_bytes=56 * 1024 * 1024, collective_id=4, has_side_effects=True
        ),
        name="backward",
    )(*in_vmem, *in_hbm, *results, *[array for array, _, _ in riders])


def reduce_kernel(n_dp, widths, *refs):
    count = len(widths)
    shares, refs = refs[:count], refs[count:]
    own_rank_ref, partner_rank_ref, mid_ref = refs[:3]
    rows_of, mine, refs = (refs[3:5], refs[5:7]), refs[7:10], refs[10:]
    names = HOME_RETURN[RETURN_FIRST:] + HOME_BACKWARD
    homes, refs = dict(zip(names, refs)), refs[len(names) :]
    totals, refs = refs[:count], refs[count:]
    result_ref, all_ref, part_ref = refs[:3]
    refs = refs[3:]
    sums, core_in, first_in, second_in, z_in = (refs[n * count : (n + 1) * count] for n in range(5))
    (
        load_sems,
        core_send,
        core_recv,
        first_send,
        first_recv,
        second_send,
        second_recv,
        z_send,
        z_recv,
        out_send,
        out_recv,
        share_sends,
        share_recvs,
        pair_sems,
        held,
        to_partner,
        of_partner,
        mixed,
        mid_block,
        held_sems,
        summed,
        matrix_sums,
        piece_sems,
        sum_sems,
    ) = refs[5 * count :]
    here = plane_here()
    plane = held.shape[1]
    z_index = lax.axis_index("dp")
    greet(
        [plane_peer(here ^ flip) for flip in (1, 2, 4)] + [{"dp": z_index ^ flip} for flip in range(1, n_dp)]
    )
    chips = (0, 2, 4, 6)
    order = [1, 2, 3, 0] if n_dp == 4 else list(range(1, n_dp)) + [0]
    loads, core_moves = {}, {}
    for n in order:
        z_to = z_index ^ n
        for a in range(count):
            for m, chip in enumerate(chips):
                loads[n, a, m] = pltpu.make_async_copy(
                    shares[a].at[z_to, here ^ chip], sums[a].at[n, m], load_sems.at[a, n, m]
                )
                loads[n, a, m].start()
                core_moves[n, a, m] = remote(
                    shares[a].at[z_to, here ^ 1 ^ chip],
                    core_in[a].at[n, m],
                    core_send.at[a, n, m],
                    core_recv.at[a, n, m],
                    plane_peer(here ^ 1),
                )
                core_moves[n, a, m].start()

    def load_rows(side):
        copies = [
            pltpu.make_async_copy(rows_of[side][expert], held.at[expert], held_sems.at[expert])
            for expert in range(2)
        ]
        for copy in copies:
            copy.start()
        return copies

    rows_here = load_rows(1)
    gathers = [
        share_context(
            part_ref.at[:, m],
            lambda place, m=m: all_ref.at[place, :, m],
            share_sends.at[m],
            share_recvs.at[m],
        )
        for m in range(2)
    ]

    def sum_of(which):
        sources = [mine[which].at[0]] + [homes[which, flip, 1] for flip in range(1, n_dp)]
        sum_matrix(which, sources, summed, matrix_sums, part_ref, piece_sems, sum_sems)

    sum_of(0)
    gathers[0][0]()
    for copy in rows_here:
        copy.wait()
    collect_into(plane, partner_rank_ref, held, 0, to_partner, lambda rows, made: made.astype(BF))
    pair = remote(to_partner, of_partner, pair_sems.at[0], pair_sems.at[1], {"dp": z_index ^ 1})
    pair.start()
    rows_here = load_rows(0)

    def add(target, *others):
        total = target[...].astype(F32)
        for other in others:
            total = total + other[...].astype(F32)
        target[...] = total.astype(BF)

    first_moves, second_moves, z_moves = {}, {}, {}
    for n in order:
        toward = 2 if n % 2 == 0 else 4
        kept = 6 - toward
        for a in range(count):
            for m in range(4):
                loads[n, a, m].wait()
                core_moves[n, a, m].wait_recv()
                add(sums[a].at[n, m], core_in[a].at[n, m])
            for slot, chip in enumerate((toward, 6)):
                first_moves[n, a, slot] = remote(
                    sums[a].at[n, chip // 2],
                    first_in[a].at[n, slot],
                    first_send.at[a, n, slot],
                    first_recv.at[a, n, slot],
                    plane_peer(here ^ toward),
                )
                first_moves[n, a, slot].start()
    sum_of(1)
    sum_of(2)
    for copy in rows_here:
        copy.wait()

    def with_mid(rows, made):
        load = pltpu.make_async_copy(mid_ref.at[rows], mid_block, held_sems.at[2])
        load.start()
        load.wait()
        return mid_block[...] + made

    collect_into(plane, own_rank_ref, held, 0, mixed, with_mid)
    for n in order:
        toward = 2 if n % 2 == 0 else 4
        kept = 6 - toward
        for a in range(count):
            for slot, chip in enumerate((0, kept)):
                first_moves[n, a, slot].wait_recv()
                add(sums[a].at[n, chip // 2], first_in[a].at[n, slot])
            second_moves[n, a] = remote(
                sums[a].at[n, kept // 2],
                second_in[a].at[n],
                second_send.at[a, n],
                second_recv.at[a, n],
                plane_peer(here ^ kept),
            )
            second_moves[n, a].start()
    gathers[1][0]()
    gathers[0][1]()
    for n in order:
        for a in range(count):
            second_moves[n, a].wait_recv()
            add(sums[a].at[n, 0], second_in[a].at[n])
            if n > 0:
                z_moves[n, a] = remote(
                    sums[a].at[n, 0], z_in[a].at[n], z_send.at[a, n], z_recv.at[a, n], {"dp": z_index ^ n}
                )
                z_moves[n, a].start()
    started = list(core_moves.values()) + list(first_moves.values())
    started += list(second_moves.values()) + list(z_moves.values())

    def pass_on(a, lane, flip, place):
        block = totals[a].at[place]
        move = remote(
            block, block, out_send.at[a, lane, place], out_recv.at[a, place], plane_peer(here ^ flip)
        )
        move.start()
        started.append(move)

    def landed(a, place):
        block = totals[a].at[place]
        remote(block, block, out_send.at[a, 0, place], out_recv.at[a, place], plane_peer(here ^ 1)).wait_recv()

    for a in range(count):
        for n in range(1, n_dp):
            z_moves[n, a].wait_recv()
        add(sums[a].at[0, 0], *[z_in[a].at[n] for n in range(1, n_dp)])
        totals[a][here] = sums[a][0, 0]
        for lane, flip in enumerate((2, 4, 1)):
            pass_on(a, lane, flip, here)
    for a in range(count):
        landed(a, here ^ 2)
        if a % 2 == 1:
            pass_on(a, 1, 4, here ^ 2)
        pass_on(a, 2, 1, here ^ 2)
        landed(a, here ^ 4)
        if a % 2 == 0:
            pass_on(a, 0, 2, here ^ 4)
        pass_on(a, 2, 1, here ^ 4)
    for a in range(count):
        landed(a, here ^ 6)
        pass_on(a, 2, 1, here ^ 6)
    gathers[1][1]()
    pair.wait()
    result_ref[...] = (mixed[...] + of_partner[...].astype(F32)).astype(BF)
    for a in range(count):
        for flip in (1, 3, 5, 7):
            landed(a, here ^ flip)
    for move in started:
        move.wait_send()
    for _, _, finish in gathers:
        finish()


def reduce_shares(shares, ranks, mid, slot_rows, mine, homes, n_dp, n_context):
    plane, rows = shares[0].shape[1:3]
    widths = tuple(share.shape[3] for share in shares)
    count = len(widths)
    vmem = pl.BlockSpec(memory_space=pltpu.VMEM)
    anywhere = pl.BlockSpec(memory_space=pl.ANY)
    shape = jax.ShapeDtypeStruct
    dma = pltpu.SemaphoreType.DMA

    def buffers(*lead):
        return [pltpu.VMEM(lead + (rows, width), BF) for width in widths]

    return pl.pallas_call(
        functools.partial(reduce_kernel, n_dp, widths),
        in_specs=[anywhere] * count + [vmem] * 2 + [anywhere] * (8 + len(homes)),
        out_specs=[vmem] * (count + 1) + [anywhere] * 2,
        out_shape=[shape((plane, rows, width), BF) for width in widths]
        + [
            shape(mid.shape, BF),
            shape((n_context, 2, 2) + homes[0].shape, BF),
            shape((2, 3) + homes[0].shape, BF),
        ],
        scratch_shapes=buffers(n_dp, 4)
        + buffers(n_dp, 4)
        + buffers(n_dp, 2)
        + buffers(n_dp)
        + buffers(n_dp)
        + [
            dma((count, n_dp, 4)),
            dma((count, n_dp, 4)),
            dma((count, n_dp, 4)),
            dma((count, n_dp, 2)),
            dma((count, n_dp, 2)),
            dma((count, n_dp)),
            dma((count, n_dp)),
            dma((count, n_dp)),
            dma((count, n_dp)),
            dma((count, 3, plane)),
            dma((count, plane)),
            dma((2, 3)),
            dma((2, n_context)),
            dma((2,)),
            pltpu.VMEM((2, plane, SLOTS, D), BF),
            pltpu.VMEM(mid.shape, BF),
            pltpu.VMEM(mid.shape, BF),
            pltpu.VMEM(mid.shape, F32),
            pltpu.VMEM((PBLK, D), F32),
            dma((3,)),
            pltpu.VMEM((n_dp,) + homes[0].shape, BF),
            pltpu.VMEM((2,) + homes[0].shape, BF),
            dma((n_dp,)),
            dma((2,)),
        ],
        compiler_params=pltpu.CompilerParams(
            vmem_limit_bytes=56 * 1024 * 1024, collective_id=5, has_side_effects=True
        ),
        name="reduce_shares",
    )(*shares, *ranks, mid, *slot_rows[0], *slot_rows[1], *mine, *homes)


def finish_kernel(n_context, apart, halves, *refs):
    (first_ref, own_first_ref), out_ref = refs[:2], refs[-1]
    seconds = refs[2:-1]
    step, experts, _ = out_ref.shape
    here = lax.axis_index("context")
    group = 16
    size = group * experts
    log_group, log_experts = group.bit_length() - 1, experts.bit_length() - 1
    to = lax.broadcasted_iota(jnp.int32, (size, size), 0)
    of = lax.broadcasted_iota(jnp.int32, (size, size), 1)
    same_row = (to >> log_experts) == (of & (group - 1))
    same_expert = (to & (experts - 1)) == (of >> log_group)
    turned = jnp.where(same_row & same_expert, 1.0, 0.0).astype(BF)

    def gathered(all_ref, own_ref, place, side, at):
        return jnp.where(here == place, own_ref[(side, 0) + at], all_ref[(place, side, 0) + at])

    def by_distance(place, side, at):
        value = seconds[0][(side, 0) + at]
        for flip in range(1, n_context):
            value = jnp.where((here ^ place) == flip, seconds[flip][(side, 0) + at], value)
        return value

    width = out_ref.shape[2] // halves
    for half in range(halves):
        at_half = (half,) if halves > 1 else ()
        for start in range(0, step, group):
            at = at_half + (slice(start, start + group),)
            rows = []
            for place in range(n_context):
                for side in range(2):
                    rows.append(gathered(first_ref, own_first_ref, place, side, at))
                    if apart:
                        rows.append(by_distance(place, side, at))
                    else:
                        rows.append(gathered(seconds[0], seconds[1], place, side, at))
            made = mxu(turned, jnp.concatenate(rows, axis=0))
            out_ref[start : start + group, :, half * width : (half + 1) * width] = made.reshape(
                group, experts, width
            )


def finish_weight(which, first, own_first, seconds):
    n_context, _, _, rows, width = first.shape
    experts = n_context * 4
    step = 32
    apart = len(seconds) == n_context
    halves = 2 if which == 2 else 1
    rows, wide = rows // halves, width * halves
    parts = [first, own_first, *seconds]
    specs = []
    for n, part in enumerate(parts):
        lead = part.shape[:-3]
        matrix = 0 if part.shape[-3] == 1 else which
        if halves > 1:
            parts[n] = part.reshape(part.shape[:-2] + (halves, rows, width))
            block = lead + (1, halves, step, width)
            specs.append(pl.BlockSpec(block, lambda j, k=len(lead), m=matrix: (0,) * k + (m, 0, j, 0)))
        else:
            block = lead + (1, step, width)
            specs.append(pl.BlockSpec(block, lambda j, k=len(lead), m=matrix: (0,) * k + (m, j, 0)))
    return pl.pallas_call(
        functools.partial(finish_kernel, n_context, apart, halves),
        grid=(rows // step,),
        in_specs=specs,
        out_specs=pl.BlockSpec((step, experts, wide), lambda j: (j, 0, 0)),
        out_shape=jax.ShapeDtypeStruct((rows, experts, wide), F32),
        compiler_params=grant(),
        cost_estimate=pl.CostEstimate(flops=2 * 10**9, bytes_accessed=30 * 10**6, transcendentals=0),
        name="finish_weight",
    )(*parts)


def flip_permute(value, axis, size, flip):
    return lax.ppermute(value, axis, [(i, i ^ flip) for i in range(size)])


def local_paired(
    inputs,
    cotangent,
    routes,
    attn_q,
    attn_k,
    attn_v,
    attn_o,
    norm_attn,
    norm_moe,
    router,
    expert_gate,
    expert_up,
    expert_down,
):
    n_context, n_expert, n_dp = lax.axis_size("context"), lax.axis_size("expert"), lax.axis_size("dp")
    plane = n_context * n_expert
    tokens = inputs.shape[1]
    block_index = lax.axis_index("context")
    z_index = lax.axis_index("dp")
    parity = z_index % 2
    prompt_len = PBLK * n_context
    x_low = inputs[0]
    cot_low = cotangent[0]
    route_rows = routes[0]

    here = lax.axis_index("expert") * n_context + block_index
    part_rows = attn_q.shape[0] // plane

    def part_of(shard):
        return lax.dynamic_slice_in_dim(shard, here * part_rows, part_rows, 0).astype(BF)

    part_in = jnp.concatenate(
        [part_of(attn_q), part_of(attn_k), part_of(attn_v), part_of(router)]
        + [part_of(norm_attn)[:, None], part_of(norm_moe)[:, None]]
        + [jnp.zeros((part_rows, 128 - EXPERTS - 2), BF)],
        axis=1,
    )
    qkv_width = D + 2 * KVH * HD
    weights = (expert_gate, expert_up, expert_down)
    own_ranks, own_rows, own_columns, partner_rows, partner_columns, whole_in, w_out, *weight_halves = (
        gather_parts(route_rows.T, part_in, part_of(attn_o), weights, cot_low, n_dp, n_context, plane)
    )
    partner_cot = [weight_halves.pop()]
    whole_in = whole_in.reshape(-1, part_in.shape[1])
    w_out = w_out.reshape(-1, D)
    pieces = {(which, 0, i): (weight_halves[which], (0, i)) for which in range(3) for i in range(2)}

    def riding(names):
        return [
            (weight_halves[which], flip % 2 if i is None else (flip % 2, i), flip) for which, flip, i in names
        ]

    def pieces_of(expert):
        return [pieces[which, flip, expert] for which in range(3) for flip in range(n_dp)]

    positions = jnp.concatenate(
        [
            block_index * PBLK + jnp.arange(PBLK, dtype=jnp.int32),
            prompt_len + jnp.arange(CONT, dtype=jnp.int32),
        ]
    )
    angles = angle_table(positions)
    cos_half, sin_half = jnp.cos(angles), jnp.sin(angles)
    cosine = jnp.concatenate([cos_half, cos_half], axis=1)
    sine = jnp.concatenate([-sin_half, sin_half], axis=1)
    gains, normed_one, qkv, keys_values, attended, logs, normed_two, logits, mid_rows, cot_half, *moved = (
        front(prompt_len, n_dp, x_low, cosine, sine, whole_in, w_out, cot_low, riding(RIDE_FRONT))
    )
    partner_cot.append(cot_half)
    for (which, flip, expert), piece in zip(RIDE_FRONT, moved):
        if expert is None:
            pieces.update({(which, flip, i): (piece, i) for i in range(2)})
        else:
            pieces[which, flip, expert] = (piece, None)

    gates, gates_here, landed, staged, arrived = dispatch_rows(
        normed_two, cot_low, partner_cot, own_rows, partner_rows, logits, own_ranks, riding(RIDE_DISPATCH), n_dp
    )
    pieces.update({name: (piece, None) for name, piece in zip(RIDE_DISPATCH, arrived)})

    def slots_of(arrays):
        flat = [array.reshape(plane * SLOTS, D) for array in arrays]
        return (flat[0], flat[3]), (flat[1], flat[2])

    parted = lambda arrays: [array.reshape(plane, SLOTS, D) for array in arrays]
    rows, cots = slots_of(landed)
    first, first_dots, first_shares, landed, arrived = run_expert(
        "first_expert", 0, 6, rows, cots, gates_here, pieces_of(0), staged, riding(RIDE_FIRST)
    )
    pieces.update({name: (piece, None) for name, piece in zip(RIDE_FIRST, arrived)})
    rows, cots = slots_of(landed)

    def homing(names, *shares):
        return [(shares[i][which], flip, flip) for which, flip, i in names]

    second, second_dots, second_shares, early, homes = run_expert(
        "second_expert",
        1,
        7,
        rows,
        cots,
        gates_here,
        pieces_of(1),
        parted(first)[1:4],
        homing(HOME_SECOND, first_shares),
    )

    second = parted(second)
    grad_rows, grad_logits, part_first, late, homes_second = return_rows(
        own_columns,
        partner_columns,
        first_dots,
        second_dots,
        own_ranks,
        gates,
        early[1:3],
        second[2:4],
        [parted(first)[0], second[1]],
        homing(HOME_RETURN, first_shares, second_shares),
        HOME_RETURN,
        first_shares,
        homes,
        n_dp,
    )
    grad_inputs, grad_wout, grad_wqkv, grad_small, all_first, *homes = backward(
        prompt_len,
        n_dp,
        (
            grad_logits,
            cot_low,
            x_low,
            gains,
            attended,
            qkv,
            keys_values,
            logs,
            normed_one,
            cosine,
            sine,
        ),
        (mid_rows, grad_rows, w_out, whole_in, normed_two, part_first),
        second[0:1],
        homing(HOME_BACKWARD, first_shares, second_shares),
    )
    last, homes = homes[0], list(homes_second[RETURN_FIRST:]) + list(homes[1:])
    out_own, out_partner = [late[0], last], [early[0], late[1]]

    parts = lambda share: share.reshape(n_dp, plane, -1, share.shape[1])
    total_qkv, total_out, total_small, result, all_second, part_second = reduce_shares(
        [parts(grad_wqkv), parts(grad_wout), parts(grad_small)],
        (own_columns, partner_columns),
        mid_rows,
        (out_own, out_partner),
        second_shares,
        homes,
        n_dp,
        n_context,
    )
    own = part_second[:, 2:]
    across = flip_permute(own, "context", n_context, 2)
    beside = flip_permute(own, "context", n_context, 1)
    grad_gate, grad_up = (
        finish_weight(which, all_first, part_first, (all_second, part_second)) for which in range(2)
    )
    across, beside, grad_gate, grad_up = lax.optimization_barrier((across, beside, grad_gate, grad_up))
    apart = (own, beside, across, flip_permute(across, "context", n_context, 1))
    total_qkv = total_qkv.reshape(-1, qkv_width).astype(F32)
    total_out = total_out.reshape(-1, D).astype(F32)
    total_small = total_small.reshape(-1, 128).astype(F32)
    return (
        result[None],
        grad_inputs[None],
        total_qkv[:, :D],
        total_qkv[:, D : D + KVH * HD],
        total_qkv[:, D + KVH * HD :],
        total_out,
        total_small[:, EXPERTS],
        total_small[:, EXPERTS + 1],
        total_small[:, :EXPERTS],
        grad_gate,
        grad_up,
        finish_weight(2, all_first, part_first, apart),
    )


def paired_plan(mesh):
    n_expert, n_context, n_dp = mesh.shape["expert"], mesh.shape["context"], mesh.shape["dp"]
    owners = 2 * n_expert * n_context
    small_axes = all(size & (size - 1) == 0 for size in (n_expert, n_context, n_dp))
    return small_axes and n_dp % 2 == 0 and EXPERTS == 2 * owners


def solution(mesh):
    in_specs = (
        P(("expert", "dp"), "context", None),
        P(("expert", "dp"), "context", None),
        P(("expert", "dp"), "context", None),
        P("dp", None),
        P("dp", None),
        P("dp", None),
        P("dp", None),
        P("dp"),
        P("dp"),
        P("dp", None),
        P("dp", "expert", None),
        P("dp", "expert", None),
        P("dp", "expert", None),
    )
    out_specs = (
        P(("expert", "dp"), "context", None),
        P(("expert", "dp"), "context", None),
        P("dp", None),
        P("dp", None),
        P("dp", None),
        P("dp", None),
        P("dp"),
        P("dp"),
        P("dp", None),
        P("dp", "expert", None),
        P("dp", "expert", None),
        P("dp", "expert", None),
    )
    chosen = local_paired if paired_plan(mesh) else local
    return jax.shard_map(chosen, mesh=mesh, in_specs=in_specs, out_specs=out_specs, check_vma=False)
```

```python
import functools
import math

import jax
import jax.numpy as jnp
from jax import lax
from jax.experimental import pallas as pl
from jax.experimental.pallas import tpu as pltpu
from jax.sharding import PartitionSpec as P

D = 1536
HEADS = 12
KVH = 2
HD = 128
EXPERTS = 32
TOP = 4
PBLK = 256
CONT = 512
CAP = 103


epsilon = 1e-06
rope_base = 1000000.0
masked_score = -1e30


def rms_scale(values, gain):
    return values * lax.rsqrt(jnp.mean(values * values, axis=-1, keepdims=True) + epsilon) * gain


def angle_table(positions):
    steps_half = jnp.arange(HD // 2, dtype=jnp.float32)
    inverse = jnp.exp(steps_half * (-2.0 * math.log(rope_base) / HD))
    return positions.astype(jnp.float32)[..., None] * inverse


def rotary(values, angles, direction):
    halfway = values.shape[-1] // 2
    cosine = jnp.cos(angles)[..., None, :]
    sine_part = direction * jnp.sin(angles)[..., None, :]
    leading = values[..., :halfway]
    trailing = values[..., halfway:]
    return jnp.concatenate(
        [leading * cosine - trailing * sine_part, trailing * cosine + leading * sine_part], axis=-1
    )


def visible(query_pos, key_pos, prompt_len):
    query_cont = jnp.arange(query_pos.shape[0]) >= PBLK
    key_prompt = jnp.arange(key_pos.shape[0]) < prompt_len
    return (key_pos[None, :] <= query_pos[:, None]) & (key_prompt[None, :] | query_cont[:, None])


def gating(logit_rows, route_rows):
    picker = (route_rows[:, :, None] == jnp.arange(EXPERTS, dtype=jnp.int32)[None, None, :]).astype(
        logit_rows.dtype
    )
    chosen = jnp.sum(picker * logit_rows[:, None, :], axis=-1)
    return jax.nn.softmax(chosen, axis=-1)


def gated(gate_pre, up_pre):
    return jax.nn.silu(gate_pre) * up_pre


def expert_slots(flat_experts):
    picker = (flat_experts[:, None] == jnp.arange(EXPERTS, dtype=jnp.int32)[None, :]).astype(
        jnp.int32
    )
    earlier = jnp.cumsum(picker, axis=0) - picker
    return jnp.sum(earlier * picker, axis=1)


def local(
    inputs,
    cotangent,
    routes,
    attn_q,
    attn_k,
    attn_v,
    attn_o,
    norm_attn,
    norm_moe,
    router,
    expert_gate,
    expert_up,
    expert_down,
):
    low_type = jnp.bfloat16
    full_type = jnp.float32
    w_query, w_key, w_value, w_out, gain_first, gain_second, w_router, w_gate, w_up, w_down = (
        lax.all_gather(attn_q.astype(low_type), "dp", axis=0, tiled=True),
        lax.all_gather(attn_k.astype(low_type), "dp", axis=0, tiled=True),
        lax.all_gather(attn_v.astype(low_type), "dp", axis=0, tiled=True),
        lax.all_gather(attn_o.astype(low_type), "dp", axis=0, tiled=True),
        lax.all_gather(norm_attn.astype(low_type), "dp", axis=0, tiled=True),
        lax.all_gather(norm_moe.astype(low_type), "dp", axis=0, tiled=True),
        lax.all_gather(router.astype(low_type), "dp", axis=0, tiled=True),
        lax.all_gather(expert_gate.astype(low_type), "dp", axis=0, tiled=True),
        lax.all_gather(expert_up.astype(low_type), "dp", axis=0, tiled=True),
        lax.all_gather(expert_down.astype(low_type), "dp", axis=0, tiled=True),
    )
    n_context = lax.axis_size("context")
    n_expert = lax.axis_size("expert")
    block_index = lax.axis_index("context")
    prompt_len = PBLK * n_context
    tokens = inputs.shape[1]
    local_experts = w_gate.shape[1]
    group_width = HEADS // KVH
    score_scale = 1.0 / math.sqrt(HD)
    gain_one = gain_first.astype(full_type)
    gain_two = gain_second.astype(full_type)
    x_rows = inputs[0].astype(full_type)
    positions = jnp.concatenate(
        [
            block_index * PBLK + jnp.arange(PBLK, dtype=jnp.int32),
            prompt_len + jnp.arange(CONT, dtype=jnp.int32),
        ]
    )
    angles = angle_table(positions)
    normed_one = rms_scale(x_rows, gain_one).astype(low_type)
    q_proj = jnp.dot(normed_one, w_query, preferred_element_type=full_type)
    k_proj = jnp.dot(normed_one, w_key, preferred_element_type=full_type)
    v_proj = jnp.dot(normed_one, w_value, preferred_element_type=full_type)
    queries = (rotary(q_proj.reshape(tokens, HEADS, HD), angles, 1.0) * score_scale).astype(
        low_type
    )
    queries = queries.reshape(tokens, KVH, group_width, HD)
    keys_own = rotary(k_proj.reshape(tokens, KVH, HD), angles, 1.0).astype(low_type)
    values_own = v_proj.astype(low_type).reshape(tokens, KVH, HD)
    prompt_keys, prompt_values = (
        lax.all_gather(keys_own[:PBLK], "context", axis=0, tiled=True),
        lax.all_gather(values_own[:PBLK], "context", axis=0, tiled=True),
    )
    all_keys = jnp.concatenate([prompt_keys, keys_own[PBLK:]], axis=0)
    all_values = jnp.concatenate([prompt_values, values_own[PBLK:]], axis=0)
    key_pos = jnp.concatenate(
        [jnp.arange(prompt_len, dtype=jnp.int32), prompt_len + jnp.arange(CONT, dtype=jnp.int32)]
    )
    allowed = visible(positions, key_pos, prompt_len)
    head_outs = []
    log_totals = []
    for kv_head in range(KVH):
        scores = jnp.einsum(
            "tgn,kn->gtk",
            queries[:, kv_head],
            all_keys[:, kv_head],
            preferred_element_type=full_type,
        )
        scores = jnp.where(allowed[None], scores, masked_score)
        top_score = jnp.max(scores, axis=-1, keepdims=True)
        unnormed = jnp.exp(scores - top_score)
        totals = jnp.sum(unnormed, axis=-1, keepdims=True)
        attn_probs = (unnormed / totals).astype(low_type)
        head_outs.append(
            jnp.einsum(
                "gtk,kn->tgn", attn_probs, all_values[:, kv_head], preferred_element_type=full_type
            )
        )
        log_totals.append(top_score + jnp.log(totals))
    attended_low = jnp.stack(head_outs, axis=1).reshape(tokens, D).astype(low_type)
    mid_rows = x_rows + jnp.dot(attended_low, w_out, preferred_element_type=full_type)
    normed_two = rms_scale(mid_rows, gain_two).astype(low_type)
    logits = jnp.dot(normed_two, w_router, preferred_element_type=full_type)
    route_rows = routes[0]
    gate_weights = gating(logits, route_rows)
    flat_experts = route_rows.reshape(-1)
    slot_rank = expert_slots(flat_experts)
    destination = (
        flat_experts % local_experts * n_expert + flat_experts // local_experts
    ) * CAP + slot_rank
    capacity_rows = local_experts * n_expert * CAP
    assignments = tokens * TOP
    source = (
        jnp.full((capacity_rows,), assignments, dtype=jnp.int32)
        .at[destination]
        .set(jnp.arange(assignments, dtype=jnp.int32))
    )
    filled = source < assignments
    source_row = jnp.minimum(source, assignments - 1)
    send_rows = jnp.where(filled[:, None], normed_two[source_row // TOP], jnp.zeros((), low_type))
    received = lax.all_to_all(
        send_rows.reshape(local_experts, n_expert, CAP, D),
        "expert",
        split_axis=1,
        concat_axis=1,
        tiled=True,
    )
    received = received.reshape(local_experts, n_expert * CAP, D)
    gate_pre = jnp.einsum("lrd,dlf->lrf", received, w_gate, preferred_element_type=full_type)
    up_pre = jnp.einsum("lrd,dlf->lrf", received, w_up, preferred_element_type=full_type)
    activation = gated(gate_pre, up_pre).astype(low_type)
    expert_rows = jnp.einsum(
        "lrf,fld->lrd", activation, w_down, preferred_element_type=full_type
    ).astype(low_type)
    returned = lax.all_to_all(
        expert_rows.reshape(local_experts, n_expert, CAP, D),
        "expert",
        split_axis=1,
        concat_axis=1,
        tiled=True,
    )
    returned = returned.reshape(capacity_rows, D)
    picked = returned[destination].reshape(tokens, TOP, D)
    moe_out = jnp.sum(gate_weights[:, :, None] * picked.astype(full_type), axis=1)
    result = (mid_rows + moe_out).astype(low_type)
    grad_out = cotangent[0].astype(full_type)
    slot_grads = (
        (gate_weights[:, :, None] * grad_out[:, None, :]).reshape(assignments, D).astype(low_type)
    )
    send_grads = jnp.where(filled[:, None], slot_grads[source_row], jnp.zeros((), low_type))
    grad_rows = lax.all_to_all(
        send_grads.reshape(local_experts, n_expert, CAP, D),
        "expert",
        split_axis=1,
        concat_axis=1,
        tiled=True,
    )
    grad_rows = grad_rows.reshape(local_experts, n_expert * CAP, D)
    grad_gates = jnp.sum(picked.astype(full_type) * grad_out[:, None, :], axis=-1)
    grad_wdown = jnp.einsum("lrf,lrd->fld", activation, grad_rows, preferred_element_type=full_type)
    grad_act = jnp.einsum("lrd,fld->lrf", grad_rows, w_down, preferred_element_type=full_type)
    primal_gate, gated_back = jax.vjp(gated, gate_pre, up_pre)
    grad_gpre, grad_upre = gated_back(grad_act)
    grad_gpre = grad_gpre.astype(low_type)
    grad_upre = grad_upre.astype(low_type)
    grad_wgate = jnp.einsum("lrd,lrf->dlf", received, grad_gpre, preferred_element_type=full_type)
    grad_wup = jnp.einsum("lrd,lrf->dlf", received, grad_upre, preferred_element_type=full_type)
    grad_recv = jnp.einsum("lrf,dlf->lrd", grad_gpre, w_gate, preferred_element_type=full_type)
    grad_recv = (
        grad_recv + jnp.einsum("lrf,dlf->lrd", grad_upre, w_up, preferred_element_type=full_type)
    ).astype(low_type)
    back_rows = lax.all_to_all(
        grad_recv.reshape(local_experts, n_expert, CAP, D),
        "expert",
        split_axis=1,
        concat_axis=1,
        tiled=True,
    )
    back_rows = back_rows.reshape(capacity_rows, D)
    grad_normed_two = jnp.sum(
        back_rows[destination].reshape(tokens, TOP, D).astype(full_type), axis=1
    )

    def gate_of(logit_rows):
        return gating(logit_rows, route_rows)

    primal_gates, gate_back = jax.vjp(gate_of, logits)
    grad_logits = gate_back(grad_gates)[0].astype(low_type)
    grad_wrouter = jnp.einsum(
        "td,te->de", normed_two, grad_logits, preferred_element_type=full_type
    )
    grad_normed_two = grad_normed_two + jnp.einsum(
        "te,de->td", grad_logits, w_router, preferred_element_type=full_type
    )
    primal_two, norm_back_two = jax.vjp(rms_scale, mid_rows, gain_two)
    grad_mid_norm, grad_gain_two = norm_back_two(grad_normed_two)
    grad_mid = grad_out + grad_mid_norm
    grad_attn = grad_mid.astype(low_type)
    grad_wout = jnp.einsum("td,te->de", attended_low, grad_attn, preferred_element_type=full_type)
    grad_attended = jnp.einsum(
        "te,de->td", grad_attn, w_out, preferred_element_type=full_type
    ).astype(low_type)
    grad_attended = grad_attended.reshape(tokens, KVH, group_width, HD)
    query_grads = []
    key_grads = []
    value_grads = []
    for kv_head in range(KVH):
        scores = jnp.einsum(
            "tgn,kn->gtk",
            queries[:, kv_head],
            all_keys[:, kv_head],
            preferred_element_type=full_type,
        )
        scores = jnp.where(allowed[None], scores, masked_score)
        exact_probs = jnp.exp(scores - log_totals[kv_head])
        grad_probs = jnp.einsum(
            "tgn,kn->gtk",
            grad_attended[:, kv_head],
            all_values[:, kv_head],
            preferred_element_type=full_type,
        )
        row_dots = jnp.sum(exact_probs * grad_probs, axis=-1, keepdims=True)
        grad_scores = (exact_probs * (grad_probs - row_dots)).astype(low_type)
        query_grads.append(
            jnp.einsum(
                "gtk,kn->tgn", grad_scores, all_keys[:, kv_head], preferred_element_type=full_type
            )
        )
        key_grads.append(
            jnp.einsum(
                "gtk,tgn->kn", grad_scores, queries[:, kv_head], preferred_element_type=full_type
            )
        )
        value_grads.append(
            jnp.einsum(
                "gtk,tgn->kn",
                exact_probs.astype(low_type),
                grad_attended[:, kv_head],
                preferred_element_type=full_type,
            )
        )
    grad_queries = jnp.stack(query_grads, axis=1).reshape(tokens, HEADS, HD)
    grad_keys = jnp.stack(key_grads, axis=1)
    grad_values = jnp.stack(value_grads, axis=1)
    prompt_key_grad, prompt_value_grad = (
        lax.psum_scatter(
            grad_keys[:prompt_len].astype(jnp.bfloat16), "context", scatter_dimension=0, tiled=True
        ).astype(jnp.float32),
        lax.psum_scatter(
            grad_values[:prompt_len].astype(jnp.bfloat16),
            "context",
            scatter_dimension=0,
            tiled=True,
        ).astype(jnp.float32),
    )
    own_key_grad = jnp.concatenate([prompt_key_grad, grad_keys[prompt_len:]], axis=0)
    own_value_grad = jnp.concatenate([prompt_value_grad, grad_values[prompt_len:]], axis=0)
    grad_qproj = (
        rotary(grad_queries * score_scale, angles, -1.0).reshape(tokens, D).astype(low_type)
    )
    grad_kproj = rotary(own_key_grad, angles, -1.0).reshape(tokens, KVH * HD).astype(low_type)
    grad_vproj = own_value_grad.reshape(tokens, KVH * HD).astype(low_type)
    grad_wquery = jnp.einsum("td,te->de", normed_one, grad_qproj, preferred_element_type=full_type)
    grad_wkey = jnp.einsum("td,te->de", normed_one, grad_kproj, preferred_element_type=full_type)
    grad_wvalue = jnp.einsum("td,te->de", normed_one, grad_vproj, preferred_element_type=full_type)
    grad_normed_one = jnp.einsum("te,de->td", grad_qproj, w_query, preferred_element_type=full_type)
    grad_normed_one = grad_normed_one + jnp.einsum(
        "te,de->td", grad_kproj, w_key, preferred_element_type=full_type
    )
    grad_normed_one = grad_normed_one + jnp.einsum(
        "te,de->td", grad_vproj, w_value, preferred_element_type=full_type
    )
    primal_one, norm_back_one = jax.vjp(rms_scale, x_rows, gain_one)
    grad_x_norm, grad_gain_one = norm_back_one(grad_normed_one)
    grad_inputs = (grad_mid + grad_x_norm).astype(low_type)
    shares = (
        lax.psum_scatter(
            grad_wquery.astype(jnp.bfloat16), "dp", scatter_dimension=0, tiled=True
        ).astype(jnp.float32),
        lax.psum_scatter(
            grad_wkey.astype(jnp.bfloat16), "dp", scatter_dimension=0, tiled=True
        ).astype(jnp.float32),
        lax.psum_scatter(
            grad_wvalue.astype(jnp.bfloat16), "dp", scatter_dimension=0, tiled=True
        ).astype(jnp.float32),
        lax.psum_scatter(
            grad_wout.astype(jnp.bfloat16), "dp", scatter_dimension=0, tiled=True
        ).astype(jnp.float32),
        lax.psum_scatter(
            grad_gain_one.astype(jnp.bfloat16), "dp", scatter_dimension=0, tiled=True
        ).astype(jnp.float32),
        lax.psum_scatter(
            grad_gain_two.astype(jnp.bfloat16), "dp", scatter_dimension=0, tiled=True
        ).astype(jnp.float32),
        lax.psum_scatter(
            grad_wrouter.astype(jnp.bfloat16), "dp", scatter_dimension=0, tiled=True
        ).astype(jnp.float32),
        lax.psum_scatter(
            grad_wgate.astype(jnp.bfloat16), "dp", scatter_dimension=0, tiled=True
        ).astype(jnp.float32),
        lax.psum_scatter(
            grad_wup.astype(jnp.bfloat16), "dp", scatter_dimension=0, tiled=True
        ).astype(jnp.float32),
        lax.psum_scatter(
            grad_wdown.astype(jnp.bfloat16), "dp", scatter_dimension=0, tiled=True
        ).astype(jnp.float32),
    )
    dense_sum = lax.psum(
        (shares[0], shares[1], shares[2], shares[3], shares[4], shares[5], shares[6]),
        ("expert", "context"),
    )
    expert_sum = (
        lax.psum(shares[7].astype(jnp.bfloat16), "context").astype(jnp.float32),
        lax.psum(shares[8].astype(jnp.bfloat16), "context").astype(jnp.float32),
        lax.psum(shares[9].astype(jnp.bfloat16), "context").astype(jnp.float32),
    )
    totals_all = tuple(dense_sum) + tuple(expert_sum)
    return (
        result[None],
        grad_inputs[None],
        totals_all[0],
        totals_all[1],
        totals_all[2],
        totals_all[3],
        totals_all[4],
        totals_all[5],
        totals_all[6],
        totals_all[7],
        totals_all[8],
        totals_all[9],
    )


BF = jnp.bfloat16
F32 = jnp.float32
SLOTS = 112
MESH_ID = pl.DeviceIdType.MESH
PLANE = ("expert", "context")
VMEM_BYTES = 60 * 1024 * 1024


def mxu(lhs, rhs, contract=((1,), (0,))):
    return lax.dot_general(lhs, rhs, (contract, ((), ())), preferred_element_type=F32)


def grant(bytes_wanted=VMEM_BYTES):
    return pltpu.CompilerParams(vmem_limit_bytes=bytes_wanted)


def turn(values, cosine, sine):
    return values * cosine + pltpu.roll(values, HD // 2, 1) * sine


def row_blocks(prompt_len):
    blocks = [(0, prompt_len)]
    for start in range(0, CONT, PBLK):
        blocks.append((PBLK + start, prompt_len + start + PBLK))
    return blocks


def masked_scores(scores, first_row, block_index):
    tail = scores if first_row == 0 else scores[:, -PBLK:]
    row = lax.broadcasted_iota(jnp.int32, tail.shape, 0)
    column = lax.broadcasted_iota(jnp.int32, tail.shape, 1)
    limit = row + block_index * PBLK if first_row == 0 else row
    tail = jnp.where(column <= limit, tail, masked_score)
    return tail if first_row == 0 else jnp.concatenate([scores[:, :-PBLK], tail], axis=1)


def segment_matrix(parts, transposed):
    shape = (parts * SLOTS, parts) if transposed else (parts, parts * SLOTS)
    long = lax.broadcasted_iota(jnp.int32, shape, 0 if transposed else 1)
    short = lax.broadcasted_iota(jnp.int32, shape, 1 if transposed else 0)
    inside = (long >= short * SLOTS) & (long < (short + 1) * SLOTS)
    return jnp.where(inside, 1.0, 0.0).astype(BF)


def slot_matrix(ranks, parts, transposed):
    if transposed:
        spread = mxu(segment_matrix(parts, True), ranks)
        slot = lax.broadcasted_iota(jnp.int32, (parts * SLOTS, 1), 0)
    else:
        spread = mxu(ranks, segment_matrix(parts, False))
        slot = lax.broadcasted_iota(jnp.int32, (1, parts * SLOTS), 1)
    for part in range(parts - 1, 0, -1):
        slot = jnp.where(slot >= part * SLOTS, slot - SLOTS, slot)
    return jnp.where(spread == slot.astype(F32), 1.0, 0.0).astype(BF)


def collect_into(plane, rank_ref, held, base, target, finish):
    def block(n, carry):
        rows = pl.ds(pl.multiple_of(n * PBLK, PBLK), PBLK)
        made = jnp.zeros((PBLK, D), F32)
        for expert in range(2):
            chooser = slot_matrix(rank_ref[expert, rows, :], plane, False)
            made = made + mxu(chooser, held[base + expert].reshape(plane * SLOTS, D))
        target[rows, :] = finish(rows, made)
        return carry

    lax.fori_loop(0, target.shape[0] // PBLK, block, 0)


def plane_exchange(slot, source, target, local_sems, send_sems, recv_sems, bounce=None):
    here = plane_here()
    plane = source.shape[0]
    own_first = target.at[here] if bounce is None else bounce.at[slot]

    def begin():
        pltpu.make_async_copy(source.at[here], own_first, local_sems.at[slot]).start()

        def one(flip, carry):
            peer = here ^ flip
            remote(
                source.at[peer],
                target.at[here],
                send_sems.at[slot, peer],
                recv_sems.at[slot, here],
                plane_peer(peer),
            ).start()
            return carry

        lax.fori_loop(1, plane, one, 0)

    def finish():
        pltpu.make_async_copy(source.at[here], own_first, local_sems.at[slot]).wait()
        if bounce is not None:
            onward = pltpu.make_async_copy(own_first, target.at[here], local_sems.at[slot])
            onward.start()
            onward.wait()

        def one(flip, carry):
            peer = here ^ flip
            done = remote(
                source.at[peer],
                target.at[peer],
                send_sems.at[slot, peer],
                recv_sems.at[slot, peer],
                plane_peer(peer),
            )
            done.wait_send()
            done.wait_recv()
            return carry

        lax.fori_loop(1, plane, one, 0)

    return begin, finish


ALL_FLIPS = (2, 3, 1)
RIDE_FRONT = ((0, 2, 1), (0, 3, 0), (0, 1, 0))
RIDE_DISPATCH = ((1, 2, 0), (1, 3, 0), (2, 2, 0), (2, 3, 0), (1, 1, 0), (2, 1, 0))
DISPATCH_FIRST = 4
RIDE_FIRST = ((0, 3, 1), (0, 1, 1)) + tuple((m, f, 1) for m in (1, 2) for f in ALL_FLIPS)
HOME_SECOND = tuple((m, f, 0) for m in (0, 1) for f in (2, 3)) + tuple((m, 1, 0) for m in range(3))
HOME_RETURN = ((2, 2, 0), (2, 3, 0), (0, 2, 1), (0, 3, 1))
RETURN_FIRST = 2
HOME_BACKWARD = tuple((m, f, 1) for m in (1, 2) for f in (2, 3)) + tuple((m, 1, 1) for m in range(3))


def pick(array, index):
    return array if index is None else array.at[index]


def picked_shape(array, index):
    if index is None:
        return array.shape
    return array.shape[len(index) if isinstance(index, tuple) else 1 :]


def dp_moves(sources, targets, riders, sends, recvs):
    z_index = lax.axis_index("dp")
    return [
        remote(pick(source, index), target, sends.at[n], recvs.at[n], {"dp": z_index ^ flip})
        for n, (source, target, (index, flip)) in enumerate(zip(sources, targets, riders))
    ]


def dp_peers(n_dp):
    return [{"dp": lax.axis_index("dp") ^ flip} for flip in range(1, n_dp)]


def expert_kernel(plane, n_dp, half_steps, number, n_carried, picks, riders, *refs):
    (xo_ref, xp_ref, go_ref, gp_ref, gates_ref), refs = refs[:5], refs[5:]
    pieces, refs = refs[: 3 * n_dp], refs[3 * n_dp :]
    carried, refs = refs[:n_carried], refs[n_carried:]
    sources, refs = refs[: len(riders)], refs[len(riders) :]
    (yo_ref, yp_ref, bo_ref, bp_ref, dots_ref, gate_ref, up_ref, down_ref), refs = refs[:8], refs[8:]
    landed, refs = refs[:n_carried], refs[n_carried:]
    targets, refs = refs[: len(riders)], refs[len(riders) :]
    (wg_ref, wu_ref, wd_ref, x_all, de_all, a_all, dg_all, du_all, stage, bounce), sems = refs[:10], refs[10:]
    weight_sems, store_sems, local_sems, send_sems, recv_sems, ride_send, ride_recv = sems
    weights = (wg_ref, wu_ref, wd_ref)
    z_index = lax.axis_index("dp")
    step = pl.program_id(0)
    own = step < half_steps
    rows_of_step = xo_ref.shape[0]
    exchanges = [
        plane_exchange(n, source, target, local_sems, send_sems, recv_sems, bounce)
        for n, (source, target) in enumerate(zip(carried, landed))
    ]
    moves = dp_moves(sources, targets, riders, ride_send, ride_recv)

    @pl.when(step == 0)
    def _():
        here = plane_here()
        greet([plane_peer(here ^ flip) for flip in range(1, plane)] + dp_peers(n_dp))
        loads = []
        for n, piece in enumerate(pieces):
            source = pick(piece, picks[n])
            size = source.shape[0]
            start = pl.multiple_of((z_index ^ (n % n_dp)) * size, 64)
            loads.append(
                pltpu.make_async_copy(source, weights[n // n_dp].at[pl.ds(start, size)], weight_sems.at[n])
            )
            loads[-1].start()
        for begin, _ in exchanges:
            begin()
        for move in moves:
            move.start()
        for load in loads:
            load.wait()

    rows = jnp.where(own, xo_ref[...], xp_ref[...])
    cot = jnp.where(own, go_ref[...], gp_ref[...])
    places = rows_of_step // SLOTS
    first_place = lax.rem(step, half_steps) * places
    at = (SLOTS, 128)
    diagonal = lax.broadcasted_iota(jnp.int32, at, 0) == lax.broadcasted_iota(jnp.int32, at, 1)
    columns = []
    for n in range(places):
        own_row = gates_ref[first_place + n, number : number + 1, :]
        row = jnp.where(own, own_row, gates_ref[first_place + n, 2 + number : 3 + number, :])
        columns.append(jnp.sum(jnp.where(diagonal, row, 0.0), axis=-1, keepdims=True))
    share = jnp.concatenate(columns, axis=0)
    place = pl.ds(pl.multiple_of(step * rows_of_step, 32), rows_of_step)
    x_all[place, :] = rows
    gate_pre = mxu(rows, wg_ref[...])
    up_pre = mxu(rows, wu_ref[...])
    sigma = 1.0 / (1.0 + jnp.exp(-gate_pre))
    silu = gate_pre * sigma
    act = (silu * up_pre).astype(BF)
    a_all[place, :] = act
    cot_full = cot.astype(F32)
    weighted = (cot_full * share).astype(BF)
    de_all[place, :] = weighted
    result = mxu(act, wd_ref[...])
    dots = jnp.sum(result.astype(BF).astype(F32) * cot_full, axis=-1, keepdims=True)
    scaled = (result * share).astype(BF)
    grad_act = mxu(weighted, wd_ref[...], ((1,), (1,)))
    grad_gate = (grad_act * up_pre * sigma * (1.0 + gate_pre * (1.0 - sigma))).astype(BF)
    grad_up = (grad_act * silu).astype(BF)
    dg_all[place, :] = grad_gate
    du_all[place, :] = grad_up
    back = mxu(grad_gate, wg_ref[...], ((1,), (1,))) + mxu(grad_up, wu_ref[...], ((1,), (1,)))
    back = back.astype(BF)

    @pl.when(own)
    def _():
        yo_ref[...] = scaled
        bo_ref[...] = back

    @pl.when(jnp.logical_not(own))
    def _():
        yp_ref[...] = scaled
        bp_ref[...] = back

    for n in range(places):
        column = dots[n * SLOTS : (n + 1) * SLOTS]
        dots_ref[step // half_steps, first_place + n] = jnp.sum(
            jnp.where(diagonal, column, 0.0), axis=0, keepdims=True
        )

    @pl.when(step == 2 * half_steps - 1)
    def _():
        quarter = D // n_dp
        hidden = a_all.shape[1]

        def of_rows(q, carry):
            columns = pl.ds(pl.multiple_of(q * quarter, 128), quarter)
            stores = []
            for n, (grads, out_ref) in enumerate(((dg_all, gate_ref), (du_all, up_ref))):
                stage[n] = mxu(x_all[:, columns], grads[...], ((0,), (0,))).astype(BF)
                stores.append(pltpu.make_async_copy(stage.at[n], out_ref.at[z_index ^ q], store_sems.at[n]))
                stores[-1].start()
            for store in stores:
                store.wait()
            return carry

        lax.fori_loop(0, n_dp, of_rows, 0)
        size = hidden // n_dp
        for q in range(0, n_dp, 2):
            made = mxu(a_all[:, q * size : (q + 2) * size], de_all[...], ((0,), (0,))).astype(BF)
            stores = []
            for half in range(2):
                part = made[half * size : (half + 1) * size]
                stage[half, :size] = part[:, :hidden]
                stage[half, size:] = part[:, hidden:]
                stores.append(
                    pltpu.make_async_copy(
                        stage.at[half], down_ref.at[z_index ^ (q + half)], store_sems.at[half]
                    )
                )
                stores[-1].start()
            for store in stores:
                store.wait()
        for _, finish in exchanges:
            finish()
        for move in moves:
            move.wait()


def run_expert(name, which, number, rows, cots, gates, pieces, carried, riders):
    half_rows = rows[0].shape[0]
    half_steps = 4
    step_rows = half_rows // half_steps
    plane = carried[0].shape[0]
    n_dp = lax.axis_size("dp")
    hidden = picked_shape(*pieces[0])[1]
    own_map = lambda j: (jnp.minimum(j, half_steps - 1), 0)
    par_map = lambda j: (jnp.maximum(j - half_steps, 0), 0)
    anywhere = pl.BlockSpec(memory_space=pl.ANY)

    def pair(width):
        return [pl.BlockSpec((step_rows, width), own_map), pl.BlockSpec((step_rows, width), par_map)]

    shape = jax.ShapeDtypeStruct
    share = shape((n_dp, D // n_dp, hidden), BF)
    dma = pltpu.SemaphoreType.DMA
    all_rows = 2 * half_rows
    results = pl.pallas_call(
        functools.partial(
            expert_kernel,
            plane,
            n_dp,
            half_steps,
            which,
            len(carried),
            [index for _, index in pieces],
            [(index, flip) for _, index, flip in riders],
        ),
        grid=(2 * half_steps,),
        in_specs=pair(D)
        + pair(D)
        + [pl.BlockSpec(gates.shape, lambda j: (0, 0, 0))]
        + [anywhere] * (len(pieces) + len(carried) + len(riders)),
        out_specs=pair(D)
        + pair(D)
        + [pl.BlockSpec((2, plane, 1, 128), lambda j: (0, 0, 0, 0))]
        + [anywhere] * (3 + len(carried) + len(riders)),
        out_shape=[shape((half_rows, D), BF)] * 4
        + [shape((2, plane, 1, 128), F32)]
        + [share] * 3
        + [shape(array.shape, BF) for array in carried]
        + [shape(picked_shape(array, index), BF) for array, index, _ in riders],
        scratch_shapes=[
            pltpu.VMEM((D, hidden), BF),
            pltpu.VMEM((D, hidden), BF),
            pltpu.VMEM((hidden, D), BF),
            pltpu.VMEM((all_rows, D), BF),
            pltpu.VMEM((all_rows, D), BF),
            pltpu.VMEM((all_rows, hidden), BF),
            pltpu.VMEM((all_rows, hidden), BF),
            pltpu.VMEM((all_rows, hidden), BF),
            pltpu.VMEM((2, D // n_dp, hidden), BF),
            pltpu.VMEM((len(carried), SLOTS, D), BF),
            dma((len(pieces),)),
            dma((2,)),
            dma((len(carried),)),
            dma((len(carried), plane)),
            dma((len(carried), plane)),
            dma((len(riders),)),
            dma((len(riders),)),
        ],
        compiler_params=pltpu.CompilerParams(
            vmem_limit_bytes=56 * 1024 * 1024, collective_id=number, has_side_effects=True
        ),
        name=name,
    )(*rows, *cots, gates, *[a for a, _ in pieces], *carried, *[a for a, _, _ in riders])
    last = 8 + len(carried)
    return results[:4], results[4], results[5:8], results[8:last], results[last:]


def plane_peer(index):
    n_context = lax.axis_size("context")
    return {"expert": index // n_context, "context": index % n_context}


def plane_here():
    return lax.axis_index("expert") * lax.axis_size("context") + lax.axis_index("context")


def greet(peers):
    barrier = pltpu.get_barrier_semaphore()
    for peer in peers:
        pl.semaphore_signal(barrier, inc=1, device_id=peer, device_id_type=MESH_ID)
    pl.semaphore_wait(barrier, len(peers))


def remote(source, target, send, receive, peer):
    return pltpu.make_async_remote_copy(
        src_ref=source,
        dst_ref=target,
        send_sem=send,
        recv_sem=receive,
        device_id=peer,
        device_id_type=MESH_ID,
    )


def cast_halves(source_ref, halves_ref, loaded, made, load_sems, store_sems):
    rows, experts, width = source_ref.shape
    mine = experts // lax.axis_size("context")
    group = 8
    first = lax.axis_index("context") * mine
    start = pl.multiple_of(first // group * group, group)
    step = loaded.shape[1] * loaded.shape[3] // width
    lower = lax.rem(first, group) == 0
    even = lax.rem(lax.axis_index("dp"), 2) == 0
    steps = rows // step

    def load(n):
        slot = lax.rem(n, 2)
        block = source_ref.at[pl.ds(pl.multiple_of(n * step, step), step), pl.ds(start, group), :]
        return pltpu.make_async_copy(block, loaded.at[slot], load_sems.at[slot])

    def store(n, half):
        slot = lax.rem(n, 2)
        block = halves_ref.at[half, :, pl.ds(pl.multiple_of(n * step, step), step), :]
        return pltpu.make_async_copy(made.at[slot, half], block, store_sems.at[slot, half])

    load(0).start()

    def body(n, carry):
        @pl.when(n + 1 < steps)
        def _():
            load(n + 1).start()

        load(n).wait()

        @pl.when(n >= 2)
        def _():
            for half in range(2):
                store(n - 2, half).wait()

        slot = lax.rem(n, 2)
        block = loaded[slot]
        kept = jnp.where(lower, block[:, :mine, :], block[:, group - mine :, :])
        by_expert = jnp.swapaxes(kept, 0, 1).astype(BF)
        low, high = by_expert[: mine // 2], by_expert[mine // 2 :]
        made[slot, 0] = jnp.where(even, low, high)
        made[slot, 1] = jnp.where(even, high, low)
        for half in range(2):
            store(n, half).start()
        return carry

    lax.fori_loop(0, steps, body, 0)
    for n in (steps - 2, steps - 1):
        for half in range(2):
            store(n, half).wait()


def rank_tables(routes, plane, row_ref, column_ref):
    tokens = routes.shape[1]
    expert = lax.broadcasted_iota(jnp.int32, (EXPERTS, tokens), 0)
    named = jnp.zeros((EXPERTS, tokens), F32)
    for k in range(TOP):
        named = named + jnp.where(routes[k : k + 1, :] == expert, 1.0, 0.0)
    before = lax.broadcasted_iota(jnp.int32, (tokens, tokens), 0) < lax.broadcasted_iota(
        jnp.int32, (tokens, tokens), 1
    )
    count = mxu(named.astype(BF), jnp.where(before, 1.0, 0.0).astype(BF))
    ranks = jnp.where(named > 0, count, -1.0)
    low = ranks.astype(BF)
    owned = EXPERTS // plane
    parity = lax.rem(lax.axis_index("dp"), 2)
    for i in range(2):
        place = lax.broadcasted_iota(jnp.int32, (plane, EXPERTS), 0) * owned + parity * 2 + i
        column = lax.broadcasted_iota(jnp.int32, (plane, EXPERTS), 1)
        chosen = jnp.where(place == column, 1.0, 0.0).astype(BF)
        row_ref[i] = mxu(chosen, low).astype(BF)
        column_ref[i] = mxu(low, chosen, ((0,), (1,))).astype(BF)
    one = lax.broadcasted_iota(jnp.int32, (EXPERTS, EXPERTS), 0) == lax.broadcasted_iota(
        jnp.int32, (EXPERTS, EXPERTS), 1
    )
    return mxu(low, jnp.where(one, 1.0, 0.0).astype(BF), ((0,), (0,)))


def gather_kernel(
    n_dp,
    plane,
    routes_ref,
    in_ref,
    out_ref,
    gate_ref,
    up_ref,
    down_ref,
    cot_ref,
    ranks_ref,
    own_row_ref,
    own_column_ref,
    partner_row_ref,
    partner_column_ref,
    whole_in_ref,
    whole_out_ref,
    gate_halves_ref,
    up_halves_ref,
    down_halves_ref,
    cot_partner_ref,
    gate_piece_ref,
    partner_routes,
    loaded,
    made,
    loaded_wide,
    made_wide,
    load_sems,
    store_sems,
    local_sems,
    z_send,
    sends,
    recvs,
    route_sems,
):
    here = plane_here()
    z_index = lax.axis_index("dp")
    parts, wholes = (in_ref, out_ref), (whole_in_ref, whole_out_ref)
    z_peer = lambda flip: {"dp": z_index ^ flip}
    greet([z_peer(flip) for flip in range(1, n_dp)] + [plane_peer(here ^ flip) for flip in (1, 2, 4)])
    routing = remote(routes_ref, partner_routes, route_sems.at[0], route_sems.at[1], z_peer(1))
    routing.start()
    keep = [
        pltpu.make_async_copy(part, whole.at[z_index, here], local_sems.at[a])
        for a, (part, whole) in enumerate(zip(parts, wholes))
    ]
    for copy in keep:
        copy.start()
    started = []
    for a in range(2):
        for flip in range(1, n_dp):
            started.append(
                remote(
                    parts[a],
                    wholes[a].at[z_index, here],
                    z_send.at[a, flip],
                    recvs.at[a, z_index, here],
                    z_peer(flip),
                )
            )
            started[-1].start()

    half = cot_partner_ref.shape[0]
    cot_pair = remote(
        cot_ref.at[pl.ds(0, half)], cot_partner_ref, route_sems.at[2], route_sems.at[3], z_peer(1)
    )
    cot_pair.start()

    def pass_on(a, lane, flip, z_from, place, source=None):
        block = wholes[a].at[z_from, place]
        move = remote(
            block if source is None else source,
            block,
            sends.at[a, lane, z_from, place],
            recvs.at[a, z_from, place],
            plane_peer(here ^ flip),
        )
        move.start()
        started.append(move)

    def landed(a, z_from, place):
        block = wholes[a].at[z_from, place]
        remote(block, block, z_send.at[a, 0], recvs.at[a, z_from, place], z_peer(1)).wait_recv()

    froms = [z_index ^ flip for flip in range(n_dp)]
    for a in range(2):
        for lane, flip in enumerate((2, 4, 1)):
            pass_on(a, lane, flip, z_index, here, parts[a])
    ranks_ref[...] = rank_tables(routes_ref[...], plane, own_row_ref, own_column_ref)
    cast_halves(gate_ref, gate_halves_ref, loaded, made, load_sems, store_sems)
    gate_move = remote(
        gate_halves_ref.at[0, 0], gate_piece_ref, route_sems.at[4], route_sems.at[5], z_peer(2)
    )
    gate_move.start()
    for a in range(2):
        for z_from in froms[1:]:
            landed(a, z_from, here)
            for lane, flip in enumerate((2, 4, 1)):
                pass_on(a, lane, flip, z_from, here)
    cast_halves(up_ref, up_halves_ref, loaded, made, load_sems, store_sems)
    for a in range(2):
        for n, z_from in enumerate(froms):
            landed(a, z_from, here ^ 2)
            if n % 2 == 1:
                pass_on(a, 1, 4, z_from, here ^ 2)
            pass_on(a, 2, 1, z_from, here ^ 2)
            landed(a, z_from, here ^ 4)
            if n % 2 == 0:
                pass_on(a, 0, 2, z_from, here ^ 4)
            pass_on(a, 2, 1, z_from, here ^ 4)
    routing.wait()
    rank_tables(partner_routes[...], plane, partner_row_ref, partner_column_ref)
    cast_halves(down_ref, down_halves_ref, loaded_wide, made_wide, load_sems, store_sems)
    for a in range(2):
        for z_from in froms:
            landed(a, z_from, here ^ 6)
            pass_on(a, 2, 1, z_from, here ^ 6)
    for a in range(2):
        for place in (1, 3, 5, 7):
            for z_from in froms:
                landed(a, z_from, here ^ place)
    for move in started:
        move.wait_send()
    for copy in keep:
        copy.wait()
    cot_pair.wait()
    gate_move.wait()


def gather_parts(routes, part_in, part_out, weights, cot, n_dp, n_context, plane):
    tokens = routes.shape[1]
    vmem = pl.BlockSpec(memory_space=pltpu.VMEM)
    anywhere = pl.BlockSpec(memory_space=pl.ANY)
    shape = jax.ShapeDtypeStruct
    dma = pltpu.SemaphoreType.DMA
    row, column = shape((2, plane, tokens), BF), shape((2, tokens, plane), BF)
    mine = weights[0].shape[1] // n_context
    rows, width = 64, weights[0].shape[2]
    return pl.pallas_call(
        functools.partial(gather_kernel, n_dp, plane),
        in_specs=[vmem] + [anywhere] * 6,
        out_specs=[vmem] * 5 + [anywhere] * 7,
        out_shape=[shape((tokens, EXPERTS), F32), row, column, row, column]
        + [shape((n_dp, plane) + part.shape, BF) for part in (part_in, part_out)]
        + [shape((2, mine // 2, w.shape[0], w.shape[2]), BF) for w in weights]
        + [shape((tokens // 2, D), BF), shape(weights[0].shape[::2], BF)],
        scratch_shapes=[
            pltpu.VMEM(routes.shape, routes.dtype),
            pltpu.VMEM((2, rows, 8, width), F32),
            pltpu.VMEM((2, 2, mine // 2, rows, width), BF),
            pltpu.VMEM((2, rows // 2, 8, 2 * width), F32),
            pltpu.VMEM((2, 2, mine // 2, rows // 2, 2 * width), BF),
            dma((2,)),
            dma((2, 2)),
            dma((2,)),
            dma((2, n_dp)),
            dma((2, 3, n_dp, plane)),
            dma((2, n_dp, plane)),
            dma((6,)),
        ],
        compiler_params=pltpu.CompilerParams(
            vmem_limit_bytes=60 * 1024 * 1024, collective_id=3, has_side_effects=True
        ),
        name="gather_parts",
    )(routes, part_in, part_out, *weights, cot)


def front_kernel(n_dp, prompt_len, riders, *refs):
    (x_ref, cos_ref, sin_ref, w_in_ref, w_out_ref, cot_ref), refs = refs[:6], refs[6:]
    sources, refs = refs[: len(riders)], refs[len(riders) :]
    (gains_ref, log_ref, logits_ref), refs = refs[:3], refs[3:]
    saved, (mid_ref, cot_partner_ref), refs = refs[:5], refs[5:7], refs[7:]
    targets, refs = refs[: len(riders)], refs[len(riders) :]
    (
        normed_one_ref,
        qkv_ref,
        kv_ref,
        attended_ref,
        normed_two_ref,
        save_sems,
        columns_buf,
        small,
        w_out,
        mid_block,
        load_sems,
        column_sems,
        pair_sems,
        kv_send,
        kv_recv,
        ride_send,
        ride_recv,
    ) = refs
    block_index = lax.axis_index("context")
    n_context = prompt_len // PBLK
    tokens = x_ref.shape[0]
    width = qkv_ref.shape[1]
    greet([context_peer(flip) for flip in range(1, n_context)] + dp_peers(n_dp))
    held = (normed_one_ref, qkv_ref, kv_ref, attended_ref, normed_two_ref)
    saves = [pltpu.make_async_copy(buf, out, save_sems.at[n]) for n, (buf, out) in enumerate(zip(held, saved))]
    load_small = pltpu.make_async_copy(w_in_ref.at[:, pl.ds(width, 128)], small, load_sems.at[0])
    load_out = pltpu.make_async_copy(w_out_ref, w_out, load_sems.at[1])
    step_width = columns_buf.shape[2]
    steps = width // step_width
    kv_steps = (width - D) // step_width

    def place_of(n):
        return lax.rem(n + steps - kv_steps, steps)

    def load_columns(n):
        slot = lax.rem(n, 2)
        start = pl.multiple_of(place_of(n) * step_width, step_width)
        return pltpu.make_async_copy(
            w_in_ref.at[:, pl.ds(start, step_width)], columns_buf.at[slot], column_sems.at[slot]
        )

    load_small.start()
    load_columns(0).start()
    load_out.start()
    rest = cot_partner_ref.shape[0]
    pair = remote(
        cot_ref.at[pl.ds(tokens - rest, rest)],
        cot_partner_ref,
        pair_sems.at[0],
        pair_sems.at[1],
        {"dp": lax.axis_index("dp") ^ 1},
    )
    pair.start()
    moves = dp_moves(sources, targets, riders, ride_send, ride_recv)
    for move in moves:
        move.start()
    load_small.wait()
    picked = lax.broadcasted_iota(jnp.int32, (8, 128), 1) - lax.broadcasted_iota(jnp.int32, (8, 128), 0)
    gains_ref[...] = mxu(jnp.where(picked == EXPERTS, 1.0, 0.0).astype(BF), small[...], ((1,), (1,)))

    def normed(rows, gain):
        scale = lax.rsqrt(jnp.mean(rows * rows, axis=-1, keepdims=True) + epsilon)
        return (rows * scale * gain).astype(BF)

    def block_rows(n):
        return pl.ds(pl.multiple_of(n * PBLK, PBLK), PBLK)

    def first_norm(n, carry):
        rows = block_rows(n)
        normed_one_ref[rows, :] = normed(x_ref[rows, :].astype(F32), gains_ref[0:1, :])
        return carry

    lax.fori_loop(0, tokens // PBLK, first_norm, 0)

    def project(n, carry):
        @pl.when(n + 1 < steps)
        def _():
            load_columns(n + 1).start()

        load_columns(n).wait()
        place = place_of(n)
        product = mxu(normed_one_ref[...], columns_buf[lax.rem(n, 2)])
        is_value = place == steps - kv_steps // 2
        cosine = jnp.where(is_value, 1.0, cos_ref[...])
        sine = jnp.where(is_value, 0.0, sin_ref[...])
        factor = jnp.where(place < steps - kv_steps, 1.0 / math.sqrt(HD), 1.0)
        for half in range(step_width // HD):
            part = product[:, half * HD : (half + 1) * HD]
            start = pl.multiple_of(place * step_width + half * HD, HD)
            qkv_ref[:, pl.ds(start, HD)] = (turn(part, cosine, sine) * factor).astype(BF)
        return carry

    lax.fori_loop(0, kv_steps, project, 0)
    own_keys = pl.ds(pl.multiple_of(block_index * PBLK, PBLK), PBLK)
    kv_ref[own_keys, :] = qkv_ref[:PBLK, D:]
    kv_ref[prompt_len:, :] = qkv_ref[PBLK:, D:]
    kv_moves = [
        remote(
            kv_ref.at[own_keys],
            kv_ref.at[own_keys],
            kv_send.at[flip],
            kv_recv.at[flip],
            context_peer(flip),
        )
        for flip in range(1, n_context)
    ]
    for move in kv_moves:
        move.start()
    lax.fori_loop(kv_steps, steps, project, 0)
    for move in kv_moves:
        move.wait()
    for save in saves[:3]:
        save.start()
    log_ref[...] = jnp.zeros_like(log_ref)

    def through_head(head, carry):
        columns = pl.ds(pl.multiple_of(head * HD, HD), HD)
        group = head // (HEADS // KVH)
        key_columns = pl.ds(pl.multiple_of(group * HD, HD), HD)
        value_columns = pl.ds(pl.multiple_of(KVH * HD + group * HD, HD), HD)
        for first_row, keys in row_blocks(prompt_len):
            rows = slice(first_row, first_row + PBLK)
            scores = mxu(qkv_ref[rows, columns], kv_ref[:keys, key_columns], ((1,), (1,)))
            scores = masked_scores(scores, first_row, block_index)
            top = jnp.max(scores, axis=-1, keepdims=True)
            unnormed = jnp.exp(scores - top)
            total = jnp.sum(unnormed, axis=-1, keepdims=True)
            mixed = mxu(unnormed.astype(BF), kv_ref[:keys, value_columns]) / total
            attended_ref[rows, columns] = mixed.astype(BF)
            lane = lax.broadcasted_iota(jnp.int32, (PBLK, log_ref.shape[1]), 1)
            log_ref[rows, :] = jnp.where(lane == head, top + jnp.log(total), log_ref[rows, :])
        return carry

    lax.fori_loop(0, HEADS, through_head, 0)
    saves[3].start()
    load_out.wait()

    def second_norm(n, carry):
        rows = block_rows(n)
        mid = x_ref[rows, :].astype(F32) + mxu(attended_ref[rows, :], w_out[...])
        mid_block[...] = mid
        store = pltpu.make_async_copy(mid_block, mid_ref.at[rows], load_sems.at[2])
        store.start()
        low = normed(mid, gains_ref[1:2, :])
        normed_two_ref[rows, :] = low
        logits_ref[rows, :] = mxu(low, small[...])
        store.wait()
        return carry

    lax.fori_loop(0, tokens // PBLK, second_norm, 0)
    saves[4].start()
    pair.wait()
    for move in moves:
        move.wait()
    for save in saves:
        save.wait()


def front(prompt_len, n_dp, x_low, cosine, sine, w_in, w_out, cot, riders):
    tokens = x_low.shape[0]
    width = D + 2 * KVH * HD
    key_rows = prompt_len + CONT
    n_context = prompt_len // PBLK
    vmem = pl.BlockSpec(memory_space=pltpu.VMEM)
    anywhere = pl.BlockSpec(memory_space=pl.ANY)
    shape = jax.ShapeDtypeStruct
    dma = pltpu.SemaphoreType.DMA
    return pl.pallas_call(
        functools.partial(front_kernel, n_dp, prompt_len, [(index, flip) for _, index, flip in riders]),
        in_specs=[vmem] * 3 + [anywhere] * (3 + len(riders)),
        out_specs=[vmem] * 3 + [anywhere] * (7 + len(riders)),
        out_shape=[
            shape((8, D), F32),
            shape((tokens, 128), F32),
            shape((tokens, 128), F32),
            shape((tokens, D), BF),
            shape((tokens, width), BF),
            shape((key_rows, 2 * KVH * HD), BF),
            shape((tokens, D), BF),
            shape((tokens, D), BF),
            shape((tokens, D), F32),
            shape((tokens // 2, D), BF),
        ]
        + [shape(picked_shape(array, index), BF) for array, index, _ in riders],
        scratch_shapes=[
            pltpu.VMEM((tokens, D), BF),
            pltpu.VMEM((tokens, width), BF),
            pltpu.VMEM((key_rows, 2 * KVH * HD), BF),
            pltpu.VMEM((tokens, D), BF),
            pltpu.VMEM((tokens, D), BF),
            dma((5,)),
            pltpu.VMEM((2, D, 2 * HD), BF),
            pltpu.VMEM((D, 128), BF),
            pltpu.VMEM((D, D), BF),
            pltpu.VMEM((PBLK, D), F32),
            dma((3,)),
            dma((2,)),
            dma((2,)),
            dma((n_context,)),
            dma((n_context,)),
            dma((len(riders),)),
            dma((len(riders),)),
        ],
        compiler_params=pltpu.CompilerParams(
            vmem_limit_bytes=56 * 1024 * 1024, collective_id=8, has_side_effects=True
        ),
        name="front",
    )(x_low, cosine, sine, w_in, w_out, cot, *[array for array, _, _ in riders])


def dispatch_kernel(plane, n_dp, riders, *refs):
    normed_ref, cot_ref, own_rank_ref, partner_rank_ref, logits_ref, ranks_ref = refs[:6]
    cot_halves, refs = refs[6:8], refs[8:]
    sources, refs = refs[: len(riders)], refs[len(riders) :]
    gates_ref, gates_here_ref, refs = refs[0], refs[1], refs[2:]
    landed, staged, targets = refs[:4], refs[4:8], refs[8 : 8 + len(riders)]
    (
        stage,
        normed_partner,
        pair_sems,
        stage_sems,
        local_sems,
        send_sems,
        recv_sems,
        ride_send,
        ride_recv,
        all_gates,
        other_gates,
        partner_gates,
        gate_sems,
        gate_send,
        gate_recv,
        cot_partner,
        cot_sems,
    ) = refs[8 + len(riders) :]
    here = plane_here()
    greet([plane_peer(here ^ flip) for flip in range(1, plane)] + dp_peers(n_dp))
    partner = {"dp": lax.axis_index("dp") ^ 1}
    gate_pair = remote(other_gates, partner_gates, gate_sems.at[0], gate_sems.at[1], partner)
    pair = remote(normed_ref, normed_partner, pair_sems.at[0], pair_sems.at[1], partner)
    pair.start()
    moves = dp_moves(sources, targets, riders, ride_send, ride_recv)
    first = cot_halves[0].shape[0]
    places = (pl.ds(0, first), pl.ds(first, cot_halves[1].shape[0]))
    cot_loads = [
        pltpu.make_async_copy(part, cot_partner.at[place], cot_sems.at[n])
        for n, (part, place) in enumerate(zip(cot_halves, places))
    ]
    for load in cot_loads:
        load.start()
    plans = (
        (0, normed_ref, own_rank_ref),
        (1, cot_ref, own_rank_ref),
        (2, cot_partner, partner_rank_ref),
        (3, normed_partner, partner_rank_ref),
    )
    exchanges = [
        plane_exchange(n, stage.at[n], landed[n], local_sems, send_sems, recv_sems) for n in range(4)
    ]
    copies = [pltpu.make_async_copy(stage.at[4 + n], staged[n], stage_sems.at[n]) for n in range(4)]

    def slot_gates():
        ranks = ranks_ref[...]
        parity = lax.rem(lax.axis_index("dp"), 2)
        named = ranks >= 0
        logits = jnp.where(named, logits_ref[:, :EXPERTS], masked_score)
        top = jnp.max(logits, axis=-1, keepdims=True)
        raised = jnp.where(named, jnp.exp(logits - top), 0.0)
        gates = raised / jnp.sum(raised, axis=-1, keepdims=True)
        gates_ref[...] = gates
        slot = lax.broadcasted_iota(jnp.int32, (ranks.shape[0], 128), 1).astype(F32)
        owned = EXPERTS // plane
        for place in range(plane):
            for i in range(2):
                rows = []
                for expert in (place * owned + i, place * owned + 2 + i):
                    hit = ranks[:, expert : expert + 1] == slot
                    rows.append(
                        jnp.sum(jnp.where(hit, gates[:, expert : expert + 1], 0.0), axis=0, keepdims=True)
                    )
                all_gates[place, i : i + 1, :] = jnp.where(parity == 0, rows[0], rows[1])
                other_gates[place, i : i + 1, :] = jnp.where(parity == 0, rows[1], rows[0])

    for expert in range(2):
        for n, rows_ref, rank_ref in plans:
            if expert == 0 and n == 2:
                for load in cot_loads:
                    load.wait()
            if expert == 0 and n == 3:
                for move in moves[:DISPATCH_FIRST]:
                    move.start()
                slot_gates()
                gate_pair.start()
                pair.wait()
                for move in moves[DISPATCH_FIRST:]:
                    move.start()
            chooser = slot_matrix(rank_ref[expert], plane, True)
            stage[4 * expert + n] = mxu(chooser, rows_ref[...]).astype(BF).reshape(plane, SLOTS, D)
            if expert == 0:
                exchanges[n][0]()
            else:
                copies[n].start()
    gate_pair.wait()
    all_gates[:, 2:4, :] = partner_gates[...]
    gates_here_ref[here] = all_gates[here]
    gate_moves = [
        remote(
            all_gates.at[here ^ flip],
            gates_here_ref.at[here],
            gate_send.at[flip],
            gate_recv.at[flip],
            plane_peer(here ^ flip),
        )
        for flip in range(1, plane)
    ]
    for move in gate_moves:
        move.start()
    for copy in copies:
        copy.wait()
    for _, finish in exchanges:
        finish()
    for move in gate_moves + moves:
        move.wait()


def dispatch_rows(normed, cot, cot_halves, own_ranks, partner_ranks, logits, ranks, riders, n_dp):
    plane, tokens = own_ranks.shape[1:]
    vmem = pl.BlockSpec(memory_space=pltpu.VMEM)
    anywhere = pl.BlockSpec(memory_space=pl.ANY)
    shape = jax.ShapeDtypeStruct
    dma = pltpu.SemaphoreType.DMA
    results = pl.pallas_call(
        functools.partial(dispatch_kernel, plane, n_dp, [(index, flip) for _, index, flip in riders]),
        in_specs=[vmem] * 6 + [anywhere] * (2 + len(riders)),
        out_specs=[vmem] * 2 + [anywhere] * (8 + len(riders)),
        out_shape=[shape(ranks.shape, F32), shape((plane, 4, 128), F32)]
        + [shape((plane, SLOTS, D), BF)] * 8
        + [shape(picked_shape(array, index), BF) for array, index, _ in riders],
        scratch_shapes=[
            pltpu.VMEM((8, plane, SLOTS, D), BF),
            pltpu.VMEM((tokens, D), BF),
            dma((2,)),
            dma((4,)),
            dma((4,)),
            dma((4, plane)),
            dma((4, plane)),
            dma((len(riders),)),
            dma((len(riders),)),
            pltpu.VMEM((plane, 4, 128), F32),
            pltpu.VMEM((plane, 2, 128), F32),
            pltpu.VMEM((plane, 2, 128), F32),
            dma((2,)),
            dma((plane,)),
            dma((plane,)),
            pltpu.VMEM((tokens, D), BF),
            dma((2,)),
        ],
        compiler_params=pltpu.CompilerParams(
            vmem_limit_bytes=56 * 1024 * 1024, collective_id=1, has_side_effects=True
        ),
        cost_estimate=pl.CostEstimate(flops=2 * 10**10, bytes_accessed=4 * 10**8, transcendentals=0),
        name="dispatch_rows",
    )(
        normed, cot, own_ranks, partner_ranks, logits, ranks, *cot_halves, *[a for a, _, _ in riders]
    )
    return results[0], results[1], results[2:6], results[6:10], results[10:]


def sum_matrix(which, sources, summed, sums, part_ref, piece_sems, sum_sems):
    copies = [pltpu.make_async_copy(source, summed.at[n], piece_sems.at[n]) for n, source in enumerate(sources)]
    for copy in copies:
        copy.start()
    for copy in copies:
        copy.wait()
    parity = lax.rem(lax.axis_index("dp"), 2)
    stores = []
    for side in range(2):
        total = summed[side].astype(F32)
        for n in range(side + 2, len(sources), 2):
            total = total + summed[n].astype(F32)
        sums[side] = total.astype(BF)
        place = parity if side == 0 else 1 - parity
        stores.append(pltpu.make_async_copy(sums.at[side], part_ref.at[place, which], sum_sems.at[side]))
        stores[-1].start()
    for store in stores:
        store.wait()


def return_kernel(
    plane,
    n_dp,
    n_results,
    riders,
    names,
    own_rank_ref,
    partner_rank_ref,
    first_dots_ref,
    second_dots_ref,
    ranks_ref,
    gates_ref,
    *refs,
):
    early, back = refs[0:2], refs[2:4]
    results, refs = refs[4 : 4 + n_results], refs[4 + n_results :]
    sources, refs = refs[: len(riders)], refs[len(riders) :]
    mine, refs = refs[:3], refs[3:]
    arrived, refs = refs[: len(HOME_SECOND)], refs[len(HOME_SECOND) :]
    total_ref, dlog_ref, part_ref = refs[:3]
    results_back, refs = refs[3 : 3 + n_results], refs[3 + n_results :]
    targets = refs[: len(riders)]
    homes = dict(zip(HOME_SECOND, arrived))
    homes.update(zip(names, targets))
    (
        held,
        to_partner,
        of_partner,
        load_sems,
        pair_sems,
        local_sems,
        send_sems,
        recv_sems,
        ride_send,
        ride_recv,
        dot_sems,
        dot_send,
        dot_recv,
        dots_ref,
        dots_here_ref,
        dots_other_ref,
        bounce,
        summed,
        sums,
        partial,
        piece_sems,
        sum_sems,
    ) = refs[len(riders) :]
    here = plane_here()
    partner = {"dp": lax.axis_index("dp") ^ 1}
    greet([plane_peer(here ^ flip) for flip in range(1, plane)] + dp_peers(n_dp))
    for n, by_side in enumerate((first_dots_ref, second_dots_ref)):
        for side in range(2):
            dots_ref[:, 2 * side + n : 2 * side + n + 1, :] = by_side[side]
    own_dots = pltpu.make_async_copy(dots_ref.at[here], dots_here_ref.at[here], dot_sems.at[0])
    own_dots.start()
    dot_moves = [
        remote(
            dots_ref.at[here ^ flip],
            dots_here_ref.at[here],
            dot_send.at[flip],
            dot_recv.at[flip],
            plane_peer(here ^ flip),
        )
        for flip in range(1, plane)
    ]
    for move in dot_moves:
        move.start()
    loads, exchanges = {}, {}
    for side in (1, 0):
        loads[side] = pltpu.make_async_copy(early[side], held.at[2 * side], load_sems.at[side])
        loads[side].start()
        exchanges[side] = plane_exchange(
            side, back[side], held.at[2 * side + 1], local_sems, send_sems, recv_sems
        )
    exchanges[1][0]()
    later = [
        plane_exchange(2 + n, results[n], results_back[n], local_sems, send_sems, recv_sems, bounce)
        for n in range(n_results)
    ]
    moves = dp_moves(sources, targets, riders, ride_send, ride_recv)
    own_dots.wait()
    for move in dot_moves:
        move.wait()
    dots_pair = remote(dots_here_ref, dots_other_ref, dot_sems.at[1], dot_sems.at[2], partner)
    dots_pair.start()

    def of_gates():
        tokens = ranks_ref.shape[0]
        parity = lax.rem(lax.axis_index("dp"), 2)
        owned = EXPERTS // plane
        slot = lax.broadcasted_iota(jnp.int32, (tokens, 128), 1).astype(F32)
        lane = lax.broadcasted_iota(jnp.int32, (tokens, EXPERTS), 1)
        made = jnp.zeros((tokens, EXPERTS), F32)
        for expert in range(EXPERTS):
            place, side, i = expert // owned, expert % owned // 2, expert % 2
            row = jnp.where(
                parity == side,
                dots_here_ref[place, i : i + 1, :],
                dots_other_ref[place, 2 + i : 3 + i, :],
            )
            hit = ranks_ref[:, expert : expert + 1] == slot
            value = jnp.sum(jnp.where(hit, row, 0.0), axis=-1, keepdims=True)
            made = jnp.where(lane == expert, value, made)
        gates = gates_ref[...]
        mean = jnp.sum(gates * made, axis=-1, keepdims=True)
        dlog_ref[...] = jnp.zeros_like(dlog_ref)
        dlog_ref[:, :EXPERTS] = (gates * (made - mean)).astype(BF)

    def sum_of(which):
        sources = [mine[which].at[0]] + [homes[which, flip, 0] for flip in range(1, n_dp)]
        sum_matrix(which, sources, summed, sums, part_ref, piece_sems, sum_sems)

    blocks = [slice(start, start + PBLK) for start in range(0, total_ref.shape[0], PBLK)]

    def collected(rank_ref, rows, side, expert):
        chooser = slot_matrix(rank_ref[expert, rows, :], plane, False)
        return mxu(chooser, held[2 * side + expert].reshape(plane * SLOTS, D))

    for move in moves[:RETURN_FIRST]:
        move.start()
    loads[1].wait()
    for rows in blocks:
        partial[rows, :] = collected(partner_rank_ref, rows, 1, 0)
    loads[0].wait()
    for rows in blocks:
        total_ref[rows, :] = collected(own_rank_ref, rows, 0, 0)
    sum_of(0)
    sum_of(1)
    exchanges[1][1]()
    exchanges[0][0]()
    pairs = []
    for n, rows in enumerate(blocks):
        to_partner[rows, :] = (partial[rows, :] + collected(partner_rank_ref, rows, 1, 1)).astype(BF)
        block = pl.ds(n * PBLK, PBLK)
        pairs.append(
            remote(to_partner.at[block], of_partner.at[block], pair_sems.at[0, n], pair_sems.at[1, n], partner)
        )
        pairs[-1].start()
    for move in moves[RETURN_FIRST:]:
        move.start()
    for begin, _ in later:
        begin()
    dots_pair.wait()
    of_gates()
    for move in moves[:RETURN_FIRST]:
        move.wait()
    sum_of(2)
    exchanges[0][1]()
    for rows in blocks:
        total_ref[rows, :] += collected(own_rank_ref, rows, 0, 1)
    for pair, rows in zip(pairs, blocks):
        pair.wait()
        total_ref[rows, :] += of_partner[rows, :].astype(F32)
    for move in moves[RETURN_FIRST:]:
        move.wait()
    for _, finish in later:
        finish()


def return_rows(
    own_ranks, partner_ranks, first_dots, second_dots, ranks, gates, early, back, results, riders, names, shares, arrived, n_dp
):
    tokens, plane = own_ranks.shape[1:]
    vmem = pl.BlockSpec(memory_space=pltpu.VMEM)
    anywhere = pl.BlockSpec(memory_space=pl.ANY)
    shape = jax.ShapeDtypeStruct
    dma = pltpu.SemaphoreType.DMA
    outcome = pl.pallas_call(
        functools.partial(
            return_kernel, plane, n_dp, len(results), [(index, flip) for _, index, flip in riders], names
        ),
        in_specs=[vmem] * 6 + [anywhere] * (7 + len(results) + len(riders) + len(arrived)),
        out_specs=[vmem] * 2 + [anywhere] * (1 + len(results) + len(riders)),
        out_shape=[shape((tokens, D), F32), shape((tokens, 128), BF), shape((2, 3) + shares[0].shape[1:], BF)]
        + [shape(rows.shape, BF) for rows in results]
        + [shape(picked_shape(array, index), BF) for array, index, _ in riders],
        scratch_shapes=[
            pltpu.VMEM((4, plane, SLOTS, D), BF),
            pltpu.VMEM((tokens, D), BF),
            pltpu.VMEM((tokens, D), BF),
            dma((2,)),
            dma((2, tokens // PBLK)),
            dma((4,)),
            dma((4, plane)),
            dma((4, plane)),
            dma((len(riders),)),
            dma((len(riders),)),
            dma((3,)),
            dma((plane,)),
            dma((plane,)),
            pltpu.VMEM((plane, 4, 128), F32),
            pltpu.VMEM((plane, 4, 128), F32),
            pltpu.VMEM((plane, 4, 128), F32),
            pltpu.VMEM((2 + len(results), SLOTS, D), BF),
            pltpu.VMEM(shares[0].shape, BF),
            pltpu.VMEM((2,) + shares[0].shape[1:], BF),
            pltpu.VMEM((tokens, D), F32),
            dma((n_dp,)),
            dma((2,)),
        ],
        compiler_params=pltpu.CompilerParams(
            vmem_limit_bytes=56 * 1024 * 1024, collective_id=2, has_side_effects=True
        ),
        cost_estimate=pl.CostEstimate(flops=3 * 10**10, bytes_accessed=4 * 10**8, transcendentals=0),
        name="return_rows",
    )(
        own_ranks,
        partner_ranks,
        first_dots,
        second_dots,
        ranks,
        gates,
        *early,
        *back,
        *results,
        *[array for array, _, _ in riders],
        *shares,
        *arrived,
    )
    last = 3 + len(results)
    return outcome[0], outcome[1], outcome[2], outcome[3:last], outcome[last:]


def normed_back(rows, gain, grads):
    scale = lax.rsqrt(jnp.mean(rows * rows, axis=-1, keepdims=True) + epsilon)
    weighted = grads * gain
    mean = jnp.mean(rows * weighted, axis=-1, keepdims=True)
    return scale * weighted - rows * (scale * scale * scale * mean), rows * scale * grads


def context_peer(flip):
    return {"context": lax.axis_index("context") ^ flip}


def share_context(part, place_of, sends, recvs):
    here = lax.axis_index("context")
    across = remote(part, place_of(here), sends.at[0], recvs.at[here], context_peer(2))
    beside = remote(part, place_of(here), sends.at[1], recvs.at[here], context_peer(1))
    block = place_of(here ^ 2)
    onward = remote(block, block, sends.at[2], recvs.at[here ^ 2], context_peer(1))

    def begin():
        across.start()
        beside.start()

    def pass_on():
        remote(part, block, sends.at[0], recvs.at[here ^ 2], context_peer(2)).wait_recv()
        onward.start()

    def finish():
        for flip in (1, 3):
            remote(part, place_of(here ^ flip), sends.at[1], recvs.at[here ^ flip], context_peer(1)).wait_recv()
        across.wait_send()
        beside.wait_send()
        onward.wait_send()

    return begin, pass_on, finish


def backward_kernel(n_dp, prompt_len, n_results, riders, *refs):
    (dlog_ref, gains_in_ref, log_ref, cos_ref, sin_ref), kept, refs = refs[:5], refs[5:11], refs[11:]
    (mid_ref, total_ref, w_out_ref, w_in_ref, normed_two_ref, part_ref), refs = refs[:6], refs[6:]
    results, refs = refs[:n_results], refs[n_results:]
    late = len(riders)
    sources, refs = refs[:late], refs[late:]
    grad_x_ref, grad_out_ref, grad_in_ref, grad_small_ref, all_ref = refs[:5]
    results_back, refs = refs[5 : 5 + n_results], refs[5 + n_results :]
    homes, refs = refs[:late], refs[late:]
    (
        weights,
        grad_mid,
        grad_attn,
        mid_block,
        grad_qkv,
        grad_kv,
        kv_send,
        kv_recv,
        stage,
        load_sems,
        store_sems,
        kv_send_sems,
        kv_recv_sems,
        home_send,
        home_recv,
        share_sends,
        share_recvs,
        small,
        gains_ref,
        bounce,
        local_sems,
        send_sems,
        recv_sems,
        cot_ref,
        qkv_ref,
        kv_ref,
        attended_ref,
        normed_ref,
        x_ref,
        kept_sems,
        mid_sems,
    ) = refs
    block_index = lax.axis_index("context")
    n_context = kv_send.shape[0]
    tokens = x_ref.shape[0]
    heads_width = HEADS * HD
    kv_width = KVH * HD
    here = plane_here()
    plane = results[0].shape[0]
    greet([plane_peer(here ^ flip) for flip in range(1, plane)] + dp_peers(n_dp))
    load_small = pltpu.make_async_copy(
        w_in_ref.at[:, pl.ds(weights.shape[1], 128)], small, load_sems.at[4]
    )
    load_small.start()
    buffers = (cot_ref, qkv_ref, kv_ref, attended_ref, normed_ref, x_ref)
    kept_loads = [
        pltpu.make_async_copy(source, buf, kept_sems.at[n]) for n, (source, buf) in enumerate(zip(kept, buffers))
    ]
    load_total = pltpu.make_async_copy(total_ref, grad_mid, load_sems.at[0])
    load_out = pltpu.make_async_copy(w_out_ref, weights.at[:, pl.ds(0, D)], load_sems.at[1])
    load_in = pltpu.make_async_copy(w_in_ref.at[:, pl.ds(0, weights.shape[1])], weights, load_sems.at[2])
    load_total.start()
    load_out.start()
    for load in kept_loads:
        load.start()
    homing = dp_moves(sources, homes, riders, home_send, home_recv)
    for move in homing:
        move.start()
    begin_all, pass_on, finish = share_context(
        part_ref, lambda place: all_ref.at[place], share_sends, share_recvs
    )
    begin_all()
    exchanges = [
        plane_exchange(side, results[side], results_back[side], local_sems, send_sems, recv_sems, bounce)
        for side in range(n_results)
    ]
    load_small.wait()
    load_total.wait()
    load_out.wait()
    gains_ref[...] = jnp.zeros_like(gains_ref)
    kept_loads[0].wait()

    def load_mid(n):
        slot = lax.rem(n, 2)
        block = mid_ref.at[pl.ds(pl.multiple_of(n * PBLK, PBLK), PBLK)]
        return pltpu.make_async_copy(block, mid_block.at[slot], mid_sems.at[slot])

    load_mid(0).start()

    def block_rows(n):
        return pl.ds(pl.multiple_of(n * PBLK, PBLK), PBLK)

    def through_norm(n, carry):
        rows = block_rows(n)

        @pl.when(n + 1 < tokens // PBLK)
        def _():
            load_mid(n + 1).start()

        load_mid(n).wait()
        grads = grad_mid[rows, :] + mxu(dlog_ref[rows, :], small[...], ((1,), (1,)))
        by_rows, by_gain = normed_back(mid_block[lax.rem(n, 2)], gains_in_ref[1:2, :], grads)
        gains_ref[1:2, :] += jnp.sum(by_gain, axis=0, keepdims=True)
        by_mid = cot_ref[rows, :].astype(F32) + by_rows
        grad_mid[rows, :] = by_mid
        low = by_mid.astype(BF)
        grad_attn[rows, :] = low
        grad_qkv[rows, :D] = mxu(low, weights[:, :D], ((1,), (1,))).astype(BF)
        return carry

    lax.fori_loop(0, tokens // PBLK, through_norm, 0)
    load_in.start()
    for load in kept_loads[1:3]:
        load.wait()
    grad_kv[...] = jnp.zeros_like(grad_kv)

    def through_head(head, carry):
        columns = pl.ds(pl.multiple_of(head * HD, HD), HD)
        group = head // (HEADS // KVH)
        key_columns = pl.ds(pl.multiple_of(group * HD, HD), HD)
        value_columns = pl.ds(pl.multiple_of(kv_width + group * HD, HD), HD)
        for first_row, keys in row_blocks(prompt_len):
            rows = slice(first_row, first_row + PBLK)
            queries, grads = qkv_ref[rows, columns], grad_qkv[rows, columns]
            scores = mxu(queries, kv_ref[:keys, key_columns], ((1,), (1,)))
            scores = masked_scores(scores, first_row, block_index)
            lane = lax.broadcasted_iota(jnp.int32, (PBLK, log_ref.shape[1]), 1)
            logs = jnp.sum(jnp.where(lane == head, log_ref[rows, :], 0.0), axis=-1, keepdims=True)
            probs = jnp.exp(scores - logs)
            grad_probs = mxu(grads, kv_ref[:keys, value_columns], ((1,), (1,)))
            dots = jnp.sum(probs * grad_probs, axis=-1, keepdims=True)
            grad_scores = (probs * (grad_probs - dots)).astype(BF)
            grad_query = mxu(grad_scores, kv_ref[:keys, key_columns])
            grad_query = turn(grad_query, cos_ref[rows, :], -sin_ref[rows, :]) * (1.0 / math.sqrt(HD))
            grad_qkv[rows, columns] = grad_query.astype(BF)
            grad_kv[:keys, key_columns] += mxu(grad_scores, queries, ((0,), (0,)))
            grad_kv[:keys, value_columns] += mxu(probs.astype(BF), grads, ((0,), (0,)))
        return carry

    lax.fori_loop(0, HEADS, through_head, 0)

    for place in range(n_context):
        kv_send[place] = grad_kv[place * PBLK : (place + 1) * PBLK, :].astype(BF)
    kv_moves = [
        remote(
            kv_send.at[block_index ^ flip],
            kv_recv.at[flip],
            kv_send_sems.at[flip],
            kv_recv_sems.at[flip],
            context_peer(flip),
        )
        for flip in range(1, n_context)
    ]
    for move in kv_moves:
        move.start()
    for begin, _ in exchanges:
        begin()

    quarter = D // n_dp

    def quarter_rows(q):
        return pl.ds(pl.multiple_of(q * quarter, 128), quarter)

    def store_of(q, out_ref, width):
        slot = lax.rem(q, 2)
        return pltpu.make_async_copy(
            stage.at[slot, :, pl.ds(0, width)], out_ref.at[quarter_rows(q)], store_sems.at[slot]
        )

    def share_of_out(q, carry):
        made = mxu(attended_ref[:, quarter_rows(q)], grad_attn[...], ((0,), (0,)))

        @pl.when(q >= 2)
        def _():
            store_of(q - 2, grad_out_ref, D).wait()

        stage[lax.rem(q, 2), :, :D] = made.astype(BF)
        store_of(q, grad_out_ref, D).start()
        return carry

    kept_loads[3].wait()
    lax.fori_loop(0, n_dp, share_of_out, 0)
    for q in (n_dp - 2, n_dp - 1):
        store_of(q, grad_out_ref, D).wait()
    load_normed = pltpu.make_async_copy(normed_two_ref, grad_attn, load_sems.at[0])
    load_normed.start()

    for move in kv_moves:
        move.wait()
    own_rows = pl.ds(pl.multiple_of(block_index * PBLK, PBLK), PBLK)
    summed = grad_kv[own_rows, :]
    for flip in range(1, n_context):
        summed = summed + kv_recv[flip].astype(F32)
    pieces = [(0, PBLK, summed), (PBLK, tokens, grad_kv[prompt_len:, :])]
    for first, last, made in pieces:
        for group in range(KVH):
            turned = turn(
                made[:, group * HD : (group + 1) * HD], cos_ref[first:last, :], -sin_ref[first:last, :]
            )
            start = heads_width + group * HD
            grad_qkv[first:last, start : start + HD] = turned.astype(BF)
        grad_qkv[first:last, heads_width + kv_width :] = made[:, kv_width:].astype(BF)

    load_in.wait()

    width = weights.shape[1]

    def share_of_in(q, carry):
        made = mxu(normed_ref[:, quarter_rows(q)], grad_qkv[...], ((0,), (0,)))

        @pl.when(q >= 2)
        def _():
            store_of(q - 2, grad_in_ref, width).wait()

        stage[lax.rem(q, 2)] = made.astype(BF)
        store_of(q, grad_in_ref, width).start()
        return carry

    kept_loads[4].wait()
    lax.fori_loop(0, n_dp, share_of_in, 0)
    kept_loads[5].wait()

    def through_first(n, carry):
        rows = block_rows(n)
        grads = mxu(grad_qkv[rows, :], weights[...], ((1,), (1,)))
        by_rows, by_gain = normed_back(x_ref[rows, :].astype(F32), gains_in_ref[0:1, :], grads)
        gains_ref[0:1, :] += jnp.sum(by_gain, axis=0, keepdims=True)
        grad_x_ref[rows, :] = (grad_mid[rows, :] + by_rows).astype(BF)
        return carry

    pass_on()
    lax.fori_loop(0, tokens // PBLK, through_first, 0)
    for q in (n_dp - 2, n_dp - 1):
        store_of(q, grad_in_ref, width).wait()
    load_normed.wait()
    lane = lax.broadcasted_iota(jnp.int32, (8, 128), 1)
    column = lax.broadcasted_iota(jnp.int32, (8, 128), 0) + EXPERTS
    place = jnp.where((lane == column) & (column < EXPERTS + 2), 1.0, 0.0).astype(BF)
    of_router = mxu(grad_attn[...], dlog_ref[...], ((0,), (0,)))
    small[...] = (of_router + mxu(gains_ref[...].astype(BF), place, ((0,), (0,)))).astype(BF)
    store_small = pltpu.make_async_copy(small, grad_small_ref, store_sems.at[0])
    store_small.start()
    finish()
    store_small.wait()
    for _, end in exchanges:
        end()
    for move in homing:
        move.wait()


def backward(prompt_len, n_dp, in_vmem, in_hbm, results, riders):
    tokens = in_vmem[0].shape[0]
    width = D + 2 * KVH * HD
    n_context = prompt_len // PBLK
    key_rows = prompt_len + CONT
    quarter = D // n_dp
    vmem = pl.BlockSpec(memory_space=pltpu.VMEM)
    anywhere = pl.BlockSpec(memory_space=pl.ANY)
    part = in_hbm[-1]
    plane = results[0].shape[0]
    shape = jax.ShapeDtypeStruct
    return pl.pallas_call(
        functools.partial(
            backward_kernel, n_dp, prompt_len, len(results), [(index, flip) for _, index, flip in riders]
        ),
        in_specs=[vmem] * len(in_vmem) + [anywhere] * (len(in_hbm) + len(results) + len(riders)),
        out_specs=[vmem] + [anywhere] * (4 + len(results) + len(riders)),
        out_shape=[
            shape((tokens, D), BF),
            shape((D, D), BF),
            shape((D, width), BF),
            shape((D, 128), BF),
            shape((n_context,) + part.shape, BF),
        ]
        + [shape(rows.shape, BF) for rows in results]
        + [shape(picked_shape(array, index), BF) for array, index, _ in riders],
        scratch_shapes=[
            pltpu.VMEM((D, width), BF),
            pltpu.VMEM((tokens, D), F32),
            pltpu.VMEM((tokens, D), BF),
            pltpu.VMEM((2, PBLK, D), F32),
            pltpu.VMEM((tokens, width), BF),
            pltpu.VMEM((key_rows, 2 * KVH * HD), F32),
            pltpu.VMEM((n_context, PBLK, 2 * KVH * HD), BF),
            pltpu.VMEM((n_context, PBLK, 2 * KVH * HD), BF),
            pltpu.VMEM((2, quarter, width), BF),
            pltpu.SemaphoreType.DMA((5,)),
            pltpu.SemaphoreType.DMA((2,)),
            pltpu.SemaphoreType.DMA((n_context,)),
            pltpu.SemaphoreType.DMA((n_context,)),
            pltpu.SemaphoreType.DMA((len(riders),)),
            pltpu.SemaphoreType.DMA((len(riders),)),
            pltpu.SemaphoreType.DMA((3,)),
            pltpu.SemaphoreType.DMA((n_context,)),
            pltpu.VMEM((D, 128), BF),
            pltpu.VMEM((8, D), F32),
            pltpu.VMEM((len(results), SLOTS, D), BF),
            pltpu.SemaphoreType.DMA((len(results),)),
            pltpu.SemaphoreType.DMA((len(results), plane)),
            pltpu.SemaphoreType.DMA((len(results), plane)),
            *[pltpu.VMEM(array.shape, BF) for array in in_hbm[:6]],
            pltpu.SemaphoreType.DMA((6,)),
            pltpu.SemaphoreType.DMA((2,)),
        ],
        compiler_params=pltpu.CompilerParams(
            vmem_limit_bytes=56 * 1024 * 1024, collective_id=4, has_side_effects=True
        ),
        name="backward",
    )(*in_vmem, *in_hbm, *results, *[array for array, _, _ in riders])


def reduce_kernel(n_dp, widths, *refs):
    count = len(widths)
    shares, refs = refs[:count], refs[count:]
    own_rank_ref, partner_rank_ref, mid_ref = refs[:3]
    rows_of, mine, refs = (refs[3:5], refs[5:7]), refs[7:10], refs[10:]
    names = HOME_RETURN[RETURN_FIRST:] + HOME_BACKWARD
    homes, refs = dict(zip(names, refs)), refs[len(names) :]
    totals, refs = refs[:count], refs[count:]
    result_ref, all_ref, part_ref = refs[:3]
    refs = refs[3:]
    sums, core_in, first_in, second_in, z_in = (refs[n * count : (n + 1) * count] for n in range(5))
    (
        load_sems,
        core_send,
        core_recv,
        first_send,
        first_recv,
        second_send,
        second_recv,
        z_send,
        z_recv,
        out_send,
        out_recv,
        share_sends,
        share_recvs,
        pair_sems,
        held,
        to_partner,
        of_partner,
        mixed,
        mid_block,
        held_sems,
        summed,
        matrix_sums,
        piece_sems,
        sum_sems,
    ) = refs[5 * count :]
    here = plane_here()
    plane = held.shape[1]
    z_index = lax.axis_index("dp")
    greet(
        [plane_peer(here ^ flip) for flip in (1, 2, 4)] + [{"dp": z_index ^ flip} for flip in range(1, n_dp)]
    )
    chips = (0, 2, 4, 6)
    order = list(range(1, n_dp)) + [0]
    loads, core_moves = {}, {}
    for n in order:
        z_to = z_index ^ n
        for a in range(count):
            for m, chip in enumerate(chips):
                loads[n, a, m] = pltpu.make_async_copy(
                    shares[a].at[z_to, here ^ chip], sums[a].at[n, m], load_sems.at[a, n, m]
                )
                loads[n, a, m].start()
                core_moves[n, a, m] = remote(
                    shares[a].at[z_to, here ^ 1 ^ chip],
                    core_in[a].at[n, m],
                    core_send.at[a, n, m],
                    core_recv.at[a, n, m],
                    plane_peer(here ^ 1),
                )
                core_moves[n, a, m].start()

    def load_rows(side):
        copies = [
            pltpu.make_async_copy(rows_of[side][expert], held.at[expert], held_sems.at[expert])
            for expert in range(2)
        ]
        for copy in copies:
            copy.start()
        return copies

    rows_here = load_rows(1)
    gathers = [
        share_context(
            part_ref.at[:, m],
            lambda place, m=m: all_ref.at[place, :, m],
            share_sends.at[m],
            share_recvs.at[m],
        )
        for m in range(2)
    ]

    def sum_of(which):
        sources = [mine[which].at[0]] + [homes[which, flip, 1] for flip in range(1, n_dp)]
        sum_matrix(which, sources, summed, matrix_sums, part_ref, piece_sems, sum_sems)

    sum_of(0)
    gathers[0][0]()

    def add(target, *others):
        total = target[...].astype(F32)
        for other in others:
            total = total + other[...].astype(F32)
        target[...] = total.astype(BF)

    first_moves, second_moves, z_moves = {}, {}, {}
    for n in order:
        toward = 2 if n % 2 == 0 else 4
        kept = 6 - toward
        for a in range(count):
            for m in range(4):
                loads[n, a, m].wait()
                core_moves[n, a, m].wait_recv()
                add(sums[a].at[n, m], core_in[a].at[n, m])
            for slot, chip in enumerate((toward, 6)):
                first_moves[n, a, slot] = remote(
                    sums[a].at[n, chip // 2],
                    first_in[a].at[n, slot],
                    first_send.at[a, n, slot],
                    first_recv.at[a, n, slot],
                    plane_peer(here ^ toward),
                )
                first_moves[n, a, slot].start()
    for copy in rows_here:
        copy.wait()
    collect_into(plane, partner_rank_ref, held, 0, to_partner, lambda rows, made: made.astype(BF))
    pair = remote(to_partner, of_partner, pair_sems.at[0], pair_sems.at[1], {"dp": z_index ^ 1})
    pair.start()
    rows_here = load_rows(0)
    sum_of(1)
    for n in order:
        toward = 2 if n % 2 == 0 else 4
        kept = 6 - toward
        for a in range(count):
            for slot, chip in enumerate((0, kept)):
                first_moves[n, a, slot].wait_recv()
                add(sums[a].at[n, chip // 2], first_in[a].at[n, slot])
            second_moves[n, a] = remote(
                sums[a].at[n, kept // 2],
                second_in[a].at[n],
                second_send.at[a, n],
                second_recv.at[a, n],
                plane_peer(here ^ kept),
            )
            second_moves[n, a].start()
    gathers[1][0]()

    def with_mid(rows, made):
        load = pltpu.make_async_copy(mid_ref.at[rows], mid_block, held_sems.at[2])
        load.start()
        load.wait()
        return mid_block[...] + made

    for copy in rows_here:
        copy.wait()
    collect_into(plane, own_rank_ref, held, 0, mixed, with_mid)
    sum_of(2)
    gathers[0][1]()
    for n in order:
        for a in range(count):
            second_moves[n, a].wait_recv()
            add(sums[a].at[n, 0], second_in[a].at[n])
            if n > 0:
                z_moves[n, a] = remote(
                    sums[a].at[n, 0], z_in[a].at[n], z_send.at[a, n], z_recv.at[a, n], {"dp": z_index ^ n}
                )
                z_moves[n, a].start()
    started = list(core_moves.values()) + list(first_moves.values())
    started += list(second_moves.values()) + list(z_moves.values())

    def pass_on(a, lane, flip, place):
        block = totals[a].at[place]
        move = remote(
            block, block, out_send.at[a, lane, place], out_recv.at[a, place], plane_peer(here ^ flip)
        )
        move.start()
        started.append(move)

    def landed(a, place):
        block = totals[a].at[place]
        remote(block, block, out_send.at[a, 0, place], out_recv.at[a, place], plane_peer(here ^ 1)).wait_recv()

    for a in range(count):
        for n in range(1, n_dp):
            z_moves[n, a].wait_recv()
        add(sums[a].at[0, 0], *[z_in[a].at[n] for n in range(1, n_dp)])
        totals[a][here] = sums[a][0, 0]
        for lane, flip in enumerate((2, 4, 1)):
            pass_on(a, lane, flip, here)
    for a in range(count):
        landed(a, here ^ 2)
        if a % 2 == 1:
            pass_on(a, 1, 4, here ^ 2)
        pass_on(a, 2, 1, here ^ 2)
        landed(a, here ^ 4)
        if a % 2 == 0:
            pass_on(a, 0, 2, here ^ 4)
        pass_on(a, 2, 1, here ^ 4)
    for a in range(count):
        landed(a, here ^ 6)
        pass_on(a, 2, 1, here ^ 6)
    gathers[1][1]()
    pair.wait()
    result_ref[...] = (mixed[...] + of_partner[...].astype(F32)).astype(BF)
    for a in range(count):
        for flip in (1, 3, 5, 7):
            landed(a, here ^ flip)
    for move in started:
        move.wait_send()
    for _, _, finish in gathers:
        finish()


def reduce_shares(shares, ranks, mid, slot_rows, mine, homes, n_dp, n_context):
    plane, rows = shares[0].shape[1:3]
    widths = tuple(share.shape[3] for share in shares)
    count = len(widths)
    vmem = pl.BlockSpec(memory_space=pltpu.VMEM)
    anywhere = pl.BlockSpec(memory_space=pl.ANY)
    shape = jax.ShapeDtypeStruct
    dma = pltpu.SemaphoreType.DMA

    def buffers(*lead):
        return [pltpu.VMEM(lead + (rows, width), BF) for width in widths]

    return pl.pallas_call(
        functools.partial(reduce_kernel, n_dp, widths),
        in_specs=[anywhere] * count + [vmem] * 2 + [anywhere] * (8 + len(homes)),
        out_specs=[vmem] * (count + 1) + [anywhere] * 2,
        out_shape=[shape((plane, rows, width), BF) for width in widths]
        + [
            shape(mid.shape, BF),
            shape((n_context, 2, 2) + homes[0].shape, BF),
            shape((2, 3) + homes[0].shape, BF),
        ],
        scratch_shapes=buffers(n_dp, 4)
        + buffers(n_dp, 4)
        + buffers(n_dp, 2)
        + buffers(n_dp)
        + buffers(n_dp)
        + [
            dma((count, n_dp, 4)),
            dma((count, n_dp, 4)),
            dma((count, n_dp, 4)),
            dma((count, n_dp, 2)),
            dma((count, n_dp, 2)),
            dma((count, n_dp)),
            dma((count, n_dp)),
            dma((count, n_dp)),
            dma((count, n_dp)),
            dma((count, 3, plane)),
            dma((count, plane)),
            dma((2, 3)),
            dma((2, n_context)),
            dma((2,)),
            pltpu.VMEM((2, plane, SLOTS, D), BF),
            pltpu.VMEM(mid.shape, BF),
            pltpu.VMEM(mid.shape, BF),
            pltpu.VMEM(mid.shape, F32),
            pltpu.VMEM((PBLK, D), F32),
            dma((3,)),
            pltpu.VMEM((n_dp,) + homes[0].shape, BF),
            pltpu.VMEM((2,) + homes[0].shape, BF),
            dma((n_dp,)),
            dma((2,)),
        ],
        compiler_params=pltpu.CompilerParams(
            vmem_limit_bytes=56 * 1024 * 1024, collective_id=5, has_side_effects=True
        ),
        name="reduce_shares",
    )(*shares, *ranks, mid, *slot_rows[0], *slot_rows[1], *mine, *homes)


def finish_kernel(n_context, apart, halves, *refs):
    (first_ref, own_first_ref), out_ref = refs[:2], refs[-1]
    seconds = refs[2:-1]
    step, experts, _ = out_ref.shape
    here = lax.axis_index("context")
    group = 16
    size = group * experts
    log_group, log_experts = group.bit_length() - 1, experts.bit_length() - 1
    to = lax.broadcasted_iota(jnp.int32, (size, size), 0)
    of = lax.broadcasted_iota(jnp.int32, (size, size), 1)
    same_row = (to >> log_experts) == (of & (group - 1))
    same_expert = (to & (experts - 1)) == (of >> log_group)
    turned = jnp.where(same_row & same_expert, 1.0, 0.0).astype(BF)

    def gathered(all_ref, own_ref, place, side, at):
        return jnp.where(here == place, own_ref[(side, 0) + at], all_ref[(place, side, 0) + at])

    def by_distance(place, side, at):
        value = seconds[0][(side, 0) + at]
        for flip in range(1, n_context):
            value = jnp.where((here ^ place) == flip, seconds[flip][(side, 0) + at], value)
        return value

    width = out_ref.shape[2] // halves
    for half in range(halves):
        at_half = (half,) if halves > 1 else ()
        for start in range(0, step, group):
            at = at_half + (slice(start, start + group),)
            rows = []
            for place in range(n_context):
                for side in range(2):
                    rows.append(gathered(first_ref, own_first_ref, place, side, at))
                    if apart:
                        rows.append(by_distance(place, side, at))
                    else:
                        rows.append(gathered(seconds[0], seconds[1], place, side, at))
            made = mxu(turned, jnp.concatenate(rows, axis=0))
            out_ref[start : start + group, :, half * width : (half + 1) * width] = made.reshape(
                group, experts, width
            )


def finish_weight(which, first, own_first, seconds):
    n_context, _, _, rows, width = first.shape
    experts = n_context * 4
    step = 32 if which == 2 else 64
    apart = len(seconds) == n_context
    halves = 2 if which == 2 else 1
    rows, wide = rows // halves, width * halves
    parts = [first, own_first, *seconds]
    specs = []
    for n, part in enumerate(parts):
        lead = part.shape[:-3]
        matrix = 0 if part.shape[-3] == 1 else which
        if halves > 1:
            parts[n] = part.reshape(part.shape[:-2] + (halves, rows, width))
            block = lead + (1, halves, step, width)
            specs.append(pl.BlockSpec(block, lambda j, k=len(lead), m=matrix: (0,) * k + (m, 0, j, 0)))
        else:
            block = lead + (1, step, width)
            specs.append(pl.BlockSpec(block, lambda j, k=len(lead), m=matrix: (0,) * k + (m, j, 0)))
    return pl.pallas_call(
        functools.partial(finish_kernel, n_context, apart, halves),
        grid=(rows // step,),
        in_specs=specs,
        out_specs=pl.BlockSpec((step, experts, wide), lambda j: (j, 0, 0)),
        out_shape=jax.ShapeDtypeStruct((rows, experts, wide), F32),
        compiler_params=grant(),
        cost_estimate=pl.CostEstimate(flops=2 * 10**9, bytes_accessed=30 * 10**6, transcendentals=0),
        name="finish_weight",
    )(*parts)


def flip_permute(value, axis, size, flip):
    return lax.ppermute(value, axis, [(i, i ^ flip) for i in range(size)])


def local_paired(
    inputs,
    cotangent,
    routes,
    attn_q,
    attn_k,
    attn_v,
    attn_o,
    norm_attn,
    norm_moe,
    router,
    expert_gate,
    expert_up,
    expert_down,
):
    n_context, n_expert, n_dp = lax.axis_size("context"), lax.axis_size("expert"), lax.axis_size("dp")
    plane = n_context * n_expert
    tokens = inputs.shape[1]
    block_index = lax.axis_index("context")
    z_index = lax.axis_index("dp")
    parity = z_index % 2
    prompt_len = PBLK * n_context
    x_low = inputs[0]
    cot_low = cotangent[0]
    route_rows = routes[0]

    here = lax.axis_index("expert") * n_context + block_index
    part_rows = attn_q.shape[0] // plane

    def part_of(shard):
        return lax.dynamic_slice_in_dim(shard, here * part_rows, part_rows, 0).astype(BF)

    part_in = jnp.concatenate(
        [part_of(attn_q), part_of(attn_k), part_of(attn_v), part_of(router)]
        + [part_of(norm_attn)[:, None], part_of(norm_moe)[:, None]]
        + [jnp.zeros((part_rows, 128 - EXPERTS - 2), BF)],
        axis=1,
    )
    qkv_width = D + 2 * KVH * HD
    weights = (expert_gate, expert_up, expert_down)
    own_ranks, own_rows, own_columns, partner_rows, partner_columns, whole_in, w_out, *weight_halves = (
        gather_parts(route_rows.T, part_in, part_of(attn_o), weights, cot_low, n_dp, n_context, plane)
    )
    gate_piece = weight_halves.pop()
    partner_cot = [weight_halves.pop()]
    whole_in = whole_in.reshape(-1, part_in.shape[1])
    w_out = w_out.reshape(-1, D)
    pieces = {(which, 0, i): (weight_halves[which], (0, i)) for which in range(3) for i in range(2)}
    pieces[0, 2, 0] = (gate_piece, None)

    def riding(names):
        return [
            (weight_halves[which], (flip % 2, i), flip) for which, flip, i in names
        ]

    def pieces_of(expert):
        return [pieces[which, flip, expert] for which in range(3) for flip in range(n_dp)]

    positions = jnp.concatenate(
        [
            block_index * PBLK + jnp.arange(PBLK, dtype=jnp.int32),
            prompt_len + jnp.arange(CONT, dtype=jnp.int32),
        ]
    )
    angles = angle_table(positions)
    cos_half, sin_half = jnp.cos(angles), jnp.sin(angles)
    cosine = jnp.concatenate([cos_half, cos_half], axis=1)
    sine = jnp.concatenate([-sin_half, sin_half], axis=1)
    gains, logs, logits, normed_one, qkv, keys_values, attended, normed_two, mid_rows, cot_half, *moved = (
        front(prompt_len, n_dp, x_low, cosine, sine, whole_in, w_out, cot_low, riding(RIDE_FRONT))
    )
    partner_cot.append(cot_half)
    pieces.update({name: (piece, None) for name, piece in zip(RIDE_FRONT, moved)})

    gates, gates_here, landed, staged, arrived = dispatch_rows(
        normed_two, cot_low, partner_cot, own_rows, partner_rows, logits, own_ranks, riding(RIDE_DISPATCH), n_dp
    )
    pieces.update({name: (piece, None) for name, piece in zip(RIDE_DISPATCH, arrived)})

    def slots_of(arrays):
        flat = [array.reshape(plane * SLOTS, D) for array in arrays]
        return (flat[0], flat[3]), (flat[1], flat[2])

    parted = lambda arrays: [array.reshape(plane, SLOTS, D) for array in arrays]
    rows, cots = slots_of(landed)
    first, first_dots, first_shares, landed, arrived = run_expert(
        "first_expert", 0, 6, rows, cots, gates_here, pieces_of(0), staged, riding(RIDE_FIRST)
    )
    pieces.update({name: (piece, None) for name, piece in zip(RIDE_FIRST, arrived)})
    rows, cots = slots_of(landed)

    def homing(names, *shares):
        return [(shares[i][which], flip, flip) for which, flip, i in names]

    second, second_dots, second_shares, early, homes = run_expert(
        "second_expert",
        1,
        7,
        rows,
        cots,
        gates_here,
        pieces_of(1),
        parted(first)[1:4],
        homing(HOME_SECOND, first_shares),
    )

    second = parted(second)
    grad_rows, grad_logits, part_first, late, homes_second = return_rows(
        own_columns,
        partner_columns,
        first_dots,
        second_dots,
        own_ranks,
        gates,
        early[1:3],
        second[2:4],
        [parted(first)[0], second[1]],
        homing(HOME_RETURN, first_shares, second_shares),
        HOME_RETURN,
        first_shares,
        homes,
        n_dp,
    )
    grad_inputs, grad_wout, grad_wqkv, grad_small, all_first, *homes = backward(
        prompt_len,
        n_dp,
        (grad_logits, gains, logs, cosine, sine),
        (
            cot_low,
            qkv,
            keys_values,
            attended,
            normed_one,
            x_low,
            mid_rows,
            grad_rows,
            w_out,
            whole_in,
            normed_two,
            part_first,
        ),
        second[0:1],
        homing(HOME_BACKWARD, first_shares, second_shares),
    )
    last, homes = homes[0], list(homes_second[RETURN_FIRST:]) + list(homes[1:])
    out_own, out_partner = [late[0], last], [early[0], late[1]]

    parts = lambda share: share.reshape(n_dp, plane, -1, share.shape[1])
    total_qkv, total_out, total_small, result, all_second, part_second = reduce_shares(
        [parts(grad_wqkv), parts(grad_wout), parts(grad_small)],
        (own_columns, partner_columns),
        mid_rows,
        (out_own, out_partner),
        second_shares,
        homes,
        n_dp,
        n_context,
    )
    own = part_second[:, 2:]
    across = flip_permute(own, "context", n_context, 2)
    beside = flip_permute(own, "context", n_context, 1)
    grad_gate, grad_up = (
        finish_weight(which, all_first, part_first, (all_second, part_second)) for which in range(2)
    )
    across, beside, grad_gate, grad_up = lax.optimization_barrier((across, beside, grad_gate, grad_up))
    apart = (own, beside, across, flip_permute(across, "context", n_context, 1))
    total_qkv = total_qkv.reshape(-1, qkv_width).astype(F32)
    total_out = total_out.reshape(-1, D).astype(F32)
    total_small = total_small.reshape(-1, 128).astype(F32)
    return (
        result[None],
        grad_inputs[None],
        total_qkv[:, :D],
        total_qkv[:, D : D + KVH * HD],
        total_qkv[:, D + KVH * HD :],
        total_out,
        total_small[:, EXPERTS],
        total_small[:, EXPERTS + 1],
        total_small[:, :EXPERTS],
        grad_gate,
        grad_up,
        finish_weight(2, all_first, part_first, apart),
    )


def paired_plan(mesh):
    n_expert, n_context, n_dp = mesh.shape["expert"], mesh.shape["context"], mesh.shape["dp"]
    owners = 2 * n_expert * n_context
    small_axes = all(size & (size - 1) == 0 for size in (n_expert, n_context, n_dp))
    return small_axes and n_dp % 2 == 0 and EXPERTS == 2 * owners


def solution(mesh):
    in_specs = (
        P(("expert", "dp"), "context", None),
        P(("expert", "dp"), "context", None),
        P(("expert", "dp"), "context", None),
        P("dp", None),
        P("dp", None),
        P("dp", None),
        P("dp", None),
        P("dp"),
        P("dp"),
        P("dp", None),
        P("dp", "expert", None),
        P("dp", "expert", None),
        P("dp", "expert", None),
    )
    out_specs = (
        P(("expert", "dp"), "context", None),
        P(("expert", "dp"), "context", None),
        P("dp", None),
        P("dp", None),
        P("dp", None),
        P("dp", None),
        P("dp"),
        P("dp"),
        P("dp", None),
        P("dp", "expert", None),
        P("dp", "expert", None),
        P("dp", "expert", None),
    )
    chosen = local_paired if paired_plan(mesh) else local
    return jax.shard_map(chosen, mesh=mesh, in_specs=in_specs, out_specs=out_specs, check_vma=False)
```

```python
import functools
import math

import jax
import jax.numpy as jnp
from jax import lax
from jax.experimental import pallas as pl
from jax.experimental.pallas import tpu as pltpu
from jax.sharding import PartitionSpec as P

D = 1536
HEADS = 12
KVH = 2
HD = 128
EXPERTS = 32
TOP = 4
PBLK = 256
CONT = 512
CAP = 103


epsilon = 1e-06
rope_base = 1000000.0
masked_score = -1e30


def rms_scale(values, gain):
    return values * lax.rsqrt(jnp.mean(values * values, axis=-1, keepdims=True) + epsilon) * gain


def angle_table(positions):
    steps_half = jnp.arange(HD // 2, dtype=jnp.float32)
    inverse = jnp.exp(steps_half * (-2.0 * math.log(rope_base) / HD))
    return positions.astype(jnp.float32)[..., None] * inverse


def rotary(values, angles, direction):
    halfway = values.shape[-1] // 2
    cosine = jnp.cos(angles)[..., None, :]
    sine_part = direction * jnp.sin(angles)[..., None, :]
    leading = values[..., :halfway]
    trailing = values[..., halfway:]
    return jnp.concatenate(
        [leading * cosine - trailing * sine_part, trailing * cosine + leading * sine_part], axis=-1
    )


def visible(query_pos, key_pos, prompt_len):
    query_cont = jnp.arange(query_pos.shape[0]) >= PBLK
    key_prompt = jnp.arange(key_pos.shape[0]) < prompt_len
    return (key_pos[None, :] <= query_pos[:, None]) & (key_prompt[None, :] | query_cont[:, None])


def gating(logit_rows, route_rows):
    picker = (route_rows[:, :, None] == jnp.arange(EXPERTS, dtype=jnp.int32)[None, None, :]).astype(
        logit_rows.dtype
    )
    chosen = jnp.sum(picker * logit_rows[:, None, :], axis=-1)
    return jax.nn.softmax(chosen, axis=-1)


def gated(gate_pre, up_pre):
    return jax.nn.silu(gate_pre) * up_pre


def expert_slots(flat_experts):
    picker = (flat_experts[:, None] == jnp.arange(EXPERTS, dtype=jnp.int32)[None, :]).astype(
        jnp.int32
    )
    earlier = jnp.cumsum(picker, axis=0) - picker
    return jnp.sum(earlier * picker, axis=1)


def local(
    inputs,
    cotangent,
    routes,
    attn_q,
    attn_k,
    attn_v,
    attn_o,
    norm_attn,
    norm_moe,
    router,
    expert_gate,
    expert_up,
    expert_down,
):
    low_type = jnp.bfloat16
    full_type = jnp.float32
    w_query, w_key, w_value, w_out, gain_first, gain_second, w_router, w_gate, w_up, w_down = (
        lax.all_gather(attn_q.astype(low_type), "dp", axis=0, tiled=True),
        lax.all_gather(attn_k.astype(low_type), "dp", axis=0, tiled=True),
        lax.all_gather(attn_v.astype(low_type), "dp", axis=0, tiled=True),
        lax.all_gather(attn_o.astype(low_type), "dp", axis=0, tiled=True),
        lax.all_gather(norm_attn.astype(low_type), "dp", axis=0, tiled=True),
        lax.all_gather(norm_moe.astype(low_type), "dp", axis=0, tiled=True),
        lax.all_gather(router.astype(low_type), "dp", axis=0, tiled=True),
        lax.all_gather(expert_gate.astype(low_type), "dp", axis=0, tiled=True),
        lax.all_gather(expert_up.astype(low_type), "dp", axis=0, tiled=True),
        lax.all_gather(expert_down.astype(low_type), "dp", axis=0, tiled=True),
    )
    n_context = lax.axis_size("context")
    n_expert = lax.axis_size("expert")
    block_index = lax.axis_index("context")
    prompt_len = PBLK * n_context
    tokens = inputs.shape[1]
    local_experts = w_gate.shape[1]
    group_width = HEADS // KVH
    score_scale = 1.0 / math.sqrt(HD)
    gain_one = gain_first.astype(full_type)
    gain_two = gain_second.astype(full_type)
    x_rows = inputs[0].astype(full_type)
    positions = jnp.concatenate(
        [
            block_index * PBLK + jnp.arange(PBLK, dtype=jnp.int32),
            prompt_len + jnp.arange(CONT, dtype=jnp.int32),
        ]
    )
    angles = angle_table(positions)
    normed_one = rms_scale(x_rows, gain_one).astype(low_type)
    q_proj = jnp.dot(normed_one, w_query, preferred_element_type=full_type)
    k_proj = jnp.dot(normed_one, w_key, preferred_element_type=full_type)
    v_proj = jnp.dot(normed_one, w_value, preferred_element_type=full_type)
    queries = (rotary(q_proj.reshape(tokens, HEADS, HD), angles, 1.0) * score_scale).astype(
        low_type
    )
    queries = queries.reshape(tokens, KVH, group_width, HD)
    keys_own = rotary(k_proj.reshape(tokens, KVH, HD), angles, 1.0).astype(low_type)
    values_own = v_proj.astype(low_type).reshape(tokens, KVH, HD)
    prompt_keys, prompt_values = (
        lax.all_gather(keys_own[:PBLK], "context", axis=0, tiled=True),
        lax.all_gather(values_own[:PBLK], "context", axis=0, tiled=True),
    )
    all_keys = jnp.concatenate([prompt_keys, keys_own[PBLK:]], axis=0)
    all_values = jnp.concatenate([prompt_values, values_own[PBLK:]], axis=0)
    key_pos = jnp.concatenate(
        [jnp.arange(prompt_len, dtype=jnp.int32), prompt_len + jnp.arange(CONT, dtype=jnp.int32)]
    )
    allowed = visible(positions, key_pos, prompt_len)
    head_outs = []
    log_totals = []
    for kv_head in range(KVH):
        scores = jnp.einsum(
            "tgn,kn->gtk",
            queries[:, kv_head],
            all_keys[:, kv_head],
            preferred_element_type=full_type,
        )
        scores = jnp.where(allowed[None], scores, masked_score)
        top_score = jnp.max(scores, axis=-1, keepdims=True)
        unnormed = jnp.exp(scores - top_score)
        totals = jnp.sum(unnormed, axis=-1, keepdims=True)
        attn_probs = (unnormed / totals).astype(low_type)
        head_outs.append(
            jnp.einsum(
                "gtk,kn->tgn", attn_probs, all_values[:, kv_head], preferred_element_type=full_type
            )
        )
        log_totals.append(top_score + jnp.log(totals))
    attended_low = jnp.stack(head_outs, axis=1).reshape(tokens, D).astype(low_type)
    mid_rows = x_rows + jnp.dot(attended_low, w_out, preferred_element_type=full_type)
    normed_two = rms_scale(mid_rows, gain_two).astype(low_type)
    logits = jnp.dot(normed_two, w_router, preferred_element_type=full_type)
    route_rows = routes[0]
    gate_weights = gating(logits, route_rows)
    flat_experts = route_rows.reshape(-1)
    slot_rank = expert_slots(flat_experts)
    destination = (
        flat_experts % local_experts * n_expert + flat_experts // local_experts
    ) * CAP + slot_rank
    capacity_rows = local_experts * n_expert * CAP
    assignments = tokens * TOP
    source = (
        jnp.full((capacity_rows,), assignments, dtype=jnp.int32)
        .at[destination]
        .set(jnp.arange(assignments, dtype=jnp.int32))
    )
    filled = source < assignments
    source_row = jnp.minimum(source, assignments - 1)
    send_rows = jnp.where(filled[:, None], normed_two[source_row // TOP], jnp.zeros((), low_type))
    received = lax.all_to_all(
        send_rows.reshape(local_experts, n_expert, CAP, D),
        "expert",
        split_axis=1,
        concat_axis=1,
        tiled=True,
    )
    received = received.reshape(local_experts, n_expert * CAP, D)
    gate_pre = jnp.einsum("lrd,dlf->lrf", received, w_gate, preferred_element_type=full_type)
    up_pre = jnp.einsum("lrd,dlf->lrf", received, w_up, preferred_element_type=full_type)
    activation = gated(gate_pre, up_pre).astype(low_type)
    expert_rows = jnp.einsum(
        "lrf,fld->lrd", activation, w_down, preferred_element_type=full_type
    ).astype(low_type)
    returned = lax.all_to_all(
        expert_rows.reshape(local_experts, n_expert, CAP, D),
        "expert",
        split_axis=1,
        concat_axis=1,
        tiled=True,
    )
    returned = returned.reshape(capacity_rows, D)
    picked = returned[destination].reshape(tokens, TOP, D)
    moe_out = jnp.sum(gate_weights[:, :, None] * picked.astype(full_type), axis=1)
    result = (mid_rows + moe_out).astype(low_type)
    grad_out = cotangent[0].astype(full_type)
    slot_grads = (
        (gate_weights[:, :, None] * grad_out[:, None, :]).reshape(assignments, D).astype(low_type)
    )
    send_grads = jnp.where(filled[:, None], slot_grads[source_row], jnp.zeros((), low_type))
    grad_rows = lax.all_to_all(
        send_grads.reshape(local_experts, n_expert, CAP, D),
        "expert",
        split_axis=1,
        concat_axis=1,
        tiled=True,
    )
    grad_rows = grad_rows.reshape(local_experts, n_expert * CAP, D)
    grad_gates = jnp.sum(picked.astype(full_type) * grad_out[:, None, :], axis=-1)
    grad_wdown = jnp.einsum("lrf,lrd->fld", activation, grad_rows, preferred_element_type=full_type)
    grad_act = jnp.einsum("lrd,fld->lrf", grad_rows, w_down, preferred_element_type=full_type)
    primal_gate, gated_back = jax.vjp(gated, gate_pre, up_pre)
    grad_gpre, grad_upre = gated_back(grad_act)
    grad_gpre = grad_gpre.astype(low_type)
    grad_upre = grad_upre.astype(low_type)
    grad_wgate = jnp.einsum("lrd,lrf->dlf", received, grad_gpre, preferred_element_type=full_type)
    grad_wup = jnp.einsum("lrd,lrf->dlf", received, grad_upre, preferred_element_type=full_type)
    grad_recv = jnp.einsum("lrf,dlf->lrd", grad_gpre, w_gate, preferred_element_type=full_type)
    grad_recv = (
        grad_recv + jnp.einsum("lrf,dlf->lrd", grad_upre, w_up, preferred_element_type=full_type)
    ).astype(low_type)
    back_rows = lax.all_to_all(
        grad_recv.reshape(local_experts, n_expert, CAP, D),
        "expert",
        split_axis=1,
        concat_axis=1,
        tiled=True,
    )
    back_rows = back_rows.reshape(capacity_rows, D)
    grad_normed_two = jnp.sum(
        back_rows[destination].reshape(tokens, TOP, D).astype(full_type), axis=1
    )

    def gate_of(logit_rows):
        return gating(logit_rows, route_rows)

    primal_gates, gate_back = jax.vjp(gate_of, logits)
    grad_logits = gate_back(grad_gates)[0].astype(low_type)
    grad_wrouter = jnp.einsum(
        "td,te->de", normed_two, grad_logits, preferred_element_type=full_type
    )
    grad_normed_two = grad_normed_two + jnp.einsum(
        "te,de->td", grad_logits, w_router, preferred_element_type=full_type
    )
    primal_two, norm_back_two = jax.vjp(rms_scale, mid_rows, gain_two)
    grad_mid_norm, grad_gain_two = norm_back_two(grad_normed_two)
    grad_mid = grad_out + grad_mid_norm
    grad_attn = grad_mid.astype(low_type)
    grad_wout = jnp.einsum("td,te->de", attended_low, grad_attn, preferred_element_type=full_type)
    grad_attended = jnp.einsum(
        "te,de->td", grad_attn, w_out, preferred_element_type=full_type
    ).astype(low_type)
    grad_attended = grad_attended.reshape(tokens, KVH, group_width, HD)
    query_grads = []
    key_grads = []
    value_grads = []
    for kv_head in range(KVH):
        scores = jnp.einsum(
            "tgn,kn->gtk",
            queries[:, kv_head],
            all_keys[:, kv_head],
            preferred_element_type=full_type,
        )
        scores = jnp.where(allowed[None], scores, masked_score)
        exact_probs = jnp.exp(scores - log_totals[kv_head])
        grad_probs = jnp.einsum(
            "tgn,kn->gtk",
            grad_attended[:, kv_head],
            all_values[:, kv_head],
            preferred_element_type=full_type,
        )
        row_dots = jnp.sum(exact_probs * grad_probs, axis=-1, keepdims=True)
        grad_scores = (exact_probs * (grad_probs - row_dots)).astype(low_type)
        query_grads.append(
            jnp.einsum(
                "gtk,kn->tgn", grad_scores, all_keys[:, kv_head], preferred_element_type=full_type
            )
        )
        key_grads.append(
            jnp.einsum(
                "gtk,tgn->kn", grad_scores, queries[:, kv_head], preferred_element_type=full_type
            )
        )
        value_grads.append(
            jnp.einsum(
                "gtk,tgn->kn",
                exact_probs.astype(low_type),
                grad_attended[:, kv_head],
                preferred_element_type=full_type,
            )
        )
    grad_queries = jnp.stack(query_grads, axis=1).reshape(tokens, HEADS, HD)
    grad_keys = jnp.stack(key_grads, axis=1)
    grad_values = jnp.stack(value_grads, axis=1)
    prompt_key_grad, prompt_value_grad = (
        lax.psum_scatter(
            grad_keys[:prompt_len].astype(jnp.bfloat16), "context", scatter_dimension=0, tiled=True
        ).astype(jnp.float32),
        lax.psum_scatter(
            grad_values[:prompt_len].astype(jnp.bfloat16),
            "context",
            scatter_dimension=0,
            tiled=True,
        ).astype(jnp.float32),
    )
    own_key_grad = jnp.concatenate([prompt_key_grad, grad_keys[prompt_len:]], axis=0)
    own_value_grad = jnp.concatenate([prompt_value_grad, grad_values[prompt_len:]], axis=0)
    grad_qproj = (
        rotary(grad_queries * score_scale, angles, -1.0).reshape(tokens, D).astype(low_type)
    )
    grad_kproj = rotary(own_key_grad, angles, -1.0).reshape(tokens, KVH * HD).astype(low_type)
    grad_vproj = own_value_grad.reshape(tokens, KVH * HD).astype(low_type)
    grad_wquery = jnp.einsum("td,te->de", normed_one, grad_qproj, preferred_element_type=full_type)
    grad_wkey = jnp.einsum("td,te->de", normed_one, grad_kproj, preferred_element_type=full_type)
    grad_wvalue = jnp.einsum("td,te->de", normed_one, grad_vproj, preferred_element_type=full_type)
    grad_normed_one = jnp.einsum("te,de->td", grad_qproj, w_query, preferred_element_type=full_type)
    grad_normed_one = grad_normed_one + jnp.einsum(
        "te,de->td", grad_kproj, w_key, preferred_element_type=full_type
    )
    grad_normed_one = grad_normed_one + jnp.einsum(
        "te,de->td", grad_vproj, w_value, preferred_element_type=full_type
    )
    primal_one, norm_back_one = jax.vjp(rms_scale, x_rows, gain_one)
    grad_x_norm, grad_gain_one = norm_back_one(grad_normed_one)
    grad_inputs = (grad_mid + grad_x_norm).astype(low_type)
    shares = (
        lax.psum_scatter(
            grad_wquery.astype(jnp.bfloat16), "dp", scatter_dimension=0, tiled=True
        ).astype(jnp.float32),
        lax.psum_scatter(
            grad_wkey.astype(jnp.bfloat16), "dp", scatter_dimension=0, tiled=True
        ).astype(jnp.float32),
        lax.psum_scatter(
            grad_wvalue.astype(jnp.bfloat16), "dp", scatter_dimension=0, tiled=True
        ).astype(jnp.float32),
        lax.psum_scatter(
            grad_wout.astype(jnp.bfloat16), "dp", scatter_dimension=0, tiled=True
        ).astype(jnp.float32),
        lax.psum_scatter(
            grad_gain_one.astype(jnp.bfloat16), "dp", scatter_dimension=0, tiled=True
        ).astype(jnp.float32),
        lax.psum_scatter(
            grad_gain_two.astype(jnp.bfloat16), "dp", scatter_dimension=0, tiled=True
        ).astype(jnp.float32),
        lax.psum_scatter(
            grad_wrouter.astype(jnp.bfloat16), "dp", scatter_dimension=0, tiled=True
        ).astype(jnp.float32),
        lax.psum_scatter(
            grad_wgate.astype(jnp.bfloat16), "dp", scatter_dimension=0, tiled=True
        ).astype(jnp.float32),
        lax.psum_scatter(
            grad_wup.astype(jnp.bfloat16), "dp", scatter_dimension=0, tiled=True
        ).astype(jnp.float32),
        lax.psum_scatter(
            grad_wdown.astype(jnp.bfloat16), "dp", scatter_dimension=0, tiled=True
        ).astype(jnp.float32),
    )
    dense_sum = lax.psum(
        (shares[0], shares[1], shares[2], shares[3], shares[4], shares[5], shares[6]),
        ("expert", "context"),
    )
    expert_sum = (
        lax.psum(shares[7].astype(jnp.bfloat16), "context").astype(jnp.float32),
        lax.psum(shares[8].astype(jnp.bfloat16), "context").astype(jnp.float32),
        lax.psum(shares[9].astype(jnp.bfloat16), "context").astype(jnp.float32),
    )
    totals_all = tuple(dense_sum) + tuple(expert_sum)
    return (
        result[None],
        grad_inputs[None],
        totals_all[0],
        totals_all[1],
        totals_all[2],
        totals_all[3],
        totals_all[4],
        totals_all[5],
        totals_all[6],
        totals_all[7],
        totals_all[8],
        totals_all[9],
    )


BF = jnp.bfloat16
F32 = jnp.float32
SLOTS = 112
MESH_ID = pl.DeviceIdType.MESH
PLANE = ("expert", "context")
VMEM_BYTES = 60 * 1024 * 1024


def mxu(lhs, rhs, contract=((1,), (0,))):
    return lax.dot_general(lhs, rhs, (contract, ((), ())), preferred_element_type=F32)


def grant(bytes_wanted=VMEM_BYTES):
    return pltpu.CompilerParams(vmem_limit_bytes=bytes_wanted)


def turn(values, cosine, sine):
    return values * cosine + pltpu.roll(values, HD // 2, 1) * sine


def row_blocks(prompt_len):
    blocks = [(0, prompt_len)]
    for start in range(0, CONT, PBLK):
        blocks.append((PBLK + start, prompt_len + start + PBLK))
    return blocks


def masked_scores(scores, first_row, block_index):
    tail = scores if first_row == 0 else scores[:, -PBLK:]
    row = lax.broadcasted_iota(jnp.int32, tail.shape, 0)
    column = lax.broadcasted_iota(jnp.int32, tail.shape, 1)
    limit = row + block_index * PBLK if first_row == 0 else row
    tail = jnp.where(column <= limit, tail, masked_score)
    return tail if first_row == 0 else jnp.concatenate([scores[:, :-PBLK], tail], axis=1)


def segment_matrix(parts, transposed):
    shape = (parts * SLOTS, parts) if transposed else (parts, parts * SLOTS)
    long = lax.broadcasted_iota(jnp.int32, shape, 0 if transposed else 1)
    short = lax.broadcasted_iota(jnp.int32, shape, 1 if transposed else 0)
    inside = (long >= short * SLOTS) & (long < (short + 1) * SLOTS)
    return jnp.where(inside, 1.0, 0.0).astype(BF)


def slot_matrix(ranks, parts, transposed):
    if transposed:
        spread = mxu(segment_matrix(parts, True), ranks)
        slot = lax.broadcasted_iota(jnp.int32, (parts * SLOTS, 1), 0)
    else:
        spread = mxu(ranks, segment_matrix(parts, False))
        slot = lax.broadcasted_iota(jnp.int32, (1, parts * SLOTS), 1)
    for part in range(parts - 1, 0, -1):
        slot = jnp.where(slot >= part * SLOTS, slot - SLOTS, slot)
    return jnp.where(spread == slot.astype(F32), 1.0, 0.0).astype(BF)


def collect_into(plane, rank_ref, held, base, target, finish):
    def block(n, carry):
        rows = pl.ds(pl.multiple_of(n * PBLK, PBLK), PBLK)
        made = jnp.zeros((PBLK, D), F32)
        for expert in range(2):
            chooser = slot_matrix(rank_ref[expert, rows, :], plane, False)
            made = made + mxu(chooser, held[base + expert].reshape(plane * SLOTS, D))
        target[rows, :] = finish(rows, made)
        return carry

    lax.fori_loop(0, target.shape[0] // PBLK, block, 0)


def plane_exchange(slot, source, target, local_sems, send_sems, recv_sems, bounce=None):
    here = plane_here()
    plane = source.shape[0]
    own_first = target.at[here] if bounce is None else bounce.at[slot]

    def begin():
        pltpu.make_async_copy(source.at[here], own_first, local_sems.at[slot]).start()

        def one(flip, carry):
            peer = here ^ flip
            remote(
                source.at[peer],
                target.at[here],
                send_sems.at[slot, peer],
                recv_sems.at[slot, here],
                plane_peer(peer),
            ).start()
            return carry

        lax.fori_loop(1, plane, one, 0)

    def finish():
        pltpu.make_async_copy(source.at[here], own_first, local_sems.at[slot]).wait()
        if bounce is not None:
            onward = pltpu.make_async_copy(own_first, target.at[here], local_sems.at[slot])
            onward.start()
            onward.wait()

        def one(flip, carry):
            peer = here ^ flip
            done = remote(
                source.at[peer],
                target.at[peer],
                send_sems.at[slot, peer],
                recv_sems.at[slot, peer],
                plane_peer(peer),
            )
            done.wait_send()
            done.wait_recv()
            return carry

        lax.fori_loop(1, plane, one, 0)

    return begin, finish


ALL_FLIPS = (2, 3, 1)
RIDE_FRONT = ((0, 2, 1), (0, 3, 0), (0, 1, 0))
RIDE_DISPATCH = ((1, 2, 0), (1, 3, 0), (2, 2, 0), (2, 3, 0), (1, 1, 0), (2, 1, 0))
DISPATCH_FIRST = 4
RIDE_FIRST = ((0, 3, 1), (0, 1, 1)) + tuple((m, f, 1) for m in (1, 2) for f in ALL_FLIPS)
HOME_SECOND = tuple((m, f, 0) for m in (0, 1) for f in (2, 3)) + tuple((m, 1, 0) for m in range(3))
HOME_RETURN = ((2, 2, 0), (2, 3, 0), (0, 2, 1), (0, 3, 1))
RETURN_FIRST = 2
HOME_BACKWARD = tuple((m, f, 1) for m in (1, 2) for f in (2, 3)) + tuple((m, 1, 1) for m in range(3))


def pick(array, index):
    return array if index is None else array.at[index]


def picked_shape(array, index):
    if index is None:
        return array.shape
    return array.shape[len(index) if isinstance(index, tuple) else 1 :]


def dp_moves(sources, targets, riders, sends, recvs):
    z_index = lax.axis_index("dp")
    return [
        remote(pick(source, index), target, sends.at[n], recvs.at[n], {"dp": z_index ^ flip})
        for n, (source, target, (index, flip)) in enumerate(zip(sources, targets, riders))
    ]


def dp_peers(n_dp):
    return [{"dp": lax.axis_index("dp") ^ flip} for flip in range(1, n_dp)]


def expert_kernel(plane, n_dp, half_steps, number, n_carried, picks, riders, *refs):
    (xo_ref, xp_ref, go_ref, gp_ref, gates_ref), refs = refs[:5], refs[5:]
    pieces, refs = refs[: 3 * n_dp], refs[3 * n_dp :]
    carried, refs = refs[:n_carried], refs[n_carried:]
    sources, refs = refs[: len(riders)], refs[len(riders) :]
    (yo_ref, yp_ref, bo_ref, bp_ref, dots_ref, gate_ref, up_ref, down_ref), refs = refs[:8], refs[8:]
    landed, refs = refs[:n_carried], refs[n_carried:]
    targets, refs = refs[: len(riders)], refs[len(riders) :]
    (wg_ref, wu_ref, wd_ref, x_all, de_all, a_all, dg_all, du_all, stage, bounce), sems = refs[:10], refs[10:]
    weight_sems, store_sems, local_sems, send_sems, recv_sems, ride_send, ride_recv = sems
    weights = (wg_ref, wu_ref, wd_ref)
    z_index = lax.axis_index("dp")
    step = pl.program_id(0)
    own = step < half_steps
    rows_of_step = xo_ref.shape[0]
    exchanges = [
        plane_exchange(n, source, target, local_sems, send_sems, recv_sems, bounce)
        for n, (source, target) in enumerate(zip(carried, landed))
    ]
    moves = dp_moves(sources, targets, riders, ride_send, ride_recv)

    @pl.when(step == 0)
    def _():
        here = plane_here()
        greet([plane_peer(here ^ flip) for flip in range(1, plane)] + dp_peers(n_dp))
        loads = []
        for n, piece in enumerate(pieces):
            source = pick(piece, picks[n])
            size = source.shape[0]
            start = pl.multiple_of((z_index ^ (n % n_dp)) * size, 64)
            loads.append(
                pltpu.make_async_copy(source, weights[n // n_dp].at[pl.ds(start, size)], weight_sems.at[n])
            )
            loads[-1].start()
        for begin, _ in exchanges:
            begin()
        for move in moves:
            move.start()
        for load in loads:
            load.wait()

    rows = jnp.where(own, xo_ref[...], xp_ref[...])
    cot = jnp.where(own, go_ref[...], gp_ref[...])
    places = rows_of_step // SLOTS
    first_place = lax.rem(step, half_steps) * places
    at = (SLOTS, 128)
    diagonal = lax.broadcasted_iota(jnp.int32, at, 0) == lax.broadcasted_iota(jnp.int32, at, 1)
    columns = []
    for n in range(places):
        own_row = gates_ref[first_place + n, number : number + 1, :]
        row = jnp.where(own, own_row, gates_ref[first_place + n, 2 + number : 3 + number, :])
        columns.append(jnp.sum(jnp.where(diagonal, row, 0.0), axis=-1, keepdims=True))
    share = jnp.concatenate(columns, axis=0)
    place = pl.ds(pl.multiple_of(step * rows_of_step, 32), rows_of_step)
    x_all[place, :] = rows
    gate_pre = mxu(rows, wg_ref[...])
    up_pre = mxu(rows, wu_ref[...])
    sigma = 1.0 / (1.0 + jnp.exp(-gate_pre))
    silu = gate_pre * sigma
    act = (silu * up_pre).astype(BF)
    a_all[place, :] = act
    cot_full = cot.astype(F32)
    weighted = (cot_full * share).astype(BF)
    de_all[place, :] = weighted
    result = mxu(act, wd_ref[...])
    dots = jnp.sum(result.astype(BF).astype(F32) * cot_full, axis=-1, keepdims=True)
    scaled = (result * share).astype(BF)
    grad_act = mxu(weighted, wd_ref[...], ((1,), (1,)))
    grad_gate = (grad_act * up_pre * sigma * (1.0 + gate_pre * (1.0 - sigma))).astype(BF)
    grad_up = (grad_act * silu).astype(BF)
    dg_all[place, :] = grad_gate
    du_all[place, :] = grad_up
    back = mxu(grad_gate, wg_ref[...], ((1,), (1,))) + mxu(grad_up, wu_ref[...], ((1,), (1,)))
    back = back.astype(BF)

    @pl.when(own)
    def _():
        yo_ref[...] = scaled
        bo_ref[...] = back

    @pl.when(jnp.logical_not(own))
    def _():
        yp_ref[...] = scaled
        bp_ref[...] = back

    for n in range(places):
        column = dots[n * SLOTS : (n + 1) * SLOTS]
        dots_ref[step // half_steps, first_place + n] = jnp.sum(
            jnp.where(diagonal, column, 0.0), axis=0, keepdims=True
        )

    @pl.when(step == 2 * half_steps - 1)
    def _():
        quarter = D // n_dp
        hidden = a_all.shape[1]

        def of_rows(q, carry):
            columns = pl.ds(pl.multiple_of(q * quarter, 128), quarter)
            stores = []
            for n, (grads, out_ref) in enumerate(((dg_all, gate_ref), (du_all, up_ref))):
                stage[n] = mxu(x_all[:, columns], grads[...], ((0,), (0,))).astype(BF)
                stores.append(pltpu.make_async_copy(stage.at[n], out_ref.at[z_index ^ q], store_sems.at[n]))
                stores[-1].start()
            for store in stores:
                store.wait()
            return carry

        lax.fori_loop(0, n_dp, of_rows, 0)
        size = hidden // n_dp
        for q in range(0, n_dp, 2):
            made = mxu(a_all[:, q * size : (q + 2) * size], de_all[...], ((0,), (0,))).astype(BF)
            stores = []
            for half in range(2):
                part = made[half * size : (half + 1) * size]
                stage[half, :size] = part[:, :hidden]
                stage[half, size:] = part[:, hidden:]
                stores.append(
                    pltpu.make_async_copy(
                        stage.at[half], down_ref.at[z_index ^ (q + half)], store_sems.at[half]
                    )
                )
                stores[-1].start()
            for store in stores:
                store.wait()
        for _, finish in exchanges:
            finish()
        for move in moves:
            move.wait()


def run_expert(name, which, number, rows, cots, gates, pieces, carried, riders):
    half_rows = rows[0].shape[0]
    half_steps = 4
    step_rows = half_rows // half_steps
    plane = carried[0].shape[0]
    n_dp = lax.axis_size("dp")
    hidden = picked_shape(*pieces[0])[1]
    own_map = lambda j: (jnp.minimum(j, half_steps - 1), 0)
    par_map = lambda j: (jnp.maximum(j - half_steps, 0), 0)
    anywhere = pl.BlockSpec(memory_space=pl.ANY)

    def pair(width):
        return [pl.BlockSpec((step_rows, width), own_map), pl.BlockSpec((step_rows, width), par_map)]

    shape = jax.ShapeDtypeStruct
    share = shape((n_dp, D // n_dp, hidden), BF)
    dma = pltpu.SemaphoreType.DMA
    all_rows = 2 * half_rows
    results = pl.pallas_call(
        functools.partial(
            expert_kernel,
            plane,
            n_dp,
            half_steps,
            which,
            len(carried),
            [index for _, index in pieces],
            [(index, flip) for _, index, flip in riders],
        ),
        grid=(2 * half_steps,),
        in_specs=pair(D)
        + pair(D)
        + [pl.BlockSpec(gates.shape, lambda j: (0, 0, 0))]
        + [anywhere] * (len(pieces) + len(carried) + len(riders)),
        out_specs=pair(D)
        + pair(D)
        + [pl.BlockSpec((2, plane, 1, 128), lambda j: (0, 0, 0, 0))]
        + [anywhere] * (3 + len(carried) + len(riders)),
        out_shape=[shape((half_rows, D), BF)] * 4
        + [shape((2, plane, 1, 128), F32)]
        + [share] * 3
        + [shape(array.shape, BF) for array in carried]
        + [shape(picked_shape(array, index), BF) for array, index, _ in riders],
        scratch_shapes=[
            pltpu.VMEM((D, hidden), BF),
            pltpu.VMEM((D, hidden), BF),
            pltpu.VMEM((hidden, D), BF),
            pltpu.VMEM((all_rows, D), BF),
            pltpu.VMEM((all_rows, D), BF),
            pltpu.VMEM((all_rows, hidden), BF),
            pltpu.VMEM((all_rows, hidden), BF),
            pltpu.VMEM((all_rows, hidden), BF),
            pltpu.VMEM((2, D // n_dp, hidden), BF),
            pltpu.VMEM((len(carried), SLOTS, D), BF),
            dma((len(pieces),)),
            dma((2,)),
            dma((len(carried),)),
            dma((len(carried), plane)),
            dma((len(carried), plane)),
            dma((len(riders),)),
            dma((len(riders),)),
        ],
        compiler_params=pltpu.CompilerParams(
            vmem_limit_bytes=56 * 1024 * 1024, collective_id=number, has_side_effects=True
        ),
        name=name,
    )(*rows, *cots, gates, *[a for a, _ in pieces], *carried, *[a for a, _, _ in riders])
    last = 8 + len(carried)
    return results[:4], results[4], results[5:8], results[8:last], results[last:]


def plane_peer(index):
    n_context = lax.axis_size("context")
    return {"expert": index // n_context, "context": index % n_context}


def plane_here():
    return lax.axis_index("expert") * lax.axis_size("context") + lax.axis_index("context")


def greet(peers):
    barrier = pltpu.get_barrier_semaphore()
    for peer in peers:
        pl.semaphore_signal(barrier, inc=1, device_id=peer, device_id_type=MESH_ID)
    pl.semaphore_wait(barrier, len(peers))


def remote(source, target, send, receive, peer):
    return pltpu.make_async_remote_copy(
        src_ref=source,
        dst_ref=target,
        send_sem=send,
        recv_sem=receive,
        device_id=peer,
        device_id_type=MESH_ID,
    )


def cast_halves(source_ref, halves_ref, loaded, made, load_sems, store_sems):
    rows, experts, width = source_ref.shape
    mine = experts // lax.axis_size("context")
    group = 8
    first = lax.axis_index("context") * mine
    start = pl.multiple_of(first // group * group, group)
    step = loaded.shape[1] * loaded.shape[3] // width
    lower = lax.rem(first, group) == 0
    even = lax.rem(lax.axis_index("dp"), 2) == 0
    steps = rows // step

    def load(n):
        slot = lax.rem(n, 2)
        block = source_ref.at[pl.ds(pl.multiple_of(n * step, step), step), pl.ds(start, group), :]
        return pltpu.make_async_copy(block, loaded.at[slot], load_sems.at[slot])

    def store(n, half):
        slot = lax.rem(n, 2)
        block = halves_ref.at[half, :, pl.ds(pl.multiple_of(n * step, step), step), :]
        return pltpu.make_async_copy(made.at[slot, half], block, store_sems.at[slot, half])

    load(0).start()

    def body(n, carry):
        @pl.when(n + 1 < steps)
        def _():
            load(n + 1).start()

        load(n).wait()

        @pl.when(n >= 2)
        def _():
            for half in range(2):
                store(n - 2, half).wait()

        slot = lax.rem(n, 2)
        block = loaded[slot]
        kept = jnp.where(lower, block[:, :mine, :], block[:, group - mine :, :])
        by_expert = jnp.swapaxes(kept, 0, 1).astype(BF)
        low, high = by_expert[: mine // 2], by_expert[mine // 2 :]
        made[slot, 0] = jnp.where(even, low, high)
        made[slot, 1] = jnp.where(even, high, low)
        for half in range(2):
            store(n, half).start()
        return carry

    lax.fori_loop(0, steps, body, 0)
    for n in (steps - 2, steps - 1):
        for half in range(2):
            store(n, half).wait()


def rank_tables(routes, plane, row_ref, column_ref):
    tokens = routes.shape[1]
    expert = lax.broadcasted_iota(jnp.int32, (EXPERTS, tokens), 0)
    named = jnp.zeros((EXPERTS, tokens), F32)
    for k in range(TOP):
        named = named + jnp.where(routes[k : k + 1, :] == expert, 1.0, 0.0)
    before = lax.broadcasted_iota(jnp.int32, (tokens, tokens), 0) < lax.broadcasted_iota(
        jnp.int32, (tokens, tokens), 1
    )
    count = mxu(named.astype(BF), jnp.where(before, 1.0, 0.0).astype(BF))
    ranks = jnp.where(named > 0, count, -1.0)
    low = ranks.astype(BF)
    owned = EXPERTS // plane
    parity = lax.rem(lax.axis_index("dp"), 2)
    for i in range(2):
        place = lax.broadcasted_iota(jnp.int32, (plane, EXPERTS), 0) * owned + parity * 2 + i
        column = lax.broadcasted_iota(jnp.int32, (plane, EXPERTS), 1)
        chosen = jnp.where(place == column, 1.0, 0.0).astype(BF)
        row_ref[i] = mxu(chosen, low).astype(BF)
        column_ref[i] = mxu(low, chosen, ((0,), (1,))).astype(BF)
    one = lax.broadcasted_iota(jnp.int32, (EXPERTS, EXPERTS), 0) == lax.broadcasted_iota(
        jnp.int32, (EXPERTS, EXPERTS), 1
    )
    return mxu(low, jnp.where(one, 1.0, 0.0).astype(BF), ((0,), (0,)))


def gather_kernel(
    n_dp,
    plane,
    routes_ref,
    in_ref,
    out_ref,
    gate_ref,
    up_ref,
    down_ref,
    cot_ref,
    ranks_ref,
    own_row_ref,
    own_column_ref,
    partner_row_ref,
    partner_column_ref,
    whole_in_ref,
    whole_out_ref,
    gate_halves_ref,
    up_halves_ref,
    down_halves_ref,
    cot_partner_ref,
    gate_piece_ref,
    partner_routes,
    loaded,
    made,
    loaded_wide,
    made_wide,
    load_sems,
    store_sems,
    local_sems,
    z_send,
    sends,
    recvs,
    route_sems,
):
    here = plane_here()
    z_index = lax.axis_index("dp")
    parts, wholes = (in_ref, out_ref), (whole_in_ref, whole_out_ref)
    z_peer = lambda flip: {"dp": z_index ^ flip}
    greet([z_peer(flip) for flip in range(1, n_dp)] + [plane_peer(here ^ flip) for flip in (1, 2, 4)])
    routing = remote(routes_ref, partner_routes, route_sems.at[0], route_sems.at[1], z_peer(1))
    routing.start()
    keep = [
        pltpu.make_async_copy(part, whole.at[z_index, here], local_sems.at[a])
        for a, (part, whole) in enumerate(zip(parts, wholes))
    ]
    for copy in keep:
        copy.start()
    started = []
    for a in range(2):
        for flip in range(1, n_dp):
            started.append(
                remote(
                    parts[a],
                    wholes[a].at[z_index, here],
                    z_send.at[a, flip],
                    recvs.at[a, z_index, here],
                    z_peer(flip),
                )
            )
            started[-1].start()

    half = cot_partner_ref.shape[0]
    cot_pair = remote(
        cot_ref.at[pl.ds(0, half)], cot_partner_ref, route_sems.at[2], route_sems.at[3], z_peer(1)
    )
    cot_pair.start()

    def pass_on(a, lane, flip, z_from, place, source=None):
        block = wholes[a].at[z_from, place]
        move = remote(
            block if source is None else source,
            block,
            sends.at[a, lane, z_from, place],
            recvs.at[a, z_from, place],
            plane_peer(here ^ flip),
        )
        move.start()
        started.append(move)

    def landed(a, z_from, place):
        block = wholes[a].at[z_from, place]
        remote(block, block, z_send.at[a, 0], recvs.at[a, z_from, place], z_peer(1)).wait_recv()

    froms = [z_index ^ flip for flip in range(n_dp)]
    for a in range(2):
        for lane, flip in enumerate((2, 4, 1)):
            pass_on(a, lane, flip, z_index, here, parts[a])
    ranks_ref[...] = rank_tables(routes_ref[...], plane, own_row_ref, own_column_ref)
    cast_halves(gate_ref, gate_halves_ref, loaded, made, load_sems, store_sems)
    gate_move = remote(
        gate_halves_ref.at[0, 0], gate_piece_ref, route_sems.at[4], route_sems.at[5], z_peer(2)
    )
    gate_move.start()
    for a in range(2):
        for z_from in froms[1:]:
            landed(a, z_from, here)
            for lane, flip in enumerate((2, 4, 1)):
                pass_on(a, lane, flip, z_from, here)
    cast_halves(up_ref, up_halves_ref, loaded, made, load_sems, store_sems)
    for a in range(2):
        for n, z_from in enumerate(froms):
            landed(a, z_from, here ^ 2)
            if n % 2 == 1:
                pass_on(a, 1, 4, z_from, here ^ 2)
            pass_on(a, 2, 1, z_from, here ^ 2)
            landed(a, z_from, here ^ 4)
            if n % 2 == 0:
                pass_on(a, 0, 2, z_from, here ^ 4)
            pass_on(a, 2, 1, z_from, here ^ 4)
    routing.wait()
    rank_tables(partner_routes[...], plane, partner_row_ref, partner_column_ref)
    cast_halves(down_ref, down_halves_ref, loaded_wide, made_wide, load_sems, store_sems)
    for a in range(2):
        for z_from in froms:
            landed(a, z_from, here ^ 6)
            pass_on(a, 2, 1, z_from, here ^ 6)
    for a in range(2):
        for place in (1, 3, 5, 7):
            for z_from in froms:
                landed(a, z_from, here ^ place)
    for move in started:
        move.wait_send()
    for copy in keep:
        copy.wait()
    cot_pair.wait()
    gate_move.wait()


def gather_parts(routes, part_in, part_out, weights, cot, n_dp, n_context, plane):
    tokens = routes.shape[1]
    vmem = pl.BlockSpec(memory_space=pltpu.VMEM)
    anywhere = pl.BlockSpec(memory_space=pl.ANY)
    shape = jax.ShapeDtypeStruct
    dma = pltpu.SemaphoreType.DMA
    row, column = shape((2, plane, tokens), BF), shape((2, tokens, plane), BF)
    mine = weights[0].shape[1] // n_context
    rows, width = 64, weights[0].shape[2]
    return pl.pallas_call(
        functools.partial(gather_kernel, n_dp, plane),
        in_specs=[vmem] + [anywhere] * 6,
        out_specs=[vmem] * 5 + [anywhere] * 7,
        out_shape=[shape((tokens, EXPERTS), F32), row, column, row, column]
        + [shape((n_dp, plane) + part.shape, BF) for part in (part_in, part_out)]
        + [shape((2, mine // 2, w.shape[0], w.shape[2]), BF) for w in weights]
        + [shape((tokens // 2, D), BF), shape(weights[0].shape[::2], BF)],
        scratch_shapes=[
            pltpu.VMEM(routes.shape, routes.dtype),
            pltpu.VMEM((2, rows, 8, width), F32),
            pltpu.VMEM((2, 2, mine // 2, rows, width), BF),
            pltpu.VMEM((2, rows // 2, 8, 2 * width), F32),
            pltpu.VMEM((2, 2, mine // 2, rows // 2, 2 * width), BF),
            dma((2,)),
            dma((2, 2)),
            dma((2,)),
            dma((2, n_dp)),
            dma((2, 3, n_dp, plane)),
            dma((2, n_dp, plane)),
            dma((6,)),
        ],
        compiler_params=pltpu.CompilerParams(
            vmem_limit_bytes=60 * 1024 * 1024, collective_id=3, has_side_effects=True
        ),
        name="gather_parts",
    )(routes, part_in, part_out, *weights, cot)


def front_kernel(n_dp, prompt_len, riders, *refs):
    (x_ref, cos_ref, sin_ref, w_in_ref, w_out_ref, cot_ref), refs = refs[:6], refs[6:]
    sources, refs = refs[: len(riders)], refs[len(riders) :]
    (gains_ref, log_ref, logits_ref), refs = refs[:3], refs[3:]
    saved, (mid_ref, cot_partner_ref), refs = refs[:5], refs[5:7], refs[7:]
    targets, refs = refs[: len(riders)], refs[len(riders) :]
    (
        normed_one_ref,
        qkv_ref,
        kv_ref,
        attended_ref,
        normed_two_ref,
        save_sems,
        columns_buf,
        small,
        w_out,
        mid_block,
        load_sems,
        column_sems,
        pair_sems,
        kv_send,
        kv_recv,
        ride_send,
        ride_recv,
    ) = refs
    block_index = lax.axis_index("context")
    n_context = prompt_len // PBLK
    tokens = x_ref.shape[0]
    width = qkv_ref.shape[1]
    greet([context_peer(flip) for flip in range(1, n_context)] + dp_peers(n_dp))
    held = (normed_one_ref, qkv_ref, kv_ref, attended_ref, normed_two_ref)
    saves = [pltpu.make_async_copy(buf, out, save_sems.at[n]) for n, (buf, out) in enumerate(zip(held, saved))]
    load_small = pltpu.make_async_copy(w_in_ref.at[:, pl.ds(width, 128)], small, load_sems.at[0])
    load_out = pltpu.make_async_copy(w_out_ref, w_out, load_sems.at[1])
    step_width = columns_buf.shape[2]
    steps = width // step_width
    kv_steps = (width - D) // step_width

    def place_of(n):
        return lax.rem(n + steps - kv_steps, steps)

    def load_columns(n):
        slot = lax.rem(n, 2)
        start = pl.multiple_of(place_of(n) * step_width, step_width)
        return pltpu.make_async_copy(
            w_in_ref.at[:, pl.ds(start, step_width)], columns_buf.at[slot], column_sems.at[slot]
        )

    load_small.start()
    load_columns(0).start()
    load_out.start()
    rest = cot_partner_ref.shape[0]
    pair = remote(
        cot_ref.at[pl.ds(tokens - rest, rest)],
        cot_partner_ref,
        pair_sems.at[0],
        pair_sems.at[1],
        {"dp": lax.axis_index("dp") ^ 1},
    )
    pair.start()
    moves = dp_moves(sources, targets, riders, ride_send, ride_recv)
    for move in moves:
        move.start()
    load_small.wait()
    picked = lax.broadcasted_iota(jnp.int32, (8, 128), 1) - lax.broadcasted_iota(jnp.int32, (8, 128), 0)
    gains_ref[...] = mxu(jnp.where(picked == EXPERTS, 1.0, 0.0).astype(BF), small[...], ((1,), (1,)))

    def normed(rows, gain):
        scale = lax.rsqrt(jnp.mean(rows * rows, axis=-1, keepdims=True) + epsilon)
        return (rows * scale * gain).astype(BF)

    def block_rows(n):
        return pl.ds(pl.multiple_of(n * PBLK, PBLK), PBLK)

    def first_norm(n, carry):
        rows = block_rows(n)
        normed_one_ref[rows, :] = normed(x_ref[rows, :].astype(F32), gains_ref[0:1, :])
        return carry

    lax.fori_loop(0, tokens // PBLK, first_norm, 0)

    def project(n, carry):
        @pl.when(n + 1 < steps)
        def _():
            load_columns(n + 1).start()

        load_columns(n).wait()
        place = place_of(n)
        product = mxu(normed_one_ref[...], columns_buf[lax.rem(n, 2)])
        is_value = place == steps - kv_steps // 2
        cosine = jnp.where(is_value, 1.0, cos_ref[...])
        sine = jnp.where(is_value, 0.0, sin_ref[...])
        factor = jnp.where(place < steps - kv_steps, 1.0 / math.sqrt(HD), 1.0)
        for half in range(step_width // HD):
            part = product[:, half * HD : (half + 1) * HD]
            start = pl.multiple_of(place * step_width + half * HD, HD)
            qkv_ref[:, pl.ds(start, HD)] = (turn(part, cosine, sine) * factor).astype(BF)
        return carry

    lax.fori_loop(0, kv_steps, project, 0)
    own_keys = pl.ds(pl.multiple_of(block_index * PBLK, PBLK), PBLK)
    kv_ref[own_keys, :] = qkv_ref[:PBLK, D:]
    kv_ref[prompt_len:, :] = qkv_ref[PBLK:, D:]
    kv_moves = [
        remote(
            kv_ref.at[own_keys],
            kv_ref.at[own_keys],
            kv_send.at[flip],
            kv_recv.at[flip],
            context_peer(flip),
        )
        for flip in range(1, n_context)
    ]
    for move in kv_moves:
        move.start()
    lax.fori_loop(kv_steps, steps, project, 0)
    for move in kv_moves:
        move.wait()
    for save in saves[:3]:
        save.start()
    log_ref[...] = jnp.zeros_like(log_ref)

    def through_head(head, carry):
        columns = pl.ds(pl.multiple_of(head * HD, HD), HD)
        group = head // (HEADS // KVH)
        key_columns = pl.ds(pl.multiple_of(group * HD, HD), HD)
        value_columns = pl.ds(pl.multiple_of(KVH * HD + group * HD, HD), HD)
        for first_row, keys in row_blocks(prompt_len):
            rows = slice(first_row, first_row + PBLK)
            scores = mxu(qkv_ref[rows, columns], kv_ref[:keys, key_columns], ((1,), (1,)))
            scores = masked_scores(scores, first_row, block_index)
            top = jnp.max(scores, axis=-1, keepdims=True)
            unnormed = jnp.exp(scores - top)
            total = jnp.sum(unnormed, axis=-1, keepdims=True)
            mixed = mxu(unnormed.astype(BF), kv_ref[:keys, value_columns]) / total
            attended_ref[rows, columns] = mixed.astype(BF)
            lane = lax.broadcasted_iota(jnp.int32, (PBLK, log_ref.shape[1]), 1)
            log_ref[rows, :] = jnp.where(lane == head, top + jnp.log(total), log_ref[rows, :])
        return carry

    lax.fori_loop(0, HEADS, through_head, 0)
    saves[3].start()
    load_out.wait()

    def second_norm(n, carry):
        rows = block_rows(n)
        mid = x_ref[rows, :].astype(F32) + mxu(attended_ref[rows, :], w_out[...])
        mid_block[...] = mid
        store = pltpu.make_async_copy(mid_block, mid_ref.at[rows], load_sems.at[2])
        store.start()
        low = normed(mid, gains_ref[1:2, :])
        normed_two_ref[rows, :] = low
        logits_ref[rows, :] = mxu(low, small[...])
        store.wait()
        return carry

    lax.fori_loop(0, tokens // PBLK, second_norm, 0)
    saves[4].start()
    pair.wait()
    for move in moves:
        move.wait()
    for save in saves:
        save.wait()


def front(prompt_len, n_dp, x_low, cosine, sine, w_in, w_out, cot, riders):
    tokens = x_low.shape[0]
    width = D + 2 * KVH * HD
    key_rows = prompt_len + CONT
    n_context = prompt_len // PBLK
    vmem = pl.BlockSpec(memory_space=pltpu.VMEM)
    anywhere = pl.BlockSpec(memory_space=pl.ANY)
    shape = jax.ShapeDtypeStruct
    dma = pltpu.SemaphoreType.DMA
    return pl.pallas_call(
        functools.partial(front_kernel, n_dp, prompt_len, [(index, flip) for _, index, flip in riders]),
        in_specs=[vmem] * 3 + [anywhere] * (3 + len(riders)),
        out_specs=[vmem] * 3 + [anywhere] * (7 + len(riders)),
        out_shape=[
            shape((8, D), F32),
            shape((tokens, 128), F32),
            shape((tokens, 128), F32),
            shape((tokens, D), BF),
            shape((tokens, width), BF),
            shape((key_rows, 2 * KVH * HD), BF),
            shape((tokens, D), BF),
            shape((tokens, D), BF),
            shape((tokens, D), F32),
            shape((tokens // 2, D), BF),
        ]
        + [shape(picked_shape(array, index), BF) for array, index, _ in riders],
        scratch_shapes=[
            pltpu.VMEM((tokens, D), BF),
            pltpu.VMEM((tokens, width), BF),
            pltpu.VMEM((key_rows, 2 * KVH * HD), BF),
            pltpu.VMEM((tokens, D), BF),
            pltpu.VMEM((tokens, D), BF),
            dma((5,)),
            pltpu.VMEM((2, D, 2 * HD), BF),
            pltpu.VMEM((D, 128), BF),
            pltpu.VMEM((D, D), BF),
            pltpu.VMEM((PBLK, D), F32),
            dma((3,)),
            dma((2,)),
            dma((2,)),
            dma((n_context,)),
            dma((n_context,)),
            dma((len(riders),)),
            dma((len(riders),)),
        ],
        compiler_params=pltpu.CompilerParams(
            vmem_limit_bytes=56 * 1024 * 1024, collective_id=8, has_side_effects=True
        ),
        name="front",
    )(x_low, cosine, sine, w_in, w_out, cot, *[array for array, _, _ in riders])


def dispatch_kernel(plane, n_dp, riders, *refs):
    normed_ref, cot_ref, own_rank_ref, partner_rank_ref, logits_ref, ranks_ref = refs[:6]
    cot_halves, refs = refs[6:8], refs[8:]
    sources, refs = refs[: len(riders)], refs[len(riders) :]
    gates_ref, gates_here_ref, refs = refs[0], refs[1], refs[2:]
    landed, staged, targets = refs[:4], refs[4:8], refs[8 : 8 + len(riders)]
    (
        stage,
        normed_partner,
        pair_sems,
        stage_sems,
        local_sems,
        send_sems,
        recv_sems,
        ride_send,
        ride_recv,
        all_gates,
        other_gates,
        partner_gates,
        gate_sems,
        gate_send,
        gate_recv,
        cot_partner,
        cot_sems,
    ) = refs[8 + len(riders) :]
    here = plane_here()
    greet([plane_peer(here ^ flip) for flip in range(1, plane)] + dp_peers(n_dp))
    partner = {"dp": lax.axis_index("dp") ^ 1}
    gate_pair = remote(other_gates, partner_gates, gate_sems.at[0], gate_sems.at[1], partner)
    pair = remote(normed_ref, normed_partner, pair_sems.at[0], pair_sems.at[1], partner)
    pair.start()
    moves = dp_moves(sources, targets, riders, ride_send, ride_recv)
    first = cot_halves[0].shape[0]
    places = (pl.ds(0, first), pl.ds(first, cot_halves[1].shape[0]))
    cot_loads = [
        pltpu.make_async_copy(part, cot_partner.at[place], cot_sems.at[n])
        for n, (part, place) in enumerate(zip(cot_halves, places))
    ]
    for load in cot_loads:
        load.start()
    plans = (
        (0, normed_ref, own_rank_ref),
        (1, cot_ref, own_rank_ref),
        (2, cot_partner, partner_rank_ref),
        (3, normed_partner, partner_rank_ref),
    )
    exchanges = [
        plane_exchange(n, stage.at[n], landed[n], local_sems, send_sems, recv_sems) for n in range(4)
    ]
    copies = [pltpu.make_async_copy(stage.at[4 + n], staged[n], stage_sems.at[n]) for n in range(4)]

    def slot_gates():
        ranks = ranks_ref[...]
        parity = lax.rem(lax.axis_index("dp"), 2)
        named = ranks >= 0
        logits = jnp.where(named, logits_ref[:, :EXPERTS], masked_score)
        top = jnp.max(logits, axis=-1, keepdims=True)
        raised = jnp.where(named, jnp.exp(logits - top), 0.0)
        gates = raised / jnp.sum(raised, axis=-1, keepdims=True)
        gates_ref[...] = gates
        slot = lax.broadcasted_iota(jnp.int32, (ranks.shape[0], 128), 1).astype(F32)
        owned = EXPERTS // plane
        for place in range(plane):
            for i in range(2):
                rows = []
                for expert in (place * owned + i, place * owned + 2 + i):
                    hit = ranks[:, expert : expert + 1] == slot
                    rows.append(
                        jnp.sum(jnp.where(hit, gates[:, expert : expert + 1], 0.0), axis=0, keepdims=True)
                    )
                all_gates[place, i : i + 1, :] = jnp.where(parity == 0, rows[0], rows[1])
                other_gates[place, i : i + 1, :] = jnp.where(parity == 0, rows[1], rows[0])

    for expert in range(2):
        for n, rows_ref, rank_ref in plans:
            if expert == 0 and n == 2:
                for load in cot_loads:
                    load.wait()
            if expert == 0 and n == 3:
                for move in moves[:DISPATCH_FIRST]:
                    move.start()
                slot_gates()
                gate_pair.start()
                pair.wait()
                for move in moves[DISPATCH_FIRST:]:
                    move.start()
            chooser = slot_matrix(rank_ref[expert], plane, True)
            stage[4 * expert + n] = mxu(chooser, rows_ref[...]).astype(BF).reshape(plane, SLOTS, D)
            if expert == 0:
                exchanges[n][0]()
            else:
                copies[n].start()
    gate_pair.wait()
    all_gates[:, 2:4, :] = partner_gates[...]
    gates_here_ref[here] = all_gates[here]
    gate_moves = [
        remote(
            all_gates.at[here ^ flip],
            gates_here_ref.at[here],
            gate_send.at[flip],
            gate_recv.at[flip],
            plane_peer(here ^ flip),
        )
        for flip in range(1, plane)
    ]
    for move in gate_moves:
        move.start()
    for copy in copies:
        copy.wait()
    for _, finish in exchanges:
        finish()
    for move in gate_moves + moves:
        move.wait()


def dispatch_rows(normed, cot, cot_halves, own_ranks, partner_ranks, logits, ranks, riders, n_dp):
    plane, tokens = own_ranks.shape[1:]
    vmem = pl.BlockSpec(memory_space=pltpu.VMEM)
    anywhere = pl.BlockSpec(memory_space=pl.ANY)
    shape = jax.ShapeDtypeStruct
    dma = pltpu.SemaphoreType.DMA
    results = pl.pallas_call(
        functools.partial(dispatch_kernel, plane, n_dp, [(index, flip) for _, index, flip in riders]),
        in_specs=[vmem] * 6 + [anywhere] * (2 + len(riders)),
        out_specs=[vmem] * 2 + [anywhere] * (8 + len(riders)),
        out_shape=[shape(ranks.shape, F32), shape((plane, 4, 128), F32)]
        + [shape((plane, SLOTS, D), BF)] * 8
        + [shape(picked_shape(array, index), BF) for array, index, _ in riders],
        scratch_shapes=[
            pltpu.VMEM((8, plane, SLOTS, D), BF),
            pltpu.VMEM((tokens, D), BF),
            dma((2,)),
            dma((4,)),
            dma((4,)),
            dma((4, plane)),
            dma((4, plane)),
            dma((len(riders),)),
            dma((len(riders),)),
            pltpu.VMEM((plane, 4, 128), F32),
            pltpu.VMEM((plane, 2, 128), F32),
            pltpu.VMEM((plane, 2, 128), F32),
            dma((2,)),
            dma((plane,)),
            dma((plane,)),
            pltpu.VMEM((tokens, D), BF),
            dma((2,)),
        ],
        compiler_params=pltpu.CompilerParams(
            vmem_limit_bytes=56 * 1024 * 1024, collective_id=1, has_side_effects=True
        ),
        cost_estimate=pl.CostEstimate(flops=2 * 10**10, bytes_accessed=4 * 10**8, transcendentals=0),
        name="dispatch_rows",
    )(
        normed, cot, own_ranks, partner_ranks, logits, ranks, *cot_halves, *[a for a, _, _ in riders]
    )
    return results[0], results[1], results[2:6], results[6:10], results[10:]


def sum_matrix(which, sources, summed, sums, part_ref, piece_sems, sum_sems):
    copies = [pltpu.make_async_copy(source, summed.at[n], piece_sems.at[n]) for n, source in enumerate(sources)]
    for copy in copies:
        copy.start()
    for copy in copies:
        copy.wait()
    parity = lax.rem(lax.axis_index("dp"), 2)
    stores = []
    for side in range(2):
        total = summed[side].astype(F32)
        for n in range(side + 2, len(sources), 2):
            total = total + summed[n].astype(F32)
        sums[side] = total.astype(BF)
        place = parity if side == 0 else 1 - parity
        stores.append(pltpu.make_async_copy(sums.at[side], part_ref.at[place, which], sum_sems.at[side]))
        stores[-1].start()
    for store in stores:
        store.wait()


def return_kernel(
    plane,
    n_dp,
    n_results,
    riders,
    names,
    own_rank_ref,
    partner_rank_ref,
    first_dots_ref,
    second_dots_ref,
    ranks_ref,
    gates_ref,
    *refs,
):
    early, back = refs[0:2], refs[2:4]
    results, refs = refs[4 : 4 + n_results], refs[4 + n_results :]
    sources, refs = refs[: len(riders)], refs[len(riders) :]
    mine, refs = refs[:3], refs[3:]
    arrived, refs = refs[: len(HOME_SECOND)], refs[len(HOME_SECOND) :]
    saved_ref, dlog_ref, part_ref = refs[:3]
    results_back, refs = refs[3 : 3 + n_results], refs[3 + n_results :]
    targets = refs[: len(riders)]
    homes = dict(zip(HOME_SECOND, arrived))
    homes.update(zip(names, targets))
    (
        held,
        to_partner,
        of_partner,
        load_sems,
        pair_sems,
        local_sems,
        send_sems,
        recv_sems,
        ride_send,
        ride_recv,
        dot_sems,
        dot_send,
        dot_recv,
        dots_ref,
        dots_here_ref,
        dots_other_ref,
        bounce,
        summed,
        sums,
        partial,
        total_ref,
        save_sems,
        piece_sems,
        sum_sems,
    ) = refs[len(riders) :]
    here = plane_here()
    partner = {"dp": lax.axis_index("dp") ^ 1}
    greet([plane_peer(here ^ flip) for flip in range(1, plane)] + dp_peers(n_dp))
    for n, by_side in enumerate((first_dots_ref, second_dots_ref)):
        for side in range(2):
            dots_ref[:, 2 * side + n : 2 * side + n + 1, :] = by_side[side]
    own_dots = pltpu.make_async_copy(dots_ref.at[here], dots_here_ref.at[here], dot_sems.at[0])
    own_dots.start()
    dot_moves = [
        remote(
            dots_ref.at[here ^ flip],
            dots_here_ref.at[here],
            dot_send.at[flip],
            dot_recv.at[flip],
            plane_peer(here ^ flip),
        )
        for flip in range(1, plane)
    ]
    for move in dot_moves:
        move.start()
    loads, exchanges = {}, {}
    for side in (1, 0):
        loads[side] = pltpu.make_async_copy(early[side], held.at[2 * side], load_sems.at[side])
        loads[side].start()
        exchanges[side] = plane_exchange(
            side, back[side], held.at[2 * side + 1], local_sems, send_sems, recv_sems
        )
    exchanges[1][0]()
    later = [
        plane_exchange(2 + n, results[n], results_back[n], local_sems, send_sems, recv_sems, bounce)
        for n in range(n_results)
    ]
    moves = dp_moves(sources, targets, riders, ride_send, ride_recv)
    own_dots.wait()
    for move in dot_moves:
        move.wait()
    dots_pair = remote(dots_here_ref, dots_other_ref, dot_sems.at[1], dot_sems.at[2], partner)
    dots_pair.start()

    def of_gates():
        tokens = ranks_ref.shape[0]
        parity = lax.rem(lax.axis_index("dp"), 2)
        owned = EXPERTS // plane
        slot = lax.broadcasted_iota(jnp.int32, (tokens, 128), 1).astype(F32)
        lane = lax.broadcasted_iota(jnp.int32, (tokens, EXPERTS), 1)
        made = jnp.zeros((tokens, EXPERTS), F32)
        for expert in range(EXPERTS):
            place, side, i = expert // owned, expert % owned // 2, expert % 2
            row = jnp.where(
                parity == side,
                dots_here_ref[place, i : i + 1, :],
                dots_other_ref[place, 2 + i : 3 + i, :],
            )
            hit = ranks_ref[:, expert : expert + 1] == slot
            value = jnp.sum(jnp.where(hit, row, 0.0), axis=-1, keepdims=True)
            made = jnp.where(lane == expert, value, made)
        gates = gates_ref[...]
        mean = jnp.sum(gates * made, axis=-1, keepdims=True)
        dlog_ref[...] = jnp.zeros_like(dlog_ref)
        dlog_ref[:, :EXPERTS] = (gates * (made - mean)).astype(BF)

    def sum_of(which):
        sources = [mine[which].at[0]] + [homes[which, flip, 0] for flip in range(1, n_dp)]
        sum_matrix(which, sources, summed, sums, part_ref, piece_sems, sum_sems)

    blocks = [slice(start, start + PBLK) for start in range(0, total_ref.shape[0], PBLK)]

    def collected(rank_ref, rows, side, expert):
        chooser = slot_matrix(rank_ref[expert, rows, :], plane, False)
        return mxu(chooser, held[2 * side + expert].reshape(plane * SLOTS, D))

    for move in moves[:RETURN_FIRST]:
        move.start()
    loads[1].wait()
    for rows in blocks:
        partial[rows, :] = collected(partner_rank_ref, rows, 1, 0)
    loads[0].wait()
    for rows in blocks:
        total_ref[rows, :] = collected(own_rank_ref, rows, 0, 0)
    sum_of(0)
    sum_of(1)
    exchanges[1][1]()
    exchanges[0][0]()
    pairs = []
    for n, rows in enumerate(blocks):
        to_partner[rows, :] = (partial[rows, :] + collected(partner_rank_ref, rows, 1, 1)).astype(BF)
        block = pl.ds(n * PBLK, PBLK)
        pairs.append(
            remote(to_partner.at[block], of_partner.at[block], pair_sems.at[0, n], pair_sems.at[1, n], partner)
        )
        pairs[-1].start()
    for move in moves[RETURN_FIRST:]:
        move.start()
    for begin, _ in later:
        begin()
    dots_pair.wait()
    of_gates()
    for move in moves[:RETURN_FIRST]:
        move.wait()
    sum_of(2)
    exchanges[0][1]()
    for rows in blocks:
        total_ref[rows, :] += collected(own_rank_ref, rows, 0, 1)
    saves = []
    for n, (pair, rows) in enumerate(zip(pairs, blocks)):
        pair.wait()
        total_ref[rows, :] += of_partner[rows, :].astype(F32)
        block = pl.ds(n * PBLK, PBLK)
        saves.append(pltpu.make_async_copy(total_ref.at[block], saved_ref.at[block], save_sems.at[n]))
        saves[-1].start()
    for move in moves[RETURN_FIRST:]:
        move.wait()
    for _, finish in later:
        finish()
    for save in saves:
        save.wait()


def return_rows(
    own_ranks, partner_ranks, first_dots, second_dots, ranks, gates, early, back, results, riders, names, shares, arrived, n_dp
):
    tokens, plane = own_ranks.shape[1:]
    vmem = pl.BlockSpec(memory_space=pltpu.VMEM)
    anywhere = pl.BlockSpec(memory_space=pl.ANY)
    shape = jax.ShapeDtypeStruct
    dma = pltpu.SemaphoreType.DMA
    outcome = pl.pallas_call(
        functools.partial(
            return_kernel, plane, n_dp, len(results), [(index, flip) for _, index, flip in riders], names
        ),
        in_specs=[vmem] * 6 + [anywhere] * (7 + len(results) + len(riders) + len(arrived)),
        out_specs=[anywhere, vmem] + [anywhere] * (1 + len(results) + len(riders)),
        out_shape=[shape((tokens, D), F32), shape((tokens, 128), BF), shape((2, 3) + shares[0].shape[1:], BF)]
        + [shape(rows.shape, BF) for rows in results]
        + [shape(picked_shape(array, index), BF) for array, index, _ in riders],
        scratch_shapes=[
            pltpu.VMEM((4, plane, SLOTS, D), BF),
            pltpu.VMEM((tokens, D), BF),
            pltpu.VMEM((tokens, D), BF),
            dma((2,)),
            dma((2, tokens // PBLK)),
            dma((4,)),
            dma((4, plane)),
            dma((4, plane)),
            dma((len(riders),)),
            dma((len(riders),)),
            dma((3,)),
            dma((plane,)),
            dma((plane,)),
            pltpu.VMEM((plane, 4, 128), F32),
            pltpu.VMEM((plane, 4, 128), F32),
            pltpu.VMEM((plane, 4, 128), F32),
            pltpu.VMEM((2 + len(results), SLOTS, D), BF),
            pltpu.VMEM(shares[0].shape, BF),
            pltpu.VMEM((2,) + shares[0].shape[1:], BF),
            pltpu.VMEM((tokens, D), F32),
            pltpu.VMEM((tokens, D), F32),
            dma((tokens // PBLK,)),
            dma((n_dp,)),
            dma((2,)),
        ],
        compiler_params=pltpu.CompilerParams(
            vmem_limit_bytes=56 * 1024 * 1024, collective_id=2, has_side_effects=True
        ),
        cost_estimate=pl.CostEstimate(flops=3 * 10**10, bytes_accessed=4 * 10**8, transcendentals=0),
        name="return_rows",
    )(
        own_ranks,
        partner_ranks,
        first_dots,
        second_dots,
        ranks,
        gates,
        *early,
        *back,
        *results,
        *[array for array, _, _ in riders],
        *shares,
        *arrived,
    )
    last = 3 + len(results)
    return outcome[0], outcome[1], outcome[2], outcome[3:last], outcome[last:]


def normed_back(rows, gain, grads):
    scale = lax.rsqrt(jnp.mean(rows * rows, axis=-1, keepdims=True) + epsilon)
    weighted = grads * gain
    mean = jnp.mean(rows * weighted, axis=-1, keepdims=True)
    return scale * weighted - rows * (scale * scale * scale * mean), rows * scale * grads


def context_peer(flip):
    return {"context": lax.axis_index("context") ^ flip}


def share_context(part, place_of, sends, recvs):
    here = lax.axis_index("context")
    across = remote(part, place_of(here), sends.at[0], recvs.at[here], context_peer(2))
    beside = remote(part, place_of(here), sends.at[1], recvs.at[here], context_peer(1))
    block = place_of(here ^ 2)
    onward = remote(block, block, sends.at[2], recvs.at[here ^ 2], context_peer(1))

    def begin():
        across.start()
        beside.start()

    def pass_on():
        remote(part, block, sends.at[0], recvs.at[here ^ 2], context_peer(2)).wait_recv()
        onward.start()

    def finish():
        for flip in (1, 3):
            remote(part, place_of(here ^ flip), sends.at[1], recvs.at[here ^ flip], context_peer(1)).wait_recv()
        across.wait_send()
        beside.wait_send()
        onward.wait_send()

    return begin, pass_on, finish


def backward_kernel(n_dp, prompt_len, n_results, riders, *refs):
    (dlog_ref, gains_in_ref, log_ref, cos_ref, sin_ref), kept, refs = refs[:5], refs[5:11], refs[11:]
    (mid_ref, total_ref, w_out_ref, w_in_ref, normed_two_ref, part_ref), refs = refs[:6], refs[6:]
    results, refs = refs[:n_results], refs[n_results:]
    late = len(riders)
    sources, refs = refs[:late], refs[late:]
    grad_x_ref, grad_out_ref, grad_in_ref, grad_small_ref, all_ref = refs[:5]
    results_back, refs = refs[5 : 5 + n_results], refs[5 + n_results :]
    homes, refs = refs[:late], refs[late:]
    (
        weights,
        grad_mid,
        grad_attn,
        mid_block,
        grad_qkv,
        grad_kv,
        kv_send,
        kv_recv,
        stage,
        load_sems,
        store_sems,
        kv_send_sems,
        kv_recv_sems,
        home_send,
        home_recv,
        share_sends,
        share_recvs,
        small,
        gains_ref,
        bounce,
        local_sems,
        send_sems,
        recv_sems,
        cot_ref,
        qkv_ref,
        kv_ref,
        attended_ref,
        normed_ref,
        x_ref,
        kept_sems,
        mid_sems,
        grad_x,
        grad_x_sems,
    ) = refs
    block_index = lax.axis_index("context")
    n_context = kv_send.shape[0]
    tokens = x_ref.shape[0]
    heads_width = HEADS * HD
    kv_width = KVH * HD
    here = plane_here()
    plane = results[0].shape[0]
    greet([plane_peer(here ^ flip) for flip in range(1, plane)] + dp_peers(n_dp))
    load_small = pltpu.make_async_copy(
        w_in_ref.at[:, pl.ds(weights.shape[1], 128)], small, load_sems.at[4]
    )
    load_small.start()
    buffers = (cot_ref, qkv_ref, kv_ref, attended_ref, normed_ref, x_ref)
    kept_loads = [
        pltpu.make_async_copy(source, buf, kept_sems.at[n]) for n, (source, buf) in enumerate(zip(kept, buffers))
    ]
    load_total = pltpu.make_async_copy(total_ref, grad_mid, load_sems.at[0])
    load_out = pltpu.make_async_copy(w_out_ref, weights.at[:, pl.ds(0, D)], load_sems.at[1])
    load_in = pltpu.make_async_copy(w_in_ref.at[:, pl.ds(0, weights.shape[1])], weights, load_sems.at[2])
    load_total.start()
    load_out.start()
    for load in kept_loads:
        load.start()
    homing = dp_moves(sources, homes, riders, home_send, home_recv)
    for move in homing:
        move.start()
    begin_all, pass_on, finish = share_context(
        part_ref, lambda place: all_ref.at[place], share_sends, share_recvs
    )
    begin_all()
    exchanges = [
        plane_exchange(side, results[side], results_back[side], local_sems, send_sems, recv_sems, bounce)
        for side in range(n_results)
    ]
    load_small.wait()
    load_total.wait()
    load_out.wait()
    gains_ref[...] = jnp.zeros_like(gains_ref)
    kept_loads[0].wait()

    def load_mid(n):
        slot = lax.rem(n, 2)
        block = mid_ref.at[pl.ds(pl.multiple_of(n * PBLK, PBLK), PBLK)]
        return pltpu.make_async_copy(block, mid_block.at[slot], mid_sems.at[slot])

    load_mid(0).start()

    def block_rows(n):
        return pl.ds(pl.multiple_of(n * PBLK, PBLK), PBLK)

    def through_norm(n, carry):
        rows = block_rows(n)

        @pl.when(n + 1 < tokens // PBLK)
        def _():
            load_mid(n + 1).start()

        load_mid(n).wait()
        grads = grad_mid[rows, :] + mxu(dlog_ref[rows, :], small[...], ((1,), (1,)))
        by_rows, by_gain = normed_back(mid_block[lax.rem(n, 2)], gains_in_ref[1:2, :], grads)
        gains_ref[1:2, :] += jnp.sum(by_gain, axis=0, keepdims=True)
        by_mid = cot_ref[rows, :].astype(F32) + by_rows
        grad_mid[rows, :] = by_mid
        low = by_mid.astype(BF)
        grad_attn[rows, :] = low
        grad_qkv[rows, :D] = mxu(low, weights[:, :D], ((1,), (1,))).astype(BF)
        return carry

    lax.fori_loop(0, tokens // PBLK, through_norm, 0)
    load_in.start()
    for load in kept_loads[1:3]:
        load.wait()
    grad_kv[...] = jnp.zeros_like(grad_kv)

    def through_head(head, carry):
        columns = pl.ds(pl.multiple_of(head * HD, HD), HD)
        group = head // (HEADS // KVH)
        key_columns = pl.ds(pl.multiple_of(group * HD, HD), HD)
        value_columns = pl.ds(pl.multiple_of(kv_width + group * HD, HD), HD)
        for first_row, keys in row_blocks(prompt_len):
            rows = slice(first_row, first_row + PBLK)
            queries, grads = qkv_ref[rows, columns], grad_qkv[rows, columns]
            scores = mxu(queries, kv_ref[:keys, key_columns], ((1,), (1,)))
            scores = masked_scores(scores, first_row, block_index)
            lane = lax.broadcasted_iota(jnp.int32, (PBLK, log_ref.shape[1]), 1)
            logs = jnp.sum(jnp.where(lane == head, log_ref[rows, :], 0.0), axis=-1, keepdims=True)
            probs = jnp.exp(scores - logs)
            grad_probs = mxu(grads, kv_ref[:keys, value_columns], ((1,), (1,)))
            dots = jnp.sum(probs * grad_probs, axis=-1, keepdims=True)
            grad_scores = (probs * (grad_probs - dots)).astype(BF)
            grad_query = mxu(grad_scores, kv_ref[:keys, key_columns])
            grad_query = turn(grad_query, cos_ref[rows, :], -sin_ref[rows, :]) * (1.0 / math.sqrt(HD))
            grad_qkv[rows, columns] = grad_query.astype(BF)
            grad_kv[:keys, key_columns] += mxu(grad_scores, queries, ((0,), (0,)))
            grad_kv[:keys, value_columns] += mxu(probs.astype(BF), grads, ((0,), (0,)))
        return carry

    lax.fori_loop(0, HEADS, through_head, 0)

    for place in range(n_context):
        kv_send[place] = grad_kv[place * PBLK : (place + 1) * PBLK, :].astype(BF)
    kv_moves = [
        remote(
            kv_send.at[block_index ^ flip],
            kv_recv.at[flip],
            kv_send_sems.at[flip],
            kv_recv_sems.at[flip],
            context_peer(flip),
        )
        for flip in range(1, n_context)
    ]
    for move in kv_moves:
        move.start()
    for begin, _ in exchanges:
        begin()

    quarter = D // n_dp

    def quarter_rows(q):
        return pl.ds(pl.multiple_of(q * quarter, 128), quarter)

    def store_of(q, out_ref, width):
        slot = lax.rem(q, 2)
        return pltpu.make_async_copy(
            stage.at[slot, :, pl.ds(0, width)], out_ref.at[quarter_rows(q)], store_sems.at[slot]
        )

    def share_of_out(q, carry):
        made = mxu(attended_ref[:, quarter_rows(q)], grad_attn[...], ((0,), (0,)))

        @pl.when(q >= 2)
        def _():
            store_of(q - 2, grad_out_ref, D).wait()

        stage[lax.rem(q, 2), :, :D] = made.astype(BF)
        store_of(q, grad_out_ref, D).start()
        return carry

    kept_loads[3].wait()
    lax.fori_loop(0, n_dp, share_of_out, 0)
    for q in (n_dp - 2, n_dp - 1):
        store_of(q, grad_out_ref, D).wait()
    load_normed = pltpu.make_async_copy(normed_two_ref, grad_attn, load_sems.at[0])
    load_normed.start()

    for move in kv_moves:
        move.wait()
    own_rows = pl.ds(pl.multiple_of(block_index * PBLK, PBLK), PBLK)
    summed = grad_kv[own_rows, :]
    for flip in range(1, n_context):
        summed = summed + kv_recv[flip].astype(F32)
    pieces = [(0, PBLK, summed), (PBLK, tokens, grad_kv[prompt_len:, :])]
    for first, last, made in pieces:
        for group in range(KVH):
            turned = turn(
                made[:, group * HD : (group + 1) * HD], cos_ref[first:last, :], -sin_ref[first:last, :]
            )
            start = heads_width + group * HD
            grad_qkv[first:last, start : start + HD] = turned.astype(BF)
        grad_qkv[first:last, heads_width + kv_width :] = made[:, kv_width:].astype(BF)

    load_in.wait()

    width = weights.shape[1]

    def share_of_in(q, carry):
        made = mxu(normed_ref[:, quarter_rows(q)], grad_qkv[...], ((0,), (0,)))

        @pl.when(q >= 2)
        def _():
            store_of(q - 2, grad_in_ref, width).wait()

        stage[lax.rem(q, 2)] = made.astype(BF)
        store_of(q, grad_in_ref, width).start()
        return carry

    kept_loads[4].wait()
    lax.fori_loop(0, n_dp, share_of_in, 0)
    kept_loads[5].wait()

    def through_first(n, carry):
        rows = block_rows(n)
        grads = mxu(grad_qkv[rows, :], weights[...], ((1,), (1,)))
        by_rows, by_gain = normed_back(x_ref[rows, :].astype(F32), gains_in_ref[0:1, :], grads)
        gains_ref[0:1, :] += jnp.sum(by_gain, axis=0, keepdims=True)
        grad_x[rows, :] = (grad_mid[rows, :] + by_rows).astype(BF)
        pltpu.make_async_copy(grad_x.at[rows], grad_x_ref.at[rows], grad_x_sems.at[n]).start()
        return carry

    pass_on()
    lax.fori_loop(0, tokens // PBLK, through_first, 0)
    for q in (n_dp - 2, n_dp - 1):
        store_of(q, grad_in_ref, width).wait()
    load_normed.wait()
    lane = lax.broadcasted_iota(jnp.int32, (8, 128), 1)
    column = lax.broadcasted_iota(jnp.int32, (8, 128), 0) + EXPERTS
    place = jnp.where((lane == column) & (column < EXPERTS + 2), 1.0, 0.0).astype(BF)
    of_router = mxu(grad_attn[...], dlog_ref[...], ((0,), (0,)))
    small[...] = (of_router + mxu(gains_ref[...].astype(BF), place, ((0,), (0,)))).astype(BF)
    store_small = pltpu.make_async_copy(small, grad_small_ref, store_sems.at[0])
    store_small.start()
    finish()
    store_small.wait()
    for n in range(tokens // PBLK):
        pltpu.make_async_copy(grad_x.at[block_rows(n)], grad_x_ref.at[block_rows(n)], grad_x_sems.at[n]).wait()
    for _, end in exchanges:
        end()
    for move in homing:
        move.wait()


def backward(prompt_len, n_dp, in_vmem, in_hbm, results, riders):
    tokens = in_vmem[0].shape[0]
    width = D + 2 * KVH * HD
    n_context = prompt_len // PBLK
    key_rows = prompt_len + CONT
    quarter = D // n_dp
    vmem = pl.BlockSpec(memory_space=pltpu.VMEM)
    anywhere = pl.BlockSpec(memory_space=pl.ANY)
    part = in_hbm[-1]
    plane = results[0].shape[0]
    shape = jax.ShapeDtypeStruct
    return pl.pallas_call(
        functools.partial(
            backward_kernel, n_dp, prompt_len, len(results), [(index, flip) for _, index, flip in riders]
        ),
        in_specs=[vmem] * len(in_vmem) + [anywhere] * (len(in_hbm) + len(results) + len(riders)),
        out_specs=[anywhere] * (5 + len(results) + len(riders)),
        out_shape=[
            shape((tokens, D), BF),
            shape((D, D), BF),
            shape((D, width), BF),
            shape((D, 128), BF),
            shape((n_context,) + part.shape, BF),
        ]
        + [shape(rows.shape, BF) for rows in results]
        + [shape(picked_shape(array, index), BF) for array, index, _ in riders],
        scratch_shapes=[
            pltpu.VMEM((D, width), BF),
            pltpu.VMEM((tokens, D), F32),
            pltpu.VMEM((tokens, D), BF),
            pltpu.VMEM((2, PBLK, D), F32),
            pltpu.VMEM((tokens, width), BF),
            pltpu.VMEM((key_rows, 2 * KVH * HD), F32),
            pltpu.VMEM((n_context, PBLK, 2 * KVH * HD), BF),
            pltpu.VMEM((n_context, PBLK, 2 * KVH * HD), BF),
            pltpu.VMEM((2, quarter, width), BF),
            pltpu.SemaphoreType.DMA((5,)),
            pltpu.SemaphoreType.DMA((2,)),
            pltpu.SemaphoreType.DMA((n_context,)),
            pltpu.SemaphoreType.DMA((n_context,)),
            pltpu.SemaphoreType.DMA((len(riders),)),
            pltpu.SemaphoreType.DMA((len(riders),)),
            pltpu.SemaphoreType.DMA((3,)),
            pltpu.SemaphoreType.DMA((n_context,)),
            pltpu.VMEM((D, 128), BF),
            pltpu.VMEM((8, D), F32),
            pltpu.VMEM((len(results), SLOTS, D), BF),
            pltpu.SemaphoreType.DMA((len(results),)),
            pltpu.SemaphoreType.DMA((len(results), plane)),
            pltpu.SemaphoreType.DMA((len(results), plane)),
            *[pltpu.VMEM(array.shape, BF) for array in in_hbm[:6]],
            pltpu.SemaphoreType.DMA((6,)),
            pltpu.SemaphoreType.DMA((2,)),
            pltpu.VMEM((tokens, D), BF),
            pltpu.SemaphoreType.DMA((tokens // PBLK,)),
        ],
        compiler_params=pltpu.CompilerParams(
            vmem_limit_bytes=56 * 1024 * 1024, collective_id=4, has_side_effects=True
        ),
        name="backward",
    )(*in_vmem, *in_hbm, *results, *[array for array, _, _ in riders])


def reduce_kernel(n_dp, widths, *refs):
    count = len(widths)
    shares, refs = refs[:count], refs[count:]
    own_rank_ref, partner_rank_ref, mid_ref = refs[:3]
    rows_of, mine, refs = (refs[3:5], refs[5:7]), refs[7:10], refs[10:]
    names = HOME_RETURN[RETURN_FIRST:] + HOME_BACKWARD
    homes, refs = dict(zip(names, refs)), refs[len(names) :]
    totals, refs = refs[:count], refs[count:]
    result_ref, all_ref, part_ref, last_ref = refs[:4]
    refs = refs[4:]
    sums, core_in, first_in, second_in, z_in = (refs[n * count : (n + 1) * count] for n in range(5))
    (
        load_sems,
        core_send,
        core_recv,
        first_send,
        first_recv,
        second_send,
        second_recv,
        z_send,
        z_recv,
        out_send,
        out_recv,
        share_sends,
        share_recvs,
        pair_sems,
        held,
        to_partner,
        of_partner,
        mixed,
        mid_block,
        held_sems,
        summed,
        matrix_sums,
        piece_sems,
        sum_sems,
    ) = refs[5 * count :]
    here = plane_here()
    plane = held.shape[1]
    z_index = lax.axis_index("dp")
    greet(
        [plane_peer(here ^ flip) for flip in (1, 2, 4)] + [{"dp": z_index ^ flip} for flip in range(1, n_dp)]
    )
    chips = (0, 2, 4, 6)
    order = list(range(1, n_dp)) + [0]
    loads, core_moves = {}, {}
    for n in order:
        z_to = z_index ^ n
        for a in range(count):
            for m, chip in enumerate(chips):
                loads[n, a, m] = pltpu.make_async_copy(
                    shares[a].at[z_to, here ^ chip], sums[a].at[n, m], load_sems.at[a, n, m]
                )
                loads[n, a, m].start()
                core_moves[n, a, m] = remote(
                    shares[a].at[z_to, here ^ 1 ^ chip],
                    core_in[a].at[n, m],
                    core_send.at[a, n, m],
                    core_recv.at[a, n, m],
                    plane_peer(here ^ 1),
                )
                core_moves[n, a, m].start()

    def load_rows(side):
        copies = [
            pltpu.make_async_copy(rows_of[side][expert], held.at[expert], held_sems.at[expert])
            for expert in range(2)
        ]
        for copy in copies:
            copy.start()
        return copies

    rows_here = load_rows(1)
    gathers = [
        share_context(
            part_ref.at[:, m],
            lambda place, m=m: all_ref.at[place, :, m],
            share_sends.at[m],
            share_recvs.at[m],
        )
        for m in range(2)
    ]

    def sum_of(which):
        sources = [mine[which].at[0]] + [homes[which, flip, 1] for flip in range(1, n_dp)]
        target, place = (last_ref, 0) if which == 2 else (part_ref, which)
        sum_matrix(place, sources, summed, matrix_sums, target, piece_sems, sum_sems)

    sum_of(0)
    gathers[0][0]()

    def add(target, *others):
        total = target[...].astype(F32)
        for other in others:
            total = total + other[...].astype(F32)
        target[...] = total.astype(BF)

    first_moves, second_moves, z_moves = {}, {}, {}
    for n in order:
        toward = 2 if n % 2 == 0 else 4
        kept = 6 - toward
        for a in range(count):
            for m in range(4):
                loads[n, a, m].wait()
                core_moves[n, a, m].wait_recv()
                add(sums[a].at[n, m], core_in[a].at[n, m])
            for slot, chip in enumerate((toward, 6)):
                first_moves[n, a, slot] = remote(
                    sums[a].at[n, chip // 2],
                    first_in[a].at[n, slot],
                    first_send.at[a, n, slot],
                    first_recv.at[a, n, slot],
                    plane_peer(here ^ toward),
                )
                first_moves[n, a, slot].start()
    for copy in rows_here:
        copy.wait()
    collect_into(plane, partner_rank_ref, held, 0, to_partner, lambda rows, made: made.astype(BF))
    pair = remote(to_partner, of_partner, pair_sems.at[0], pair_sems.at[1], {"dp": z_index ^ 1})
    pair.start()
    rows_here = load_rows(0)
    sum_of(1)
    for n in order:
        toward = 2 if n % 2 == 0 else 4
        kept = 6 - toward
        for a in range(count):
            for slot, chip in enumerate((0, kept)):
                first_moves[n, a, slot].wait_recv()
                add(sums[a].at[n, chip // 2], first_in[a].at[n, slot])
            second_moves[n, a] = remote(
                sums[a].at[n, kept // 2],
                second_in[a].at[n],
                second_send.at[a, n],
                second_recv.at[a, n],
                plane_peer(here ^ kept),
            )
            second_moves[n, a].start()
    gathers[1][0]()

    def with_mid(rows, made):
        load = pltpu.make_async_copy(mid_ref.at[rows], mid_block, held_sems.at[2])
        load.start()
        load.wait()
        return mid_block[...] + made

    for copy in rows_here:
        copy.wait()
    collect_into(plane, own_rank_ref, held, 0, mixed, with_mid)
    sum_of(2)
    gathers[0][1]()
    for n in order:
        for a in range(count):
            second_moves[n, a].wait_recv()
            add(sums[a].at[n, 0], second_in[a].at[n])
            if n > 0:
                z_moves[n, a] = remote(
                    sums[a].at[n, 0], z_in[a].at[n], z_send.at[a, n], z_recv.at[a, n], {"dp": z_index ^ n}
                )
                z_moves[n, a].start()
    started = list(core_moves.values()) + list(first_moves.values())
    started += list(second_moves.values()) + list(z_moves.values())

    def pass_on(a, lane, flip, place):
        block = totals[a].at[place]
        move = remote(
            block, block, out_send.at[a, lane, place], out_recv.at[a, place], plane_peer(here ^ flip)
        )
        move.start()
        started.append(move)

    def landed(a, place):
        block = totals[a].at[place]
        remote(block, block, out_send.at[a, 0, place], out_recv.at[a, place], plane_peer(here ^ 1)).wait_recv()

    for a in range(count):
        for n in range(1, n_dp):
            z_moves[n, a].wait_recv()
        add(sums[a].at[0, 0], *[z_in[a].at[n] for n in range(1, n_dp)])
        totals[a][here] = sums[a][0, 0]
        for lane, flip in enumerate((2, 4, 1)):
            pass_on(a, lane, flip, here)
    for a in range(count):
        landed(a, here ^ 2)
        if a % 2 == 1:
            pass_on(a, 1, 4, here ^ 2)
        pass_on(a, 2, 1, here ^ 2)
        landed(a, here ^ 4)
        if a % 2 == 0:
            pass_on(a, 0, 2, here ^ 4)
        pass_on(a, 2, 1, here ^ 4)
    for a in range(count):
        landed(a, here ^ 6)
        pass_on(a, 2, 1, here ^ 6)
    gathers[1][1]()
    pair.wait()
    to_partner[...] = (mixed[...] + of_partner[...].astype(F32)).astype(BF)
    store_result = pltpu.make_async_copy(to_partner, result_ref, held_sems.at[2])
    store_result.start()
    for a in range(count):
        for flip in (1, 3, 5, 7):
            landed(a, here ^ flip)
    for move in started:
        move.wait_send()
    for _, _, finish in gathers:
        finish()
    store_result.wait()


def reduce_shares(shares, ranks, mid, slot_rows, mine, homes, n_dp, n_context):
    plane, rows = shares[0].shape[1:3]
    widths = tuple(share.shape[3] for share in shares)
    count = len(widths)
    vmem = pl.BlockSpec(memory_space=pltpu.VMEM)
    anywhere = pl.BlockSpec(memory_space=pl.ANY)
    shape = jax.ShapeDtypeStruct
    dma = pltpu.SemaphoreType.DMA

    def buffers(*lead):
        return [pltpu.VMEM(lead + (rows, width), BF) for width in widths]

    return pl.pallas_call(
        functools.partial(reduce_kernel, n_dp, widths),
        in_specs=[anywhere] * count + [vmem] * 2 + [anywhere] * (8 + len(homes)),
        out_specs=[vmem] * count + [anywhere] * 4,
        out_shape=[shape((plane, rows, width), BF) for width in widths]
        + [
            shape(mid.shape, BF),
            shape((n_context, 2, 2) + homes[0].shape, BF),
            shape((2, 2) + homes[0].shape, BF),
            shape((2, 1) + homes[0].shape, BF),
        ],
        scratch_shapes=buffers(n_dp, 4)
        + buffers(n_dp, 4)
        + buffers(n_dp, 2)
        + buffers(n_dp)
        + buffers(n_dp)
        + [
            dma((count, n_dp, 4)),
            dma((count, n_dp, 4)),
            dma((count, n_dp, 4)),
            dma((count, n_dp, 2)),
            dma((count, n_dp, 2)),
            dma((count, n_dp)),
            dma((count, n_dp)),
            dma((count, n_dp)),
            dma((count, n_dp)),
            dma((count, 3, plane)),
            dma((count, plane)),
            dma((2, 3)),
            dma((2, n_context)),
            dma((2,)),
            pltpu.VMEM((2, plane, SLOTS, D), BF),
            pltpu.VMEM(mid.shape, BF),
            pltpu.VMEM(mid.shape, BF),
            pltpu.VMEM(mid.shape, F32),
            pltpu.VMEM((PBLK, D), F32),
            dma((3,)),
            pltpu.VMEM((n_dp,) + homes[0].shape, BF),
            pltpu.VMEM((2,) + homes[0].shape, BF),
            dma((n_dp,)),
            dma((2,)),
        ],
        compiler_params=pltpu.CompilerParams(
            vmem_limit_bytes=56 * 1024 * 1024, collective_id=5, has_side_effects=True
        ),
        name="reduce_shares",
    )(*shares, *ranks, mid, *slot_rows[0], *slot_rows[1], *mine, *homes)


def finish_kernel(n_context, apart, halves, *refs):
    (first_ref, own_first_ref), out_ref = refs[:2], refs[-1]
    seconds = refs[2:-1]
    step, experts, _ = out_ref.shape
    here = lax.axis_index("context")
    group = 16
    size = group * experts
    log_group, log_experts = group.bit_length() - 1, experts.bit_length() - 1
    to = lax.broadcasted_iota(jnp.int32, (size, size), 0)
    of = lax.broadcasted_iota(jnp.int32, (size, size), 1)
    same_row = (to >> log_experts) == (of & (group - 1))
    same_expert = (to & (experts - 1)) == (of >> log_group)
    turned = jnp.where(same_row & same_expert, 1.0, 0.0).astype(BF)

    def gathered(all_ref, own_ref, place, side, at):
        return jnp.where(here == place, own_ref[(side, 0) + at], all_ref[(place, side, 0) + at])

    def by_distance(place, side, at):
        value = seconds[0][(side, 0) + at]
        for flip in range(1, n_context):
            value = jnp.where((here ^ place) == flip, seconds[flip][(side, 0) + at], value)
        return value

    width = out_ref.shape[2] // halves
    for half in range(halves):
        at_half = (half,) if halves > 1 else ()
        for start in range(0, step, group):
            at = at_half + (slice(start, start + group),)
            rows = []
            for place in range(n_context):
                for side in range(2):
                    rows.append(gathered(first_ref, own_first_ref, place, side, at))
                    if apart:
                        rows.append(by_distance(place, side, at))
                    else:
                        rows.append(gathered(seconds[0], seconds[1], place, side, at))
            made = mxu(turned, jnp.concatenate(rows, axis=0))
            out_ref[start : start + group, :, half * width : (half + 1) * width] = made.reshape(
                group, experts, width
            )


def finish_weight(which, first, own_first, seconds):
    n_context, _, _, rows, width = first.shape
    experts = n_context * 4
    step = 32 if which == 2 else 64
    apart = len(seconds) == n_context
    halves = 2 if which == 2 else 1
    rows, wide = rows // halves, width * halves
    parts = [first, own_first, *seconds]
    specs = []
    for n, part in enumerate(parts):
        lead = part.shape[:-3]
        matrix = 0 if part.shape[-3] == 1 else which
        if halves > 1:
            parts[n] = part.reshape(part.shape[:-2] + (halves, rows, width))
            block = lead + (1, halves, step, width)
            specs.append(pl.BlockSpec(block, lambda j, k=len(lead), m=matrix: (0,) * k + (m, 0, j, 0)))
        else:
            block = lead + (1, step, width)
            specs.append(pl.BlockSpec(block, lambda j, k=len(lead), m=matrix: (0,) * k + (m, j, 0)))
    return pl.pallas_call(
        functools.partial(finish_kernel, n_context, apart, halves),
        grid=(rows // step,),
        in_specs=specs,
        out_specs=pl.BlockSpec((step, experts, wide), lambda j: (j, 0, 0)),
        out_shape=jax.ShapeDtypeStruct((rows, experts, wide), F32),
        compiler_params=grant(),
        cost_estimate=pl.CostEstimate(flops=2 * 10**9, bytes_accessed=30 * 10**6, transcendentals=0),
        name="finish_weight",
    )(*parts)


def flip_permute(value, axis, size, flip):
    return lax.ppermute(value, axis, [(i, i ^ flip) for i in range(size)])


def local_paired(
    inputs,
    cotangent,
    routes,
    attn_q,
    attn_k,
    attn_v,
    attn_o,
    norm_attn,
    norm_moe,
    router,
    expert_gate,
    expert_up,
    expert_down,
):
    n_context, n_expert, n_dp = lax.axis_size("context"), lax.axis_size("expert"), lax.axis_size("dp")
    plane = n_context * n_expert
    tokens = inputs.shape[1]
    block_index = lax.axis_index("context")
    z_index = lax.axis_index("dp")
    parity = z_index % 2
    prompt_len = PBLK * n_context
    x_low = inputs[0]
    cot_low = cotangent[0]
    route_rows = routes[0]

    here = lax.axis_index("expert") * n_context + block_index
    part_rows = attn_q.shape[0] // plane

    def part_of(shard):
        return lax.dynamic_slice_in_dim(shard, here * part_rows, part_rows, 0).astype(BF)

    part_in = jnp.concatenate(
        [part_of(attn_q), part_of(attn_k), part_of(attn_v), part_of(router)]
        + [part_of(norm_attn)[:, None], part_of(norm_moe)[:, None]]
        + [jnp.zeros((part_rows, 128 - EXPERTS - 2), BF)],
        axis=1,
    )
    qkv_width = D + 2 * KVH * HD
    weights = (expert_gate, expert_up, expert_down)
    own_ranks, own_rows, own_columns, partner_rows, partner_columns, whole_in, w_out, *weight_halves = (
        gather_parts(route_rows.T, part_in, part_of(attn_o), weights, cot_low, n_dp, n_context, plane)
    )
    gate_piece = weight_halves.pop()
    partner_cot = [weight_halves.pop()]
    whole_in = whole_in.reshape(-1, part_in.shape[1])
    w_out = w_out.reshape(-1, D)
    pieces = {(which, 0, i): (weight_halves[which], (0, i)) for which in range(3) for i in range(2)}
    pieces[0, 2, 0] = (gate_piece, None)

    def riding(names):
        return [
            (weight_halves[which], (flip % 2, i), flip) for which, flip, i in names
        ]

    def pieces_of(expert):
        return [pieces[which, flip, expert] for which in range(3) for flip in range(n_dp)]

    positions = jnp.concatenate(
        [
            block_index * PBLK + jnp.arange(PBLK, dtype=jnp.int32),
            prompt_len + jnp.arange(CONT, dtype=jnp.int32),
        ]
    )
    angles = angle_table(positions)
    cos_half, sin_half = jnp.cos(angles), jnp.sin(angles)
    cosine = jnp.concatenate([cos_half, cos_half], axis=1)
    sine = jnp.concatenate([-sin_half, sin_half], axis=1)
    gains, logs, logits, normed_one, qkv, keys_values, attended, normed_two, mid_rows, cot_half, *moved = (
        front(prompt_len, n_dp, x_low, cosine, sine, whole_in, w_out, cot_low, riding(RIDE_FRONT))
    )
    partner_cot.append(cot_half)
    pieces.update({name: (piece, None) for name, piece in zip(RIDE_FRONT, moved)})

    gates, gates_here, landed, staged, arrived = dispatch_rows(
        normed_two, cot_low, partner_cot, own_rows, partner_rows, logits, own_ranks, riding(RIDE_DISPATCH), n_dp
    )
    pieces.update({name: (piece, None) for name, piece in zip(RIDE_DISPATCH, arrived)})

    def slots_of(arrays):
        flat = [array.reshape(plane * SLOTS, D) for array in arrays]
        return (flat[0], flat[3]), (flat[1], flat[2])

    parted = lambda arrays: [array.reshape(plane, SLOTS, D) for array in arrays]
    rows, cots = slots_of(landed)
    first, first_dots, first_shares, landed, arrived = run_expert(
        "first_expert", 0, 6, rows, cots, gates_here, pieces_of(0), staged, riding(RIDE_FIRST)
    )
    pieces.update({name: (piece, None) for name, piece in zip(RIDE_FIRST, arrived)})
    rows, cots = slots_of(landed)

    def homing(names, *shares):
        return [(shares[i][which], flip, flip) for which, flip, i in names]

    second, second_dots, second_shares, early, homes = run_expert(
        "second_expert",
        1,
        7,
        rows,
        cots,
        gates_here,
        pieces_of(1),
        parted(first)[1:4],
        homing(HOME_SECOND, first_shares),
    )

    second = parted(second)
    grad_rows, grad_logits, part_first, late, homes_second = return_rows(
        own_columns,
        partner_columns,
        first_dots,
        second_dots,
        own_ranks,
        gates,
        early[1:3],
        second[2:4],
        [parted(first)[0], second[1]],
        homing(HOME_RETURN, first_shares, second_shares),
        HOME_RETURN,
        first_shares,
        homes,
        n_dp,
    )
    grad_inputs, grad_wout, grad_wqkv, grad_small, all_first, *homes = backward(
        prompt_len,
        n_dp,
        (grad_logits, gains, logs, cosine, sine),
        (
            cot_low,
            qkv,
            keys_values,
            attended,
            normed_one,
            x_low,
            mid_rows,
            grad_rows,
            w_out,
            whole_in,
            normed_two,
            part_first,
        ),
        second[0:1],
        homing(HOME_BACKWARD, first_shares, second_shares),
    )
    last, homes = homes[0], list(homes_second[RETURN_FIRST:]) + list(homes[1:])
    out_own, out_partner = [late[0], last], [early[0], late[1]]

    parts = lambda share: share.reshape(n_dp, plane, -1, share.shape[1])
    total_qkv, total_out, total_small, result, all_second, part_second, own = reduce_shares(
        [parts(grad_wqkv), parts(grad_wout), parts(grad_small)],
        (own_columns, partner_columns),
        mid_rows,
        (out_own, out_partner),
        second_shares,
        homes,
        n_dp,
        n_context,
    )
    across = flip_permute(own, "context", n_context, 2)
    beside = flip_permute(own, "context", n_context, 1)
    grad_gate, grad_up = (
        finish_weight(which, all_first, part_first, (all_second, part_second)) for which in range(2)
    )
    across, beside, grad_gate, grad_up = lax.optimization_barrier((across, beside, grad_gate, grad_up))
    apart = (own, beside, across, flip_permute(across, "context", n_context, 1))
    total_qkv = total_qkv.reshape(-1, qkv_width).astype(F32)
    total_out = total_out.reshape(-1, D).astype(F32)
    total_small = total_small.reshape(-1, 128).astype(F32)
    return (
        result[None],
        grad_inputs[None],
        total_qkv[:, :D],
        total_qkv[:, D : D + KVH * HD],
        total_qkv[:, D + KVH * HD :],
        total_out,
        total_small[:, EXPERTS],
        total_small[:, EXPERTS + 1],
        total_small[:, :EXPERTS],
        grad_gate,
        grad_up,
        finish_weight(2, all_first, part_first, apart),
    )


def paired_plan(mesh):
    n_expert, n_context, n_dp = mesh.shape["expert"], mesh.shape["context"], mesh.shape["dp"]
    owners = 2 * n_expert * n_context
    small_axes = all(size & (size - 1) == 0 for size in (n_expert, n_context, n_dp))
    return small_axes and n_dp % 2 == 0 and EXPERTS == 2 * owners


def solution(mesh):
    in_specs = (
        P(("expert", "dp"), "context", None),
        P(("expert", "dp"), "context", None),
        P(("expert", "dp"), "context", None),
        P("dp", None),
        P("dp", None),
        P("dp", None),
        P("dp", None),
        P("dp"),
        P("dp"),
        P("dp", None),
        P("dp", "expert", None),
        P("dp", "expert", None),
        P("dp", "expert", None),
    )
    out_specs = (
        P(("expert", "dp"), "context", None),
        P(("expert", "dp"), "context", None),
        P("dp", None),
        P("dp", None),
        P("dp", None),
        P("dp", None),
        P("dp"),
        P("dp"),
        P("dp", None),
        P("dp", "expert", None),
        P("dp", "expert", None),
        P("dp", "expert", None),
    )
    chosen = local_paired if paired_plan(mesh) else local
    return jax.shard_map(chosen, mesh=mesh, in_specs=in_specs, out_specs=out_specs, check_vma=False)
```
